32 devices in a mesh: dp: 4 (over y, core), wide: 8 (over z, x).
Axes of the slice: x: 2, y: 2, z: 4, core: 2. Of those that a mesh axis runs over, the one named last changes fastest.
Arguments:
- images: bfloat16 [64, 16, 16, 1024], P(('dp', 'wide')), may hold values from -6 to 6
- pixel_mask: int32 [64, 16, 16], P(('dp', 'wide')), may hold values from 0 to 1, as said below
- cotangent: bfloat16 [64, 8, 8, 1536], P(('dp', 'wide')), may hold values from -6 to 6
- reduce_one: bfloat16 [1024, 384], P('wide'), may hold values from -0.1875 to 0.1875
- spatial_one: bfloat16 [3, 3, 384, 384], P(None, None, 'wide'), may hold values from -0.109375 to 0.109375
- expand_one: bfloat16 [384, 1536], P('wide'), may hold values from -0.3125 to 0.3125
- project_one: bfloat16 [1024, 1536], P('wide'), may hold values from -0.1875 to 0.1875
- gains_one: bfloat16 [3840], P('wide'), may hold values from 0.5 to 1.5
- shifts_one: bfloat16 [3840], P('wide'), may hold values from -1.5 to 1.5
- reduce_two: bfloat16 [1536, 384], P('wide'), may hold values from -0.15625 to 0.15625
- spatial_two: bfloat16 [3, 3, 384, 384], P(None, None, 'wide'), may hold values from -0.109375 to 0.109375
- expand_two: bfloat16 [384, 1536], P('wide'), may hold values from -0.3125 to 0.3125
- gains_two: bfloat16 [2304], P('wide'), may hold values from 0.5 to 1.5
- shifts_two: bfloat16 [2304], P('wide'), may hold values from -1.5 to 1.5
Outputs:
- activations: bfloat16 [64, 8, 8, 1536], P(('dp', 'wide'))
- grad_images: bfloat16 [64, 16, 16, 1024], P(('dp', 'wide'))
- grad_reduce_one: float32 [1024, 384], P('wide')
- grad_spatial_one: float32 [3, 3, 384, 384], P(None, None, 'wide')
- grad_expand_one: float32 [384, 1536], P('wide')
- grad_project_one: float32 [1024, 1536], P('wide')
- grad_gains_one: float32 [3840], P('wide')
- grad_shifts_one: float32 [3840], P('wide')
- grad_reduce_two: float32 [1536, 384], P('wide')
- grad_spatial_two: float32 [3, 3, 384, 384], P(None, None, 'wide')
- grad_expand_two: float32 [384, 1536], P('wide')
- grad_gains_two: float32 [2304], P('wide')
- grad_shifts_two: float32 [2304], P('wide')
The draws below stay inside these ranges and needn't reach their ends.
Inputs may be any that keep to these rules, and one draw needn't show every extreme that they name: `pixel_mask`: 1 marks a pixel that counts in the norms' statistics; the share of such pixels rises with the image's index.
All inputs are finite; a program needn't handle non-finite values.
Results may differ from the reference program's by a relative error of at most 0.023.
Values may be sent and summed in bfloat16 or wider, within the bound.
A program may use at most 128 MiB of HBM per device.

```python
import jax
import jax.numpy as jnp
from jax import lax

C_IN = 1024
C_MID = 384
C_OUT = 1536
H_IN = 16
IMAGES = 64
H_OUT = 8
GAINS_ONE = 3840
GAINS_TWO = 2304


def draw_pixel_mask(key, part):
    key = jax.random.fold_in(key, 11)
    rolls = jax.random.randint(key, (IMAGES, H_IN, H_IN), 0, 1000, dtype=jnp.int32)
    image_index = jnp.arange(IMAGES, dtype=jnp.int32)
    threshold = 150 + 750 * image_index // max(IMAGES - 1, 1)
    return (rolls < threshold[:, None, None]).astype(jnp.int32)


def level_of(stream_key, extent, shards, smallest, high):
    def one(position, blocks):
        draws = jax.random.uniform(jax.random.fold_in(jax.random.fold_in(stream_key, 6), position), (blocks,), jnp.float32, smallest / len(shards), high / len(shards))
        return jnp.repeat(jnp.exp(draws), extent[position] // blocks).reshape((-1,) + (1,) * (len(extent) - position - 1))

    level = one(*shards[0])
    for cut in shards[1:]:
        level = level * one(*cut)
    return level


def noise(own_key, shape, scale, reach, split=(), held_as=jnp.bfloat16):
    array = scale * jax.random.normal(own_key, shape, jnp.float32)
    if split:
        array = array * level_of(own_key, shape, split, -0.22, 0.18)
    return jnp.clip(array, -reach, reach).astype(held_as)


def setup_inputs(seed: int = 0) -> dict:
    key_list = jax.random.split(jax.random.key(seed), 15)
    return {
        "images": noise(key_list[0], (IMAGES, H_IN, H_IN, C_IN), 1.0, 6.0, ((0, 32),)),
        "pixel_mask": draw_pixel_mask(jax.random.fold_in(key_list[14], 71), 0),
        "cotangent": noise(key_list[2], (IMAGES, H_OUT, H_OUT, C_OUT), 1.0, 6.0, ((0, 32),)),
        "reduce_one": noise(key_list[3], (C_IN, C_MID), C_IN ** -0.5, 0.1875, ((0, 8),)),
        "spatial_one": noise(key_list[4], (3, 3, C_MID, C_MID), (9 * C_MID) ** -0.5, 0.109375, ((2, 8),)),
        "expand_one": noise(key_list[5], (C_MID, C_OUT), C_MID ** -0.5, 0.3125, ((0, 8),)),
        "project_one": noise(key_list[6], (C_IN, C_OUT), C_IN ** -0.5, 0.1875, ((0, 8),)),
        "gains_one": jnp.clip(1.0 + 0.1 * jax.random.normal(key_list[7], (GAINS_ONE,), jnp.float32), 0.5, 1.5).astype(jnp.bfloat16),
        "shifts_one": noise(key_list[8], (GAINS_ONE,), 0.3, 1.5, ((0, 8),)),
        "reduce_two": noise(key_list[9], (C_OUT, C_MID), C_OUT ** -0.5, 0.15625, ((0, 8),)),
        "spatial_two": noise(key_list[10], (3, 3, C_MID, C_MID), (9 * C_MID) ** -0.5, 0.109375, ((2, 8),)),
        "expand_two": noise(key_list[11], (C_MID, C_OUT), C_MID ** -0.5, 0.3125, ((0, 8),)),
        "gains_two": jnp.clip(1.0 + 0.1 * jax.random.normal(key_list[12], (GAINS_TWO,), jnp.float32), 0.5, 1.5).astype(jnp.bfloat16),
        "shifts_two": noise(key_list[13], (GAINS_TWO,), 0.3, 1.5, ((0, 8),)),
    }


NORM_EPS = 1e-05
HIGHEST_MODE = lax.Precision.HIGHEST

@jax.custom_vjp
def low(v):
    return lax.optimization_barrier(v.astype(jnp.bfloat16)).astype(jnp.float32)

@jax.custom_vjp
def low_back(v):
    return v

def low_keep(v):
    return (low(v), None)

def low_pass(kept, grad):
    return (grad,)

def back_keep(v):
    return (v, None)

def back_low(kept, grad):
    return (low(grad),)
low.defvjp(low_keep, low_pass)
low_back.defvjp(back_keep, back_low)

def pixel_product(source, kernel):
    return jnp.einsum('bhwc,co->bhwo', source, kernel, precision=HIGHEST_MODE)

def conv_spatial(source, kernel, stride):
    return lax.conv_general_dilated(source, kernel, (stride, stride), ((1, 1), (1, 1)), dimension_numbers=('NHWC', 'HWIO', 'NHWC'), precision=HIGHEST_MODE)

def normalize(pre, valid, count, gain, shift):
    mean_val = lax.optimization_barrier(jnp.sum(pre * valid, axis=(0, 1, 2))) / count
    variance = lax.optimization_barrier(jnp.sum(pre * pre * valid, axis=(0, 1, 2))) / count - mean_val * mean_val
    return gain * ((pre - mean_val) * lax.rsqrt(variance + NORM_EPS)) + shift

def forward(valid_hi, valid_lo, count_hi, count_lo, images, reduce_one, spatial_one, expand_one, project_one, gains_one, shifts_one, reduce_two, spatial_two, expand_two, gains_two, shifts_two):
    mid_a = C_MID
    mid_b = 2 * C_MID
    out_a = 2 * C_MID + C_OUT
    out_b = 2 * C_MID + 2 * C_OUT
    pre_one = low_back(pixel_product(images, reduce_one))
    act_one = low(jax.nn.silu(normalize(pre_one, valid_hi, count_hi, gains_one[:mid_a], shifts_one[:mid_a])))
    pre_two = low_back(conv_spatial(act_one, spatial_one, 2))
    act_two = low(jax.nn.silu(normalize(pre_two, valid_lo, count_lo, gains_one[mid_a:mid_b], shifts_one[mid_a:mid_b])))
    pre_three = low_back(pixel_product(act_two, expand_one))
    y_three = normalize(pre_three, valid_lo, count_lo, gains_one[mid_b:out_a], shifts_one[mid_b:out_a])
    pre_proj = low_back(pixel_product(images[:, ::2, ::2], project_one))
    y_proj = normalize(pre_proj, valid_lo, count_lo, gains_one[out_a:out_b], shifts_one[out_a:out_b])
    hidden = jax.nn.silu(y_three + y_proj)
    hidden_low = low(hidden)
    pre_four = low_back(pixel_product(hidden_low, reduce_two))
    act_four = low(jax.nn.silu(normalize(pre_four, valid_lo, count_lo, gains_two[:mid_a], shifts_two[:mid_a])))
    pre_five = low_back(conv_spatial(act_four, spatial_two, 1))
    act_five = low(jax.nn.silu(normalize(pre_five, valid_lo, count_lo, gains_two[mid_a:mid_b], shifts_two[mid_a:mid_b])))
    pre_six = low_back(pixel_product(act_five, expand_two))
    y_six = normalize(pre_six, valid_lo, count_lo, gains_two[mid_b:out_a], shifts_two[mid_b:out_a])
    return jax.nn.silu(y_six + hidden)

def reference(images, pixel_mask, cotangent, reduce_one, spatial_one, expand_one, project_one, gains_one, shifts_one, reduce_two, spatial_two, expand_two, gains_two, shifts_two):
    valid_hi = pixel_mask.astype(jnp.float32)[..., None]
    valid_lo = valid_hi[:, ::2, ::2]
    count_hi = jnp.maximum(jnp.sum(valid_hi), jnp.float32(1.0))
    count_lo = jnp.maximum(jnp.sum(valid_lo), jnp.float32(1.0))
    inputs = tuple((item.astype(jnp.float32) for item in (images, reduce_one, spatial_one, expand_one, project_one, gains_one, shifts_one, reduce_two, spatial_two, expand_two, gains_two, shifts_two)))

    def wrapped(*values):
        return forward(valid_hi, valid_lo, count_hi, count_lo, *values)
    output, pullback = jax.vjp(wrapped, *inputs)
    grads = pullback(cotangent.astype(jnp.float32))
    return (output.astype(jnp.bfloat16), grads[0].astype(jnp.bfloat16), grads[1], grads[2], grads[3], grads[4], grads[5], grads[6], grads[7], grads[8], grads[9], grads[10], grads[11])
```

```python
import functools
import types

import jax
import jax.numpy as jnp
from jax import lax
from jax.experimental import pallas as pl
from jax.experimental.pallas import tpu as pltpu
from jax.sharding import PartitionSpec as P

NORM_EPS = 1e-05


def pixel_product(source, kernel):
    return jnp.einsum("bhwc,co->bhwo", source, kernel, preferred_element_type=jnp.float32)


def weight_grad(source, upstream):
    return jnp.einsum("bhwc,bhwo->co", source, upstream, preferred_element_type=jnp.float32)


def input_grad(upstream, kernel):
    return jnp.einsum("bhwo,co->bhwc", upstream, kernel, preferred_element_type=jnp.float32)


def conv_spatial(source, kernel, stride):
    out_h = source.shape[1] // stride
    out_w = source.shape[2] // stride
    padded = jnp.pad(source, ((0, 0), (1, 1), (1, 1), (0, 0)))
    summed = jnp.zeros((source.shape[0], out_h, out_w, kernel.shape[3]), jnp.float32)
    for row_off in range(3):
        for col_off in range(3):
            window = padded[
                :,
                row_off : row_off + stride * out_h : stride,
                col_off : col_off + stride * out_w : stride,
            ]
            summed = summed + pixel_product(window, kernel[row_off, col_off])
    return summed


def conv_back(source, upstream, kernel, stride):
    out_h = upstream.shape[1]
    out_w = upstream.shape[2]
    padded = jnp.pad(source, ((0, 0), (1, 1), (1, 1), (0, 0)))
    grad_src = jnp.zeros(padded.shape, jnp.float32)
    kernel_rows = []
    for row_off in range(3):
        for col_off in range(3):
            window = padded[
                :,
                row_off : row_off + stride * out_h : stride,
                col_off : col_off + stride * out_w : stride,
            ]
            kernel_rows.append(weight_grad(window, upstream))
            grad_src = grad_src.at[
                :,
                row_off : row_off + stride * out_h : stride,
                col_off : col_off + stride * out_w : stride,
            ].add(input_grad(upstream, kernel[row_off, col_off]))
    kernel_grad = jnp.stack(kernel_rows).reshape(kernel.shape)
    return (kernel_grad, grad_src[:, 1:-1, 1:-1])


def norm_forward(pre, valid, count, gain, shift):
    moments = lax.psum(
        (jnp.sum(pre * valid, axis=(0, 1, 2)), jnp.sum(pre * pre * valid, axis=(0, 1, 2))),
        ("dp", "wide"),
    )
    mean_val = moments[0] / count
    variance = moments[1] / count - mean_val * mean_val
    scaler = lax.rsqrt(variance + NORM_EPS)
    normed = (pre - mean_val) * scaler
    return (gain * normed + shift, (mean_val, scaler))


def norm_backward(upstream, pre, valid, count, gain, stats):
    mean_val, scaler = stats
    sums = lax.psum(
        (jnp.sum(upstream, axis=(0, 1, 2)), jnp.sum(upstream * pre, axis=(0, 1, 2))), ("dp", "wide")
    )
    first_sum, second_sum = sums
    centred = second_sum - mean_val * first_sum
    grad_gain = scaler * centred
    grad_var = -0.5 * gain * centred * scaler * scaler * scaler
    grad_mean = -gain * scaler * first_sum - 2.0 * mean_val * grad_var
    grad_pre = gain * scaler * upstream + valid / count * (grad_mean + 2.0 * pre * grad_var)
    return (grad_pre, grad_gain, first_sum)


def silu_grad(pre_act, upstream):
    sigma = jax.nn.sigmoid(pre_act)
    return upstream * sigma * (1.0 + pre_act * (1.0 - sigma))


def own_slice(whole, local_len):
    start = lax.axis_index("wide") * local_len
    return lax.dynamic_slice_in_dim(whole, start, local_len, 0)


def shards(
    images,
    pixel_mask,
    cotangent,
    reduce_one,
    spatial_one,
    expand_one,
    project_one,
    gains_one,
    shifts_one,
    reduce_two,
    spatial_two,
    expand_two,
    gains_two,
    shifts_two,
):
    valid_hi = pixel_mask.astype(jnp.float32)[..., None]
    valid_lo = valid_hi[:, ::2, ::2]
    counts = lax.psum((jnp.sum(valid_hi), jnp.sum(valid_lo)), ("dp", "wide"))
    count_hi = jnp.maximum(counts[0], 1.0)
    count_lo = jnp.maximum(counts[1], 1.0)
    first_full = (
        lax.all_gather(reduce_one, "wide", axis=0, tiled=True),
        lax.all_gather(spatial_one, "wide", axis=2, tiled=True),
        lax.all_gather(expand_one, "wide", axis=0, tiled=True),
        lax.all_gather(project_one, "wide", axis=0, tiled=True),
        lax.all_gather(gains_one, "wide", axis=0, tiled=True),
        lax.all_gather(shifts_one, "wide", axis=0, tiled=True),
    )
    red_a, spa_a, exp_a, proj_a, gain_a, shift_a = first_full
    mid_a = red_a.shape[1]
    mid_b = 2 * mid_a
    out_a = mid_b + exp_a.shape[1]
    out_b = out_a + exp_a.shape[1]
    gain_af = gain_a.astype(jnp.float32)
    shift_af = shift_a.astype(jnp.float32)
    pre_one = pixel_product(images, red_a)
    y_one, stat_one = norm_forward(pre_one, valid_hi, count_hi, gain_af[:mid_a], shift_af[:mid_a])
    act_one = jax.nn.silu(y_one).astype(jnp.bfloat16)
    pre_two = conv_spatial(act_one, spa_a, 2)
    y_two, stat_two = norm_forward(
        pre_two, valid_lo, count_lo, gain_af[mid_a:mid_b], shift_af[mid_a:mid_b]
    )
    act_two = jax.nn.silu(y_two).astype(jnp.bfloat16)
    pre_three = pixel_product(act_two, exp_a)
    y_three, stat_three = norm_forward(
        pre_three, valid_lo, count_lo, gain_af[mid_b:out_a], shift_af[mid_b:out_a]
    )
    sampled = images[:, ::2, ::2]
    pre_proj = pixel_product(sampled, proj_a)
    y_proj, stat_proj = norm_forward(
        pre_proj, valid_lo, count_lo, gain_af[out_a:out_b], shift_af[out_a:out_b]
    )
    sum_one = y_three + y_proj
    hidden = jax.nn.silu(sum_one)
    hidden_low = hidden.astype(jnp.bfloat16)
    second_full = (
        lax.all_gather(reduce_two, "wide", axis=0, tiled=True),
        lax.all_gather(spatial_two, "wide", axis=2, tiled=True),
        lax.all_gather(expand_two, "wide", axis=0, tiled=True),
        lax.all_gather(gains_two, "wide", axis=0, tiled=True),
        lax.all_gather(shifts_two, "wide", axis=0, tiled=True),
    )
    red_b, spa_b, exp_b, gain_b, shift_b = second_full
    gain_bf = gain_b.astype(jnp.float32)
    shift_bf = shift_b.astype(jnp.float32)
    pre_four = pixel_product(hidden_low, red_b)
    y_four, stat_four = norm_forward(
        pre_four, valid_lo, count_lo, gain_bf[:mid_a], shift_bf[:mid_a]
    )
    act_four = jax.nn.silu(y_four).astype(jnp.bfloat16)
    pre_five = conv_spatial(act_four, spa_b, 1)
    y_five, stat_five = norm_forward(
        pre_five, valid_lo, count_lo, gain_bf[mid_a:mid_b], shift_bf[mid_a:mid_b]
    )
    act_five = jax.nn.silu(y_five).astype(jnp.bfloat16)
    pre_six = pixel_product(act_five, exp_b)
    y_six, stat_six = norm_forward(
        pre_six, valid_lo, count_lo, gain_bf[mid_b:out_a], shift_bf[mid_b:out_a]
    )
    sum_two = y_six + hidden
    activations = jax.nn.silu(sum_two).astype(jnp.bfloat16)
    back_two = (
        lax.all_gather(reduce_two, "wide", axis=0, tiled=True),
        lax.all_gather(spatial_two, "wide", axis=2, tiled=True),
        lax.all_gather(expand_two, "wide", axis=0, tiled=True),
        lax.all_gather(gains_two, "wide", axis=0, tiled=True),
    )
    red_b, spa_b, exp_b, gain_b = back_two
    gain_bf = gain_b.astype(jnp.float32)
    upstream = cotangent.astype(jnp.float32)
    grad_sum_two = silu_grad(sum_two, upstream)
    grad_pre6, gain_g6, shift_g6 = norm_backward(
        grad_sum_two, pre_six, valid_lo, count_lo, gain_bf[mid_b:out_a], stat_six
    )
    low_six = grad_pre6.astype(jnp.bfloat16)
    grad_exp_b = weight_grad(act_five, low_six)
    grad_act5 = input_grad(low_six, exp_b)
    grad_pre5, gain_g5, shift_g5 = norm_backward(
        silu_grad(y_five, grad_act5), pre_five, valid_lo, count_lo, gain_bf[mid_a:mid_b], stat_five
    )
    low_five = grad_pre5.astype(jnp.bfloat16)
    grad_spa_b, grad_act4 = conv_back(act_four, low_five, spa_b, 1)
    grad_pre4, gain_g4, shift_g4 = norm_backward(
        silu_grad(y_four, grad_act4), pre_four, valid_lo, count_lo, gain_bf[:mid_a], stat_four
    )
    low_four = grad_pre4.astype(jnp.bfloat16)
    grad_red_b = weight_grad(hidden_low, low_four)
    grad_hidden = grad_sum_two + input_grad(low_four, red_b)
    owned_two = (
        lax.psum_scatter(
            grad_red_b.astype(jnp.bfloat16), "wide", scatter_dimension=0, tiled=True
        ).astype(jnp.float32),
        lax.psum_scatter(
            grad_spa_b.astype(jnp.bfloat16), "wide", scatter_dimension=2, tiled=True
        ).astype(jnp.float32),
        lax.psum_scatter(
            grad_exp_b.astype(jnp.bfloat16), "wide", scatter_dimension=0, tiled=True
        ).astype(jnp.float32),
    )
    owned_two = (
        lax.psum(owned_two[0].astype(jnp.bfloat16), "dp").astype(jnp.float32),
        lax.psum(owned_two[1].astype(jnp.bfloat16), "dp").astype(jnp.float32),
        lax.psum(owned_two[2].astype(jnp.bfloat16), "dp").astype(jnp.float32),
    )
    back_one = (
        lax.all_gather(reduce_one, "wide", axis=0, tiled=True),
        lax.all_gather(spatial_one, "wide", axis=2, tiled=True),
        lax.all_gather(expand_one, "wide", axis=0, tiled=True),
        lax.all_gather(project_one, "wide", axis=0, tiled=True),
        lax.all_gather(gains_one, "wide", axis=0, tiled=True),
    )
    red_a, spa_a, exp_a, proj_a, gain_a = back_one
    gain_af = gain_a.astype(jnp.float32)
    grad_sum_one = silu_grad(sum_one, grad_hidden)
    grad_pre3, gain_g3, shift_g3 = norm_backward(
        grad_sum_one, pre_three, valid_lo, count_lo, gain_af[mid_b:out_a], stat_three
    )
    grad_prep, gain_gp, shift_gp = norm_backward(
        grad_sum_one, pre_proj, valid_lo, count_lo, gain_af[out_a:out_b], stat_proj
    )
    low_three = grad_pre3.astype(jnp.bfloat16)
    low_proj = grad_prep.astype(jnp.bfloat16)
    grad_exp_a = weight_grad(act_two, low_three)
    grad_act2 = input_grad(low_three, exp_a)
    grad_proj_a = weight_grad(sampled, low_proj)
    grad_sampled = input_grad(low_proj, proj_a)
    grad_pre2, gain_g2, shift_g2 = norm_backward(
        silu_grad(y_two, grad_act2), pre_two, valid_lo, count_lo, gain_af[mid_a:mid_b], stat_two
    )
    low_two = grad_pre2.astype(jnp.bfloat16)
    grad_spa_a, grad_act1 = conv_back(act_one, low_two, spa_a, 2)
    grad_pre1, gain_g1, shift_g1 = norm_backward(
        silu_grad(y_one, grad_act1), pre_one, valid_hi, count_hi, gain_af[:mid_a], stat_one
    )
    low_one = grad_pre1.astype(jnp.bfloat16)
    grad_red_a = weight_grad(images, low_one)
    grad_input = input_grad(low_one, red_a)
    grad_input = grad_input.at[:, ::2, ::2].add(grad_sampled)
    grad_images = grad_input.astype(jnp.bfloat16)
    owned_one = (
        lax.psum_scatter(
            grad_red_a.astype(jnp.bfloat16), "wide", scatter_dimension=0, tiled=True
        ).astype(jnp.float32),
        lax.psum_scatter(
            grad_spa_a.astype(jnp.bfloat16), "wide", scatter_dimension=2, tiled=True
        ).astype(jnp.float32),
        lax.psum_scatter(
            grad_exp_a.astype(jnp.bfloat16), "wide", scatter_dimension=0, tiled=True
        ).astype(jnp.float32),
        lax.psum_scatter(
            grad_proj_a.astype(jnp.bfloat16), "wide", scatter_dimension=0, tiled=True
        ).astype(jnp.float32),
    )
    owned_one = (
        lax.psum(owned_one[0].astype(jnp.bfloat16), "dp").astype(jnp.float32),
        lax.psum(owned_one[1].astype(jnp.bfloat16), "dp").astype(jnp.float32),
        lax.psum(owned_one[2].astype(jnp.bfloat16), "dp").astype(jnp.float32),
        lax.psum(owned_one[3].astype(jnp.bfloat16), "dp").astype(jnp.float32),
    )
    gains_grad_a = jnp.concatenate([gain_g1, gain_g2, gain_g3, gain_gp])
    shifts_grad_a = jnp.concatenate([shift_g1, shift_g2, shift_g3, shift_gp])
    gains_grad_b = jnp.concatenate([gain_g4, gain_g5, gain_g6])
    shifts_grad_b = jnp.concatenate([shift_g4, shift_g5, shift_g6])
    local_a = gains_one.shape[0]
    local_b = gains_two.shape[0]
    return (
        activations,
        grad_images,
        owned_one[0],
        owned_one[1],
        owned_one[2],
        owned_one[3],
        own_slice(gains_grad_a, local_a),
        own_slice(shifts_grad_a, local_a),
        owned_two[0],
        owned_two[1],
        owned_two[2],
        own_slice(gains_grad_b, local_b),
        own_slice(shifts_grad_b, local_b),
    )


MESH = pl.DeviceIdType.MESH
F32 = jnp.float32
BF16 = jnp.bfloat16
ALL = slice(None)
NAMES = R1, S1, E1, P1, R2, S2, E2 = range(7)
ROW, TAP, COL = range(3)
KINDS = (ROW, TAP, COL, ROW, ROW, TAP, COL)
GATHER_X_FIRST = (S1, R2, E2)
REDUCE_Y_FIRST = (S2, R1)
NORMS = N1, N2, N3, NP, N4, N5, N6 = range(7)


def nn(left, right):
    return jnp.dot(left, right, preferred_element_type=F32)


def nt(left, right):
    return lax.dot_general(left, right, (((1,), (1,)), ((), ())), preferred_element_type=F32)


def tn(left, right):
    return lax.dot_general(left, right, (((0,), (0,)), ((), ())), preferred_element_type=F32)


def half_of(kind, buf, z, x, h):
    if kind == ROW:
        return buf.at[z, x, h]
    if kind == TAP:
        return buf.at[pl.ds(4 * h, 5), z, x]
    cols = buf.shape[-1] // 2
    return buf.at[z, x, :, pl.ds(pl.multiple_of(h * cols, 128), cols)]


def thin_of(kind, buf, z, x, h):
    if kind == TAP:
        return buf.at[pl.ds(5 * h, 4), z, x]
    return half_of(kind, buf, z, x, h)


def full_of(kind, buf, z, x):
    if kind == TAP:
        return buf.at[:, z, x]
    return buf.at[z, x]


def shard_half(kind, buf, h):
    if kind == ROW:
        return buf.at[h]
    if kind == TAP:
        return buf.at[pl.ds(4 * h, 5)]
    cols = buf.shape[-1] // 2
    return buf.at[:, pl.ds(pl.multiple_of(h * cols, 128), cols)]


def shard_thin(kind, buf, h):
    if kind == TAP:
        return buf.at[pl.ds(5 * h, 4)]
    return shard_half(kind, buf, h)


def whole_shape(kind, shard):
    if kind == TAP:
        return (shard[0], 4, 2) + tuple(shard[1:])
    return (4, 2) + tuple(shard)


def half_shape(kind, shard):
    if kind == ROW:
        return tuple(shard[1:])
    if kind == TAP:
        return (5,) + tuple(shard[1:])
    return (shard[0], shard[1] // 2)


class Links:
    def __init__(self, send_sems, recv_sems, core, base):
        self.send_sems, self.recv_sems = send_sems, recv_sems
        self.dp, self.wide = lax.axis_index("dp"), lax.axis_index("wide")
        self.core = core
        self.y, self.z, self.x = self.dp // 2, self.wide // 2, self.wide % 2
        self.next_send = base

    def device(self, dy=0, dz=0, dx=0, other=False):
        core = 1 - self.core if other else self.core
        y = (self.y + dy) % 2
        z, x = (self.z + dz) % 4, (self.x + dx) % 2
        return {"dp": y * 2 + core, "wide": z * 2 + x}

    def copy(self, src, dst, slot, **to):
        sem = self.send_sems.at[self.next_send]
        self.next_send += 1
        return pltpu.make_async_remote_copy(
            src_ref=src, dst_ref=dst, send_sem=sem, recv_sem=self.recv_sems.at[slot],
            device_id=self.device(**to), device_id_type=MESH)

    def send(self, src, dst, slot, **to):
        made = self.copy(src, dst, slot, **to)
        made.start()
        return made

    def arrived(self, dst, slot):
        pltpu.make_async_remote_copy(
            src_ref=dst, dst_ref=dst, send_sem=self.send_sems.at[0], recv_sem=self.recv_sems.at[slot],
            device_id=self.device(other=True), device_id_type=MESH).wait_recv()


def slot_table(**counts):
    table, at = types.SimpleNamespace(), 0
    for key, count in counts.items():
        setattr(table, key, at)
        at += count
    table.total = at
    return table


T = slot_table(raw=1, mask=1, cot=1, pix=1, prep=1, xc2=1, act2=1, hlow=1, xc5=1, act5=1, low6=1, low5=1, low4=1, low3=1, lowp=1,
               low2=1, low1=1, gsamp=1, out_act=1, out_norm=1, out_gimg=1, out=7, hand=7, first=8, gather=35, reduce=42, norm_in=8, sums=12)


def sigmoid(v):
    return 1.0 / (1.0 + jnp.exp(-v))


def silu_back(v, up):
    sg = sigmoid(v)
    return up * sg * (1.0 + v * (1.0 - sg))


def pixel_ids(rows, cols):
    row = lax.broadcasted_iota(jnp.int32, (rows, cols), 0)
    return (row // 8) % 8, row % 8


def shifted(value, di, dj):
    step = di * 8 + dj
    if step == 0:
        return value
    rows, cols = value.shape
    rolled = pltpu.roll(value, (-step) % rows, 0)
    i, j = pixel_ids(rows, cols)
    keep = None
    for index, d in ((i, di), (j, dj)):
        if d == 0:
            continue
        this = index < 8 - d if d > 0 else index >= -d
        keep = this if keep is None else keep & this
    return jnp.where(keep, rolled, 0.0)


def mover(links, ins, outs, w, g, stash, third, fin, m, credit):
    x, y, z = links.x, links.y, links.z
    pending = []
    local_sems = m.local_sems
    shards_in = ins.weights

    def post(src, dst, slot, **to):
        made = links.send(src, dst, slot, **to)
        pending.append(made)
        return made

    def sent(made):
        made.wait_send()
        pending[:] = [other for other in pending if other is not made]

    def drain():
        for made in pending:
            made.wait_send()
        pending.clear()

    post(ins.images, m.raw.at[0], T.raw, other=True)
    post(ins.mask, m.mask.at[0], T.mask, other=True)
    own = []
    for n, name in enumerate(NAMES):
        kind, shard = KINDS[name], shards_in[name]
        if name == R1:
            made = pltpu.make_async_copy(shard, full_of(kind, w[name], z, x), local_sems.at[n])
        else:
            made = pltpu.make_async_copy(shard_half(kind, shard, y), half_of(kind, w[name], z, x, y), local_sems.at[n])
        made.start()
        own.append(made)
    first = []
    for dz, dx in ((2, 1), (2, 0), (1, 1), (3, 1), (1, 0), (3, 0), (0, 1)):
        slot = T.first + dz * 2 + dx
        first.append(post(shards_in[R1], full_of(ROW, w[R1], z, x), slot, dz=dz, dx=dx))
    post(ins.cotangent, m.cot.at[0], T.cot, other=True)

    flight = {}

    def start(name, stage):
        kind, buf, shard = KINDS[name], w[name], shards_in[name]
        slot = T.gather + 5 * name
        x_first = name in GATHER_X_FIRST
        along_x, along_y, along_z = dict(dx=1), dict(dy=1), None
        axis = ((along_x, along_z, along_y) if x_first else (along_z, along_y, along_x))[stage]
        if stage == 0:
            src, dst = shard_half(kind, shard, y), half_of(kind, buf, z, x, y)
        elif x_first:
            src = dst = half_of(kind, buf, z, ALL, y) if stage == 1 else thin_of(kind, buf, ALL, ALL, y)
        else:
            src = dst = thin_of(kind, buf, ALL, x, y) if stage == 1 else full_of(kind, buf, ALL, x)
        if axis is None:
            flight[name] = [post(src, dst, slot + dz, dz=dz) for dz in (2, 1, 3)]
        else:
            flight[name] = [post(src, dst, slot + (4 if axis is along_y else 0), **axis)]

    def landed(name):
        for made in flight[name]:
            made.wait_recv()

    order = (S1, E1, P1, R2, S2, E2)

    def finish(name):
        landed(name)
        if name != P1:
            post(w[name], w[name], T.hand + name, other=True)
            return
        links.arrived(m.pix, T.pix)

        def project(step, carry):
            off = pl.multiple_of(step * 256, 256)
            kern = w[P1][:, :, :, :, pl.ds(off, 256)].reshape(1024, 256)
            m.prep[:, pl.ds(off, 256)] = nn(m.pix[0:256, :], kern)
            return carry

        lax.fori_loop(0, 6, project, 0)
        post(m.prep, m.prep, T.prep, other=True)

    start(order[0], 0)
    start(order[1], 0)
    for made in own:
        made.wait()
    for made in first:
        made.wait_recv()
    post(w[R1], w[R1], T.hand + R1, other=True)
    for turn in range(len(order) + 2):
        for n in range(len(order)):
            stage = turn - n
            if stage in (0, 1):
                landed(order[n])
                start(order[n], stage + 1)
                if stage == 0 and n + 2 < len(order):
                    start(order[n + 2], 0)
            elif stage == 2:
                finish(order[n])
    drain()

    def allow(which):
        for to in (dict(dx=1), dict(dy=1)):
            pl.semaphore_signal(credit.at[which], inc=1, device_id=links.device(**to), device_id_type=MESH)

    allow(0)
    pl.semaphore_wait(credit.at[0], 2)

    def add(dst, others, count, take=None):
        take = take or (lambda ref, i: ref.at[i])

        def one(i, carry):
            total = take(dst, i)[...].astype(F32)
            for other in others:
                total = total + take(other, i)[...].astype(F32)
            take(dst, i)[...] = total.astype(BF16)
            return carry

        lax.fori_loop(0, count, one, 0)

    def reduce_start(name, stage):
        kind, buf, into = KINDS[name], g[name], w[name]
        slot = T.reduce + 6 * name
        if stage == 3:
            flight[name] = [post(shard_thin(kind, fin[name], y), shard_thin(kind, fin[name], y), slot + 5, dy=1)]
            return
        if name in REDUCE_Y_FIRST:
            if stage == 0:
                flight[name] = [post(half_of(kind, buf, ALL, ALL, 1 - y), half_of(kind, into, ALL, ALL, 0), slot + 4, dy=1)]
            elif stage == 1:
                flight[name] = [post(half_of(kind, buf, (z + dz) % 4, ALL, y), third[name].at[dz - 1], slot + dz, dz=dz) for dz in (2, 1, 3)]
            else:
                flight[name] = [post(half_of(kind, buf, z, 1 - x, y), stash[name], slot, dx=1)]
            return
        if stage == 0:
            flight[name] = [post(full_of(kind, buf, ALL, 1 - x), full_of(kind, into, ALL, 0), slot, dx=1)]
        elif stage == 1:
            flight[name] = [post(half_of(kind, buf, ALL, x, 1 - y), half_of(kind, into, ALL, 1, 0), slot + 4, dy=1)]
        else:
            flight[name] = [post(half_of(kind, buf, (z + dz) % 4, x, y), third[name].at[dz - 1], slot + dz, dz=dz) for dz in (2, 1, 3)]

    def reduce_next(name, stage):
        landed(name)
        if KINDS[name] == TAP and stage < 2:
            for made in flight[name]:
                sent(made)
        kind, buf, into = KINDS[name], g[name], w[name]
        if stage == 3:
            made = pltpu.make_async_copy(fin[name], outs.grads[name], local_sems.at[name])
            made.start()
            m.tail.append(made)
            post(fin[name], outs.grads[name], T.out + name, other=True)
            return
        if name in REDUCE_Y_FIRST:
            if stage == 0:
                if kind == TAP:
                    add(half_of(kind, buf, ALL, ALL, y), [half_of(kind, into, ALL, ALL, 0)], 20,
                        lambda ref, i: ref.at[i // 4, i % 4])
                else:
                    add(half_of(kind, buf, ALL, ALL, y), [half_of(kind, into, ALL, ALL, 0)], 4)
            elif stage == 1:
                mine = half_of(kind, buf, z, ALL, y)
                theirs = [third[name].at[i] for i in range(3)]
                if kind == TAP:
                    add(mine, theirs, 5)
                else:
                    add(mine, theirs, 2)
            else:
                shard_half(kind, fin[name], y)[...] = (
                    half_of(kind, buf, z, x, y)[...].astype(F32) + stash[name][...].astype(F32)).astype(BF16)
            return
        if stage == 0:
            if kind == TAP:
                add(full_of(kind, buf, ALL, x), [full_of(kind, into, ALL, 0)], 9)
            else:
                add(full_of(kind, buf, ALL, x), [full_of(kind, into, ALL, 0)], 4)
        elif stage == 1:
            add(half_of(kind, buf, ALL, x, y), [half_of(kind, into, ALL, 1, 0)], 5 if kind == TAP else 4)
        else:
            total = half_of(kind, buf, z, x, y)[...].astype(F32)
            for i in range(3):
                total = total + third[name][i].astype(F32)
            shard_half(kind, fin[name], y)[...] = total.astype(BF16)

    def columns(name, left, right):
        def one(step, carry):
            off = pl.multiple_of(step * 256, 256)
            part = tn(left, right[:, pl.ds(off, 256)])
            shape = g[name].shape[:-1] + (256,)
            g[name][..., pl.ds(off, 256)] = part.astype(BF16).reshape(shape)
            return carry

        lax.fori_loop(0, right.shape[1] // 256, one, 0)

    def taps(name, wide_ref, low_ref):
        def one(tap, carry):
            off = pl.multiple_of(tap * 384, 128)
            part = tn(wide_ref[:, pl.ds(off, 384)], low_ref[...])
            g[name][tap] = part.astype(BF16).reshape(4, 2, 48, 384)
            return carry

        lax.fori_loop(0, 9, one, 0)

    def make(name):
        if name == E2:
            links.arrived(m.act5, T.act5)
            links.arrived(m.low6, T.low6)
            columns(E2, m.act5[...], m.low6)
        elif name == S2:
            links.arrived(m.xc5, T.xc5)
            links.arrived(m.low5, T.low5)
            taps(S2, m.xc5, m.low5)
        elif name == R2:
            links.arrived(m.hlow, T.hlow)
            links.arrived(m.low4, T.low4)

            def one(step, carry):
                part = tn(m.hlow[:, pl.ds(pl.multiple_of(step * 384, 128), 384)], m.low4[...])
                g[R2][step] = part.astype(BF16).reshape(2, 2, 96, 384)
                return carry

            lax.fori_loop(0, 4, one, 0)
        elif name == E1:
            links.arrived(m.act2, T.act2)
            links.arrived(m.low3, T.low3)
            columns(E1, m.act2[...], m.low3)
        elif name == P1:
            links.arrived(m.lowp, T.lowp)

            def back(step, carry):
                kern = w[P1][step].reshape(256, 1536)
                m.gsamp[:, pl.ds(pl.multiple_of(step * 256, 256), 256)] = nt(m.lowp[...], kern)
                return carry

            lax.fori_loop(0, 4, back, 0)
            allow(1)
            post(m.gsamp, m.gsamp, T.gsamp, other=True)

            def one(step, carry):
                part = tn(m.pix[0:256, pl.ds(pl.multiple_of(step * 256, 256), 256)], m.lowp[...])
                g[P1][step] = part.astype(BF16).reshape(2, 2, 64, 1536)
                return carry

            lax.fori_loop(0, 4, one, 0)
            pl.semaphore_wait(credit.at[1], 2)
        elif name == S1:
            links.arrived(m.xc2, T.xc2)
            links.arrived(m.low2, T.low2)
            taps(S1, m.xc2, m.low2)
        else:
            links.arrived(m.low1, T.low1)

            def one(step, carry):
                part = tn(m.pix[:, pl.ds(pl.multiple_of(step * 256, 256), 256)], m.low1[...])
                g[R1][step] = part.astype(BF16).reshape(2, 2, 64, 384)
                return carry

            lax.fori_loop(0, 4, one, 0)

    back_order = (E2, S2, R2, E1, P1, S1, R1)
    for turn in range(len(back_order) + 4):
        if turn < len(back_order):
            make(back_order[turn])
            reduce_start(back_order[turn], 0)
        for n in range(len(back_order)):
            stage = turn - n - 1
            if 0 <= stage <= 3:
                reduce_next(back_order[n], stage)
                if stage < 3:
                    reduce_start(back_order[n], stage + 1)
    drain()
    for made in m.tail:
        made.wait()
    links.arrived(outs.act, T.out_act)
    links.arrived(outs.norm, T.out_norm)
    links.arrived(outs.gimg, T.out_gimg)


def runner(links, ins, outs, w, m, sums):
    x, y, z = links.x, links.y, links.z
    me = y * 8 + links.wide
    pending = []
    local_sems = m.local_sems

    def post(src, dst, slot, **to):
        made = links.send(src, dst, slot, **to)
        pending.append(made)
        return made

    def hand(ref, slot):
        post(ref, ref, slot, other=True)

    peers = [(dy, dz, dx) for dz in (2, 1, 3, 0) for dx in (1, 0) for dy in (1, 0) if (dy, dz, dx) != (0, 0, 0)]

    def total(which, rows):
        buf = sums[which]
        for r, row in enumerate(rows):
            buf[me, r:r + 1, :] = row
        slot = T.sums + which
        sem = links.next_send
        links.next_send += 1
        for dy, dz, dx in peers:
            pltpu.make_async_remote_copy(
                src_ref=buf.at[me], dst_ref=buf.at[me], send_sem=links.send_sems.at[sem], recv_sem=links.recv_sems.at[slot],
                device_id=links.device(dy=dy, dz=dz, dx=dx), device_id_type=MESH).start()
        both = pltpu.make_async_remote_copy(
            src_ref=buf.at[pl.ds(0, 15)], dst_ref=buf.at[pl.ds(0, 15)], send_sem=links.send_sems.at[sem],
            recv_sem=links.recv_sems.at[slot], device_id=links.device(other=True), device_id_type=MESH)
        both.wait_recv()
        both.wait_send()
        parts = [buf[i] for i in range(16)]
        while len(parts) > 1:
            parts = [parts[i] + parts[i + 1] for i in range(0, len(parts), 2)]
        return parts[0]

    own_norm = pltpu.make_async_copy(ins.norm, m.norm_in.at[links.wide], local_sems.at[0])
    own_norm.start()
    own_raw = pltpu.make_async_copy(ins.images, m.raw.at[1], local_sems.at[1])
    own_raw.start()
    own_mask = pltpu.make_async_copy(ins.mask, m.mask.at[1], local_sems.at[2])
    own_mask.start()
    own_cot = pltpu.make_async_copy(ins.cotangent, m.cot.at[1], local_sems.at[3])
    own_cot.start()
    for k, (dz, dx) in enumerate([(dz, dx) for dz in (2, 1, 3, 0) for dx in (1, 0) if (dz, dx) != (0, 0)]):
        post(ins.norm, m.norm_in.at[links.wide], T.norm_in + dz * 2 + dx, dz=dz, dx=dx)

    r = lax.broadcasted_iota(jnp.int32, (256, 256), 0)
    c = lax.broadcasted_iota(jnp.int32, (256, 256), 1)
    source = (2 * ((r // 8) % 8) + r // 128) * 16 + 2 * (r % 8) + (r // 64) % 2
    perm = jnp.where(c == source, 1.0, 0.0).astype(BF16)
    m.perm[...] = perm

    own_mask.wait()
    links.arrived(m.mask.at[0], T.mask)
    flags = m.mask[...].reshape(64, 16).astype(F32)
    for pq in range(4):
        p, q = pq // 2, pq % 2
        row = lax.broadcasted_iota(jnp.int32, (256, 64), 0)
        line = lax.broadcasted_iota(jnp.int32, (256, 64), 1)
        pick = jnp.where(line == (row // 64) * 16 + 2 * ((row // 8) % 8) + p, 1.0, 0.0)
        lines = nn(pick.astype(BF16), flags.astype(BF16))
        row16 = lax.broadcasted_iota(jnp.int32, (256, 16), 0)
        col16 = lax.broadcasted_iota(jnp.int32, (256, 16), 1)
        one = jnp.sum(jnp.where(col16 == 2 * (row16 % 8) + q, lines, 0.0), axis=1, keepdims=True)
        m.valid[pq * 256:(pq + 1) * 256, :] = jnp.broadcast_to(one, (256, 128))

    own_raw.wait()
    links.arrived(m.raw.at[0], T.raw)
    for b in range(4):
        picked = nn(perm, m.raw[b // 2, (b % 2) * 256:(b % 2) * 256 + 256, :]).astype(BF16)
        for pq in range(4):
            m.pix[pq * 256 + b * 64:pq * 256 + b * 64 + 64, :] = picked[pq * 64:pq * 64 + 64, :]
    hand(m.pix, T.pix)

    own_norm.wait()
    for dz in range(4):
        for dx in range(2):
            if dz or dx:
                links.arrived(m.norm_in.at[0], T.norm_in + dz * 2 + dx)
    for s in range(8):
        piece = m.norm_in[s]
        at = 0
        for ref in (m.gain_a, m.shift_a, m.gain_b, m.shift_b):
            size = ref.shape[1] // 8
            ref[:, s * size:(s + 1) * size] = piece[:, at:at + size]
            at += size

    norms = m.norms

    def set_norm(key, mean_sum, square_sum, count, gain, shift):
        ref = norms[key]
        mean = mean_sum / count
        var = square_sum / count - mean * mean
        scaler = lax.rsqrt(var + NORM_EPS)
        ref[0:1, :] = mean
        ref[1:2, :] = scaler
        ref[2:3, :] = gain
        ref[3:4, :] = gain * scaler
        ref[4:5, :] = shift - mean * (gain * scaler)

    def set_back(key, first_sum, second_sum, count, at):
        ref = norms[key]
        mean, scaler, gain = ref[0:1, :], ref[1:2, :], ref[2:3, :]
        centred = second_sum - mean * first_sum
        grad_var = -0.5 * gain * centred * scaler * scaler * scaler
        grad_mean = -gain * scaler * first_sum - 2.0 * mean * grad_var
        ref[5:6, :] = grad_mean / count
        ref[6:7, :] = 2.0 * grad_var / count
        size = ref.shape[1]
        gain_at, shift_at = at
        m.norm_out[:, gain_at:gain_at + size] = scaler * centred
        m.norm_out[:, shift_at:shift_at + size] = first_sum

    def rows_of(key, at, size):
        ref = norms[key]
        return [ref[k:k + 1, pl.ds(at, size)] for k in range(8)]

    def norm_of(key, pre, at, size):
        ref = norms[key]
        return pre * ref[3:4, pl.ds(at, size)] + ref[4:5, pl.ds(at, size)]

    def back_of(key, pre, up, valid, at, size):
        ref = norms[key]
        return ref[3:4, pl.ds(at, size)] * up + valid * (ref[5:6, pl.ds(at, size)] + ref[6:7, pl.ds(at, size)] * pre)

    def valid_of(rows, cols):
        one = m.valid[rows, :]
        return jnp.concatenate([one] * (cols // 128), axis=1) if cols > 128 else one

    def colsum(v):
        return jnp.sum(v, axis=0, keepdims=True)

    lo = pl.ds(0, 256)
    stat = m.stat

    def chunks(rows, width, body):
        def one(step, carry):
            return body(pl.ds(pl.multiple_of(step * 64, 64), 64), carry)

        zero = jnp.zeros((1, width), F32)
        return lax.fori_loop(0, rows // 64, one, (zero, zero))

    links.arrived(w[R1], T.hand + R1)

    def layer1(step, carry):
        rows = pl.ds(pl.multiple_of(step * 256, 256), 256)
        pre = nn(m.pix[rows, :], w[R1][...].reshape(1024, 384))
        m.pre1[rows, :] = pre
        weighed = pre * valid_of(rows, 384)
        return carry[0] + colsum(weighed), carry[1] + colsum(weighed * pre)

    zero = jnp.zeros((1, 384), F32)
    first, second = lax.fori_loop(0, 4, layer1, (zero, zero))
    hi_here = jnp.concatenate([colsum(m.valid[...])] * 3, axis=1)
    lo_here = jnp.concatenate([colsum(m.valid[lo, :])] * 3, axis=1)
    got = total(0, [first, second, hi_here, lo_here])
    count_hi = jnp.maximum(got[2:3, :], 1.0)
    count_lo = jnp.maximum(got[3:4, :], 1.0)
    count_wide = jnp.concatenate([count_lo] * 4, axis=1)
    set_norm(N1, got[0:1, :], got[1:2, :], count_hi, m.gain_a[:, 0:384], m.shift_a[:, 0:384])

    def activate1(rows, carry):
        v = norm_of(N1, m.pre1[rows, :], 0, 384)
        m.up1[rows, :] = v * sigmoid(v)
        return carry

    chunks(1024, 384, activate1)
    for tap in range(9):
        a, b = tap // 3, tap % 3
        pq = (0 if a == 1 else 2) + (0 if b == 1 else 1)
        block = m.up1[pq * 256:pq * 256 + 256, :]
        block = shifted(block, -1 if a == 0 else 0, -1 if b == 0 else 0)
        m.xc2[:, tap * 384:(tap + 1) * 384] = block.astype(BF16)
    hand(m.xc2, T.xc2)

    def statistics(pre, rows, width):
        weighed = pre * valid_of(rows, width)
        return colsum(weighed), colsum(weighed * pre)

    links.arrived(w[S1], T.hand + S1)
    pre = nn(m.xc2[...], w[S1][...].reshape(3456, 384))
    m.pre2[...] = pre
    got = total(1, statistics(pre, lo, 384))
    set_norm(N2, got[0:1, :], got[1:2, :], count_lo, m.gain_a[:, 384:768], m.shift_a[:, 384:768])

    def activate2(rows, carry):
        v = norm_of(N2, m.pre2[rows, :], 0, 384)
        m.act2[rows, :] = (v * sigmoid(v)).astype(BF16)
        return carry

    chunks(256, 384, activate2)
    hand(m.act2, T.act2)

    def wide_loop(body, size=256):
        def one(step, carry):
            body(pl.multiple_of(step * size, size))
            return carry

        lax.fori_loop(0, 1536 // size, one, 0)

    def keep_stats(ref, at, size, k):
        first, second = statistics(ref[:, pl.ds(at, size)], lo, size)
        stat[k:k + 1, pl.ds(at, size)] = first
        stat[k + 1:k + 2, pl.ds(at, size)] = second

    links.arrived(w[E1], T.hand + E1)

    def layer3(at):
        m.pre3[:, pl.ds(at, 256)] = nn(m.act2[...], w[E1][:, :, :, pl.ds(at, 256)].reshape(384, 256))
        keep_stats(m.pre3, at, 256, 0)

    wide_loop(layer3)
    links.arrived(m.prep, T.prep)
    wide_loop(lambda at: keep_stats(m.prep, at, 256, 2))
    got = total(2, [stat[k:k + 1, :] for k in range(4)])
    set_norm(N3, got[0:1, :], got[1:2, :], count_wide, m.gain_a[:, 768:2304], m.shift_a[:, 768:2304])
    set_norm(NP, got[2:3, :], got[3:4, :], count_wide, m.gain_a[:, 2304:3840], m.shift_a[:, 2304:3840])

    def sum_one(at, size):
        cols = pl.ds(at, size)
        return norm_of(N3, m.pre3[:, cols], at, size) + norm_of(NP, m.prep[:, cols], at, size)

    def make_hidden(at):
        v = sum_one(at, 128)
        hidden = v * sigmoid(v)
        m.hidden[:, pl.ds(at, 128)] = hidden
        m.hlow[:, pl.ds(at, 128)] = hidden.astype(BF16)

    wide_loop(make_hidden, 128)
    hand(m.hlow, T.hlow)

    links.arrived(w[R2], T.hand + R2)
    pre = nn(m.hlow[...], w[R2][...].reshape(1536, 384))
    m.pre4[...] = pre
    got = total(3, statistics(pre, lo, 384))
    set_norm(N4, got[0:1, :], got[1:2, :], count_lo, m.gain_b[:, 0:384], m.shift_b[:, 0:384])

    def activate4(rows, carry):
        v = norm_of(N4, m.pre4[rows, :], 0, 384)
        m.small[rows, :] = v * sigmoid(v)
        return carry

    chunks(256, 384, activate4)
    for tap in range(9):
        m.xc5[:, tap * 384:(tap + 1) * 384] = shifted(m.small[...], tap // 3 - 1, tap % 3 - 1).astype(BF16)
    hand(m.xc5, T.xc5)
    links.arrived(w[S2], T.hand + S2)
    pre = nn(m.xc5[...], w[S2][...].reshape(3456, 384))
    m.pre5[...] = pre
    got = total(4, statistics(pre, lo, 384))
    set_norm(N5, got[0:1, :], got[1:2, :], count_lo, m.gain_b[:, 384:768], m.shift_b[:, 384:768])

    def activate5(rows, carry):
        v = norm_of(N5, m.pre5[rows, :], 0, 384)
        m.act5[rows, :] = (v * sigmoid(v)).astype(BF16)
        return carry

    chunks(256, 384, activate5)
    hand(m.act5, T.act5)
    links.arrived(w[E2], T.hand + E2)

    def layer6(at):
        m.pre6[:, pl.ds(at, 256)] = nn(m.act5[...], w[E2][:, :, :, pl.ds(at, 256)].reshape(384, 256))
        keep_stats(m.pre6, at, 256, 0)

    wide_loop(layer6)
    got = total(5, [stat[k:k + 1, :] for k in range(2)])
    set_norm(N6, got[0:1, :], got[1:2, :], count_wide, m.gain_b[:, 768:2304], m.shift_b[:, 768:2304])
    own_cot.wait()
    links.arrived(m.cot.at[0], T.cot)

    def top(at):
        cols = pl.ds(at, 128)
        pre = m.pre6[:, cols]
        v = norm_of(N6, pre, at, 128) + m.hidden[:, cols]
        sg = sigmoid(v)
        m.acts[:, cols] = (v * sg).astype(BF16)
        up = m.cot[:, :, cols].reshape(256, 128).astype(F32)
        up = up * sg * (1.0 + v * (1.0 - sg))
        m.hidden[:, cols] = up
        stat[0:1, cols] = colsum(up)
        stat[1:2, cols] = colsum(up * pre)

    wide_loop(top, 128)
    out_act = pltpu.make_async_copy(m.acts.at[pl.ds(128, 128)], outs.act, local_sems.at[4])
    out_act.start()
    post(m.acts.at[pl.ds(0, 128)], outs.act, T.out_act, other=True)
    got = total(6, [stat[k:k + 1, :] for k in range(2)])
    b_gain, b_shift = 7680, 9984
    set_back(N6, got[0:1, :], got[1:2, :], count_wide, (b_gain + 768, b_shift + 768))

    def low6(at):
        cols = pl.ds(at, 128)
        m.low6[:, cols] = back_of(N6, m.pre6[:, cols], m.hidden[:, cols], valid_of(lo, 128), at, 128).astype(BF16)

    wide_loop(low6, 128)
    hand(m.low6, T.low6)
    m.small[...] = nt(m.low6[...], w[E2][...].reshape(384, 1536))

    def narrow_up(key, pre):
        def one(rows, carry):
            kept = pre[rows, :]
            up = silu_back(norm_of(key, kept, 0, 384), m.small[rows, :])
            m.small[rows, :] = up
            return carry[0] + colsum(up), carry[1] + colsum(up * kept)

        return chunks(256, 384, one)

    def narrow_low(key, pre, low, slot):
        def one(rows, carry):
            got = back_of(key, pre[rows, :], m.small[rows, :], valid_of(rows, 384), 0, 384)
            m.small[rows, :] = got
            low[rows, :] = got.astype(BF16)
            return carry

        chunks(256, 384, one)
        hand(low, slot)

    got = total(7, narrow_up(N5, m.pre5))
    set_back(N5, got[0:1, :], got[1:2, :], count_lo, (b_gain + 384, b_shift + 384))
    narrow_low(N5, m.pre5, m.low5, T.low5)
    grad = jnp.zeros((256, 384), F32)
    for tap in range(9):
        moved = shifted(m.small[...], 1 - tap // 3, 1 - tap % 3).astype(BF16)
        grad = grad + nt(moved, w[S2][tap].reshape(384, 384))
    m.small[...] = grad
    got = total(8, narrow_up(N4, m.pre4))
    set_back(N4, got[0:1, :], got[1:2, :], count_lo, (b_gain, b_shift))
    narrow_low(N4, m.pre4, m.low4, T.low4)

    def below(step, carry):
        at = pl.multiple_of(step * 384, 128)
        cols = pl.ds(at, 384)
        grad = m.hidden[:, cols] + nt(m.low4[...], w[R2][step].reshape(384, 384))
        up = silu_back(sum_one(at, 384), grad)
        m.pre6[:, cols] = up
        stat[0:1, cols] = colsum(up)
        stat[1:2, cols] = colsum(up * m.pre3[:, cols])
        stat[2:3, cols] = colsum(up * m.prep[:, cols])
        return carry

    lax.fori_loop(0, 4, below, 0)
    got = total(9, [stat[k:k + 1, :] for k in range(3)])
    a_gain, a_shift = 0, 3840
    set_back(N3, got[0:1, :], got[1:2, :], count_wide, (a_gain + 768, a_shift + 768))
    set_back(NP, got[0:1, :], got[2:3, :], count_wide, (a_gain + 2304, a_shift + 2304))

    def low3(at):
        cols = pl.ds(at, 128)
        up, valid = m.pre6[:, cols], valid_of(lo, 128)
        m.low3[:, cols] = back_of(N3, m.pre3[:, cols], up, valid, at, 128).astype(BF16)
        m.lowp[:, cols] = back_of(NP, m.prep[:, cols], up, valid, at, 128).astype(BF16)

    wide_loop(low3, 128)
    hand(m.low3, T.low3)
    hand(m.lowp, T.lowp)
    m.small[...] = nt(m.low3[...], w[E1][...].reshape(384, 1536))
    got = total(10, narrow_up(N2, m.pre2))
    set_back(N2, got[0:1, :], got[1:2, :], count_lo, (a_gain + 384, a_shift + 384))
    narrow_low(N2, m.pre2, m.low2, T.low2)
    for pq in range(4):
        p, q = pq // 2, pq % 2
        grad = jnp.zeros((256, 384), F32)
        for a in ((1,) if p == 0 else (0, 2)):
            for b in ((1,) if q == 0 else (0, 2)):
                moved = shifted(m.small[...], 1 if a == 0 else 0, 1 if b == 0 else 0).astype(BF16)
                grad = grad + nt(moved, w[S1][a * 3 + b].reshape(384, 384))
        m.up1[pq * 256:pq * 256 + 256, :] = grad

    def up1(rows, carry):
        kept = m.pre1[rows, :]
        up = silu_back(norm_of(N1, kept, 0, 384), m.up1[rows, :])
        m.up1[rows, :] = up
        return carry[0] + colsum(up), carry[1] + colsum(up * kept)

    got = total(11, chunks(1024, 384, up1))
    set_back(N1, got[0:1, :], got[1:2, :], count_hi, (a_gain, a_shift))
    out_norm = pltpu.make_async_copy(m.norm_out, outs.norm, local_sems.at[5])
    out_norm.start()
    post(m.norm_out, outs.norm, T.out_norm, other=True)

    def low1(rows, carry):
        got = back_of(N1, m.pre1[rows, :], m.up1[rows, :], valid_of(rows, 384), 0, 384)
        m.low1[rows, :] = got.astype(BF16)
        return carry

    chunks(1024, 384, low1)
    hand(m.low1, T.low1)
    links.arrived(m.gsamp, T.gsamp)
    for pq in range(4):
        grad = nt(m.low1[pq * 256:pq * 256 + 256, :], w[R1][...].reshape(1024, 384))
        if pq == 0:
            grad = grad + m.gsamp[...]
        m.pixg[pq * 256:pq * 256 + 256, :] = grad.astype(BF16)
    for b in range(4):
        block = jnp.concatenate([m.pixg[pq * 256 + b * 64:pq * 256 + b * 64 + 64, :] for pq in range(4)], axis=0)
        m.raw[b // 2, (b % 2) * 256:(b % 2) * 256 + 256, :] = tn(m.perm[...], block).astype(BF16)
    out_img = pltpu.make_async_copy(m.raw.at[1], outs.gimg, local_sems.at[6])
    out_img.start()
    post(m.raw.at[0], outs.gimg, T.out_gimg, other=True)
    for name in NAMES:
        links.arrived(outs.grads[name], T.out + name)
    out_act.wait()
    out_norm.wait()
    out_img.wait()
    for made in pending:
        made.wait_send()


SUM_ROWS = ((4, 384), (2, 384), (4, 1536), (2, 384), (2, 384), (2, 1536), (2, 1536), (2, 384), (2, 384), (3, 1536), (2, 384), (2, 384))


def fused_kernel(sizes, keys, *refs):
    groups, at = [], 0
    for size in sizes:
        groups.append(refs[at:at + size])
        at += size
    taken, shards_in, given, made, w, g, fin, third, stash, kept, norms, sums, rest = groups
    dp, wide = lax.axis_index("dp"), lax.axis_index("wide")
    core = dp % 2
    send_sems, recv_sems, local_sems, credit = rest
    barrier = pltpu.get_barrier_semaphore()
    greet = Links(send_sems, recv_sems, core, 0)
    everyone = [dict(other=True)] + [
        dict(dy=dy, dz=dz, dx=dx) for dy in (0, 1) for dz in range(4) for dx in (0, 1) if (dy, dz, dx) != (0, 0, 0)]
    for to in everyone:
        pl.semaphore_signal(barrier, inc=1, device_id=greet.device(**to), device_id_type=MESH)
    pl.semaphore_wait(barrier, len(everyone))

    images, mask, cotangent, norm = taken
    act, gimg, norm_out = given
    ins = types.SimpleNamespace(images=images, mask=mask, cotangent=cotangent, norm=norm, weights=shards_in)
    outs = types.SimpleNamespace(act=act, gimg=gimg, norm=norm_out, grads=made)
    m = types.SimpleNamespace(**dict(zip(keys, kept)), norms=norms, local_sems=local_sems, tail=[])

    @pl.when(core == 0)
    def _():
        mover(Links(send_sems, recv_sems, 0, 1), ins, outs, w, g, dict(zip(REDUCE_Y_FIRST, stash)), third, fin, m, credit)

    @pl.when(core == 1)
    def _():
        runner(Links(send_sems, recv_sems, 1, 1), ins, outs, w, m, sums)


def fused_shards(images, pixel_mask, cotangent, reduce_one, spatial_one, expand_one, project_one, gains_one, shifts_one,
                 reduce_two, spatial_two, expand_two, gains_two, shifts_two):
    def split(weight):
        return weight.reshape(2, weight.shape[0] // 2, weight.shape[1])

    def join(weight):
        return weight.reshape(9, weight.shape[2], weight.shape[3])

    weights = (split(reduce_one), join(spatial_one), expand_one, split(project_one), split(reduce_two), join(spatial_two), expand_two)
    norm = jnp.concatenate([gains_one, shifts_one, gains_two, shifts_two]).astype(F32).reshape(1, -1)
    taken = [images.reshape(512, 1024), pixel_mask.reshape(32, 16), cotangent.reshape(128, 1536), norm]
    given = [jax.ShapeDtypeStruct((128, 1536), BF16), jax.ShapeDtypeStruct((512, 1024), BF16), jax.ShapeDtypeStruct((1, 12288), F32)]
    made = [jax.ShapeDtypeStruct(v.shape, BF16) for v in weights]
    whole = [pltpu.VMEM(whole_shape(KINDS[n], v.shape), BF16) for n, v in enumerate(weights)]
    fin = [pltpu.VMEM(v.shape, BF16) for v in weights]
    halves = [half_shape(KINDS[n], v.shape) for n, v in enumerate(weights)]
    stash = [pltpu.VMEM(halves[n], BF16) for n in REDUCE_Y_FIRST]
    third = []
    for n, half in enumerate(halves):
        if n in REDUCE_Y_FIRST:
            half = (half[0], 2) + half[1:] if KINDS[n] == TAP else (2,) + half
        third.append(pltpu.VMEM((3,) + half, BF16))
    bf = dict(raw=(2, 512, 1024), cot=(2, 128, 1536), pix=(1024, 1024), perm=(256, 256), xc2=(256, 3456), xc5=(256, 3456),
              act2=(256, 384), act5=(256, 384), hlow=(256, 1536), acts=(256, 1536), low6=(256, 1536), low5=(256, 384), low4=(256, 384),
              low3=(256, 1536), lowp=(256, 1536), low2=(256, 384), low1=(1024, 384), pixg=(1024, 1024))
    f32 = dict(norm_in=(8, 1, 1536), gain_a=(1, 3840), shift_a=(1, 3840), gain_b=(1, 2304), shift_b=(1, 2304), norm_out=(1, 12288),
               valid=(1024, 128), stat=(8, 1536), pre1=(1024, 384), up1=(1024, 384), pre2=(256, 384), pre3=(256, 1536), prep=(256, 1536),
               hidden=(256, 1536), pre4=(256, 384), pre5=(256, 384), pre6=(256, 1536), small=(256, 384), gsamp=(256, 1024))
    kept = {k: pltpu.VMEM(v, BF16) for k, v in bf.items()} | {k: pltpu.VMEM(v, F32) for k, v in f32.items()}
    kept |= dict(mask=pltpu.VMEM((2, 32, 16), jnp.int32))
    norms = [pltpu.VMEM((8, width), F32) for width in (384, 384, 1536, 1536, 384, 384, 1536)]
    sums = [pltpu.VMEM((16, rows, width), F32) for rows, width in SUM_ROWS]
    rest = [pltpu.SemaphoreType.DMA((120,)), pltpu.SemaphoreType.DMA((T.total,)), pltpu.SemaphoreType.DMA((8,)),
            pltpu.SemaphoreType.REGULAR((2,))]
    groups = [taken, weights, given, made, whole, whole, fin, third, stash, list(kept.values()), norms, sums, rest]
    anywhere = pl.BlockSpec(memory_space=pl.ANY)
    got = pl.pallas_call(
        functools.partial(fused_kernel, [len(group) for group in groups], list(kept)),
        out_shape=given + made,
        in_specs=[anywhere] * (len(taken) + len(weights)),
        out_specs=[anywhere] * (len(given) + len(made)),
        scratch_shapes=[v for group in groups[4:] for v in group],
        compiler_params=pltpu.CompilerParams(collective_id=0, has_side_effects=True, vmem_limit_bytes=63 * 2**20),
    )(*taken, *weights)
    act, gimg, norms, *grads = got
    grads = [v.astype(F32).reshape(like.shape) for v, like in zip(
        grads, (reduce_one, spatial_one, expand_one, project_one, reduce_two, spatial_two, expand_two))]
    flat = norms.reshape(-1)
    local_a, local_b = gains_one.shape[0], gains_two.shape[0]
    return (
        act.reshape(cotangent.shape),
        gimg.reshape(images.shape),
        grads[0], grads[1], grads[2], grads[3],
        own_slice(flat[:3840], local_a),
        own_slice(flat[3840:7680], local_a),
        grads[4], grads[5], grads[6],
        own_slice(flat[7680:9984], local_b),
        own_slice(flat[9984:], local_b),
    )


def solution(mesh):
    fused = mesh.shape["dp"] == 4 and mesh.shape["wide"] == 8
    in_specs = (
        P(("dp", "wide"), None, None, None),
        P(("dp", "wide"), None, None),
        P(("dp", "wide"), None, None, None),
        P("wide", None),
        P(None, None, "wide", None),
        P("wide", None),
        P("wide", None),
        P("wide"),
        P("wide"),
        P("wide", None),
        P(None, None, "wide", None),
        P("wide", None),
        P("wide"),
        P("wide"),
    )
    out_specs = (
        P(("dp", "wide"), None, None, None),
        P(("dp", "wide"), None, None, None),
        P("wide", None),
        P(None, None, "wide", None),
        P("wide", None),
        P("wide", None),
        P("wide"),
        P("wide"),
        P("wide", None),
        P(None, None, "wide", None),
        P("wide", None),
        P("wide"),
        P("wide"),
    )
    return jax.shard_map(fused_shards if fused else shards, mesh=mesh, in_specs=in_specs, out_specs=out_specs, check_vma=False)
```

```python
import functools
import types

import jax
import jax.numpy as jnp
from jax import lax
from jax.experimental import pallas as pl
from jax.experimental.pallas import tpu as pltpu
from jax.sharding import PartitionSpec as P

NORM_EPS = 1e-05


def pixel_product(source, kernel):
    return jnp.einsum("bhwc,co->bhwo", source, kernel, preferred_element_type=jnp.float32)


def weight_grad(source, upstream):
    return jnp.einsum("bhwc,bhwo->co", source, upstream, preferred_element_type=jnp.float32)


def input_grad(upstream, kernel):
    return jnp.einsum("bhwo,co->bhwc", upstream, kernel, preferred_element_type=jnp.float32)


def conv_spatial(source, kernel, stride):
    out_h = source.shape[1] // stride
    out_w = source.shape[2] // stride
    padded = jnp.pad(source, ((0, 0), (1, 1), (1, 1), (0, 0)))
    summed = jnp.zeros((source.shape[0], out_h, out_w, kernel.shape[3]), jnp.float32)
    for row_off in range(3):
        for col_off in range(3):
            window = padded[
                :,
                row_off : row_off + stride * out_h : stride,
                col_off : col_off + stride * out_w : stride,
            ]
            summed = summed + pixel_product(window, kernel[row_off, col_off])
    return summed


def conv_back(source, upstream, kernel, stride):
    out_h = upstream.shape[1]
    out_w = upstream.shape[2]
    padded = jnp.pad(source, ((0, 0), (1, 1), (1, 1), (0, 0)))
    grad_src = jnp.zeros(padded.shape, jnp.float32)
    kernel_rows = []
    for row_off in range(3):
        for col_off in range(3):
            window = padded[
                :,
                row_off : row_off + stride * out_h : stride,
                col_off : col_off + stride * out_w : stride,
            ]
            kernel_rows.append(weight_grad(window, upstream))
            grad_src = grad_src.at[
                :,
                row_off : row_off + stride * out_h : stride,
                col_off : col_off + stride * out_w : stride,
            ].add(input_grad(upstream, kernel[row_off, col_off]))
    kernel_grad = jnp.stack(kernel_rows).reshape(kernel.shape)
    return (kernel_grad, grad_src[:, 1:-1, 1:-1])


def norm_forward(pre, valid, count, gain, shift):
    moments = lax.psum(
        (jnp.sum(pre * valid, axis=(0, 1, 2)), jnp.sum(pre * pre * valid, axis=(0, 1, 2))),
        ("dp", "wide"),
    )
    mean_val = moments[0] / count
    variance = moments[1] / count - mean_val * mean_val
    scaler = lax.rsqrt(variance + NORM_EPS)
    normed = (pre - mean_val) * scaler
    return (gain * normed + shift, (mean_val, scaler))


def norm_backward(upstream, pre, valid, count, gain, stats):
    mean_val, scaler = stats
    sums = lax.psum(
        (jnp.sum(upstream, axis=(0, 1, 2)), jnp.sum(upstream * pre, axis=(0, 1, 2))), ("dp", "wide")
    )
    first_sum, second_sum = sums
    centred = second_sum - mean_val * first_sum
    grad_gain = scaler * centred
    grad_var = -0.5 * gain * centred * scaler * scaler * scaler
    grad_mean = -gain * scaler * first_sum - 2.0 * mean_val * grad_var
    grad_pre = gain * scaler * upstream + valid / count * (grad_mean + 2.0 * pre * grad_var)
    return (grad_pre, grad_gain, first_sum)


def silu_grad(pre_act, upstream):
    sigma = jax.nn.sigmoid(pre_act)
    return upstream * sigma * (1.0 + pre_act * (1.0 - sigma))


def own_slice(whole, local_len):
    start = lax.axis_index("wide") * local_len
    return lax.dynamic_slice_in_dim(whole, start, local_len, 0)


def shards(
    images,
    pixel_mask,
    cotangent,
    reduce_one,
    spatial_one,
    expand_one,
    project_one,
    gains_one,
    shifts_one,
    reduce_two,
    spatial_two,
    expand_two,
    gains_two,
    shifts_two,
):
    valid_hi = pixel_mask.astype(jnp.float32)[..., None]
    valid_lo = valid_hi[:, ::2, ::2]
    counts = lax.psum((jnp.sum(valid_hi), jnp.sum(valid_lo)), ("dp", "wide"))
    count_hi = jnp.maximum(counts[0], 1.0)
    count_lo = jnp.maximum(counts[1], 1.0)
    first_full = (
        lax.all_gather(reduce_one, "wide", axis=0, tiled=True),
        lax.all_gather(spatial_one, "wide", axis=2, tiled=True),
        lax.all_gather(expand_one, "wide", axis=0, tiled=True),
        lax.all_gather(project_one, "wide", axis=0, tiled=True),
        lax.all_gather(gains_one, "wide", axis=0, tiled=True),
        lax.all_gather(shifts_one, "wide", axis=0, tiled=True),
    )
    red_a, spa_a, exp_a, proj_a, gain_a, shift_a = first_full
    mid_a = red_a.shape[1]
    mid_b = 2 * mid_a
    out_a = mid_b + exp_a.shape[1]
    out_b = out_a + exp_a.shape[1]
    gain_af = gain_a.astype(jnp.float32)
    shift_af = shift_a.astype(jnp.float32)
    pre_one = pixel_product(images, red_a)
    y_one, stat_one = norm_forward(pre_one, valid_hi, count_hi, gain_af[:mid_a], shift_af[:mid_a])
    act_one = jax.nn.silu(y_one).astype(jnp.bfloat16)
    pre_two = conv_spatial(act_one, spa_a, 2)
    y_two, stat_two = norm_forward(
        pre_two, valid_lo, count_lo, gain_af[mid_a:mid_b], shift_af[mid_a:mid_b]
    )
    act_two = jax.nn.silu(y_two).astype(jnp.bfloat16)
    pre_three = pixel_product(act_two, exp_a)
    y_three, stat_three = norm_forward(
        pre_three, valid_lo, count_lo, gain_af[mid_b:out_a], shift_af[mid_b:out_a]
    )
    sampled = images[:, ::2, ::2]
    pre_proj = pixel_product(sampled, proj_a)
    y_proj, stat_proj = norm_forward(
        pre_proj, valid_lo, count_lo, gain_af[out_a:out_b], shift_af[out_a:out_b]
    )
    sum_one = y_three + y_proj
    hidden = jax.nn.silu(sum_one)
    hidden_low = hidden.astype(jnp.bfloat16)
    second_full = (
        lax.all_gather(reduce_two, "wide", axis=0, tiled=True),
        lax.all_gather(spatial_two, "wide", axis=2, tiled=True),
        lax.all_gather(expand_two, "wide", axis=0, tiled=True),
        lax.all_gather(gains_two, "wide", axis=0, tiled=True),
        lax.all_gather(shifts_two, "wide", axis=0, tiled=True),
    )
    red_b, spa_b, exp_b, gain_b, shift_b = second_full
    gain_bf = gain_b.astype(jnp.float32)
    shift_bf = shift_b.astype(jnp.float32)
    pre_four = pixel_product(hidden_low, red_b)
    y_four, stat_four = norm_forward(
        pre_four, valid_lo, count_lo, gain_bf[:mid_a], shift_bf[:mid_a]
    )
    act_four = jax.nn.silu(y_four).astype(jnp.bfloat16)
    pre_five = conv_spatial(act_four, spa_b, 1)
    y_five, stat_five = norm_forward(
        pre_five, valid_lo, count_lo, gain_bf[mid_a:mid_b], shift_bf[mid_a:mid_b]
    )
    act_five = jax.nn.silu(y_five).astype(jnp.bfloat16)
    pre_six = pixel_product(act_five, exp_b)
    y_six, stat_six = norm_forward(
        pre_six, valid_lo, count_lo, gain_bf[mid_b:out_a], shift_bf[mid_b:out_a]
    )
    sum_two = y_six + hidden
    activations = jax.nn.silu(sum_two).astype(jnp.bfloat16)
    back_two = (
        lax.all_gather(reduce_two, "wide", axis=0, tiled=True),
        lax.all_gather(spatial_two, "wide", axis=2, tiled=True),
        lax.all_gather(expand_two, "wide", axis=0, tiled=True),
        lax.all_gather(gains_two, "wide", axis=0, tiled=True),
    )
    red_b, spa_b, exp_b, gain_b = back_two
    gain_bf = gain_b.astype(jnp.float32)
    upstream = cotangent.astype(jnp.float32)
    grad_sum_two = silu_grad(sum_two, upstream)
    grad_pre6, gain_g6, shift_g6 = norm_backward(
        grad_sum_two, pre_six, valid_lo, count_lo, gain_bf[mid_b:out_a], stat_six
    )
    low_six = grad_pre6.astype(jnp.bfloat16)
    grad_exp_b = weight_grad(act_five, low_six)
    grad_act5 = input_grad(low_six, exp_b)
    grad_pre5, gain_g5, shift_g5 = norm_backward(
        silu_grad(y_five, grad_act5), pre_five, valid_lo, count_lo, gain_bf[mid_a:mid_b], stat_five
    )
    low_five = grad_pre5.astype(jnp.bfloat16)
    grad_spa_b, grad_act4 = conv_back(act_four, low_five, spa_b, 1)
    grad_pre4, gain_g4, shift_g4 = norm_backward(
        silu_grad(y_four, grad_act4), pre_four, valid_lo, count_lo, gain_bf[:mid_a], stat_four
    )
    low_four = grad_pre4.astype(jnp.bfloat16)
    grad_red_b = weight_grad(hidden_low, low_four)
    grad_hidden = grad_sum_two + input_grad(low_four, red_b)
    owned_two = (
        lax.psum_scatter(
            grad_red_b.astype(jnp.bfloat16), "wide", scatter_dimension=0, tiled=True
        ).astype(jnp.float32),
        lax.psum_scatter(
            grad_spa_b.astype(jnp.bfloat16), "wide", scatter_dimension=2, tiled=True
        ).astype(jnp.float32),
        lax.psum_scatter(
            grad_exp_b.astype(jnp.bfloat16), "wide", scatter_dimension=0, tiled=True
        ).astype(jnp.float32),
    )
    owned_two = (
        lax.psum(owned_two[0].astype(jnp.bfloat16), "dp").astype(jnp.float32),
        lax.psum(owned_two[1].astype(jnp.bfloat16), "dp").astype(jnp.float32),
        lax.psum(owned_two[2].astype(jnp.bfloat16), "dp").astype(jnp.float32),
    )
    back_one = (
        lax.all_gather(reduce_one, "wide", axis=0, tiled=True),
        lax.all_gather(spatial_one, "wide", axis=2, tiled=True),
        lax.all_gather(expand_one, "wide", axis=0, tiled=True),
        lax.all_gather(project_one, "wide", axis=0, tiled=True),
        lax.all_gather(gains_one, "wide", axis=0, tiled=True),
    )
    red_a, spa_a, exp_a, proj_a, gain_a = back_one
    gain_af = gain_a.astype(jnp.float32)
    grad_sum_one = silu_grad(sum_one, grad_hidden)
    grad_pre3, gain_g3, shift_g3 = norm_backward(
        grad_sum_one, pre_three, valid_lo, count_lo, gain_af[mid_b:out_a], stat_three
    )
    grad_prep, gain_gp, shift_gp = norm_backward(
        grad_sum_one, pre_proj, valid_lo, count_lo, gain_af[out_a:out_b], stat_proj
    )
    low_three = grad_pre3.astype(jnp.bfloat16)
    low_proj = grad_prep.astype(jnp.bfloat16)
    grad_exp_a = weight_grad(act_two, low_three)
    grad_act2 = input_grad(low_three, exp_a)
    grad_proj_a = weight_grad(sampled, low_proj)
    grad_sampled = input_grad(low_proj, proj_a)
    grad_pre2, gain_g2, shift_g2 = norm_backward(
        silu_grad(y_two, grad_act2), pre_two, valid_lo, count_lo, gain_af[mid_a:mid_b], stat_two
    )
    low_two = grad_pre2.astype(jnp.bfloat16)
    grad_spa_a, grad_act1 = conv_back(act_one, low_two, spa_a, 2)
    grad_pre1, gain_g1, shift_g1 = norm_backward(
        silu_grad(y_one, grad_act1), pre_one, valid_hi, count_hi, gain_af[:mid_a], stat_one
    )
    low_one = grad_pre1.astype(jnp.bfloat16)
    grad_red_a = weight_grad(images, low_one)
    grad_input = input_grad(low_one, red_a)
    grad_input = grad_input.at[:, ::2, ::2].add(grad_sampled)
    grad_images = grad_input.astype(jnp.bfloat16)
    owned_one = (
        lax.psum_scatter(
            grad_red_a.astype(jnp.bfloat16), "wide", scatter_dimension=0, tiled=True
        ).astype(jnp.float32),
        lax.psum_scatter(
            grad_spa_a.astype(jnp.bfloat16), "wide", scatter_dimension=2, tiled=True
        ).astype(jnp.float32),
        lax.psum_scatter(
            grad_exp_a.astype(jnp.bfloat16), "wide", scatter_dimension=0, tiled=True
        ).astype(jnp.float32),
        lax.psum_scatter(
            grad_proj_a.astype(jnp.bfloat16), "wide", scatter_dimension=0, tiled=True
        ).astype(jnp.float32),
    )
    owned_one = (
        lax.psum(owned_one[0].astype(jnp.bfloat16), "dp").astype(jnp.float32),
        lax.psum(owned_one[1].astype(jnp.bfloat16), "dp").astype(jnp.float32),
        lax.psum(owned_one[2].astype(jnp.bfloat16), "dp").astype(jnp.float32),
        lax.psum(owned_one[3].astype(jnp.bfloat16), "dp").astype(jnp.float32),
    )
    gains_grad_a = jnp.concatenate([gain_g1, gain_g2, gain_g3, gain_gp])
    shifts_grad_a = jnp.concatenate([shift_g1, shift_g2, shift_g3, shift_gp])
    gains_grad_b = jnp.concatenate([gain_g4, gain_g5, gain_g6])
    shifts_grad_b = jnp.concatenate([shift_g4, shift_g5, shift_g6])
    local_a = gains_one.shape[0]
    local_b = gains_two.shape[0]
    return (
        activations,
        grad_images,
        owned_one[0],
        owned_one[1],
        owned_one[2],
        owned_one[3],
        own_slice(gains_grad_a, local_a),
        own_slice(shifts_grad_a, local_a),
        owned_two[0],
        owned_two[1],
        owned_two[2],
        own_slice(gains_grad_b, local_b),
        own_slice(shifts_grad_b, local_b),
    )


MESH = pl.DeviceIdType.MESH
F32 = jnp.float32
BF16 = jnp.bfloat16
ALL = slice(None)
NAMES = R1, S1, E1, P1, R2, S2, E2 = range(7)
ROW, TAP, COL = range(3)
KINDS = (ROW, TAP, COL, ROW, ROW, TAP, COL)
NORMS = N1, N2, N3, NP, N4, N5, N6 = range(7)


def nn(left, right):
    return jnp.dot(left, right, preferred_element_type=F32)


def nt(left, right):
    return lax.dot_general(left, right, (((1,), (1,)), ((), ())), preferred_element_type=F32)


def tn(left, right):
    return lax.dot_general(left, right, (((0,), (0,)), ((), ())), preferred_element_type=F32)


def whole_shape(kind, shard):
    if kind == TAP:
        return (shard[0], 4, 2) + tuple(shard[1:])
    return (4, 2) + tuple(shard)


class Links:
    def __init__(self, send_sems, recv_sems, core, base):
        self.send_sems, self.recv_sems = send_sems, recv_sems
        self.dp, self.wide = lax.axis_index("dp"), lax.axis_index("wide")
        self.core = core
        self.y, self.z, self.x = self.dp // 2, self.wide // 2, self.wide % 2
        self.next_send = base

    def device(self, dy=0, dz=0, dx=0, other=False):
        core = 1 - self.core if other else self.core
        y = (self.y + dy) % 2
        z, x = (self.z + dz) % 4, (self.x + dx) % 2
        return {"dp": y * 2 + core, "wide": z * 2 + x}

    def copy(self, src, dst, slot, **to):
        sem = self.send_sems.at[self.next_send]
        self.next_send += 1
        return pltpu.make_async_remote_copy(
            src_ref=src, dst_ref=dst, send_sem=sem, recv_sem=self.recv_sems.at[slot],
            device_id=self.device(**to), device_id_type=MESH)

    def send(self, src, dst, slot, **to):
        made = self.copy(src, dst, slot, **to)
        made.start()
        return made

    def arrived(self, dst, slot):
        pltpu.make_async_remote_copy(
            src_ref=dst, dst_ref=dst, send_sem=self.send_sems.at[0], recv_sem=self.recv_sems.at[slot],
            device_id=self.device(other=True), device_id_type=MESH).wait_recv()


def slot_table(**counts):
    table, at = types.SimpleNamespace(), 0
    for key, count in counts.items():
        setattr(table, key, at)
        at += count
    table.total = at
    return table


T = slot_table(raw=1, mask=1, cot=1, pix=1, xc2=1, act2=1, hlow=1, xc5=1, act5=1, low6=1, low5=1, low4=1, low3=1, lowp=1, low2=1,
               low1=1, gsamp=1, out_act=1, out_norm=1, out_gimg=1, samp_y=1, act1=1, act1_y=1, act4_y=1, low5_y=1, low2_y=1, lowp_y=1,
               out=7, hand=20, gather=100, reduce=72, norm_in=8, sums=12)


def sigmoid(v):
    return 1.0 / (1.0 + jnp.exp(-v))


def silu_back(v, up):
    sg = sigmoid(v)
    return up * sg * (1.0 + v * (1.0 - sg))


def pixel_ids(rows, cols):
    row = lax.broadcasted_iota(jnp.int32, (rows, cols), 0)
    return (row // 8) % 8, row % 8


def shifted(value, di, dj):
    step = di * 8 + dj
    if step == 0:
        return value
    rows, cols = value.shape
    rolled = pltpu.roll(value, (-step) % rows, 0)
    i, j = pixel_ids(rows, cols)
    keep = None
    for index, d in ((i, di), (j, dj)):
        if d == 0:
            continue
        this = index < 8 - d if d > 0 else index >= -d
        keep = this if keep is None else keep & this
    return jnp.where(keep, rolled, 0.0)


A, B, C, D, E = range(5)
PIECES = (
    (R1, 0, 1, B), (S1, 0, 1, C), (S1, 2, 1, C), (S1, 4, 1, C), (S1, 6, 1, C), (S1, 8, 1, D), (E1, 0, 384, C), (E1, 768, 384, B),
    (P1, 0, 512, C), (P1, 512, 512, D), (P1, 1024, 512, D), (R2, 0, 1, B), (R2, 2, 1, D), (S2, 0, 1, A), (S2, 2, 1, D), (S2, 4, 1, A),
    (S2, 6, 1, D), (S2, 8, 1, D), (E2, 0, 384, B), (E2, 768, 384, A))
ACT1 = len(PIECES)
GATHER_PLAN = (
    (13, 0), (0, 0), (15, 0), (19, 0), (1, 0), (2, 0), (3, 0), (0, 1), (4, 0), (1, 1), (5, 0), (2, 1), (6, 0), (0, 2), (7, 0), (1, 2),
    (8, 0), (3, 1), (9, 0), (4, 1), (2, 2), (0, 3), (5, 1), (1, 3), (6, 1), (3, 2), (8, 1), (10, 0), (5, 3), (2, 3), (4, 2), (9, 1),
    (3, 3), (6, 2), (11, 0), (4, 3), (12, 0), (7, 1), (8, 2), (10, 1), (6, 3), (13, 1), (9, 3), (14, 0), (11, 1), (7, 2), (20, 0),
    (15, 1), (8, 3), (10, 3), (12, 1), (16, 0), (7, 3), (11, 2), (17, 0), (12, 3), (14, 1), (13, 2), (18, 0), (19, 1), (11, 3),
    (16, 1), (15, 2), (14, 3), (13, 3), (17, 1), (18, 1), (16, 3), (15, 3), (17, 3), (19, 2), (18, 2), (19, 3), (18, 3))
SUMMED = (
    (E2, 0, 0), (S2, 0, 2), (S2, 2, 2), (S2, 4, 1), (R2, 0, 0), (E1, 0, 0), (P1, 0, 384), (P1, 384, 384), (S1, 0, 2), (S1, 2, 2),
    (S1, 4, 1), (R1, 0, 0))
LOWP = len(SUMMED)
REDUCE_PLAN = (
    (0, 0), (0, 1), (1, 0), (4, 0), (0, 2), (2, 0), (1, 1), (3, 0), (5, 0), (2, 1), (4, 1), (3, 1), (12, 0), (4, 2), (6, 0), (3, 4),
    (0, 3), (1, 2), (2, 2), (5, 1), (0, 4), (1, 4), (4, 3), (2, 4), (6, 1), (7, 0), (11, 0), (4, 4), (5, 2), (8, 0), (7, 1), (9, 0),
    (6, 2), (10, 0), (5, 3), (8, 1), (6, 4), (11, 1), (9, 1), (5, 4), (7, 2), (10, 1), (8, 2), (7, 4), (11, 2), (9, 2), (8, 4),
    (10, 4), (11, 3), (9, 4), (11, 4))


def piece_of(piece, buf, z, x, h):
    name, first, count, order = piece
    kind = KINDS[name]
    if kind == COL or name == P1:
        if kind == COL:
            cols = pl.ds(first, 2 * count) if h is ALL else pl.ds(pl.multiple_of(first + h * count, 128), count)
            return buf.at[z, x, :, cols]
        return buf.at[z, x, h, :, pl.ds(first, count)]
    if name == R1:
        return buf.at[z, x, h]
    part = pl.ds(first, 1) if first == 8 else pl.ds(first, 2) if h is ALL else pl.ds(first + h, 1)
    return buf.at[part, z, x] if kind == TAP else buf.at[z, x, part]


def shard_of(piece, buf, h):
    name, first, count, order = piece
    kind = KINDS[name]
    if kind == COL:
        cols = pl.ds(first, 2 * count) if h is ALL else pl.ds(pl.multiple_of(first + h * count, 128), count)
        return buf.at[:, cols]
    if name == P1:
        return buf.at[h, :, pl.ds(first, count)]
    if name == R1:
        return buf.at[h]
    return buf.at[pl.ds(first, 1) if first == 8 else pl.ds(first, 2) if h is ALL else pl.ds(first + h, 1)]


def columns_of(ref, h):
    return pl.ds(pl.multiple_of(h * (ref.shape[-1] // 2), 128), ref.shape[-1] // 2)


def mover(links, ins, outs, w, g, third, fin, m, credit):
    x, y, z = links.x, links.y, links.z
    pending = []
    local_sems = m.local_sems

    def post(src, dst, slot, **to):
        made = links.send(src, dst, slot, **to)
        pending.append(made)
        return made

    def drain():
        for made in pending:
            made.wait_send()
        pending.clear()

    post(ins.images, m.raw.at[0], T.raw, other=True)
    post(ins.mask, m.mask.at[0], T.mask, other=True)
    own = []
    for n, piece in enumerate(PIECES):
        h = ALL if piece[3] in (D, E) else y
        made = pltpu.make_async_copy(shard_of(piece, ins.weights[piece[0]], h), piece_of(piece, w[piece[0]], z, x, h), local_sems.at[n])
        made.start()
        own.append(made)

    flight = {}

    def along_z(src, dst, slot):
        return [post(src, dst, slot + dz, dz=dz) for dz in (2, 1, 3)]

    def gather(n, stage):
        piece = PIECES[n]
        buf, shard, order, slot = w[piece[0]], ins.weights[piece[0]], piece[3], T.gather + 5 * n
        if stage == 0:
            h = ALL if order in (D, E) else y
            src, dst = shard_of(piece, shard, h), piece_of(piece, buf, z, x, h)
        else:
            if order == A:
                part = (z, ALL, y) if stage == 1 else (ALL, ALL, y)
            elif order == B:
                part = (ALL, x, y) if stage == 1 else (ALL, x, ALL)
            elif order == C:
                part = (ALL, x, y) if stage == 1 else (ALL, ALL, y)
            elif order == D:
                part = (ALL, x, ALL)
            else:
                part = (z, ALL, ALL)
            src = dst = piece_of(piece, buf, *part)
        axis = ((1, 3, 2), (3, 2, 1), (3, 1, 2), (3, 1), (1, 3))[order][stage]
        if axis == 3:
            flight[n] = along_z(src, dst, slot)
        elif axis == 2:
            flight[n] = [post(src, dst, slot + 4, dy=1)]
        else:
            flight[n] = [post(src, dst, slot, dx=1)]

    def landed(n):
        for made in flight[n]:
            made.wait_recv()

    def gathered(n):
        piece = PIECES[n]
        if piece[0] != P1:
            whole = piece_of(piece, w[piece[0]], ALL, ALL, ALL)
            post(whole, whole, T.hand + n, other=True)
            return
        if not m.seen:
            links.arrived(m.pix, T.pix)
            m.seen.append(n)

        def project(step, carry):
            off = pl.multiple_of(piece[1] + step * 256, 256)
            kern = w[P1][:, :, :, :, pl.ds(off, 256)].reshape(1024, 256)
            m.prep[:, pl.ds(off, 256)] = nn(m.pix[0:256, :], kern)
            return carry

        lax.fori_loop(0, 2, project, 0)
        cols = m.prep.at[:, pl.ds(piece[1], 512)]
        post(cols, cols, T.hand + n, other=True)

    waited = False
    for n, stage in GATHER_PLAN:
        if stage and not waited:
            for made in own:
                made.wait()
            waited = True
        if n == ACT1:
            links.arrived(m.act1.at[y], T.act1)
            post(m.act1.at[y], m.act1.at[y], T.act1_y, dy=1)
            continue
        if stage:
            landed(n)
        if stage == 3:
            gathered(n)
        else:
            gather(n, stage)
    post(ins.cotangent, m.cot.at[0], T.cot, other=True)
    drain()

    def allow(which):
        for to in (dict(dx=1), dict(dy=1)):
            pl.semaphore_signal(credit.at[which], inc=1, device_id=links.device(**to), device_id_type=MESH)

    allow(0)
    pl.semaphore_wait(credit.at[0], 2)

    links.arrived(m.act1.at[1 - y], T.act1_y)
    for tap in range(9):
        a, b = tap // 3, tap % 3
        pq = (0 if a == 1 else 2) + (0 if b == 1 else 1)
        block = m.act1[1 - y, pq * 256:pq * 256 + 256, :].astype(F32)
        m.xc2[1 - y, :, tap * 384:(tap + 1) * 384] = shifted(block, -1 if a == 0 else 0, -1 if b == 0 else 0).astype(BF16)
    links.arrived(m.act4.at[1 - y], T.act4_y)
    for tap in range(9):
        block = m.act4[1 - y].astype(F32)
        m.xc5[1 - y, :, tap * 384:(tap + 1) * 384] = shifted(block, tap // 3 - 1, tap % 3 - 1).astype(BF16)

    def add(count, take, other):
        def one(i, carry):
            into = take(i)
            into[...] = (into[...].astype(F32) + other(i)[...].astype(F32)).astype(BF16)
            return carry

        lax.fori_loop(0, count, one, 0)

    def settle(count, take, parts, into):
        def one(i, carry):
            got = take(i)[...].astype(F32)
            for part in parts:
                got = got + part(i)[...].astype(F32)
            into(i)[...] = got.astype(BF16)
            return carry

        lax.fori_loop(0, count, one, 0)

    def scatter_z(n, src_at, name_third, slot):
        flight[n] = [post(src_at((z + dz) % 4), name_third(dz - 1), slot + dz, dz=dz) for dz in (2, 1, 3)]

    def reduce_tap(n, stage, issue):
        name, first, count = SUMMED[n]
        buf, into, slot = g[name], w[name], T.reduce + 6 * n
        part = pl.ds(first, count)

        def tap_of(i):
            return 8 if first == 4 else 2 * (first + i) + y

        if stage == 0 and issue:
            flight[n] = [post(buf.at[part, :, 1 - x], into.at[part, :, 0], slot, dx=1)]
        elif stage == 0:
            add(count * 4, lambda i: buf.at[first + i // 4, i % 4, x], lambda i: into.at[first + i // 4, i % 4, 0])
        elif stage == 1 and issue:
            scatter_z(n, lambda at: buf.at[part, at, x], lambda k: third[name].at[k, part], slot)
        elif stage == 1:
            settle(count, lambda i: buf.at[first + i, z, x], [lambda i, k=k: third[name].at[k, first + i] for k in range(3)],
                   lambda i: fin[name].at[tap_of(i)])
        elif stage == 2 and issue:
            flight[n] = [post(fin[name].at[tap_of(i)], fin[name].at[tap_of(i)], slot + 4 + i, dy=1) for i in range(count)]

    def reduce_project(n, stage, issue):
        name, first, count = SUMMED[n]
        buf, into, slot = g[P1], w[P1], T.reduce + 6 * n
        cols = pl.ds(first, count)
        mine = pl.ds(pl.multiple_of(768 * y + first, 128), count)
        if stage == 0 and issue:
            flight[n] = [post(buf.at[:, 1 - x, :, :, cols], into.at[:, 0, :, :, cols], slot, dx=1)]
        elif stage == 0:
            add(8, lambda i: buf.at[i // 2, x, i % 2, :, cols], lambda i: into.at[i // 2, 0, i % 2, :, cols])
        elif stage == 1 and issue:
            scatter_z(n, lambda at: buf.at[at, x, :, :, cols], lambda k: third[P1].at[k, :, :, cols], slot)
        elif stage == 1:
            settle(2, lambda i: buf.at[z, x, i, :, cols], [lambda i, k=k: third[P1].at[k, i, :, cols] for k in range(3)],
                   lambda i: fin[P1].at[i, :, mine])
        elif stage == 2 and issue:
            flight[n] = [post(fin[P1].at[:, :, mine], fin[P1].at[:, :, mine], slot + 4, dy=1)]

    def reduce_plain(n, stage, issue):
        name = SUMMED[n][0]
        buf, into, slot = g[name], w[name], T.reduce + 6 * n
        if KINDS[name] == COL:
            def half(ref, at, h):
                return ref.at[at + (slice(None), columns_of(ref, h))]
        elif name == R2:
            def half(ref, at, h):
                return ref.at[at + (pl.ds(2 * h, 2),)]
        else:
            def half(ref, at, h):
                return ref.at[at + (pl.ds(h, 1),)]

        if stage == 0 and issue:
            flight[n] = [post(half(buf, (ALL, ALL), 1 - y), half(into, (ALL, ALL), 0), slot + 4, dy=1)]
        elif stage == 0:
            add(8, lambda i: half(buf, (i // 2, i % 2), y), lambda i: half(into, (i // 2, i % 2), 0))
        elif stage == 1 and issue:
            flight[n] = [post(half(buf, (ALL, 1 - x), y), half(into, (ALL, 0), 1), slot, dx=1)]
        elif stage == 1:
            add(4, lambda i: half(buf, (i, x), y), lambda i: half(into, (i, 0), 1))
        elif stage == 2 and issue:
            scatter_z(n, lambda at: half(buf, (at, x), y), lambda k: third[name].at[k], slot)
        elif stage == 2:
            settle(1, lambda i: half(buf, (z, x), y), [lambda i, k=k: third[name].at[k] for k in range(3)],
                   lambda i: half(fin[name], (), y))
        elif stage == 3 and issue:
            flight[n] = [post(half(fin[name], (), y), half(fin[name], (), y), slot + 5, dy=1)]

    def reducer(n):
        name = SUMMED[n][0]
        return reduce_project if name == P1 else reduce_tap if KINDS[name] == TAP else reduce_plain

    def columns(name, left, right):
        def one(step, carry):
            off = pl.multiple_of(step * 256, 256)
            part = tn(left, right[:, pl.ds(off, 256)])
            g[name][..., pl.ds(off, 256)] = part.astype(BF16).reshape(g[name].shape[:-1] + (256,))
            return carry

        lax.fori_loop(0, right.shape[1] // 256, one, 0)

    def taps(name, windows, low):
        def one(k, carry):
            tap = jnp.where(k == 4, 8, 2 * k + y)
            off = pl.multiple_of(tap * 384, 128)
            part = tn(windows[:, :, pl.ds(off, 384)].reshape(512, 384), low[...].reshape(512, 384))
            g[name][k] = part.astype(BF16).reshape(4, 2, 48, 384)
            return carry

        lax.fori_loop(0, 5, one, 0)

    def make(name):
        if name == E2:
            links.arrived(m.act5, T.act5)
            links.arrived(m.low6, T.low6)
            columns(E2, m.act5[...], m.low6)
        elif name == S2:
            links.arrived(m.xc5.at[y], T.xc5)
            links.arrived(m.low5.at[y], T.low5)
            links.arrived(m.low5.at[1 - y], T.low5_y)
            taps(S2, m.xc5, m.low5)
        elif name == R2:
            links.arrived(m.hlow, T.hlow)
            links.arrived(m.low4, T.low4)

            def one(step, carry):
                part = tn(m.hlow[:, pl.ds(pl.multiple_of(step * 384, 128), 384)], m.low4[...])
                g[R2][step] = part.astype(BF16).reshape(2, 4, 48, 384)
                return carry

            lax.fori_loop(0, 4, one, 0)
        elif name == E1:
            links.arrived(m.act2, T.act2)
            links.arrived(m.low3, T.low3)
            columns(E1, m.act2[...], m.low3)
        elif name == P1:
            links.arrived(m.samp.at[1 - y], T.samp_y)
            links.arrived(m.lowp_y, T.lowp_y)
            mine = columns_of(m.lowp, y)

            def one(step, carry):
                cols = pl.ds(pl.multiple_of(step * 256, 256), 256)
                part = tn(m.pix[0:256, cols], m.lowp[:, mine]) + tn(m.samp[1 - y, :, cols], m.lowp_y[...])
                g[P1][step] = part.astype(BF16).reshape(2, 2, 64, 768)
                return carry

            lax.fori_loop(0, 4, one, 0)
            pl.semaphore_wait(credit.at[1], 2)
        elif name == S1:
            links.arrived(m.xc2.at[y], T.xc2)
            links.arrived(m.low2.at[y], T.low2)
            links.arrived(m.low2.at[1 - y], T.low2_y)
            taps(S1, m.xc2, m.low2)
        else:
            links.arrived(m.low1, T.low1)

            def one(step, carry):
                part = tn(m.pix[:, pl.ds(pl.multiple_of(step * 256, 256), 256)], m.low1[...])
                g[R1][step] = part.astype(BF16).reshape(2, 2, 64, 384)
                return carry

            lax.fori_loop(0, 4, one, 0)

    def swap_projection():
        links.arrived(m.lowp, T.lowp)
        theirs = m.lowp.at[:, columns_of(m.lowp, 1 - y)]
        post(theirs, m.lowp_y, T.lowp_y, dy=1)

        def back(step, carry):
            kern = w[P1][step].reshape(256, 1536)
            m.gsamp[:, pl.ds(pl.multiple_of(step * 256, 256), 256)] = nt(m.lowp[...], kern)
            return carry

        lax.fori_loop(0, 4, back, 0)
        allow(1)
        post(m.gsamp, m.gsamp, T.gsamp, other=True)

    made_already = set()
    left = {name: sum(piece[0] == name for piece in SUMMED) for name in NAMES}
    for n, stage in REDUCE_PLAN:
        if n == LOWP:
            swap_projection()
            continue
        name = SUMMED[n][0]
        if name not in made_already:
            made_already.add(name)
            make(name)
        work = reducer(n)
        if stage:
            landed(n)
            last = {reduce_tap: 2, reduce_project: 2, reduce_plain: 3}[work]
            work(n, last if stage == 4 and SUMMED[n][1:] != (4, 1) else 1 if stage == 4 else stage - 1, False)
        if stage < 4:
            work(n, stage, True)
            continue
        left[name] -= 1
        if left[name] == 0:
            made = pltpu.make_async_copy(fin[name], outs.grads[name], local_sems.at[name])
            made.start()
            m.tail.append(made)
            post(fin[name], outs.grads[name], T.out + name, other=True)
    drain()
    for made in m.tail:
        made.wait()
    links.arrived(outs.act, T.out_act)
    links.arrived(outs.norm, T.out_norm)
    links.arrived(outs.gimg, T.out_gimg)


def runner(links, ins, outs, w, m, sums):
    x, y, z = links.x, links.y, links.z
    me = y * 8 + links.wide
    pending = []
    local_sems = m.local_sems

    def post(src, dst, slot, **to):
        made = links.send(src, dst, slot, **to)
        pending.append(made)
        return made

    def hand(ref, slot):
        post(ref, ref, slot, other=True)

    def weight(name):
        for n, piece in enumerate(PIECES):
            if piece[0] == name:
                links.arrived(piece_of(piece, w[name], ALL, ALL, ALL), T.hand + n)

    peers = [(dy, dz, dx) for dz in (2, 1, 3, 0) for dx in (1, 0) for dy in (1, 0) if (dy, dz, dx) != (0, 0, 0)]

    def total(which, rows):
        buf = sums[which]
        for r, row in enumerate(rows):
            buf[me, r:r + 1, :] = row
        slot = T.sums + which
        sem = links.next_send
        links.next_send += 1
        for dy, dz, dx in peers:
            pltpu.make_async_remote_copy(
                src_ref=buf.at[me], dst_ref=buf.at[me], send_sem=links.send_sems.at[sem], recv_sem=links.recv_sems.at[slot],
                device_id=links.device(dy=dy, dz=dz, dx=dx), device_id_type=MESH).start()
        both = pltpu.make_async_remote_copy(
            src_ref=buf.at[pl.ds(0, 15)], dst_ref=buf.at[pl.ds(0, 15)], send_sem=links.send_sems.at[sem],
            recv_sem=links.recv_sems.at[slot], device_id=links.device(other=True), device_id_type=MESH)
        both.wait_recv()
        both.wait_send()
        parts = [buf[i] for i in range(16)]
        while len(parts) > 1:
            parts = [parts[i] + parts[i + 1] for i in range(0, len(parts), 2)]
        return parts[0]

    own_norm = pltpu.make_async_copy(ins.norm, m.norm_in.at[links.wide], local_sems.at[0])
    own_norm.start()
    own_raw = pltpu.make_async_copy(ins.images, m.raw.at[1], local_sems.at[1])
    own_raw.start()
    own_mask = pltpu.make_async_copy(ins.mask, m.mask.at[1], local_sems.at[2])
    own_mask.start()
    own_cot = pltpu.make_async_copy(ins.cotangent, m.cot.at[1], local_sems.at[3])
    own_cot.start()
    for k, (dz, dx) in enumerate([(dz, dx) for dz in (2, 1, 3, 0) for dx in (1, 0) if (dz, dx) != (0, 0)]):
        post(ins.norm, m.norm_in.at[links.wide], T.norm_in + dz * 2 + dx, dz=dz, dx=dx)

    lo = pl.ds(0, 256)
    r = lax.broadcasted_iota(jnp.int32, (256, 256), 0)
    c = lax.broadcasted_iota(jnp.int32, (256, 256), 1)
    source = (2 * ((r // 8) % 8) + r // 128) * 16 + 2 * (r % 8) + (r // 64) % 2
    perm = jnp.where(c == source, 1.0, 0.0).astype(BF16)
    m.perm[...] = perm

    own_mask.wait()
    links.arrived(m.mask.at[0], T.mask)
    flags = m.mask[...].reshape(64, 16).astype(F32)
    for pq in range(4):
        p, q = pq // 2, pq % 2
        row = lax.broadcasted_iota(jnp.int32, (256, 64), 0)
        line = lax.broadcasted_iota(jnp.int32, (256, 64), 1)
        pick = jnp.where(line == (row // 64) * 16 + 2 * ((row // 8) % 8) + p, 1.0, 0.0)
        lines = nn(pick.astype(BF16), flags.astype(BF16))
        row16 = lax.broadcasted_iota(jnp.int32, (256, 16), 0)
        col16 = lax.broadcasted_iota(jnp.int32, (256, 16), 1)
        one = jnp.sum(jnp.where(col16 == 2 * (row16 % 8) + q, lines, 0.0), axis=1, keepdims=True)
        m.valid[pq * 256:(pq + 1) * 256, :] = jnp.broadcast_to(one, (256, 128))

    own_raw.wait()
    links.arrived(m.raw.at[0], T.raw)
    for b in range(4):
        picked = nn(perm, m.raw[b // 2, (b % 2) * 256:(b % 2) * 256 + 256, :]).astype(BF16)
        for pq in range(4):
            m.pix[pq * 256 + b * 64:pq * 256 + b * 64 + 64, :] = picked[pq * 64:pq * 64 + 64, :]
    hand(m.pix, T.pix)
    post(m.pix.at[lo], m.samp.at[y], T.samp_y, dy=1, other=True)

    own_norm.wait()
    for dz in range(4):
        for dx in range(2):
            if dz or dx:
                links.arrived(m.norm_in.at[0], T.norm_in + dz * 2 + dx)
    for s in range(8):
        piece = m.norm_in[s]
        at = 0
        for ref in (m.gain_a, m.shift_a, m.gain_b, m.shift_b):
            size = ref.shape[1] // 8
            ref[:, s * size:(s + 1) * size] = piece[:, at:at + size]
            at += size

    norms = m.norms

    def set_norm(key, mean_sum, square_sum, count, gain, shift):
        ref = norms[key]
        mean = mean_sum / count
        var = square_sum / count - mean * mean
        scaler = lax.rsqrt(var + NORM_EPS)
        ref[0:1, :] = mean
        ref[1:2, :] = scaler
        ref[2:3, :] = gain
        ref[3:4, :] = gain * scaler
        ref[4:5, :] = shift - mean * (gain * scaler)

    def set_back(key, first_sum, second_sum, count, at):
        ref = norms[key]
        mean, scaler, gain = ref[0:1, :], ref[1:2, :], ref[2:3, :]
        centred = second_sum - mean * first_sum
        grad_var = -0.5 * gain * centred * scaler * scaler * scaler
        grad_mean = -gain * scaler * first_sum - 2.0 * mean * grad_var
        ref[5:6, :] = grad_mean / count
        ref[6:7, :] = 2.0 * grad_var / count
        size = ref.shape[1]
        gain_at, shift_at = at
        m.norm_out[:, gain_at:gain_at + size] = scaler * centred
        m.norm_out[:, shift_at:shift_at + size] = first_sum

    def rows_of(key, at, size):
        ref = norms[key]
        return [ref[k:k + 1, pl.ds(at, size)] for k in range(8)]

    def norm_of(key, pre, at, size):
        ref = norms[key]
        return pre * ref[3:4, pl.ds(at, size)] + ref[4:5, pl.ds(at, size)]

    def back_of(key, pre, up, valid, at, size):
        ref = norms[key]
        return ref[3:4, pl.ds(at, size)] * up + valid * (ref[5:6, pl.ds(at, size)] + ref[6:7, pl.ds(at, size)] * pre)

    def valid_of(rows, cols):
        one = m.valid[rows, :]
        return jnp.concatenate([one] * (cols // 128), axis=1) if cols > 128 else one

    def colsum(v):
        return jnp.sum(v, axis=0, keepdims=True)

    stat = m.stat

    def chunks(rows, width, body):
        def one(step, carry):
            return body(pl.ds(pl.multiple_of(step * 64, 64), 64), carry)

        zero = jnp.zeros((1, width), F32)
        return lax.fori_loop(0, rows // 64, one, (zero, zero))

    weight(R1)

    def layer1(step, carry):
        rows = pl.ds(pl.multiple_of(step * 256, 256), 256)
        pre = nn(m.pix[rows, :], w[R1][...].reshape(1024, 384))
        m.pre1[rows, :] = pre
        weighed = pre * valid_of(rows, 384)
        return carry[0] + colsum(weighed), carry[1] + colsum(weighed * pre)

    zero = jnp.zeros((1, 384), F32)
    first, second = lax.fori_loop(0, 4, layer1, (zero, zero))
    hi_here = jnp.concatenate([colsum(m.valid[...])] * 3, axis=1)
    lo_here = jnp.concatenate([colsum(m.valid[lo, :])] * 3, axis=1)
    got = total(0, [first, second, hi_here, lo_here])
    count_hi = jnp.maximum(got[2:3, :], 1.0)
    count_lo = jnp.maximum(got[3:4, :], 1.0)
    count_wide = jnp.concatenate([count_lo] * 4, axis=1)
    set_norm(N1, got[0:1, :], got[1:2, :], count_hi, m.gain_a[:, 0:384], m.shift_a[:, 0:384])

    def activate1(rows, carry):
        v = norm_of(N1, m.pre1[rows, :], 0, 384)
        act = v * sigmoid(v)
        m.up1[rows, :] = act
        m.act1[y, rows, :] = act.astype(BF16)
        return carry

    chunks(1024, 384, activate1)
    hand(m.act1.at[y], T.act1)
    for tap in range(9):
        a, b = tap // 3, tap % 3
        pq = (0 if a == 1 else 2) + (0 if b == 1 else 1)
        block = m.up1[pq * 256:pq * 256 + 256, :]
        block = shifted(block, -1 if a == 0 else 0, -1 if b == 0 else 0)
        m.xc2[y, :, tap * 384:(tap + 1) * 384] = block.astype(BF16)
    hand(m.xc2.at[y], T.xc2)

    def statistics(pre, rows, width):
        weighed = pre * valid_of(rows, width)
        return colsum(weighed), colsum(weighed * pre)

    weight(S1)
    pre = nn(m.xc2[y], w[S1][...].reshape(3456, 384))
    m.pre2[...] = pre
    got = total(1, statistics(pre, lo, 384))
    set_norm(N2, got[0:1, :], got[1:2, :], count_lo, m.gain_a[:, 384:768], m.shift_a[:, 384:768])

    def activate2(rows, carry):
        v = norm_of(N2, m.pre2[rows, :], 0, 384)
        m.act2[rows, :] = (v * sigmoid(v)).astype(BF16)
        return carry

    chunks(256, 384, activate2)
    hand(m.act2, T.act2)

    def wide_loop(body, size=256):
        def one(step, carry):
            body(pl.multiple_of(step * size, size))
            return carry

        lax.fori_loop(0, 1536 // size, one, 0)

    def keep_stats(ref, at, size, k):
        first, second = statistics(ref[:, pl.ds(at, size)], lo, size)
        stat[k:k + 1, pl.ds(at, size)] = first
        stat[k + 1:k + 2, pl.ds(at, size)] = second

    weight(E1)

    def layer3(at):
        m.pre3[:, pl.ds(at, 256)] = nn(m.act2[...], w[E1][:, :, :, pl.ds(at, 256)].reshape(384, 256))
        keep_stats(m.pre3, at, 256, 0)

    wide_loop(layer3)
    for n, piece in enumerate(PIECES):
        if piece[0] == P1:
            links.arrived(m.prep.at[:, pl.ds(piece[1], 512)], T.hand + n)
    wide_loop(lambda at: keep_stats(m.prep, at, 256, 2))
    got = total(2, [stat[k:k + 1, :] for k in range(4)])
    set_norm(N3, got[0:1, :], got[1:2, :], count_wide, m.gain_a[:, 768:2304], m.shift_a[:, 768:2304])
    set_norm(NP, got[2:3, :], got[3:4, :], count_wide, m.gain_a[:, 2304:3840], m.shift_a[:, 2304:3840])

    def sum_one(at, size):
        cols = pl.ds(at, size)
        return norm_of(N3, m.pre3[:, cols], at, size) + norm_of(NP, m.prep[:, cols], at, size)

    def make_hidden(at):
        v = sum_one(at, 128)
        hidden = v * sigmoid(v)
        m.hidden[:, pl.ds(at, 128)] = hidden
        m.hlow[:, pl.ds(at, 128)] = hidden.astype(BF16)

    wide_loop(make_hidden, 128)
    hand(m.hlow, T.hlow)

    weight(R2)
    pre = nn(m.hlow[...], w[R2][...].reshape(1536, 384))
    m.pre4[...] = pre
    got = total(3, statistics(pre, lo, 384))
    set_norm(N4, got[0:1, :], got[1:2, :], count_lo, m.gain_b[:, 0:384], m.shift_b[:, 0:384])

    def activate4(rows, carry):
        v = norm_of(N4, m.pre4[rows, :], 0, 384)
        act = v * sigmoid(v)
        m.small[rows, :] = act
        m.act4[y, rows, :] = act.astype(BF16)
        return carry

    chunks(256, 384, activate4)
    post(m.act4.at[y], m.act4.at[y], T.act4_y, dy=1, other=True)
    for tap in range(9):
        m.xc5[y, :, tap * 384:(tap + 1) * 384] = shifted(m.small[...], tap // 3 - 1, tap % 3 - 1).astype(BF16)
    hand(m.xc5.at[y], T.xc5)
    weight(S2)
    pre = nn(m.xc5[y], w[S2][...].reshape(3456, 384))
    m.pre5[...] = pre
    got = total(4, statistics(pre, lo, 384))
    set_norm(N5, got[0:1, :], got[1:2, :], count_lo, m.gain_b[:, 384:768], m.shift_b[:, 384:768])

    def activate5(rows, carry):
        v = norm_of(N5, m.pre5[rows, :], 0, 384)
        m.act5[rows, :] = (v * sigmoid(v)).astype(BF16)
        return carry

    chunks(256, 384, activate5)
    hand(m.act5, T.act5)
    weight(E2)

    def layer6(at):
        m.pre6[:, pl.ds(at, 256)] = nn(m.act5[...], w[E2][:, :, :, pl.ds(at, 256)].reshape(384, 256))
        keep_stats(m.pre6, at, 256, 0)

    wide_loop(layer6)
    got = total(5, [stat[k:k + 1, :] for k in range(2)])
    set_norm(N6, got[0:1, :], got[1:2, :], count_wide, m.gain_b[:, 768:2304], m.shift_b[:, 768:2304])
    own_cot.wait()
    links.arrived(m.cot.at[0], T.cot)

    def top(at):
        cols = pl.ds(at, 128)
        pre = m.pre6[:, cols]
        v = norm_of(N6, pre, at, 128) + m.hidden[:, cols]
        sg = sigmoid(v)
        m.acts[:, cols] = (v * sg).astype(BF16)
        up = m.cot[:, :, cols].reshape(256, 128).astype(F32)
        up = up * sg * (1.0 + v * (1.0 - sg))
        m.hidden[:, cols] = up
        stat[0:1, cols] = colsum(up)
        stat[1:2, cols] = colsum(up * pre)

    wide_loop(top, 128)
    out_act = pltpu.make_async_copy(m.acts.at[pl.ds(128, 128)], outs.act, local_sems.at[4])
    out_act.start()
    post(m.acts.at[pl.ds(0, 128)], outs.act, T.out_act, other=True)
    got = total(6, [stat[k:k + 1, :] for k in range(2)])
    b_gain, b_shift = 7680, 9984
    set_back(N6, got[0:1, :], got[1:2, :], count_wide, (b_gain + 768, b_shift + 768))

    def low6(at):
        cols = pl.ds(at, 128)
        m.low6[:, cols] = back_of(N6, m.pre6[:, cols], m.hidden[:, cols], valid_of(lo, 128), at, 128).astype(BF16)

    wide_loop(low6, 128)
    hand(m.low6, T.low6)
    m.small[...] = nt(m.low6[...], w[E2][...].reshape(384, 1536))

    def narrow_up(key, pre):
        def one(rows, carry):
            kept = pre[rows, :]
            up = silu_back(norm_of(key, kept, 0, 384), m.small[rows, :])
            m.small[rows, :] = up
            return carry[0] + colsum(up), carry[1] + colsum(up * kept)

        return chunks(256, 384, one)

    def narrow_low(key, pre, low, slot, far=None):
        def one(rows, carry):
            got = back_of(key, pre[rows, :], m.small[rows, :], valid_of(rows, 384), 0, 384)
            m.small[rows, :] = got
            low[rows, :] = got.astype(BF16)
            return carry

        chunks(256, 384, one)
        hand(low, slot)
        if far is not None:
            post(low, low, far, dy=1, other=True)

    got = total(7, narrow_up(N5, m.pre5))
    set_back(N5, got[0:1, :], got[1:2, :], count_lo, (b_gain + 384, b_shift + 384))
    narrow_low(N5, m.pre5, m.low5.at[y], T.low5, T.low5_y)
    grad = jnp.zeros((256, 384), F32)
    for tap in range(9):
        moved = shifted(m.small[...], 1 - tap // 3, 1 - tap % 3).astype(BF16)
        grad = grad + nt(moved, w[S2][tap].reshape(384, 384))
    m.small[...] = grad
    got = total(8, narrow_up(N4, m.pre4))
    set_back(N4, got[0:1, :], got[1:2, :], count_lo, (b_gain, b_shift))
    narrow_low(N4, m.pre4, m.low4, T.low4)

    def below(step, carry):
        at = pl.multiple_of(step * 384, 128)
        cols = pl.ds(at, 384)
        grad = m.hidden[:, cols] + nt(m.low4[...], w[R2][step].reshape(384, 384))
        up = silu_back(sum_one(at, 384), grad)
        m.pre6[:, cols] = up
        stat[0:1, cols] = colsum(up)
        stat[1:2, cols] = colsum(up * m.pre3[:, cols])
        stat[2:3, cols] = colsum(up * m.prep[:, cols])
        return carry

    lax.fori_loop(0, 4, below, 0)
    got = total(9, [stat[k:k + 1, :] for k in range(3)])
    a_gain, a_shift = 0, 3840
    set_back(N3, got[0:1, :], got[1:2, :], count_wide, (a_gain + 768, a_shift + 768))
    set_back(NP, got[0:1, :], got[2:3, :], count_wide, (a_gain + 2304, a_shift + 2304))

    def low3(at):
        cols = pl.ds(at, 128)
        up, valid = m.pre6[:, cols], valid_of(lo, 128)
        m.low3[:, cols] = back_of(N3, m.pre3[:, cols], up, valid, at, 128).astype(BF16)
        m.lowp[:, cols] = back_of(NP, m.prep[:, cols], up, valid, at, 128).astype(BF16)

    wide_loop(low3, 128)
    hand(m.low3, T.low3)
    hand(m.lowp, T.lowp)
    m.small[...] = nt(m.low3[...], w[E1][...].reshape(384, 1536))
    got = total(10, narrow_up(N2, m.pre2))
    set_back(N2, got[0:1, :], got[1:2, :], count_lo, (a_gain + 384, a_shift + 384))
    narrow_low(N2, m.pre2, m.low2.at[y], T.low2, T.low2_y)
    for pq in range(4):
        p, q = pq // 2, pq % 2
        grad = jnp.zeros((256, 384), F32)
        for a in ((1,) if p == 0 else (0, 2)):
            for b in ((1,) if q == 0 else (0, 2)):
                moved = shifted(m.small[...], 1 if a == 0 else 0, 1 if b == 0 else 0).astype(BF16)
                grad = grad + nt(moved, w[S1][a * 3 + b].reshape(384, 384))
        m.up1[pq * 256:pq * 256 + 256, :] = grad

    def up1(rows, carry):
        kept = m.pre1[rows, :]
        up = silu_back(norm_of(N1, kept, 0, 384), m.up1[rows, :])
        m.up1[rows, :] = up
        return carry[0] + colsum(up), carry[1] + colsum(up * kept)

    got = total(11, chunks(1024, 384, up1))
    set_back(N1, got[0:1, :], got[1:2, :], count_hi, (a_gain, a_shift))
    out_norm = pltpu.make_async_copy(m.norm_out, outs.norm, local_sems.at[5])
    out_norm.start()
    post(m.norm_out, outs.norm, T.out_norm, other=True)

    def low1(rows, carry):
        got = back_of(N1, m.pre1[rows, :], m.up1[rows, :], valid_of(rows, 384), 0, 384)
        m.low1[rows, :] = got.astype(BF16)
        return carry

    chunks(1024, 384, low1)
    hand(m.low1, T.low1)
    links.arrived(m.gsamp, T.gsamp)
    for pq in range(4):
        grad = nt(m.low1[pq * 256:pq * 256 + 256, :], w[R1][...].reshape(1024, 384))
        if pq == 0:
            grad = grad + m.gsamp[...]
        m.pixg[pq * 256:pq * 256 + 256, :] = grad.astype(BF16)
    for b in range(4):
        block = jnp.concatenate([m.pixg[pq * 256 + b * 64:pq * 256 + b * 64 + 64, :] for pq in range(4)], axis=0)
        m.raw[b // 2, (b % 2) * 256:(b % 2) * 256 + 256, :] = tn(m.perm[...], block).astype(BF16)
    out_img = pltpu.make_async_copy(m.raw.at[1], outs.gimg, local_sems.at[6])
    out_img.start()
    post(m.raw.at[0], outs.gimg, T.out_gimg, other=True)
    for name in NAMES:
        links.arrived(outs.grads[name], T.out + name)
    out_act.wait()
    out_norm.wait()
    out_img.wait()
    for made in pending:
        made.wait_send()


SUM_ROWS = ((4, 384), (2, 384), (4, 1536), (2, 384), (2, 384), (2, 1536), (2, 1536), (2, 384), (2, 384), (3, 1536), (2, 384), (2, 384))


def fused_kernel(sizes, keys, *refs):
    groups, at = [], 0
    for size in sizes:
        groups.append(refs[at:at + size])
        at += size
    taken, shards_in, given, made, w, g, fin, third, kept, norms, sums, rest = groups
    dp, wide = lax.axis_index("dp"), lax.axis_index("wide")
    core = dp % 2
    send_sems, recv_sems, local_sems, credit = rest
    barrier = pltpu.get_barrier_semaphore()
    greet = Links(send_sems, recv_sems, core, 0)
    everyone = [dict(other=True), dict(dy=1, other=True)] + [
        dict(dy=dy, dz=dz, dx=dx) for dy in (0, 1) for dz in range(4) for dx in (0, 1) if (dy, dz, dx) != (0, 0, 0)]
    for to in everyone:
        pl.semaphore_signal(barrier, inc=1, device_id=greet.device(**to), device_id_type=MESH)
    pl.semaphore_wait(barrier, len(everyone))

    images, mask, cotangent, norm = taken
    act, gimg, norm_out = given
    ins = types.SimpleNamespace(images=images, mask=mask, cotangent=cotangent, norm=norm, weights=shards_in)
    outs = types.SimpleNamespace(act=act, gimg=gimg, norm=norm_out, grads=made)
    m = types.SimpleNamespace(**dict(zip(keys, kept)), norms=norms, local_sems=local_sems, tail=[], seen=[])

    @pl.when(core == 0)
    def _():
        mover(Links(send_sems, recv_sems, 0, 1), ins, outs, w, g, third, fin, m, credit)

    @pl.when(core == 1)
    def _():
        runner(Links(send_sems, recv_sems, 1, 1), ins, outs, w, m, sums)


def fused_shards(images, pixel_mask, cotangent, reduce_one, spatial_one, expand_one, project_one, gains_one, shifts_one,
                 reduce_two, spatial_two, expand_two, gains_two, shifts_two):
    def split(weight, parts=2):
        return weight.reshape(parts, weight.shape[0] // parts, weight.shape[1])

    def join(weight):
        return weight.reshape(9, weight.shape[2], weight.shape[3])

    weights = (split(reduce_one), join(spatial_one), expand_one, split(project_one), split(reduce_two, 4), join(spatial_two), expand_two)
    norm = jnp.concatenate([gains_one, shifts_one, gains_two, shifts_two]).astype(F32).reshape(1, -1)
    taken = [images.reshape(512, 1024), pixel_mask.reshape(32, 16), cotangent.reshape(128, 1536), norm]
    given = [jax.ShapeDtypeStruct((128, 1536), BF16), jax.ShapeDtypeStruct((512, 1024), BF16), jax.ShapeDtypeStruct((1, 12288), F32)]
    made = [jax.ShapeDtypeStruct(v.shape, BF16) for v in weights]
    whole = [pltpu.VMEM(whole_shape(KINDS[n], v.shape), BF16) for n, v in enumerate(weights)]
    fin = [pltpu.VMEM(v.shape, BF16) for v in weights]
    partial = list(whole)
    partial[S1] = partial[S2] = pltpu.VMEM((5, 4, 2, 48, 384), BF16)
    partial[P1] = pltpu.VMEM((4, 2, 2, 64, 768), BF16)
    halves = ((1, 64, 384), (5, 48, 384), (48, 768), (2, 64, 768), (2, 48, 384), (5, 48, 384), (48, 768))
    third = [pltpu.VMEM((3,) + half, BF16) for half in halves]
    bf = dict(raw=(2, 512, 1024), cot=(2, 128, 1536), pix=(1024, 1024), perm=(256, 256), xc2=(2, 256, 3456), xc5=(2, 256, 3456),
              act2=(256, 384), act5=(256, 384), hlow=(256, 1536), acts=(256, 1536), low6=(256, 1536), low5=(2, 256, 384), low4=(256, 384),
              low3=(256, 1536), lowp=(256, 1536), low2=(2, 256, 384), low1=(1024, 384), pixg=(1024, 1024),
              samp=(2, 256, 1024), act1=(2, 1024, 384), act4=(2, 256, 384), lowp_y=(256, 768))
    f32 = dict(norm_in=(8, 1, 1536), gain_a=(1, 3840), shift_a=(1, 3840), gain_b=(1, 2304), shift_b=(1, 2304), norm_out=(1, 12288),
               valid=(1024, 128), stat=(8, 1536), pre1=(1024, 384), up1=(1024, 384), pre2=(256, 384), pre3=(256, 1536), prep=(256, 1536),
               hidden=(256, 1536), pre4=(256, 384), pre5=(256, 384), pre6=(256, 1536), small=(256, 384), gsamp=(256, 1024))
    kept = {k: pltpu.VMEM(v, BF16) for k, v in bf.items()} | {k: pltpu.VMEM(v, F32) for k, v in f32.items()}
    kept |= dict(mask=pltpu.VMEM((2, 32, 16), jnp.int32))
    norms = [pltpu.VMEM((8, width), F32) for width in (384, 384, 1536, 1536, 384, 384, 1536)]
    sums = [pltpu.VMEM((16, rows, width), F32) for rows, width in SUM_ROWS]
    rest = [pltpu.SemaphoreType.DMA((256,)), pltpu.SemaphoreType.DMA((T.total,)), pltpu.SemaphoreType.DMA((24,)),
            pltpu.SemaphoreType.REGULAR((2,))]
    groups = [taken, weights, given, made, whole, partial, fin, third, list(kept.values()), norms, sums, rest]
    anywhere = pl.BlockSpec(memory_space=pl.ANY)
    got = pl.pallas_call(
        functools.partial(fused_kernel, [len(group) for group in groups], list(kept)),
        out_shape=given + made,
        in_specs=[anywhere] * (len(taken) + len(weights)),
        out_specs=[anywhere] * (len(given) + len(made)),
        scratch_shapes=[v for group in groups[4:] for v in group],
        compiler_params=pltpu.CompilerParams(collective_id=0, has_side_effects=True, vmem_limit_bytes=63 * 2**20),
    )(*taken, *weights)
    act, gimg, norms, *grads = got
    grads = [v.astype(F32).reshape(like.shape) for v, like in zip(
        grads, (reduce_one, spatial_one, expand_one, project_one, reduce_two, spatial_two, expand_two))]
    flat = norms.reshape(-1)
    local_a, local_b = gains_one.shape[0], gains_two.shape[0]
    return (
        act.reshape(cotangent.shape),
        gimg.reshape(images.shape),
        grads[0], grads[1], grads[2], grads[3],
        own_slice(flat[:3840], local_a),
        own_slice(flat[3840:7680], local_a),
        grads[4], grads[5], grads[6],
        own_slice(flat[7680:9984], local_b),
        own_slice(flat[9984:], local_b),
    )


def solution(mesh):
    fused = mesh.shape["dp"] == 4 and mesh.shape["wide"] == 8
    in_specs = (
        P(("dp", "wide"), None, None, None),
        P(("dp", "wide"), None, None),
        P(("dp", "wide"), None, None, None),
        P("wide", None),
        P(None, None, "wide", None),
        P("wide", None),
        P("wide", None),
        P("wide"),
        P("wide"),
        P("wide", None),
        P(None, None, "wide", None),
        P("wide", None),
        P("wide"),
        P("wide"),
    )
    out_specs = (
        P(("dp", "wide"), None, None, None),
        P(("dp", "wide"), None, None, None),
        P("wide", None),
        P(None, None, "wide", None),
        P("wide", None),
        P("wide", None),
        P("wide"),
        P("wide"),
        P("wide", None),
        P(None, None, "wide", None),
        P("wide", None),
        P("wide"),
        P("wide"),
    )
    return jax.shard_map(fused_shards if fused else shards, mesh=mesh, in_specs=in_specs, out_specs=out_specs, check_vma=False)
```

```python
import functools
import types

import jax
import jax.numpy as jnp
from jax import lax
from jax.experimental import pallas as pl
from jax.experimental.pallas import tpu as pltpu
from jax.sharding import PartitionSpec as P

NORM_EPS = 1e-05


def pixel_product(source, kernel):
    return jnp.einsum("bhwc,co->bhwo", source, kernel, preferred_element_type=jnp.float32)


def weight_grad(source, upstream):
    return jnp.einsum("bhwc,bhwo->co", source, upstream, preferred_element_type=jnp.float32)


def input_grad(upstream, kernel):
    return jnp.einsum("bhwo,co->bhwc", upstream, kernel, preferred_element_type=jnp.float32)


def conv_spatial(source, kernel, stride):
    out_h = source.shape[1] // stride
    out_w = source.shape[2] // stride
    padded = jnp.pad(source, ((0, 0), (1, 1), (1, 1), (0, 0)))
    summed = jnp.zeros((source.shape[0], out_h, out_w, kernel.shape[3]), jnp.float32)
    for row_off in range(3):
        for col_off in range(3):
            window = padded[
                :,
                row_off : row_off + stride * out_h : stride,
                col_off : col_off + stride * out_w : stride,
            ]
            summed = summed + pixel_product(window, kernel[row_off, col_off])
    return summed


def conv_back(source, upstream, kernel, stride):
    out_h = upstream.shape[1]
    out_w = upstream.shape[2]
    padded = jnp.pad(source, ((0, 0), (1, 1), (1, 1), (0, 0)))
    grad_src = jnp.zeros(padded.shape, jnp.float32)
    kernel_rows = []
    for row_off in range(3):
        for col_off in range(3):
            window = padded[
                :,
                row_off : row_off + stride * out_h : stride,
                col_off : col_off + stride * out_w : stride,
            ]
            kernel_rows.append(weight_grad(window, upstream))
            grad_src = grad_src.at[
                :,
                row_off : row_off + stride * out_h : stride,
                col_off : col_off + stride * out_w : stride,
            ].add(input_grad(upstream, kernel[row_off, col_off]))
    kernel_grad = jnp.stack(kernel_rows).reshape(kernel.shape)
    return (kernel_grad, grad_src[:, 1:-1, 1:-1])


def norm_forward(pre, valid, count, gain, shift):
    moments = lax.psum(
        (jnp.sum(pre * valid, axis=(0, 1, 2)), jnp.sum(pre * pre * valid, axis=(0, 1, 2))),
        ("dp", "wide"),
    )
    mean_val = moments[0] / count
    variance = moments[1] / count - mean_val * mean_val
    scaler = lax.rsqrt(variance + NORM_EPS)
    normed = (pre - mean_val) * scaler
    return (gain * normed + shift, (mean_val, scaler))


def norm_backward(upstream, pre, valid, count, gain, stats):
    mean_val, scaler = stats
    sums = lax.psum(
        (jnp.sum(upstream, axis=(0, 1, 2)), jnp.sum(upstream * pre, axis=(0, 1, 2))), ("dp", "wide")
    )
    first_sum, second_sum = sums
    centred = second_sum - mean_val * first_sum
    grad_gain = scaler * centred
    grad_var = -0.5 * gain * centred * scaler * scaler * scaler
    grad_mean = -gain * scaler * first_sum - 2.0 * mean_val * grad_var
    grad_pre = gain * scaler * upstream + valid / count * (grad_mean + 2.0 * pre * grad_var)
    return (grad_pre, grad_gain, first_sum)


def silu_grad(pre_act, upstream):
    sigma = jax.nn.sigmoid(pre_act)
    return upstream * sigma * (1.0 + pre_act * (1.0 - sigma))


def own_slice(whole, local_len):
    start = lax.axis_index("wide") * local_len
    return lax.dynamic_slice_in_dim(whole, start, local_len, 0)


def shards(
    images,
    pixel_mask,
    cotangent,
    reduce_one,
    spatial_one,
    expand_one,
    project_one,
    gains_one,
    shifts_one,
    reduce_two,
    spatial_two,
    expand_two,
    gains_two,
    shifts_two,
):
    valid_hi = pixel_mask.astype(jnp.float32)[..., None]
    valid_lo = valid_hi[:, ::2, ::2]
    counts = lax.psum((jnp.sum(valid_hi), jnp.sum(valid_lo)), ("dp", "wide"))
    count_hi = jnp.maximum(counts[0], 1.0)
    count_lo = jnp.maximum(counts[1], 1.0)
    first_full = (
        lax.all_gather(reduce_one, "wide", axis=0, tiled=True),
        lax.all_gather(spatial_one, "wide", axis=2, tiled=True),
        lax.all_gather(expand_one, "wide", axis=0, tiled=True),
        lax.all_gather(project_one, "wide", axis=0, tiled=True),
        lax.all_gather(gains_one, "wide", axis=0, tiled=True),
        lax.all_gather(shifts_one, "wide", axis=0, tiled=True),
    )
    red_a, spa_a, exp_a, proj_a, gain_a, shift_a = first_full
    mid_a = red_a.shape[1]
    mid_b = 2 * mid_a
    out_a = mid_b + exp_a.shape[1]
    out_b = out_a + exp_a.shape[1]
    gain_af = gain_a.astype(jnp.float32)
    shift_af = shift_a.astype(jnp.float32)
    pre_one = pixel_product(images, red_a)
    y_one, stat_one = norm_forward(pre_one, valid_hi, count_hi, gain_af[:mid_a], shift_af[:mid_a])
    act_one = jax.nn.silu(y_one).astype(jnp.bfloat16)
    pre_two = conv_spatial(act_one, spa_a, 2)
    y_two, stat_two = norm_forward(
        pre_two, valid_lo, count_lo, gain_af[mid_a:mid_b], shift_af[mid_a:mid_b]
    )
    act_two = jax.nn.silu(y_two).astype(jnp.bfloat16)
    pre_three = pixel_product(act_two, exp_a)
    y_three, stat_three = norm_forward(
        pre_three, valid_lo, count_lo, gain_af[mid_b:out_a], shift_af[mid_b:out_a]
    )
    sampled = images[:, ::2, ::2]
    pre_proj = pixel_product(sampled, proj_a)
    y_proj, stat_proj = norm_forward(
        pre_proj, valid_lo, count_lo, gain_af[out_a:out_b], shift_af[out_a:out_b]
    )
    sum_one = y_three + y_proj
    hidden = jax.nn.silu(sum_one)
    hidden_low = hidden.astype(jnp.bfloat16)
    second_full = (
        lax.all_gather(reduce_two, "wide", axis=0, tiled=True),
        lax.all_gather(spatial_two, "wide", axis=2, tiled=True),
        lax.all_gather(expand_two, "wide", axis=0, tiled=True),
        lax.all_gather(gains_two, "wide", axis=0, tiled=True),
        lax.all_gather(shifts_two, "wide", axis=0, tiled=True),
    )
    red_b, spa_b, exp_b, gain_b, shift_b = second_full
    gain_bf = gain_b.astype(jnp.float32)
    shift_bf = shift_b.astype(jnp.float32)
    pre_four = pixel_product(hidden_low, red_b)
    y_four, stat_four = norm_forward(
        pre_four, valid_lo, count_lo, gain_bf[:mid_a], shift_bf[:mid_a]
    )
    act_four = jax.nn.silu(y_four).astype(jnp.bfloat16)
    pre_five = conv_spatial(act_four, spa_b, 1)
    y_five, stat_five = norm_forward(
        pre_five, valid_lo, count_lo, gain_bf[mid_a:mid_b], shift_bf[mid_a:mid_b]
    )
    act_five = jax.nn.silu(y_five).astype(jnp.bfloat16)
    pre_six = pixel_product(act_five, exp_b)
    y_six, stat_six = norm_forward(
        pre_six, valid_lo, count_lo, gain_bf[mid_b:out_a], shift_bf[mid_b:out_a]
    )
    sum_two = y_six + hidden
    activations = jax.nn.silu(sum_two).astype(jnp.bfloat16)
    back_two = (
        lax.all_gather(reduce_two, "wide", axis=0, tiled=True),
        lax.all_gather(spatial_two, "wide", axis=2, tiled=True),
        lax.all_gather(expand_two, "wide", axis=0, tiled=True),
        lax.all_gather(gains_two, "wide", axis=0, tiled=True),
    )
    red_b, spa_b, exp_b, gain_b = back_two
    gain_bf = gain_b.astype(jnp.float32)
    upstream = cotangent.astype(jnp.float32)
    grad_sum_two = silu_grad(sum_two, upstream)
    grad_pre6, gain_g6, shift_g6 = norm_backward(
        grad_sum_two, pre_six, valid_lo, count_lo, gain_bf[mid_b:out_a], stat_six
    )
    low_six = grad_pre6.astype(jnp.bfloat16)
    grad_exp_b = weight_grad(act_five, low_six)
    grad_act5 = input_grad(low_six, exp_b)
    grad_pre5, gain_g5, shift_g5 = norm_backward(
        silu_grad(y_five, grad_act5), pre_five, valid_lo, count_lo, gain_bf[mid_a:mid_b], stat_five
    )
    low_five = grad_pre5.astype(jnp.bfloat16)
    grad_spa_b, grad_act4 = conv_back(act_four, low_five, spa_b, 1)
    grad_pre4, gain_g4, shift_g4 = norm_backward(
        silu_grad(y_four, grad_act4), pre_four, valid_lo, count_lo, gain_bf[:mid_a], stat_four
    )
    low_four = grad_pre4.astype(jnp.bfloat16)
    grad_red_b = weight_grad(hidden_low, low_four)
    grad_hidden = grad_sum_two + input_grad(low_four, red_b)
    owned_two = (
        lax.psum_scatter(
            grad_red_b.astype(jnp.bfloat16), "wide", scatter_dimension=0, tiled=True
        ).astype(jnp.float32),
        lax.psum_scatter(
            grad_spa_b.astype(jnp.bfloat16), "wide", scatter_dimension=2, tiled=True
        ).astype(jnp.float32),
        lax.psum_scatter(
            grad_exp_b.astype(jnp.bfloat16), "wide", scatter_dimension=0, tiled=True
        ).astype(jnp.float32),
    )
    owned_two = (
        lax.psum(owned_two[0].astype(jnp.bfloat16), "dp").astype(jnp.float32),
        lax.psum(owned_two[1].astype(jnp.bfloat16), "dp").astype(jnp.float32),
        lax.psum(owned_two[2].astype(jnp.bfloat16), "dp").astype(jnp.float32),
    )
    back_one = (
        lax.all_gather(reduce_one, "wide", axis=0, tiled=True),
        lax.all_gather(spatial_one, "wide", axis=2, tiled=True),
        lax.all_gather(expand_one, "wide", axis=0, tiled=True),
        lax.all_gather(project_one, "wide", axis=0, tiled=True),
        lax.all_gather(gains_one, "wide", axis=0, tiled=True),
    )
    red_a, spa_a, exp_a, proj_a, gain_a = back_one
    gain_af = gain_a.astype(jnp.float32)
    grad_sum_one = silu_grad(sum_one, grad_hidden)
    grad_pre3, gain_g3, shift_g3 = norm_backward(
        grad_sum_one, pre_three, valid_lo, count_lo, gain_af[mid_b:out_a], stat_three
    )
    grad_prep, gain_gp, shift_gp = norm_backward(
        grad_sum_one, pre_proj, valid_lo, count_lo, gain_af[out_a:out_b], stat_proj
    )
    low_three = grad_pre3.astype(jnp.bfloat16)
    low_proj = grad_prep.astype(jnp.bfloat16)
    grad_exp_a = weight_grad(act_two, low_three)
    grad_act2 = input_grad(low_three, exp_a)
    grad_proj_a = weight_grad(sampled, low_proj)
    grad_sampled = input_grad(low_proj, proj_a)
    grad_pre2, gain_g2, shift_g2 = norm_backward(
        silu_grad(y_two, grad_act2), pre_two, valid_lo, count_lo, gain_af[mid_a:mid_b], stat_two
    )
    low_two = grad_pre2.astype(jnp.bfloat16)
    grad_spa_a, grad_act1 = conv_back(act_one, low_two, spa_a, 2)
    grad_pre1, gain_g1, shift_g1 = norm_backward(
        silu_grad(y_one, grad_act1), pre_one, valid_hi, count_hi, gain_af[:mid_a], stat_one
    )
    low_one = grad_pre1.astype(jnp.bfloat16)
    grad_red_a = weight_grad(images, low_one)
    grad_input = input_grad(low_one, red_a)
    grad_input = grad_input.at[:, ::2, ::2].add(grad_sampled)
    grad_images = grad_input.astype(jnp.bfloat16)
    owned_one = (
        lax.psum_scatter(
            grad_red_a.astype(jnp.bfloat16), "wide", scatter_dimension=0, tiled=True
        ).astype(jnp.float32),
        lax.psum_scatter(
            grad_spa_a.astype(jnp.bfloat16), "wide", scatter_dimension=2, tiled=True
        ).astype(jnp.float32),
        lax.psum_scatter(
            grad_exp_a.astype(jnp.bfloat16), "wide", scatter_dimension=0, tiled=True
        ).astype(jnp.float32),
        lax.psum_scatter(
            grad_proj_a.astype(jnp.bfloat16), "wide", scatter_dimension=0, tiled=True
        ).astype(jnp.float32),
    )
    owned_one = (
        lax.psum(owned_one[0].astype(jnp.bfloat16), "dp").astype(jnp.float32),
        lax.psum(owned_one[1].astype(jnp.bfloat16), "dp").astype(jnp.float32),
        lax.psum(owned_one[2].astype(jnp.bfloat16), "dp").astype(jnp.float32),
        lax.psum(owned_one[3].astype(jnp.bfloat16), "dp").astype(jnp.float32),
    )
    gains_grad_a = jnp.concatenate([gain_g1, gain_g2, gain_g3, gain_gp])
    shifts_grad_a = jnp.concatenate([shift_g1, shift_g2, shift_g3, shift_gp])
    gains_grad_b = jnp.concatenate([gain_g4, gain_g5, gain_g6])
    shifts_grad_b = jnp.concatenate([shift_g4, shift_g5, shift_g6])
    local_a = gains_one.shape[0]
    local_b = gains_two.shape[0]
    return (
        activations,
        grad_images,
        owned_one[0],
        owned_one[1],
        owned_one[2],
        owned_one[3],
        own_slice(gains_grad_a, local_a),
        own_slice(shifts_grad_a, local_a),
        owned_two[0],
        owned_two[1],
        owned_two[2],
        own_slice(gains_grad_b, local_b),
        own_slice(shifts_grad_b, local_b),
    )


MESH = pl.DeviceIdType.MESH
F32 = jnp.float32
BF16 = jnp.bfloat16
ALL = slice(None)
NAMES = R1, S1, E1, P1, R2, S2, E2 = range(7)
ROW, TAP, COL = range(3)
KINDS = (ROW, TAP, COL, ROW, ROW, TAP, COL)
NORMS = N1, N2, N3, NP, N4, N5, N6 = range(7)


def nn(left, right):
    return jnp.dot(left, right, preferred_element_type=F32)


def nt(left, right):
    return lax.dot_general(left, right, (((1,), (1,)), ((), ())), preferred_element_type=F32)


def tn(left, right):
    return lax.dot_general(left, right, (((0,), (0,)), ((), ())), preferred_element_type=F32)


def whole_shape(kind, shard):
    if kind == TAP:
        return (shard[0], 4, 2) + tuple(shard[1:])
    return (4, 2) + tuple(shard)


class Links:
    def __init__(self, send_sems, recv_sems, core, base):
        self.send_sems, self.recv_sems = send_sems, recv_sems
        self.dp, self.wide = lax.axis_index("dp"), lax.axis_index("wide")
        self.core = core
        self.y, self.z, self.x = self.dp // 2, self.wide // 2, self.wide % 2
        self.next_send = base

    def device(self, dy=0, dz=0, dx=0, other=False):
        core = 1 - self.core if other else self.core
        y = (self.y + dy) % 2
        z, x = (self.z + dz) % 4, (self.x + dx) % 2
        return {"dp": y * 2 + core, "wide": z * 2 + x}

    def copy(self, src, dst, slot, **to):
        sem = self.send_sems.at[self.next_send]
        self.next_send += 1
        return pltpu.make_async_remote_copy(
            src_ref=src, dst_ref=dst, send_sem=sem, recv_sem=self.recv_sems.at[slot],
            device_id=self.device(**to), device_id_type=MESH)

    def send(self, src, dst, slot, **to):
        made = self.copy(src, dst, slot, **to)
        made.start()
        return made

    def arrived(self, dst, slot):
        pltpu.make_async_remote_copy(
            src_ref=dst, dst_ref=dst, send_sem=self.send_sems.at[0], recv_sem=self.recv_sems.at[slot],
            device_id=self.device(other=True), device_id_type=MESH).wait_recv()


def slot_table(**counts):
    table, at = types.SimpleNamespace(), 0
    for key, count in counts.items():
        setattr(table, key, at)
        at += count
    table.total = at
    return table


T = slot_table(raw=1, mask=1, cot=1, pix=1, xc2=1, act2=1, hlow=1, xc5=1, act5=1, low6=1, low5=1, low4=1, low3=1, lowp=1, low2=1,
               low1=1, gsamp=1, out_act=1, out_norm=1, out_gimg=1, samp_y=1, act1=1, act1_y=1, act4_y=1, low5_y=1, low2_y=1, lowp_y=1,
               out=7, hand=32, gather=5 * 32, reduce=6 * 16, norm_in=8, sums=12)


def sigmoid(v):
    return 1.0 / (1.0 + jnp.exp(-v))


def silu_back(v, up):
    sg = sigmoid(v)
    return up * sg * (1.0 + v * (1.0 - sg))


def pixel_ids(rows, cols):
    row = lax.broadcasted_iota(jnp.int32, (rows, cols), 0)
    return (row // 8) % 8, row % 8


def shifted(value, di, dj):
    step = di * 8 + dj
    if step == 0:
        return value
    rows, cols = value.shape
    rolled = pltpu.roll(value, (-step) % rows, 0)
    i, j = pixel_ids(rows, cols)
    keep = None
    for index, d in ((i, di), (j, dj)):
        if d == 0:
            continue
        this = index < 8 - d if d > 0 else index >= -d
        keep = this if keep is None else keep & this
    return jnp.where(keep, rolled, 0.0)


A, B, C, D, E = range(5)
PIECES = (
    (R1, 0, 1, C), (S1, 0, 1, A), (S1, 2, 1, C), (S1, 4, 1, B), (S1, 6, 1, B), (S1, 8, 1, D), (E1, 0, 384, B), (E1, 768, 384, B),
    (P1, 0, 512, B), (P1, 512, 512, B), (P1, 1024, 512, A), (R2, 0, 1, D), (R2, 2, 1, E), (S2, 0, 1, B), (S2, 2, 1, B), (S2, 4, 1,
    A), (S2, 6, 1, B), (S2, 8, 1, E), (E2, 0, 384, C), (E2, 768, 384, B))
GATHER_PLAN = (
    (3, 0), (0, 0), (7, 0), (4, 0), (10, 0), (12, 0), (15, 0), (3, 1), (2, 0), (1, 0), (8, 0), (0, 1), (5, 0), (7, 1), (3, 2), (6,
    0), (4, 1), (9, 0), (0, 2), (1, 1), (2, 1), (7, 2), (4, 2), (10, 1), (8, 1), (3, 3), (2, 2), (6, 1), (0, 3), (13, 0), (5, 1),
    (7, 3), (9, 1), (14, 0), (8, 2), (4, 3), (1, 2), (5, 3), (11, 0), (2, 3), (6, 2), (16, 0), (9, 2), (10, 2), (15, 1), (12, 1),
    (8, 3), (13, 1), (1, 3), (6, 3), (19, 0), (18, 0), (17, 0), (14, 1), (11, 1), (10, 3), (9, 3), (13, 2), (11, 3), (14, 2), (17,
    1), (16, 1), (15, 2), (13, 3), (12, 3), (16, 2), (14, 3), (19, 1), (18, 1), (15, 3), (17, 3), (16, 3), (19, 2), (18, 2), (19,
    3), (18, 3))
MAKE, OTHER = -1, -2
SUMMED = (
    (E2, 0, 384, (3, 2, 1)), (E2, 768, 384, (1, 3, 2)), (R2, 0, 2, (1, 2, 3)), (E1, 0, 384, (1, 2, 3)), (E1, 768, 384, (1, 3, 2)),
    (R1, 0, 1, (2, 1, 3)), (S2, 0, 2, (3, 1)), (S2, 2, 2, (3, 1)), (S2, 4, 1, (3, 1)), (S1, 0, 2, (1, 3)), (S1, 2, 2, (1, 3)),
    (S1, 4, 1, (1, 3)), (P1, 0, 256, (1, 3)), (P1, 256, 256, (1, 3)), (P1, 512, 256, (1, 3)))
REDUCE_PLAN = (
    (OTHER, 1), (MAKE, E2), (0, 0), (OTHER, 0), (1, 0), (1, 1), (MAKE, S2), (7, 0), (MAKE, R2), (2, 0), (0, 1), (6, 0), (MAKE,
    E1), (1, 2), (4, 0), (OTHER, 2), (OTHER, 3), (3, 0), (2, 1), (7, 1), (1, 3), (8, 0), (4, 1), (MAKE, P1), (12, 0), (3, 1), (2,
    2), (MAKE, R1), (14, 0), (MAKE, S1), (13, 0), (3, 2), (12, 1), (0, 2), (5, 0), (14, 1), (10, 0), (0, 3), (3, 3), (9, 0), (13,
    1), (1, 4), (12, 2), (5, 1), (10, 1), (4, 2), (8, 1), (12, 3), (9, 1), (2, 3), (11, 0), (5, 2), (7, 2), (14, 2), (6, 1), (8,
    2), (10, 2), (13, 2), (4, 3), (2, 4), (11, 1), (0, 4), (9, 2), (3, 4), (6, 2), (5, 3), (10, 3), (4, 4), (6, 3), (13, 3), (7,
    3), (14, 3), (9, 3), (11, 2), (5, 4))
def piece_of(piece, buf, z, x, h):
    name, first, count, order = piece
    kind = KINDS[name]
    if kind == COL or name == P1:
        if kind == COL:
            cols = pl.ds(first, 2 * count) if h is ALL else pl.ds(pl.multiple_of(first + h * count, 128), count)
            return buf.at[z, x, :, cols]
        return buf.at[z, x, h, :, pl.ds(first, count)]
    if name == R1:
        return buf.at[z, x, h]
    part = pl.ds(first, 1) if first == 8 else pl.ds(first, 2) if h is ALL else pl.ds(first + h, 1)
    return buf.at[part, z, x] if kind == TAP else buf.at[z, x, part]


def shard_of(piece, buf, h):
    name, first, count, order = piece
    kind = KINDS[name]
    if kind == COL:
        cols = pl.ds(first, 2 * count) if h is ALL else pl.ds(pl.multiple_of(first + h * count, 128), count)
        return buf.at[:, cols]
    if name == P1:
        return buf.at[h, :, pl.ds(first, count)]
    if name == R1:
        return buf.at[h]
    return buf.at[pl.ds(first, 1) if first == 8 else pl.ds(first, 2) if h is ALL else pl.ds(first + h, 1)]


def columns_of(ref, h):
    return pl.ds(pl.multiple_of(h * (ref.shape[-1] // 2), 128), ref.shape[-1] // 2)


def mover(links, ins, outs, w, g, third, fin, m, credit):
    x, y, z = links.x, links.y, links.z
    pending = []
    local_sems = m.local_sems

    def post(src, dst, slot, **to):
        made = links.send(src, dst, slot, **to)
        pending.append(made)
        return made

    def drain():
        for made in pending:
            made.wait_send()
        pending.clear()

    post(ins.images, m.raw.at[0], T.raw, other=True)
    post(ins.mask, m.mask.at[0], T.mask, other=True)
    own = []
    for n, piece in enumerate(PIECES):
        h = ALL if piece[3] in (D, E) else y
        made = pltpu.make_async_copy(shard_of(piece, ins.weights[piece[0]], h), piece_of(piece, w[piece[0]], z, x, h), local_sems.at[n])
        made.start()
        own.append(made)

    flight = {}

    def along_z(src, dst, slot):
        return [post(src, dst, slot + dz, dz=dz) for dz in (2, 1, 3)]

    def gather(n, stage):
        piece = PIECES[n]
        buf, shard, order, slot = w[piece[0]], ins.weights[piece[0]], piece[3], T.gather + 5 * n
        if stage == 0:
            h = ALL if order in (D, E) else y
            src, dst = shard_of(piece, shard, h), piece_of(piece, buf, z, x, h)
        else:
            if order == A:
                part = (z, ALL, y) if stage == 1 else (ALL, ALL, y)
            elif order == B:
                part = (ALL, x, y) if stage == 1 else (ALL, x, ALL)
            elif order == C:
                part = (ALL, x, y) if stage == 1 else (ALL, ALL, y)
            elif order == D:
                part = (ALL, x, ALL)
            else:
                part = (z, ALL, ALL)
            src = dst = piece_of(piece, buf, *part)
        axis = ((1, 3, 2), (3, 2, 1), (3, 1, 2), (3, 1), (1, 3))[order][stage]
        if axis == 3:
            flight[n] = along_z(src, dst, slot)
        elif axis == 2:
            flight[n] = [post(src, dst, slot + 4, dy=1)]
        else:
            flight[n] = [post(src, dst, slot, dx=1)]

    def landed(n):
        for made in flight[n]:
            made.wait_recv()

    def gathered(n):
        piece = PIECES[n]
        if piece[0] != P1:
            whole = piece_of(piece, w[piece[0]], ALL, ALL, ALL)
            post(whole, whole, T.hand + n, other=True)
            return
        if not m.seen:
            links.arrived(m.pix, T.pix)
            m.seen.append(n)

        def project(step, carry):
            off = pl.multiple_of(piece[1] + step * 256, 256)
            kern = w[P1][:, :, :, :, pl.ds(off, 256)].reshape(1024, 256)
            m.prep[:, pl.ds(off, 256)] = nn(m.pix[0:256, :], kern)
            return carry

        lax.fori_loop(0, piece[2] // 256, project, 0)
        cols = m.prep.at[:, pl.ds(piece[1], piece[2])]
        post(cols, cols, T.hand + n, other=True)

    waited = False
    for n, stage in GATHER_PLAN:
        if stage and not waited:
            for made in own:
                made.wait()
            waited = True
        if stage:
            landed(n)
        if stage == 3:
            gathered(n)
        else:
            gather(n, stage)
    post(ins.cotangent, m.cot.at[0], T.cot, other=True)
    drain()

    def allow(which):
        for to in (dict(dx=1), dict(dy=1)):
            pl.semaphore_signal(credit.at[which], inc=1, device_id=links.device(**to), device_id_type=MESH)

    allow(0)
    links.arrived(m.act1.at[y], T.act1)
    post(m.act1.at[y], m.act1.at[y], T.act1_y, dy=1)
    post(m.pix.at[pl.ds(0, 256)], m.samp.at[y], T.samp_y, dy=1)
    pl.semaphore_wait(credit.at[0], 2)

    def windows_one():
        links.arrived(m.act1.at[1 - y], T.act1_y)
        for tap in range(9):
            a, b = tap // 3, tap % 3
            pq = (0 if a == 1 else 2) + (0 if b == 1 else 1)
            block = m.act1[1 - y, pq * 256:pq * 256 + 256, :].astype(F32)
            m.xc2[1 - y, :, tap * 384:(tap + 1) * 384] = shifted(block, -1 if a == 0 else 0, -1 if b == 0 else 0).astype(BF16)

    def windows_two():
        links.arrived(m.act4.at[1 - y], T.act4_y)
        for tap in range(9):
            block = m.act4[1 - y].astype(F32)
            m.xc5[1 - y, :, tap * 384:(tap + 1) * 384] = shifted(block, tap // 3 - 1, tap % 3 - 1).astype(BF16)

    def add(into, own, others):
        got = own[...].astype(F32)
        for other in others:
            got = got + other[...].astype(F32)
        into[...] = got.astype(BF16)

    def reduce(n, stage):
        name, first, count, order = SUMMED[n]
        kind, buf, into, last = KINDS[name], g[name], w[name], fin[name]
        slot = T.reduce + 6 * n
        paired = len(order) == 2
        done = order[:stage]

        def pick(ref, zi, xi, h):
            if kind == TAP:
                return ref.at[pl.ds(first, count), zi, xi]
            if name == P1:
                return ref.at[zi, xi, :, :, pl.ds(first, count)]
            if kind == COL:
                cols = pl.ds(first, 2 * count) if h is ALL else pl.ds(pl.multiple_of(first + h * count, 128), count)
                return ref.at[zi, xi, :, cols]
            return ref.at[zi, xi] if h is ALL else ref.at[zi, xi, pl.ds(h * count, count)]

        def pick_z(k, xi, h):
            ref = third[name].at[k]
            if kind == TAP:
                return ref.at[pl.ds(first, count), xi]
            if name == P1:
                return ref.at[xi, :, :, pl.ds(first, count)]
            if kind == COL:
                thin = ref.shape[-1] < buf.shape[-1]
                return ref.at[xi, :, pl.ds(first, 2 * count) if h is ALL else pl.ds(first // 2 if thin else first, count)]
            return ref.at[xi]

        def pick_last(i):
            if kind == TAP:
                return last.at[8 if first == 4 else 2 * (first + i) + y]
            if name == P1:
                return last.at[:, :, pl.ds(pl.multiple_of(768 * y + first, 128), count)]
            if kind == COL:
                return last.at[:, pl.ds(pl.multiple_of(first + y * count, 128), count)]
            return last.at[pl.ds(y * count, count)]

        def held(axes):
            return z if 3 in axes else ALL, x if 1 in axes else ALL, y if 2 in axes else ALL

        def landing(axes, axis, zi):
            if axis == 1:
                return pick(into, zi, 0, ALL if paired or 2 not in axes else 1)
            return pick(into, zi, 1 if 1 in axes else ALL, 0)

        if stage:
            for made in flight[n]:
                made.wait_recv()
        if 0 < stage <= len(order):
            before, axis = order[:stage - 1], order[stage - 1]
            zi, xi, h = held(done)
            taps_here = count if kind == TAP else 1
            many_z, many_x = 4 if zi is ALL else 1, 2 if xi is ALL else 1

            def one(i, carry):
                tap, cell = i // (many_z * many_x), i % (many_z * many_x)
                at_z, at_x = cell // many_x if zi is ALL else zi, cell % many_x if xi is ALL else xi

                def inner(ref):
                    return ref.at[tap] if kind == TAP else ref

                own = inner(pick(buf, at_z, at_x, h))
                if axis == 3:
                    others = [inner(pick_z(k, 0 if 1 in before else at_x, ALL if 2 not in before else 0)) for k in range(3)]
                else:
                    land_x = 0 if axis == 1 else 1 if 1 in before else at_x
                    land_h = (ALL if paired or 2 not in before else 1) if axis == 1 else 0
                    others = [inner(pick(into, at_z, land_x, land_h))]
                add(pick_last(tap) if stage == len(order) else own, own, others)
                return carry

            lax.fori_loop(0, taps_here * many_z * many_x, one, 0)
        if stage < len(order):
            axis = order[stage]
            zi, xi, h = held(done)
            if axis == 1:
                flight[n] = [post(pick(buf, zi, 1 - x, h), landing(done, 1, zi), slot, dx=1)]
            elif axis == 2:
                flight[n] = [post(pick(buf, zi, xi, 1 - y), landing(done, 2, zi), slot + 4, dy=1)]
            else:
                flight[n] = [post(pick(buf, (z + dz) % 4, xi, h), pick_z(dz - 1, 0 if 1 in done else ALL, ALL if 2 not in done else 0),
                                  slot + dz, dz=dz) for dz in (2, 1, 3)]
        elif stage == len(order) and not (kind == TAP and first == 4):
            parts = [pick_last(i) for i in range(count if kind == TAP else 1)]
            flight[n] = [post(part, part, slot + (5 if kind != TAP else 4 + i), dy=1) for i, part in enumerate(parts)]
        else:
            left[name] -= 1
            if left[name] == 0:
                made = pltpu.make_async_copy(last, outs.grads[name], local_sems.at[name])
                made.start()
                m.tail.append(made)
                post(last, outs.grads[name], T.out + name, other=True)

    def columns(name, left, right):
        def one(step, carry):
            off = pl.multiple_of(step * 256, 256)
            part = tn(left, right[:, pl.ds(off, 256)])
            g[name][..., pl.ds(off, 256)] = part.astype(BF16).reshape(g[name].shape[:-1] + (256,))
            return carry

        lax.fori_loop(0, right.shape[1] // 256, one, 0)

    def taps(name, windows, low):
        def one(k, carry):
            tap = jnp.where(k == 4, 8, 2 * k + y)
            off = pl.multiple_of(tap * 384, 128)
            part = tn(windows[:, :, pl.ds(off, 384)].reshape(512, 384), low[...].reshape(512, 384))
            g[name][k] = part.astype(BF16).reshape(4, 2, 48, 384)
            return carry

        lax.fori_loop(0, 5, one, 0)

    def make(name):
        if name == E2:
            links.arrived(m.act5, T.act5)
            links.arrived(m.low6, T.low6)
            columns(E2, m.act5[...], m.low6)
        elif name == S2:
            links.arrived(m.xc5.at[y], T.xc5)
            links.arrived(m.low5.at[y], T.low5)
            links.arrived(m.low5.at[1 - y], T.low5_y)
            taps(S2, m.xc5, m.low5)
        elif name == R2:
            links.arrived(m.hlow, T.hlow)
            links.arrived(m.low4, T.low4)

            def one(step, carry):
                part = tn(m.hlow[:, pl.ds(pl.multiple_of(step * 384, 128), 384)], m.low4[...])
                g[R2][step] = part.astype(BF16).reshape(2, 4, 48, 384)
                return carry

            lax.fori_loop(0, 4, one, 0)
        elif name == E1:
            links.arrived(m.act2, T.act2)
            links.arrived(m.low3, T.low3)
            columns(E1, m.act2[...], m.low3)
        elif name == P1:
            links.arrived(m.samp.at[1 - y], T.samp_y)
            links.arrived(m.lowp_y, T.lowp_y)
            mine = columns_of(m.lowp, y)

            def one(step, carry):
                cols = pl.ds(pl.multiple_of(step * 256, 256), 256)
                part = tn(m.pix[0:256, cols], m.lowp[:, mine]) + tn(m.samp[1 - y, :, cols], m.lowp_y[...])
                g[P1][step] = part.astype(BF16).reshape(2, 2, 64, 768)
                return carry

            lax.fori_loop(0, 4, one, 0)
        elif name == S1:
            links.arrived(m.xc2.at[y], T.xc2)
            links.arrived(m.low2.at[y], T.low2)
            links.arrived(m.low2.at[1 - y], T.low2_y)
            taps(S1, m.xc2, m.low2)
        else:
            links.arrived(m.low1, T.low1)

            def one(step, carry):
                part = tn(m.pix[:, pl.ds(pl.multiple_of(step * 256, 256), 256)], m.low1[...])
                g[R1][step] = part.astype(BF16).reshape(2, 2, 64, 384)
                return carry

            lax.fori_loop(0, 4, one, 0)

    def swap_projection():
        links.arrived(m.lowp, T.lowp)
        theirs = m.lowp.at[:, columns_of(m.lowp, 1 - y)]
        post(theirs, m.lowp_y, T.lowp_y, dy=1)

    def project_back():
        def back(step, carry):
            kern = w[P1][step].reshape(256, 1536)
            m.gsamp[:, pl.ds(pl.multiple_of(step * 256, 256), 256)] = nt(m.lowp[...], kern)
            return carry

        lax.fori_loop(0, 4, back, 0)
        allow(1)
        post(m.gsamp, m.gsamp, T.gsamp, other=True)
        pl.semaphore_wait(credit.at[1], 2)

    left = [sum(piece[0] == name for piece in SUMMED) for name in NAMES]
    for n, stage in REDUCE_PLAN:
        if n == MAKE:
            make(stage)
        elif n == OTHER:
            (windows_one, windows_two, swap_projection, project_back)[stage]()
        else:
            reduce(n, stage)
    drain()
    for made in m.tail:
        made.wait()
    links.arrived(outs.act, T.out_act)
    links.arrived(outs.norm, T.out_norm)
    links.arrived(outs.gimg, T.out_gimg)


def runner(links, ins, outs, w, m, sums):
    x, y, z = links.x, links.y, links.z
    me = y * 8 + links.wide
    pending = []
    local_sems = m.local_sems

    def post(src, dst, slot, **to):
        made = links.send(src, dst, slot, **to)
        pending.append(made)
        return made

    def hand(ref, slot):
        post(ref, ref, slot, other=True)

    def weight(name):
        for n, piece in enumerate(PIECES):
            if piece[0] == name:
                links.arrived(piece_of(piece, w[name], ALL, ALL, ALL), T.hand + n)

    peers = [(dy, dz, dx) for dz in (2, 1, 3, 0) for dx in (1, 0) for dy in (1, 0) if (dy, dz, dx) != (0, 0, 0)]

    def total(which, rows):
        buf = sums[which]
        for r, row in enumerate(rows):
            buf[me, r:r + 1, :] = row
        slot = T.sums + which
        sem = links.next_send
        links.next_send += 1
        for dy, dz, dx in peers:
            pltpu.make_async_remote_copy(
                src_ref=buf.at[me], dst_ref=buf.at[me], send_sem=links.send_sems.at[sem], recv_sem=links.recv_sems.at[slot],
                device_id=links.device(dy=dy, dz=dz, dx=dx), device_id_type=MESH).start()
        both = pltpu.make_async_remote_copy(
            src_ref=buf.at[pl.ds(0, 15)], dst_ref=buf.at[pl.ds(0, 15)], send_sem=links.send_sems.at[sem],
            recv_sem=links.recv_sems.at[slot], device_id=links.device(other=True), device_id_type=MESH)
        both.wait_recv()
        both.wait_send()
        parts = [buf[i] for i in range(16)]
        while len(parts) > 1:
            parts = [parts[i] + parts[i + 1] for i in range(0, len(parts), 2)]
        return parts[0]

    own_norm = pltpu.make_async_copy(ins.norm, m.norm_in.at[links.wide], local_sems.at[0])
    own_norm.start()
    own_raw = pltpu.make_async_copy(ins.images, m.raw.at[1], local_sems.at[1])
    own_raw.start()
    own_mask = pltpu.make_async_copy(ins.mask, m.mask.at[1], local_sems.at[2])
    own_mask.start()
    own_cot = pltpu.make_async_copy(ins.cotangent, m.cot.at[1], local_sems.at[3])
    own_cot.start()
    for k, (dz, dx) in enumerate([(dz, dx) for dz in (2, 1, 3, 0) for dx in (1, 0) if (dz, dx) != (0, 0)]):
        post(ins.norm, m.norm_in.at[links.wide], T.norm_in + dz * 2 + dx, dz=dz, dx=dx)

    lo = pl.ds(0, 256)
    r = lax.broadcasted_iota(jnp.int32, (256, 256), 0)
    c = lax.broadcasted_iota(jnp.int32, (256, 256), 1)
    source = (2 * ((r // 8) % 8) + r // 128) * 16 + 2 * (r % 8) + (r // 64) % 2
    perm = jnp.where(c == source, 1.0, 0.0).astype(BF16)
    m.perm[...] = perm

    own_mask.wait()
    links.arrived(m.mask.at[0], T.mask)
    flags = m.mask[...].reshape(64, 16).astype(F32)
    for pq in range(4):
        p, q = pq // 2, pq % 2
        row = lax.broadcasted_iota(jnp.int32, (256, 64), 0)
        line = lax.broadcasted_iota(jnp.int32, (256, 64), 1)
        pick = jnp.where(line == (row // 64) * 16 + 2 * ((row // 8) % 8) + p, 1.0, 0.0)
        lines = nn(pick.astype(BF16), flags.astype(BF16))
        row16 = lax.broadcasted_iota(jnp.int32, (256, 16), 0)
        col16 = lax.broadcasted_iota(jnp.int32, (256, 16), 1)
        one = jnp.sum(jnp.where(col16 == 2 * (row16 % 8) + q, lines, 0.0), axis=1, keepdims=True)
        m.valid[pq * 256:(pq + 1) * 256, :] = jnp.broadcast_to(one, (256, 128))

    own_raw.wait()
    links.arrived(m.raw.at[0], T.raw)
    for b in range(4):
        picked = nn(perm, m.raw[b // 2, (b % 2) * 256:(b % 2) * 256 + 256, :]).astype(BF16)
        for pq in range(4):
            m.pix[pq * 256 + b * 64:pq * 256 + b * 64 + 64, :] = picked[pq * 64:pq * 64 + 64, :]
    pix_sent = links.send(m.pix, m.pix, T.pix, other=True)

    own_norm.wait()
    for dz in range(4):
        for dx in range(2):
            if dz or dx:
                links.arrived(m.norm_in.at[0], T.norm_in + dz * 2 + dx)
    for s in range(8):
        piece = m.norm_in[s]
        at = 0
        for ref in (m.gain_a, m.shift_a, m.gain_b, m.shift_b):
            size = ref.shape[1] // 8
            ref[:, s * size:(s + 1) * size] = piece[:, at:at + size]
            at += size

    norms = m.norms

    def set_norm(key, mean_sum, square_sum, count, gain, shift):
        ref = norms[key]
        mean = mean_sum / count
        var = square_sum / count - mean * mean
        scaler = lax.rsqrt(var + NORM_EPS)
        ref[0:1, :] = mean
        ref[1:2, :] = scaler
        ref[2:3, :] = gain
        ref[3:4, :] = gain * scaler
        ref[4:5, :] = shift - mean * (gain * scaler)

    def set_back(key, first_sum, second_sum, count, at):
        ref = norms[key]
        mean, scaler, gain = ref[0:1, :], ref[1:2, :], ref[2:3, :]
        centred = second_sum - mean * first_sum
        grad_var = -0.5 * gain * centred * scaler * scaler * scaler
        grad_mean = -gain * scaler * first_sum - 2.0 * mean * grad_var
        ref[5:6, :] = grad_mean / count
        ref[6:7, :] = 2.0 * grad_var / count
        size = ref.shape[1]
        gain_at, shift_at = at
        m.norm_out[:, gain_at:gain_at + size] = scaler * centred
        m.norm_out[:, shift_at:shift_at + size] = first_sum

    def rows_of(key, at, size):
        ref = norms[key]
        return [ref[k:k + 1, pl.ds(at, size)] for k in range(8)]

    def norm_of(key, pre, at, size):
        ref = norms[key]
        return pre * ref[3:4, pl.ds(at, size)] + ref[4:5, pl.ds(at, size)]

    def back_of(key, pre, up, valid, at, size):
        ref = norms[key]
        return ref[3:4, pl.ds(at, size)] * up + valid * (ref[5:6, pl.ds(at, size)] + ref[6:7, pl.ds(at, size)] * pre)

    def valid_of(rows, cols):
        one = m.valid[rows, :]
        return jnp.concatenate([one] * (cols // 128), axis=1) if cols > 128 else one

    def colsum(v):
        return jnp.sum(v, axis=0, keepdims=True)

    stat = m.stat

    def chunks(rows, width, body):
        def one(step, carry):
            return body(pl.ds(pl.multiple_of(step * 64, 64), 64), carry)

        zero = jnp.zeros((1, width), F32)
        return lax.fori_loop(0, rows // 64, one, (zero, zero))

    weight(R1)

    def layer1(step, carry):
        rows = pl.ds(pl.multiple_of(step * 256, 256), 256)
        pre = nn(m.pix[rows, :], w[R1][...].reshape(1024, 384))
        m.pre1[rows, :] = pre
        weighed = pre * valid_of(rows, 384)
        return carry[0] + colsum(weighed), carry[1] + colsum(weighed * pre)

    zero = jnp.zeros((1, 384), F32)
    first, second = lax.fori_loop(0, 4, layer1, (zero, zero))
    hi_here = jnp.concatenate([colsum(m.valid[...])] * 3, axis=1)
    lo_here = jnp.concatenate([colsum(m.valid[lo, :])] * 3, axis=1)
    got = total(0, [first, second, hi_here, lo_here])
    count_hi = jnp.maximum(got[2:3, :], 1.0)
    count_lo = jnp.maximum(got[3:4, :], 1.0)
    count_wide = jnp.concatenate([count_lo] * 4, axis=1)
    set_norm(N1, got[0:1, :], got[1:2, :], count_hi, m.gain_a[:, 0:384], m.shift_a[:, 0:384])

    def activate1(rows, carry):
        v = norm_of(N1, m.pre1[rows, :], 0, 384)
        act = v * sigmoid(v)
        m.up1[rows, :] = act
        m.act1[y, rows, :] = act.astype(BF16)
        return carry

    chunks(1024, 384, activate1)
    hand(m.act1.at[y], T.act1)
    for tap in range(9):
        a, b = tap // 3, tap % 3
        pq = (0 if a == 1 else 2) + (0 if b == 1 else 1)
        block = m.up1[pq * 256:pq * 256 + 256, :]
        block = shifted(block, -1 if a == 0 else 0, -1 if b == 0 else 0)
        m.xc2[y, :, tap * 384:(tap + 1) * 384] = block.astype(BF16)
    hand(m.xc2.at[y], T.xc2)

    def statistics(pre, rows, width):
        weighed = pre * valid_of(rows, width)
        return colsum(weighed), colsum(weighed * pre)

    weight(S1)
    pre = nn(m.xc2[y], w[S1][...].reshape(3456, 384))
    m.pre2[...] = pre
    got = total(1, statistics(pre, lo, 384))
    set_norm(N2, got[0:1, :], got[1:2, :], count_lo, m.gain_a[:, 384:768], m.shift_a[:, 384:768])

    def activate2(rows, carry):
        v = norm_of(N2, m.pre2[rows, :], 0, 384)
        m.act2[rows, :] = (v * sigmoid(v)).astype(BF16)
        return carry

    chunks(256, 384, activate2)
    hand(m.act2, T.act2)

    def wide_loop(body, size=256):
        def one(step, carry):
            body(pl.multiple_of(step * size, size))
            return carry

        lax.fori_loop(0, 1536 // size, one, 0)

    def keep_stats(ref, at, size, k):
        first, second = statistics(ref[:, pl.ds(at, size)], lo, size)
        stat[k:k + 1, pl.ds(at, size)] = first
        stat[k + 1:k + 2, pl.ds(at, size)] = second

    weight(E1)

    def layer3(at):
        m.pre3[:, pl.ds(at, 256)] = nn(m.act2[...], w[E1][:, :, :, pl.ds(at, 256)].reshape(384, 256))
        keep_stats(m.pre3, at, 256, 0)

    wide_loop(layer3)
    for n, piece in enumerate(PIECES):
        if piece[0] == P1:
            links.arrived(m.prep.at[:, pl.ds(piece[1], piece[2])], T.hand + n)
    wide_loop(lambda at: keep_stats(m.prep, at, 256, 2))
    got = total(2, [stat[k:k + 1, :] for k in range(4)])
    set_norm(N3, got[0:1, :], got[1:2, :], count_wide, m.gain_a[:, 768:2304], m.shift_a[:, 768:2304])
    set_norm(NP, got[2:3, :], got[3:4, :], count_wide, m.gain_a[:, 2304:3840], m.shift_a[:, 2304:3840])

    def sum_one(at, size):
        cols = pl.ds(at, size)
        return norm_of(N3, m.pre3[:, cols], at, size) + norm_of(NP, m.prep[:, cols], at, size)

    def make_hidden(at):
        v = sum_one(at, 128)
        hidden = v * sigmoid(v)
        m.hidden[:, pl.ds(at, 128)] = hidden
        m.hlow[:, pl.ds(at, 128)] = hidden.astype(BF16)

    wide_loop(make_hidden, 128)
    hand(m.hlow, T.hlow)

    weight(R2)
    pre = nn(m.hlow[...], w[R2][...].reshape(1536, 384))
    m.pre4[...] = pre
    got = total(3, statistics(pre, lo, 384))
    set_norm(N4, got[0:1, :], got[1:2, :], count_lo, m.gain_b[:, 0:384], m.shift_b[:, 0:384])

    def activate4(rows, carry):
        v = norm_of(N4, m.pre4[rows, :], 0, 384)
        act = v * sigmoid(v)
        m.small[rows, :] = act
        m.act4[y, rows, :] = act.astype(BF16)
        return carry

    chunks(256, 384, activate4)
    post(m.act4.at[y], m.act4.at[y], T.act4_y, dy=1, other=True)
    for tap in range(9):
        m.xc5[y, :, tap * 384:(tap + 1) * 384] = shifted(m.small[...], tap // 3 - 1, tap % 3 - 1).astype(BF16)
    hand(m.xc5.at[y], T.xc5)
    weight(S2)
    pre = nn(m.xc5[y], w[S2][...].reshape(3456, 384))
    m.pre5[...] = pre
    got = total(4, statistics(pre, lo, 384))
    set_norm(N5, got[0:1, :], got[1:2, :], count_lo, m.gain_b[:, 384:768], m.shift_b[:, 384:768])

    def activate5(rows, carry):
        v = norm_of(N5, m.pre5[rows, :], 0, 384)
        m.act5[rows, :] = (v * sigmoid(v)).astype(BF16)
        return carry

    chunks(256, 384, activate5)
    hand(m.act5, T.act5)
    weight(E2)

    def layer6(at):
        m.pre6[:, pl.ds(at, 256)] = nn(m.act5[...], w[E2][:, :, :, pl.ds(at, 256)].reshape(384, 256))
        keep_stats(m.pre6, at, 256, 0)

    wide_loop(layer6)
    got = total(5, [stat[k:k + 1, :] for k in range(2)])
    set_norm(N6, got[0:1, :], got[1:2, :], count_wide, m.gain_b[:, 768:2304], m.shift_b[:, 768:2304])
    own_cot.wait()
    links.arrived(m.cot.at[0], T.cot)

    def top(at):
        cols = pl.ds(at, 128)
        pre = m.pre6[:, cols]
        v = norm_of(N6, pre, at, 128) + m.hidden[:, cols]
        sg = sigmoid(v)
        m.acts[:, cols] = (v * sg).astype(BF16)
        up = m.cot[:, :, cols].reshape(256, 128).astype(F32)
        up = up * sg * (1.0 + v * (1.0 - sg))
        m.hidden[:, cols] = up
        stat[0:1, cols] = colsum(up)
        stat[1:2, cols] = colsum(up * pre)

    wide_loop(top, 128)
    out_act = pltpu.make_async_copy(m.acts.at[pl.ds(128, 128)], outs.act, local_sems.at[4])
    out_act.start()
    post(m.acts.at[pl.ds(0, 128)], outs.act, T.out_act, other=True)
    got = total(6, [stat[k:k + 1, :] for k in range(2)])
    b_gain, b_shift = 7680, 9984
    set_back(N6, got[0:1, :], got[1:2, :], count_wide, (b_gain + 768, b_shift + 768))

    def low6(at):
        cols = pl.ds(at, 128)
        m.low6[:, cols] = back_of(N6, m.pre6[:, cols], m.hidden[:, cols], valid_of(lo, 128), at, 128).astype(BF16)

    wide_loop(low6, 128)
    hand(m.low6, T.low6)
    m.small[...] = nt(m.low6[...], w[E2][...].reshape(384, 1536))

    def narrow_up(key, pre):
        def one(rows, carry):
            kept = pre[rows, :]
            up = silu_back(norm_of(key, kept, 0, 384), m.small[rows, :])
            m.small[rows, :] = up
            return carry[0] + colsum(up), carry[1] + colsum(up * kept)

        return chunks(256, 384, one)

    def narrow_low(key, pre, low, slot, far=None):
        def one(rows, carry):
            got = back_of(key, pre[rows, :], m.small[rows, :], valid_of(rows, 384), 0, 384)
            m.small[rows, :] = got
            low[rows, :] = got.astype(BF16)
            return carry

        chunks(256, 384, one)
        hand(low, slot)
        if far is not None:
            post(low, low, far, dy=1, other=True)

    got = total(7, narrow_up(N5, m.pre5))
    set_back(N5, got[0:1, :], got[1:2, :], count_lo, (b_gain + 384, b_shift + 384))
    narrow_low(N5, m.pre5, m.low5.at[y], T.low5, T.low5_y)
    grad = jnp.zeros((256, 384), F32)
    for tap in range(9):
        moved = shifted(m.small[...], 1 - tap // 3, 1 - tap % 3).astype(BF16)
        grad = grad + nt(moved, w[S2][tap].reshape(384, 384))
    m.small[...] = grad
    got = total(8, narrow_up(N4, m.pre4))
    set_back(N4, got[0:1, :], got[1:2, :], count_lo, (b_gain, b_shift))
    narrow_low(N4, m.pre4, m.low4, T.low4)

    def below(step, carry):
        at = pl.multiple_of(step * 384, 128)
        cols = pl.ds(at, 384)
        grad = m.hidden[:, cols] + nt(m.low4[...], w[R2][step].reshape(384, 384))
        up = silu_back(sum_one(at, 384), grad)
        m.pre6[:, cols] = up
        stat[0:1, cols] = colsum(up)
        stat[1:2, cols] = colsum(up * m.pre3[:, cols])
        stat[2:3, cols] = colsum(up * m.prep[:, cols])
        return carry

    lax.fori_loop(0, 4, below, 0)
    got = total(9, [stat[k:k + 1, :] for k in range(3)])
    a_gain, a_shift = 0, 3840
    set_back(N3, got[0:1, :], got[1:2, :], count_wide, (a_gain + 768, a_shift + 768))
    set_back(NP, got[0:1, :], got[2:3, :], count_wide, (a_gain + 2304, a_shift + 2304))

    def low3(at):
        cols = pl.ds(at, 128)
        up, valid = m.pre6[:, cols], valid_of(lo, 128)
        m.low3[:, cols] = back_of(N3, m.pre3[:, cols], up, valid, at, 128).astype(BF16)
        m.lowp[:, cols] = back_of(NP, m.prep[:, cols], up, valid, at, 128).astype(BF16)

    wide_loop(low3, 128)
    hand(m.low3, T.low3)
    hand(m.lowp, T.lowp)
    m.small[...] = nt(m.low3[...], w[E1][...].reshape(384, 1536))
    got = total(10, narrow_up(N2, m.pre2))
    set_back(N2, got[0:1, :], got[1:2, :], count_lo, (a_gain + 384, a_shift + 384))
    narrow_low(N2, m.pre2, m.low2.at[y], T.low2, T.low2_y)
    for pq in range(4):
        p, q = pq // 2, pq % 2
        grad = jnp.zeros((256, 384), F32)
        for a in ((1,) if p == 0 else (0, 2)):
            for b in ((1,) if q == 0 else (0, 2)):
                moved = shifted(m.small[...], 1 if a == 0 else 0, 1 if b == 0 else 0).astype(BF16)
                grad = grad + nt(moved, w[S1][a * 3 + b].reshape(384, 384))
        m.up1[pq * 256:pq * 256 + 256, :] = grad

    def up1(rows, carry):
        kept = m.pre1[rows, :]
        up = silu_back(norm_of(N1, kept, 0, 384), m.up1[rows, :])
        m.up1[rows, :] = up
        return carry[0] + colsum(up), carry[1] + colsum(up * kept)

    got = total(11, chunks(1024, 384, up1))
    set_back(N1, got[0:1, :], got[1:2, :], count_hi, (a_gain, a_shift))
    out_norm = pltpu.make_async_copy(m.norm_out, outs.norm, local_sems.at[5])
    out_norm.start()
    post(m.norm_out, outs.norm, T.out_norm, other=True)

    def low1(rows, carry):
        got = back_of(N1, m.pre1[rows, :], m.up1[rows, :], valid_of(rows, 384), 0, 384)
        m.low1[rows, :] = got.astype(BF16)
        return carry

    chunks(1024, 384, low1)
    hand(m.low1, T.low1)
    links.arrived(m.gsamp, T.gsamp)
    pix_sent.wait_send()
    for pq in range(4):
        grad = nt(m.low1[pq * 256:pq * 256 + 256, :], w[R1][...].reshape(1024, 384))
        if pq == 0:
            grad = grad + m.gsamp[...]
        m.pix[pq * 256:pq * 256 + 256, :] = grad.astype(BF16)
    for b in range(4):
        block = jnp.concatenate([m.pix[pq * 256 + b * 64:pq * 256 + b * 64 + 64, :] for pq in range(4)], axis=0)
        m.raw[b // 2, (b % 2) * 256:(b % 2) * 256 + 256, :] = tn(m.perm[...], block).astype(BF16)
    out_img = pltpu.make_async_copy(m.raw.at[1], outs.gimg, local_sems.at[6])
    out_img.start()
    post(m.raw.at[0], outs.gimg, T.out_gimg, other=True)
    for name in NAMES:
        links.arrived(outs.grads[name], T.out + name)
    out_act.wait()
    out_norm.wait()
    out_img.wait()
    for made in pending:
        made.wait_send()


SUM_ROWS = ((4, 384), (2, 384), (4, 1536), (2, 384), (2, 384), (2, 1536), (2, 1536), (2, 384), (2, 384), (3, 1536), (2, 384), (2, 384))


def fused_kernel(sizes, keys, *refs):
    groups, at = [], 0
    for size in sizes:
        groups.append(refs[at:at + size])
        at += size
    taken, shards_in, given, made, w, g, fin, third, kept, norms, sums, rest = groups
    dp, wide = lax.axis_index("dp"), lax.axis_index("wide")
    core = dp % 2
    send_sems, recv_sems, local_sems, credit = rest
    barrier = pltpu.get_barrier_semaphore()
    greet = Links(send_sems, recv_sems, core, 0)
    everyone = [dict(other=True), dict(dy=1, other=True)] + [
        dict(dy=dy, dz=dz, dx=dx) for dy in (0, 1) for dz in range(4) for dx in (0, 1) if (dy, dz, dx) != (0, 0, 0)]
    for to in everyone:
        pl.semaphore_signal(barrier, inc=1, device_id=greet.device(**to), device_id_type=MESH)
    pl.semaphore_wait(barrier, len(everyone))

    images, mask, cotangent, norm = taken
    act, gimg, norm_out = given
    ins = types.SimpleNamespace(images=images, mask=mask, cotangent=cotangent, norm=norm, weights=shards_in)
    outs = types.SimpleNamespace(act=act, gimg=gimg, norm=norm_out, grads=made)
    m = types.SimpleNamespace(**dict(zip(keys, kept)), norms=norms, local_sems=local_sems, tail=[], seen=[])

    @pl.when(core == 0)
    def _():
        mover(Links(send_sems, recv_sems, 0, 1), ins, outs, w, g, third, fin, m, credit)

    @pl.when(core == 1)
    def _():
        runner(Links(send_sems, recv_sems, 1, 1), ins, outs, w, m, sums)


def finish_kernel(sizes, *refs):
    act, gimg, norms = refs[:3]
    grads, out_act, out_gimg = refs[3:10], refs[10], refs[11]
    out_grads, out_norms = refs[12:19], refs[19:23]
    low, high, row, parts = refs[23:30], refs[30:37], refs[37], refs[38:42]
    held_act, held_gimg, in_sems, out_sems = refs[42:]
    passing = [pltpu.make_async_copy(gimg, held_gimg, in_sems.at[0]), pltpu.make_async_copy(act, held_act, in_sems.at[9])]
    copies = []
    coming = [pltpu.make_async_copy(v, into, in_sems.at[2 + n]) for n, (v, into) in enumerate(zip(grads, low))]
    norm_in = pltpu.make_async_copy(norms, row, in_sems.at[1])
    norm_in.start()
    for made in coming + passing:
        made.start()
    norm_in.wait()
    wide = lax.axis_index("wide")
    at = 0
    for n, size in enumerate((sizes[0], sizes[0], sizes[1], sizes[1])):
        for s in range(8):
            @pl.when(wide == s)
            def _(n=n, size=size, start=at + s * size):
                parts[n][...] = row[:, start:start + size]
        at += 8 * size
        made = pltpu.make_async_copy(parts[n].at[0], out_norms[n], out_sems.at[1 + n])
        made.start()
        copies.append(made)
    for n, (source, into, out) in enumerate(zip(low, high, out_grads)):
        coming[n].wait()
        for i in range(source.shape[0] if len(source.shape) == 3 else 1):
            part = i if len(source.shape) == 3 else slice(None)
            into[part] = source[part].astype(F32)
        made = pltpu.make_async_copy(into, out, out_sems.at[5 + n])
        made.start()
        copies.append(made)
    for n, (source, out) in enumerate(((held_gimg, out_gimg), (held_act, out_act))):
        passing[n].wait()
        made = pltpu.make_async_copy(source, out, out_sems.at[(0, 12)[n]])
        made.start()
        copies.append(made)
    for made in copies:
        made.wait()


def fused_shards(images, pixel_mask, cotangent, reduce_one, spatial_one, expand_one, project_one, gains_one, shifts_one,
                 reduce_two, spatial_two, expand_two, gains_two, shifts_two):
    def split(weight, parts=2):
        return weight.reshape(parts, weight.shape[0] // parts, weight.shape[1])

    def join(weight):
        return weight.reshape(9, weight.shape[2], weight.shape[3])

    weights = (split(reduce_one), join(spatial_one), expand_one, split(project_one), split(reduce_two, 4), join(spatial_two), expand_two)
    local_a, local_b = gains_one.shape[0], gains_two.shape[0]
    row, at = 0.0, 0
    for part in (gains_one, shifts_one, gains_two, shifts_two):
        row = row + jnp.pad(part.astype(F32), (at, 2 * (local_a + local_b) - at - part.shape[0]))
        at += part.shape[0]
    norm = row.reshape(1, -1)
    taken = [images.reshape(512, 1024), pixel_mask.reshape(32, 16), cotangent.reshape(128, 1536), norm]
    given = [jax.ShapeDtypeStruct((128, 1536), BF16), jax.ShapeDtypeStruct((512, 1024), BF16), jax.ShapeDtypeStruct((1, 12288), F32)]
    made = [jax.ShapeDtypeStruct(v.shape, BF16) for v in weights]
    whole = [pltpu.VMEM(whole_shape(KINDS[n], v.shape), BF16) for n, v in enumerate(weights)]
    fin = [pltpu.VMEM(v.shape, BF16) for v in weights]
    partial = list(whole)
    partial[S1] = partial[S2] = pltpu.VMEM((5, 4, 2, 48, 384), BF16)
    partial[P1] = pltpu.VMEM((4, 2, 2, 64, 768), BF16)
    cells = [(5, 48, 384) if KINDS[n] == TAP else (2, 64, 768) if n == P1 else v.shape for n, v in enumerate(weights)]
    third = []
    for n, cell in enumerate(cells):
        orders = [piece[3] for piece in SUMMED if piece[0] == n]
        both = 2 if any(order.index(3) < order.index(1) for order in orders) else 1
        whole_y = any(2 in order and order.index(3) < order.index(2) for order in orders)
        if KINDS[n] == TAP:
            shape = (3, 5, both, 48, 384)
        elif n == P1 or whole_y:
            shape = (3, both) + cell
        elif KINDS[n] == COL:
            shape = (3, both, cell[0], cell[1] // 2)
        else:
            shape = (3, both, cell[0] // 2) + cell[1:]
        third.append(pltpu.VMEM(shape, BF16))
    bf = dict(raw=(2, 512, 1024), cot=(2, 128, 1536), pix=(1024, 1024), perm=(256, 256), xc2=(2, 256, 3456), xc5=(2, 256, 3456),
              act2=(256, 384), act5=(256, 384), hlow=(256, 1536), acts=(256, 1536), low6=(256, 1536), low5=(2, 256, 384), low4=(256, 384),
              low3=(256, 1536), lowp=(256, 1536), low2=(2, 256, 384), low1=(1024, 384),
              samp=(2, 256, 1024), act1=(2, 1024, 384), act4=(2, 256, 384), lowp_y=(256, 768))
    f32 = dict(norm_in=(8, 1, 1536), gain_a=(1, 3840), shift_a=(1, 3840), gain_b=(1, 2304), shift_b=(1, 2304), norm_out=(1, 12288),
               valid=(1024, 128), stat=(8, 1536), pre1=(1024, 384), up1=(1024, 384), pre2=(256, 384), pre3=(256, 1536), prep=(256, 1536),
               hidden=(256, 1536), pre4=(256, 384), pre5=(256, 384), pre6=(256, 1536), small=(256, 384), gsamp=(256, 1024))
    kept = {k: pltpu.VMEM(v, BF16) for k, v in bf.items()} | {k: pltpu.VMEM(v, F32) for k, v in f32.items()}
    kept |= dict(mask=pltpu.VMEM((2, 32, 16), jnp.int32))
    norms = [pltpu.VMEM((8, width), F32) for width in (384, 384, 1536, 1536, 384, 384, 1536)]
    sums = [pltpu.VMEM((16, rows, width), F32) for rows, width in SUM_ROWS]
    rest = [pltpu.SemaphoreType.DMA((256,)), pltpu.SemaphoreType.DMA((T.total,)), pltpu.SemaphoreType.DMA((24,)),
            pltpu.SemaphoreType.REGULAR((2,))]
    groups = [taken, weights, given, made, whole, partial, fin, third, list(kept.values()), norms, sums, rest]
    anywhere = pl.BlockSpec(memory_space=pl.ANY)
    got = pl.pallas_call(
        functools.partial(fused_kernel, [len(group) for group in groups], list(kept)),
        out_shape=given + made,
        in_specs=[anywhere] * (len(taken) + len(weights)),
        out_specs=[anywhere] * (len(given) + len(made)),
        scratch_shapes=[v for group in groups[4:] for v in group],
        compiler_params=pltpu.CompilerParams(collective_id=0, has_side_effects=True, vmem_limit_bytes=63 * 2**20),
    )(*taken, *weights)
    act, gimg, norms, *grads = got
    finished = pl.pallas_call(
        functools.partial(finish_kernel, (local_a, local_b)),
        out_shape=[act, gimg] + [jax.ShapeDtypeStruct(v.shape, F32) for v in grads]
        + [jax.ShapeDtypeStruct((size,), F32) for size in (local_a, local_a, local_b, local_b)],
        in_specs=[anywhere] * 10,
        out_specs=[anywhere] * 13,
        scratch_shapes=[pltpu.VMEM(v.shape, BF16) for v in grads] + [pltpu.VMEM(v.shape, F32) for v in grads]
        + [pltpu.VMEM(norms.shape, F32)] + [pltpu.VMEM((1, size), F32) for size in (local_a, local_a, local_b, local_b)]
        + [pltpu.VMEM(act.shape, BF16), pltpu.VMEM(gimg.shape, BF16), pltpu.SemaphoreType.DMA((10,)), pltpu.SemaphoreType.DMA((13,))],
        compiler_params=pltpu.CompilerParams(vmem_limit_bytes=60 * 2**20),
    )(act, gimg, norms, *grads)
    act, gimg = finished[:2]
    grads = [v.reshape(like.shape) for v, like in zip(
        finished[2:9], (reduce_one, spatial_one, expand_one, project_one, reduce_two, spatial_two, expand_two))]
    norm_grads = finished[9:]
    return (
        act.reshape(cotangent.shape),
        gimg.reshape(images.shape),
        grads[0], grads[1], grads[2], grads[3], norm_grads[0], norm_grads[1],
        grads[4], grads[5], grads[6], norm_grads[2], norm_grads[3],
    )


def solution(mesh):
    fused = mesh.shape["dp"] == 4 and mesh.shape["wide"] == 8
    in_specs = (
        P(("dp", "wide"), None, None, None),
        P(("dp", "wide"), None, None),
        P(("dp", "wide"), None, None, None),
        P("wide", None),
        P(None, None, "wide", None),
        P("wide", None),
        P("wide", None),
        P("wide"),
        P("wide"),
        P("wide", None),
        P(None, None, "wide", None),
        P("wide", None),
        P("wide"),
        P("wide"),
    )
    out_specs = (
        P(("dp", "wide"), None, None, None),
        P(("dp", "wide"), None, None, None),
        P("wide", None),
        P(None, None, "wide", None),
        P("wide", None),
        P("wide", None),
        P("wide"),
        P("wide"),
        P("wide", None),
        P(None, None, "wide", None),
        P("wide", None),
        P("wide"),
        P("wide"),
    )
    return jax.shard_map(fused_shards if fused else shards, mesh=mesh, in_specs=in_specs, out_specs=out_specs, check_vma=False)
```

```python
import functools
import types

import jax
import jax.numpy as jnp
from jax import lax
from jax.experimental import pallas as pl
from jax.experimental.pallas import tpu as pltpu
from jax.sharding import PartitionSpec as P

NORM_EPS = 1e-05


def pixel_product(source, kernel):
    return jnp.einsum("bhwc,co->bhwo", source, kernel, preferred_element_type=jnp.float32)


def weight_grad(source, upstream):
    return jnp.einsum("bhwc,bhwo->co", source, upstream, preferred_element_type=jnp.float32)


def input_grad(upstream, kernel):
    return jnp.einsum("bhwo,co->bhwc", upstream, kernel, preferred_element_type=jnp.float32)


def conv_spatial(source, kernel, stride):
    out_h = source.shape[1] // stride
    out_w = source.shape[2] // stride
    padded = jnp.pad(source, ((0, 0), (1, 1), (1, 1), (0, 0)))
    summed = jnp.zeros((source.shape[0], out_h, out_w, kernel.shape[3]), jnp.float32)
    for row_off in range(3):
        for col_off in range(3):
            window = padded[
                :,
                row_off : row_off + stride * out_h : stride,
                col_off : col_off + stride * out_w : stride,
            ]
            summed = summed + pixel_product(window, kernel[row_off, col_off])
    return summed


def conv_back(source, upstream, kernel, stride):
    out_h = upstream.shape[1]
    out_w = upstream.shape[2]
    padded = jnp.pad(source, ((0, 0), (1, 1), (1, 1), (0, 0)))
    grad_src = jnp.zeros(padded.shape, jnp.float32)
    kernel_rows = []
    for row_off in range(3):
        for col_off in range(3):
            window = padded[
                :,
                row_off : row_off + stride * out_h : stride,
                col_off : col_off + stride * out_w : stride,
            ]
            kernel_rows.append(weight_grad(window, upstream))
            grad_src = grad_src.at[
                :,
                row_off : row_off + stride * out_h : stride,
                col_off : col_off + stride * out_w : stride,
            ].add(input_grad(upstream, kernel[row_off, col_off]))
    kernel_grad = jnp.stack(kernel_rows).reshape(kernel.shape)
    return (kernel_grad, grad_src[:, 1:-1, 1:-1])


def norm_forward(pre, valid, count, gain, shift):
    moments = lax.psum(
        (jnp.sum(pre * valid, axis=(0, 1, 2)), jnp.sum(pre * pre * valid, axis=(0, 1, 2))),
        ("dp", "wide"),
    )
    mean_val = moments[0] / count
    variance = moments[1] / count - mean_val * mean_val
    scaler = lax.rsqrt(variance + NORM_EPS)
    normed = (pre - mean_val) * scaler
    return (gain * normed + shift, (mean_val, scaler))


def norm_backward(upstream, pre, valid, count, gain, stats):
    mean_val, scaler = stats
    sums = lax.psum(
        (jnp.sum(upstream, axis=(0, 1, 2)), jnp.sum(upstream * pre, axis=(0, 1, 2))), ("dp", "wide")
    )
    first_sum, second_sum = sums
    centred = second_sum - mean_val * first_sum
    grad_gain = scaler * centred
    grad_var = -0.5 * gain * centred * scaler * scaler * scaler
    grad_mean = -gain * scaler * first_sum - 2.0 * mean_val * grad_var
    grad_pre = gain * scaler * upstream + valid / count * (grad_mean + 2.0 * pre * grad_var)
    return (grad_pre, grad_gain, first_sum)


def silu_grad(pre_act, upstream):
    sigma = jax.nn.sigmoid(pre_act)
    return upstream * sigma * (1.0 + pre_act * (1.0 - sigma))


def own_slice(whole, local_len):
    start = lax.axis_index("wide") * local_len
    return lax.dynamic_slice_in_dim(whole, start, local_len, 0)


def shards(
    images,
    pixel_mask,
    cotangent,
    reduce_one,
    spatial_one,
    expand_one,
    project_one,
    gains_one,
    shifts_one,
    reduce_two,
    spatial_two,
    expand_two,
    gains_two,
    shifts_two,
):
    valid_hi = pixel_mask.astype(jnp.float32)[..., None]
    valid_lo = valid_hi[:, ::2, ::2]
    counts = lax.psum((jnp.sum(valid_hi), jnp.sum(valid_lo)), ("dp", "wide"))
    count_hi = jnp.maximum(counts[0], 1.0)
    count_lo = jnp.maximum(counts[1], 1.0)
    first_full = (
        lax.all_gather(reduce_one, "wide", axis=0, tiled=True),
        lax.all_gather(spatial_one, "wide", axis=2, tiled=True),
        lax.all_gather(expand_one, "wide", axis=0, tiled=True),
        lax.all_gather(project_one, "wide", axis=0, tiled=True),
        lax.all_gather(gains_one, "wide", axis=0, tiled=True),
        lax.all_gather(shifts_one, "wide", axis=0, tiled=True),
    )
    red_a, spa_a, exp_a, proj_a, gain_a, shift_a = first_full
    mid_a = red_a.shape[1]
    mid_b = 2 * mid_a
    out_a = mid_b + exp_a.shape[1]
    out_b = out_a + exp_a.shape[1]
    gain_af = gain_a.astype(jnp.float32)
    shift_af = shift_a.astype(jnp.float32)
    pre_one = pixel_product(images, red_a)
    y_one, stat_one = norm_forward(pre_one, valid_hi, count_hi, gain_af[:mid_a], shift_af[:mid_a])
    act_one = jax.nn.silu(y_one).astype(jnp.bfloat16)
    pre_two = conv_spatial(act_one, spa_a, 2)
    y_two, stat_two = norm_forward(
        pre_two, valid_lo, count_lo, gain_af[mid_a:mid_b], shift_af[mid_a:mid_b]
    )
    act_two = jax.nn.silu(y_two).astype(jnp.bfloat16)
    pre_three = pixel_product(act_two, exp_a)
    y_three, stat_three = norm_forward(
        pre_three, valid_lo, count_lo, gain_af[mid_b:out_a], shift_af[mid_b:out_a]
    )
    sampled = images[:, ::2, ::2]
    pre_proj = pixel_product(sampled, proj_a)
    y_proj, stat_proj = norm_forward(
        pre_proj, valid_lo, count_lo, gain_af[out_a:out_b], shift_af[out_a:out_b]
    )
    sum_one = y_three + y_proj
    hidden = jax.nn.silu(sum_one)
    hidden_low = hidden.astype(jnp.bfloat16)
    second_full = (
        lax.all_gather(reduce_two, "wide", axis=0, tiled=True),
        lax.all_gather(spatial_two, "wide", axis=2, tiled=True),
        lax.all_gather(expand_two, "wide", axis=0, tiled=True),
        lax.all_gather(gains_two, "wide", axis=0, tiled=True),
        lax.all_gather(shifts_two, "wide", axis=0, tiled=True),
    )
    red_b, spa_b, exp_b, gain_b, shift_b = second_full
    gain_bf = gain_b.astype(jnp.float32)
    shift_bf = shift_b.astype(jnp.float32)
    pre_four = pixel_product(hidden_low, red_b)
    y_four, stat_four = norm_forward(
        pre_four, valid_lo, count_lo, gain_bf[:mid_a], shift_bf[:mid_a]
    )
    act_four = jax.nn.silu(y_four).astype(jnp.bfloat16)
    pre_five = conv_spatial(act_four, spa_b, 1)
    y_five, stat_five = norm_forward(
        pre_five, valid_lo, count_lo, gain_bf[mid_a:mid_b], shift_bf[mid_a:mid_b]
    )
    act_five = jax.nn.silu(y_five).astype(jnp.bfloat16)
    pre_six = pixel_product(act_five, exp_b)
    y_six, stat_six = norm_forward(
        pre_six, valid_lo, count_lo, gain_bf[mid_b:out_a], shift_bf[mid_b:out_a]
    )
    sum_two = y_six + hidden
    activations = jax.nn.silu(sum_two).astype(jnp.bfloat16)
    back_two = (
        lax.all_gather(reduce_two, "wide", axis=0, tiled=True),
        lax.all_gather(spatial_two, "wide", axis=2, tiled=True),
        lax.all_gather(expand_two, "wide", axis=0, tiled=True),
        lax.all_gather(gains_two, "wide", axis=0, tiled=True),
    )
    red_b, spa_b, exp_b, gain_b = back_two
    gain_bf = gain_b.astype(jnp.float32)
    upstream = cotangent.astype(jnp.float32)
    grad_sum_two = silu_grad(sum_two, upstream)
    grad_pre6, gain_g6, shift_g6 = norm_backward(
        grad_sum_two, pre_six, valid_lo, count_lo, gain_bf[mid_b:out_a], stat_six
    )
    low_six = grad_pre6.astype(jnp.bfloat16)
    grad_exp_b = weight_grad(act_five, low_six)
    grad_act5 = input_grad(low_six, exp_b)
    grad_pre5, gain_g5, shift_g5 = norm_backward(
        silu_grad(y_five, grad_act5), pre_five, valid_lo, count_lo, gain_bf[mid_a:mid_b], stat_five
    )
    low_five = grad_pre5.astype(jnp.bfloat16)
    grad_spa_b, grad_act4 = conv_back(act_four, low_five, spa_b, 1)
    grad_pre4, gain_g4, shift_g4 = norm_backward(
        silu_grad(y_four, grad_act4), pre_four, valid_lo, count_lo, gain_bf[:mid_a], stat_four
    )
    low_four = grad_pre4.astype(jnp.bfloat16)
    grad_red_b = weight_grad(hidden_low, low_four)
    grad_hidden = grad_sum_two + input_grad(low_four, red_b)
    owned_two = (
        lax.psum_scatter(
            grad_red_b.astype(jnp.bfloat16), "wide", scatter_dimension=0, tiled=True
        ).astype(jnp.float32),
        lax.psum_scatter(
            grad_spa_b.astype(jnp.bfloat16), "wide", scatter_dimension=2, tiled=True
        ).astype(jnp.float32),
        lax.psum_scatter(
            grad_exp_b.astype(jnp.bfloat16), "wide", scatter_dimension=0, tiled=True
        ).astype(jnp.float32),
    )
    owned_two = (
        lax.psum(owned_two[0].astype(jnp.bfloat16), "dp").astype(jnp.float32),
        lax.psum(owned_two[1].astype(jnp.bfloat16), "dp").astype(jnp.float32),
        lax.psum(owned_two[2].astype(jnp.bfloat16), "dp").astype(jnp.float32),
    )
    back_one = (
        lax.all_gather(reduce_one, "wide", axis=0, tiled=True),
        lax.all_gather(spatial_one, "wide", axis=2, tiled=True),
        lax.all_gather(expand_one, "wide", axis=0, tiled=True),
        lax.all_gather(project_one, "wide", axis=0, tiled=True),
        lax.all_gather(gains_one, "wide", axis=0, tiled=True),
    )
    red_a, spa_a, exp_a, proj_a, gain_a = back_one
    gain_af = gain_a.astype(jnp.float32)
    grad_sum_one = silu_grad(sum_one, grad_hidden)
    grad_pre3, gain_g3, shift_g3 = norm_backward(
        grad_sum_one, pre_three, valid_lo, count_lo, gain_af[mid_b:out_a], stat_three
    )
    grad_prep, gain_gp, shift_gp = norm_backward(
        grad_sum_one, pre_proj, valid_lo, count_lo, gain_af[out_a:out_b], stat_proj
    )
    low_three = grad_pre3.astype(jnp.bfloat16)
    low_proj = grad_prep.astype(jnp.bfloat16)
    grad_exp_a = weight_grad(act_two, low_three)
    grad_act2 = input_grad(low_three, exp_a)
    grad_proj_a = weight_grad(sampled, low_proj)
    grad_sampled = input_grad(low_proj, proj_a)
    grad_pre2, gain_g2, shift_g2 = norm_backward(
        silu_grad(y_two, grad_act2), pre_two, valid_lo, count_lo, gain_af[mid_a:mid_b], stat_two
    )
    low_two = grad_pre2.astype(jnp.bfloat16)
    grad_spa_a, grad_act1 = conv_back(act_one, low_two, spa_a, 2)
    grad_pre1, gain_g1, shift_g1 = norm_backward(
        silu_grad(y_one, grad_act1), pre_one, valid_hi, count_hi, gain_af[:mid_a], stat_one
    )
    low_one = grad_pre1.astype(jnp.bfloat16)
    grad_red_a = weight_grad(images, low_one)
    grad_input = input_grad(low_one, red_a)
    grad_input = grad_input.at[:, ::2, ::2].add(grad_sampled)
    grad_images = grad_input.astype(jnp.bfloat16)
    owned_one = (
        lax.psum_scatter(
            grad_red_a.astype(jnp.bfloat16), "wide", scatter_dimension=0, tiled=True
        ).astype(jnp.float32),
        lax.psum_scatter(
            grad_spa_a.astype(jnp.bfloat16), "wide", scatter_dimension=2, tiled=True
        ).astype(jnp.float32),
        lax.psum_scatter(
            grad_exp_a.astype(jnp.bfloat16), "wide", scatter_dimension=0, tiled=True
        ).astype(jnp.float32),
        lax.psum_scatter(
            grad_proj_a.astype(jnp.bfloat16), "wide", scatter_dimension=0, tiled=True
        ).astype(jnp.float32),
    )
    owned_one = (
        lax.psum(owned_one[0].astype(jnp.bfloat16), "dp").astype(jnp.float32),
        lax.psum(owned_one[1].astype(jnp.bfloat16), "dp").astype(jnp.float32),
        lax.psum(owned_one[2].astype(jnp.bfloat16), "dp").astype(jnp.float32),
        lax.psum(owned_one[3].astype(jnp.bfloat16), "dp").astype(jnp.float32),
    )
    gains_grad_a = jnp.concatenate([gain_g1, gain_g2, gain_g3, gain_gp])
    shifts_grad_a = jnp.concatenate([shift_g1, shift_g2, shift_g3, shift_gp])
    gains_grad_b = jnp.concatenate([gain_g4, gain_g5, gain_g6])
    shifts_grad_b = jnp.concatenate([shift_g4, shift_g5, shift_g6])
    local_a = gains_one.shape[0]
    local_b = gains_two.shape[0]
    return (
        activations,
        grad_images,
        owned_one[0],
        owned_one[1],
        owned_one[2],
        owned_one[3],
        own_slice(gains_grad_a, local_a),
        own_slice(shifts_grad_a, local_a),
        owned_two[0],
        owned_two[1],
        owned_two[2],
        own_slice(gains_grad_b, local_b),
        own_slice(shifts_grad_b, local_b),
    )


MESH = pl.DeviceIdType.MESH
F32 = jnp.float32
BF16 = jnp.bfloat16
ALL = slice(None)
NAMES = R1, S1, E1, P1, R2, S2, E2 = range(7)
ROW, TAP, COL = range(3)
KINDS = (ROW, TAP, COL, ROW, ROW, TAP, COL)
NORMS = N1, N2, N3, NP, N4, N5, N6 = range(7)


def nn(left, right):
    return jnp.dot(left, right, preferred_element_type=F32)


def nt(left, right):
    return lax.dot_general(left, right, (((1,), (1,)), ((), ())), preferred_element_type=F32)


def tn(left, right):
    return lax.dot_general(left, right, (((0,), (0,)), ((), ())), preferred_element_type=F32)


def whole_shape(kind, shard):
    if kind == TAP:
        return (shard[0], 4, 2) + tuple(shard[1:])
    return (4, 2) + tuple(shard)


class Links:
    def __init__(self, send_sems, recv_sems, core, base):
        self.send_sems, self.recv_sems = send_sems, recv_sems
        self.dp, self.wide = lax.axis_index("dp"), lax.axis_index("wide")
        self.core = core
        self.y, self.z, self.x = self.dp // 2, self.wide // 2, self.wide % 2
        self.next_send = base

    def device(self, dy=0, dz=0, dx=0, other=False):
        core = 1 - self.core if other else self.core
        y = (self.y + dy) % 2
        z, x = (self.z + dz) % 4, (self.x + dx) % 2
        return {"dp": y * 2 + core, "wide": z * 2 + x}

    def copy(self, src, dst, slot, **to):
        sem = self.send_sems.at[self.next_send]
        self.next_send += 1
        return pltpu.make_async_remote_copy(
            src_ref=src, dst_ref=dst, send_sem=sem, recv_sem=self.recv_sems.at[slot],
            device_id=self.device(**to), device_id_type=MESH)

    def send(self, src, dst, slot, **to):
        made = self.copy(src, dst, slot, **to)
        made.start()
        return made

    def arrived(self, dst, slot):
        pltpu.make_async_remote_copy(
            src_ref=dst, dst_ref=dst, send_sem=self.send_sems.at[0], recv_sem=self.recv_sems.at[slot],
            device_id=self.device(other=True), device_id_type=MESH).wait_recv()


def slot_table(**counts):
    table, at = types.SimpleNamespace(), 0
    for key, count in counts.items():
        setattr(table, key, at)
        at += count
    table.total = at
    return table


T = slot_table(raw=1, mask=1, cot=1, pix=1, xc2=1, act2=1, hlow=1, xc5=1, act5=1, low6=1, low5=1, low4=1, low3=1, lowp=1, low2=1,
               low1=1, gsamp=1, out_act=1, out_norm=1, out_gimg=1, samp_y=1, act1=1, act1_y=1, act4_y=1, low5_y=1, low2_y=1, lowp_own=1, lowp_y=6,
               out=7, hand=28, gather=8 * 28, reduce=6 * 16, norm_in=8, sums=24)


def sigmoid(v):
    return 1.0 / (1.0 + jnp.exp(-v))


def silu_back(v, up):
    sg = sigmoid(v)
    return up * sg * (1.0 + v * (1.0 - sg))


def pixel_ids(rows, cols):
    row = lax.broadcasted_iota(jnp.int32, (rows, cols), 0)
    return (row // 8) % 8, row % 8


def shifted(value, di, dj):
    step = di * 8 + dj
    if step == 0:
        return value
    rows, cols = value.shape
    rolled = pltpu.roll(value, (-step) % rows, 0)
    i, j = pixel_ids(rows, cols)
    keep = None
    for index, d in ((i, di), (j, dj)):
        if d == 0:
            continue
        this = index < 8 - d if d > 0 else index >= -d
        keep = this if keep is None else keep & this
    return jnp.where(keep, rolled, 0.0)


A, B, C, D, E = range(5)
MAKE, MAKE_P1, OTHER = -1, -2, -3
PIECES = (
    (R1, 0, 1, C), (S1, 0, 1, C), (S1, 2, 1, B), (S1, 4, 1, C), (S1, 6, 1, C), (S1, 8, 1, D), (E1, 0, 384, B), (E1, 768, 384, C),
    (P1, 0, 256, D), (P1, 256, 256, D), (P1, 512, 256, B), (P1, 768, 256, C), (P1, 1024, 256, A), (P1, 1280, 256, C), (R2, 0, 1,
    A), (R2, 2, 1, B), (S2, 0, 1, B), (S2, 2, 1, A), (S2, 4, 1, B), (S2, 6, 1, A), (S2, 8, 1, E), (E2, 0, 384, D), (E2, 768, 384,
    E))
GATHER_PLAN = (
    (13, 0), (0, 0), (2, 0), (4, 0), (14, 0), (12, 0), (13, 1), (3, 0), (11, 0), (6, 0), (5, 0), (17, 0), (0, 1), (1, 0), (19, 0),
    (7, 0), (9, 0), (20, 0), (2, 1), (13, 2), (10, 0), (8, 0), (4, 1), (3, 1), (0, 2), (12, 1), (15, 0), (2, 2), (13, 3), (4, 2),
    (16, 0), (3, 2), (5, 1), (1, 1), (11, 1), (6, 1), (0, 3), (7, 1), (2, 3), (14, 1), (18, 0), (5, 3), (4, 3), (9, 1), (19, 1),
    (1, 2), (3, 3), (6, 2), (10, 1), (7, 2), (1, 3), (8, 1), (9, 3), (11, 2), (6, 3), (10, 2), (17, 1), (12, 2), (15, 1), (7, 3),
    (22, 0), (16, 1), (11, 3), (21, 0), (8, 3), (14, 2), (10, 3), (12, 3), (15, 2), (16, 2), (20, 1), (18, 1), (19, 2), (14, 3),
    (15, 3), (17, 2), (18, 2), (22, 1), (19, 3), (16, 3), (21, 1), (17, 3), (20, 3), (18, 3), (21, 3), (22, 3), (OTHER, 0),
    (OTHER, 1))
SUMMED = (
    (E2, 0, 384, (3, 1, 2)), (E2, 768, 384, (3, 1, 2)), (R2, 0, 2, (2, 3, 1)), (E1, 0, 384, (1, 2, 3)), (E1, 768, 384, (2, 1, 3)),
    (R1, 0, 1, (2, 1, 3)), (S2, 0, 2, (1, 3)), (S2, 2, 2, (3, 1)), (S2, 4, 1, (1, 3)), (S1, 0, 1, (1, 3)), (S1, 1, 1, (1, 3)),
    (S1, 2, 1, (1, 3)), (S1, 3, 1, (1, 3)), (S1, 4, 1, (1, 3)), (P1, 0, 256, (1, 3)), (P1, 256, 256, (1, 3)), (P1, 512, 256, (1,
    3)))
REDUCE_PLAN = (
    (OTHER, 0), (MAKE, E2), (0, 0), (OTHER, 1), (1, 0), (MAKE, R2), (2, 0), (MAKE, S2), (6, 0), (7, 0), (0, 1), (1, 1), (MAKE,
    E1), (3, 0), (OTHER, 2), (6, 1), (4, 0), (0, 2), (OTHER, 3), (2, 1), (MAKE_P1, 0), (14, 0), (MAKE_P1, 2), (1, 2), (7, 1), (3,
    1), (16, 0), (6, 2), (MAKE, S1), (11, 0), (1, 3), (0, 3), (14, 1), (7, 2), (MAKE, R1), (6, 3), (5, 0), (12, 0), (1, 4), (3,
    2), (7, 3), (2, 2), (11, 1), (0, 4), (10, 0), (MAKE_P1, 1), (16, 1), (9, 0), (12, 1), (4, 1), (14, 2), (3, 3), (2, 3), (15,
    0), (10, 1), (11, 2), (5, 1), (3, 4), (14, 3), (2, 4), (9, 1), (4, 2), (16, 2), (11, 3), (13, 0), (12, 2), (8, 0), (15, 1),
    (16, 3), (10, 2), (12, 3), (9, 2), (5, 2), (4, 3), (10, 3), (9, 3), (13, 1), (8, 1), (15, 2), (4, 4), (5, 3), (13, 2), (15,
    3), (5, 4), (8, 2))
PARTS_P1 = 3
def piece_of(piece, buf, z, x, h):
    name, first, count, order = piece
    kind = KINDS[name]
    if kind == COL or name == P1:
        if kind == COL:
            cols = pl.ds(first, 2 * count) if h is ALL else pl.ds(pl.multiple_of(first + h * count, 128), count)
            return buf.at[z, x, :, cols]
        return buf.at[z, x, h, :, pl.ds(first, count)]
    if name == R1:
        return buf.at[z, x, h]
    part = pl.ds(first, 1) if first == 8 else pl.ds(first, 2) if h is ALL else pl.ds(first + h, 1)
    return buf.at[part, z, x] if kind == TAP else buf.at[z, x, part]


def shard_of(piece, buf, h):
    name, first, count, order = piece
    kind = KINDS[name]
    if kind == COL:
        cols = pl.ds(first, 2 * count) if h is ALL else pl.ds(pl.multiple_of(first + h * count, 128), count)
        return buf.at[:, cols]
    if name == P1:
        return buf.at[h, :, pl.ds(first, count)]
    if name == R1:
        return buf.at[h]
    return buf.at[pl.ds(first, 1) if first == 8 else pl.ds(first, 2) if h is ALL else pl.ds(first + h, 1)]


def columns_of(ref, h):
    return pl.ds(pl.multiple_of(h * (ref.shape[-1] // 2), 128), ref.shape[-1] // 2)


def mover(links, ins, outs, w, g, third, fin, m, credit):
    x, y, z = links.x, links.y, links.z
    pending = []
    local_sems = m.local_sems

    def post(src, dst, slot, **to):
        made = links.send(src, dst, slot, **to)
        pending.append(made)
        return made

    def drain():
        for made in pending:
            made.wait_send()
        pending.clear()

    post(ins.images, m.raw.at[0], T.raw, other=True)
    post(ins.mask, m.mask.at[0], T.mask, other=True)
    own = []
    for n, piece in enumerate(PIECES):
        made = pltpu.make_async_copy(shard_of(piece, ins.weights[piece[0]], ALL), piece_of(piece, w[piece[0]], z, x, ALL), local_sems.at[n])
        made.start()
        own.append(made)

    flight = {}

    def along_z(src, dst, slot):
        return [post(src, dst, slot + dz, dz=dz) for dz in (2, 1, 3)]

    def gather(n, stage):
        piece = PIECES[n]
        buf, shard, order, slot = w[piece[0]], ins.weights[piece[0]], piece[3], T.gather + 8 * n
        if stage == 0:
            h = ALL if order in (D, E) else y
            src, dst = shard_of(piece, shard, h), piece_of(piece, buf, z, x, h)
        else:
            if order == A:
                part = (z, ALL, y) if stage == 1 else (ALL, ALL, y)
            elif order == B:
                part = (ALL, x, y) if stage == 1 else (ALL, x, ALL)
            elif order == C:
                part = (ALL, x, y) if stage == 1 else (ALL, ALL, y)
            elif order == D:
                part = (ALL, x, ALL)
            else:
                part = (z, ALL, ALL)
            src = dst = piece_of(piece, buf, *part)
        axis = ((1, 3, 2), (3, 2, 1), (3, 1, 2), (3, 1), (1, 3))[order][stage]
        if axis == 3:
            flight[n] = along_z(src, dst, slot)
        elif axis == 2:
            both = x if order == B else ALL
            flight[n] = []
            for dz in (1, 2, 3):
                part = piece_of(piece, buf, (z + dz) % 4, both, y)
                flight[n].append(post(part, part, slot + 4 + dz, dy=1))
            if order != B:
                part = piece_of(piece, buf, z, 1 - x, y)
                flight[n].append(post(part, part, slot + 4, dy=1))
        else:
            flight[n] = [post(src, dst, slot, dx=1)]

    def landed(n):
        for made in flight[n]:
            made.wait_recv()

    def gathered(n):
        piece = PIECES[n]
        if piece[0] != P1:
            whole = piece_of(piece, w[piece[0]], ALL, ALL, ALL)
            post(whole, whole, T.hand + n, other=True)
            return
        if not m.seen:
            links.arrived(m.pix, T.pix)
            m.seen.append(0)

        cols = pl.ds(piece[1], piece[2])
        m.prep[:, cols] = nn(m.pix[0:256, :], w[P1][:, :, :, :, cols].reshape(1024, piece[2]))
        cols = m.prep.at[:, pl.ds(piece[1], piece[2])]
        post(cols, cols, T.hand + n, other=True)

    def swap_act1():
        links.arrived(m.act1.at[y], T.act1)
        post(m.act1.at[y], m.act1.at[y], T.act1_y, dy=1)

    def swap_pix():
        if not m.seen:
            links.arrived(m.pix, T.pix)
            m.seen.append(0)
        post(m.pix.at[pl.ds(0, 256)], m.samp.at[y], T.samp_y, dy=1)

    waited = False
    for n, stage in GATHER_PLAN:
        if n == OTHER:
            (swap_act1, swap_pix)[stage]()
            continue
        if stage and not waited:
            for made in own:
                made.wait()
            waited = True
        if stage:
            landed(n)
        if stage == 3:
            gathered(n)
        else:
            gather(n, stage)
    post(ins.cotangent, m.cot.at[0], T.cot, other=True)
    drain()

    for to in (dict(dx=1), dict(dy=1)):
        pl.semaphore_signal(credit.at[0], inc=1, device_id=links.device(**to), device_id_type=MESH)
    pl.semaphore_wait(credit.at[0], 2)

    def windows_one():
        links.arrived(m.act1.at[1 - y], T.act1_y)
        for tap in range(9):
            a, b = tap // 3, tap % 3
            pq = (0 if a == 1 else 2) + (0 if b == 1 else 1)
            block = m.act1[1 - y, pq * 256:pq * 256 + 256, :].astype(F32)
            m.xc2[1 - y, :, tap * 384:(tap + 1) * 384] = shifted(block, -1 if a == 0 else 0, -1 if b == 0 else 0).astype(BF16)

    def windows_two():
        links.arrived(m.act4.at[1 - y], T.act4_y)
        for tap in range(9):
            block = m.act4[1 - y].astype(F32)
            m.xc5[1 - y, :, tap * 384:(tap + 1) * 384] = shifted(block, tap // 3 - 1, tap % 3 - 1).astype(BF16)

    def add(into, own, others):
        got = own[...].astype(F32)
        for other in others:
            got = got + other[...].astype(F32)
        into[...] = got.astype(BF16)

    def reduce(n, stage):
        name, first, count, order = SUMMED[n]
        kind, buf, into, last = KINDS[name], g[name], w[name], fin[name]
        slot = T.reduce + 6 * n
        paired = len(order) == 2
        done = order[:stage]

        def pick(ref, zi, xi, h):
            if kind == TAP:
                return ref.at[pl.ds(first, count), zi, xi]
            if name == P1:
                return ref.at[zi, xi, :, :, pl.ds(first, count)]
            if kind == COL:
                cols = pl.ds(first, 2 * count) if h is ALL else pl.ds(pl.multiple_of(first + h * count, 128), count)
                return ref.at[zi, xi, :, cols]
            return ref.at[zi, xi] if h is ALL else ref.at[zi, xi, pl.ds(h * count, count)]

        def pick_z(k, xi, h):
            ref = third[name].at[k]
            if kind == TAP:
                return ref.at[pl.ds(first, count), xi]
            if name == P1:
                return ref.at[xi, :, :, pl.ds(first, count)]
            if kind == COL:
                thin = ref.shape[-1] < buf.shape[-1]
                return ref.at[xi, :, pl.ds(first, 2 * count) if h is ALL else pl.ds(first // 2 if thin else first, count)]
            return ref.at[xi]

        def pick_last(i):
            if kind == TAP:
                return last.at[8 if first == 4 else 2 * (first + i) + y]
            if name == P1:
                return last.at[:, :, pl.ds(pl.multiple_of(768 * y + first, 128), count)]
            if kind == COL:
                return last.at[:, pl.ds(pl.multiple_of(first + y * count, 128), count)]
            return last.at[pl.ds(y * count, count)]

        def held(axes):
            return z if 3 in axes else ALL, x if 1 in axes else ALL, y if 2 in axes else ALL

        def landing(axes, axis, zi):
            if name == P1:
                return m.land.at[zi, :, :, pl.ds(first, count)]
            if axis == 1:
                return pick(into, zi, 0, ALL if paired or 2 not in axes else 1)
            return pick(into, zi, 1 if 1 in axes else ALL, 0)

        if stage:
            for made in flight[n]:
                made.wait_recv()
        if 0 < stage <= len(order):
            before, axis = order[:stage - 1], order[stage - 1]
            zi, xi, h = held(done)
            taps_here = count if kind == TAP else 1
            many_z, many_x = 4 if zi is ALL else 1, 2 if xi is ALL else 1

            def one(i, carry):
                tap, cell = i // (many_z * many_x), i % (many_z * many_x)
                at_z, at_x = cell // many_x if zi is ALL else zi, cell % many_x if xi is ALL else xi

                def inner(ref):
                    return ref.at[tap] if kind == TAP else ref

                own = inner(pick(buf, at_z, at_x, h))
                if axis == 3:
                    others = [inner(pick_z(k, 0 if 1 in before else at_x, ALL if 2 not in before else 0)) for k in range(3)]
                else:
                    land_x = 0 if axis == 1 else 1 if 1 in before else at_x
                    land_h = (ALL if paired or 2 not in before else 1) if axis == 1 else 0
                    others = [m.land.at[at_z, :, :, pl.ds(first, count)] if name == P1 else inner(pick(into, at_z, land_x, land_h))]
                add(pick_last(tap) if stage == len(order) else own, own, others)
                return carry

            lax.fori_loop(0, taps_here * many_z * many_x, one, 0)
        if stage < len(order):
            axis = order[stage]
            zi, xi, h = held(done)
            if axis == 1:
                flight[n] = [post(pick(buf, zi, 1 - x, h), landing(done, 1, zi), slot, dx=1)]
            elif axis == 2:
                flight[n] = [post(pick(buf, zi, xi, 1 - y), landing(done, 2, zi), slot + 4, dy=1)]
            else:
                flight[n] = [post(pick(buf, (z + dz) % 4, xi, h), pick_z(dz - 1, 0 if 1 in done else ALL, ALL if 2 not in done else 0),
                                  slot + dz, dz=dz) for dz in (2, 1, 3)]
        elif stage == len(order) and not (kind == TAP and first == 4):
            parts = [pick_last(i) for i in range(count if kind == TAP else 1)]
            flight[n] = [post(part, part, slot + (5 if kind != TAP else 4 + i), dy=1) for i, part in enumerate(parts)]
        else:
            left[name] -= 1
            if left[name] == 0:
                made = pltpu.make_async_copy(last, outs.grads[name], local_sems.at[name])
                made.start()
                m.tail.append(made)
                post(last, outs.grads[name], T.out + name, other=True)

    def columns(name, left, right):
        def one(step, carry):
            off = pl.multiple_of(step * 256, 256)
            part = tn(left, right[:, pl.ds(off, 256)])
            g[name][..., pl.ds(off, 256)] = part.astype(BF16).reshape(g[name].shape[:-1] + (256,))
            return carry

        lax.fori_loop(0, right.shape[1] // 256, one, 0)

    def taps(name, windows, low):
        def one(k, carry):
            tap = jnp.where(k == 4, 8, 2 * k + y)
            off = pl.multiple_of(tap * 384, 128)
            part = tn(windows[:, :, pl.ds(off, 384)].reshape(512, 384), low[...].reshape(512, 384))
            g[name][k] = part.astype(BF16).reshape(4, 2, 48, 384)
            return carry

        lax.fori_loop(0, 5, one, 0)

    def make(name):
        if name == E2:
            links.arrived(m.act5, T.act5)
            links.arrived(m.low6, T.low6)
            columns(E2, m.act5[...], m.low6)
        elif name == S2:
            links.arrived(m.xc5.at[y], T.xc5)
            links.arrived(m.low5.at[y], T.low5)
            links.arrived(m.low5.at[1 - y], T.low5_y)
            taps(S2, m.xc5, m.low5)
        elif name == R2:
            links.arrived(m.hlow, T.hlow)
            links.arrived(m.low4, T.low4)

            def one(step, carry):
                part = tn(m.hlow[:, pl.ds(pl.multiple_of(step * 384, 128), 384)], m.low4[...])
                g[R2][step] = part.astype(BF16).reshape(2, 4, 48, 384)
                return carry

            lax.fori_loop(0, 4, one, 0)
        elif name == E1:
            links.arrived(m.act2, T.act2)
            links.arrived(m.low3, T.low3)
            columns(E1, m.act2[...], m.low3)
        elif name == S1:
            links.arrived(m.xc2.at[y], T.xc2)
            links.arrived(m.low2.at[y], T.low2)
            links.arrived(m.low2.at[1 - y], T.low2_y)
            taps(S1, m.xc2, m.low2)
        else:
            links.arrived(m.low1, T.low1)

            def one(step, carry):
                part = tn(m.pix[:, pl.ds(pl.multiple_of(step * 256, 256), 256)], m.low1[...])
                g[R1][step] = part.astype(BF16).reshape(2, 2, 64, 384)
                return carry

            lax.fori_loop(0, 4, one, 0)

    def swap_projection():
        theirs = m.lowp.at[:, columns_of(m.lowp, 1 - y)]
        links.arrived(theirs, T.lowp)
        for k in range(PARTS_P1):
            size = 768 // PARTS_P1
            cols = pl.ds(pl.multiple_of((1 - y) * 768 + k * size, 128), size)
            post(m.lowp.at[:, cols], m.lowp_y.at[:, pl.ds(k * size, size)], T.lowp_y + k, dy=1)

    def project_back():
        links.arrived(m.lowp.at[:, columns_of(m.lowp, y)], T.lowp_own)

        def back(step, carry):
            kern = w[P1][step].reshape(256, 1536)
            m.gsamp[:, pl.ds(pl.multiple_of(step * 256, 256), 256)] = nt(m.lowp[...], kern)
            return carry

        lax.fori_loop(0, 4, back, 0)
        post(m.gsamp, m.gsamp, T.gsamp, other=True)

    def make_projection(k):
        size = 768 // PARTS_P1
        if k == 0:
            links.arrived(m.samp.at[1 - y], T.samp_y)
        links.arrived(m.lowp_y.at[:, pl.ds(k * size, size)], T.lowp_y + k)
        mine = m.lowp[:, pl.ds(pl.multiple_of(y * 768 + k * size, 128), size)]
        theirs = m.lowp_y[:, pl.ds(k * size, size)]

        def one(step, carry):
            cols = pl.ds(pl.multiple_of(step * 256, 256), 256)
            part = tn(m.pix[0:256, cols], mine) + tn(m.samp[1 - y, :, cols], theirs)
            g[P1][step, :, :, :, pl.ds(k * size, size)] = part.astype(BF16).reshape(2, 2, 64, size)
            return carry

        lax.fori_loop(0, 4, one, 0)

    left = [sum(piece[0] == name for piece in SUMMED) for name in NAMES]
    for n, stage in REDUCE_PLAN:
        if n == MAKE:
            make(stage)
        elif n == OTHER:
            (windows_one, windows_two, swap_projection, project_back)[stage]()
        elif n == MAKE_P1:
            make_projection(stage)
        else:
            reduce(n, stage)
    drain()
    for made in m.tail:
        made.wait()
    links.arrived(outs.act, T.out_act)
    links.arrived(outs.norm, T.out_norm)
    links.arrived(outs.gimg, T.out_gimg)


def runner(links, ins, outs, w, m, sums):
    x, y, z = links.x, links.y, links.z
    me = y * 8 + links.wide
    pending = []
    local_sems = m.local_sems

    def post(src, dst, slot, **to):
        made = links.send(src, dst, slot, **to)
        pending.append(made)
        return made

    def hand(ref, slot):
        post(ref, ref, slot, other=True)

    def weight(name):
        for n, piece in enumerate(PIECES):
            if piece[0] == name:
                links.arrived(piece_of(piece, w[name], ALL, ALL, ALL), T.hand + n)

    peers = [(dy, dz, dx) for dz in (2, 1, 3, 0) for dx in (1, 0) for dy in (1, 0) if (dy, dz, dx) != (0, 0, 0)]

    quad = [(dy, 0, dx) for dy, dx in ((1, 1), (0, 1), (1, 0))]
    along = [(0, dz, 0) for dz in (2, 1, 3)]

    def spread(buf, mine, slot, to):
        sem = links.next_send
        links.next_send += 1
        for dy, dz, dx in to:
            pltpu.make_async_remote_copy(
                src_ref=buf.at[mine], dst_ref=buf.at[mine], send_sem=links.send_sems.at[sem], recv_sem=links.recv_sems.at[slot],
                device_id=links.device(dy=dy, dz=dz, dx=dx), device_id_type=MESH).start()
        others = buf.at[pl.ds(0, len(to))]
        return pltpu.make_async_remote_copy(
            src_ref=others, dst_ref=others, send_sem=links.send_sems.at[sem],
            recv_sem=links.recv_sems.at[slot], device_id=links.device(other=True), device_id_type=MESH)

    def added(parts):
        while len(parts) > 1:
            parts = [parts[i] + parts[i + 1] for i in range(0, len(parts), 2)]
        return parts[0]

    def total(which, rows):
        buf = sums[which]
        if rows[0].shape[1] < 1536:
            for r, row in enumerate(rows):
                buf[me, r:r + 1, :] = row
            waiting = spread(buf, me, T.sums + which, peers)
            waiting.wait_recv()
            waiting.wait_send()
            return added([buf[i] for i in range(16)])
        mine = y * 2 + x
        for r, row in enumerate(rows):
            buf[mine, r:r + 1, :] = row
        waiting = spread(buf, mine, T.sums + which, quad)
        waiting.wait_recv()
        waiting.wait_send()
        far = sums[which + 12]
        far[z] = added([buf[i] for i in range(4)])
        waiting = spread(far, z, T.sums + 12 + which, along)
        waiting.wait_recv()
        waiting.wait_send()
        return added([far[i] for i in range(4)])

    own_norm = pltpu.make_async_copy(ins.norm, m.norm_in.at[links.wide], local_sems.at[0])
    own_norm.start()
    own_raw = pltpu.make_async_copy(ins.images, m.raw.at[1], local_sems.at[1])
    own_raw.start()
    own_mask = pltpu.make_async_copy(ins.mask, m.mask.at[1], local_sems.at[2])
    own_mask.start()
    own_cot = pltpu.make_async_copy(ins.cotangent, m.cot.at[1], local_sems.at[3])
    own_cot.start()
    for k, (dz, dx) in enumerate([(dz, dx) for dz in (2, 1, 3, 0) for dx in (1, 0) if (dz, dx) != (0, 0)]):
        post(ins.norm, m.norm_in.at[links.wide], T.norm_in + dz * 2 + dx, dz=dz, dx=dx)

    lo = pl.ds(0, 256)
    r = lax.broadcasted_iota(jnp.int32, (256, 256), 0)
    c = lax.broadcasted_iota(jnp.int32, (256, 256), 1)
    source = (2 * ((r // 8) % 8) + r // 128) * 16 + 2 * (r % 8) + (r // 64) % 2
    perm = jnp.where(c == source, 1.0, 0.0).astype(BF16)
    m.perm[...] = perm

    own_mask.wait()
    links.arrived(m.mask.at[0], T.mask)
    flags = m.mask[...].reshape(64, 16).astype(F32)
    for pq in range(4):
        p, q = pq // 2, pq % 2
        row = lax.broadcasted_iota(jnp.int32, (256, 64), 0)
        line = lax.broadcasted_iota(jnp.int32, (256, 64), 1)
        pick = jnp.where(line == (row // 64) * 16 + 2 * ((row // 8) % 8) + p, 1.0, 0.0)
        lines = nn(pick.astype(BF16), flags.astype(BF16))
        row16 = lax.broadcasted_iota(jnp.int32, (256, 16), 0)
        col16 = lax.broadcasted_iota(jnp.int32, (256, 16), 1)
        one = jnp.sum(jnp.where(col16 == 2 * (row16 % 8) + q, lines, 0.0), axis=1, keepdims=True)
        m.valid[pq * 256:(pq + 1) * 256, :] = jnp.broadcast_to(one, (256, 128))

    own_raw.wait()
    links.arrived(m.raw.at[0], T.raw)
    for b in range(4):
        picked = nn(perm, m.raw[b // 2, (b % 2) * 256:(b % 2) * 256 + 256, :]).astype(BF16)
        for pq in range(4):
            m.pix[pq * 256 + b * 64:pq * 256 + b * 64 + 64, :] = picked[pq * 64:pq * 64 + 64, :]
    pix_sent = links.send(m.pix, m.pix, T.pix, other=True)

    own_norm.wait()
    for dz in range(4):
        for dx in range(2):
            if dz or dx:
                links.arrived(m.norm_in.at[0], T.norm_in + dz * 2 + dx)
    for s in range(8):
        piece = m.norm_in[s]
        at = 0
        for ref in (m.gain_a, m.shift_a, m.gain_b, m.shift_b):
            size = ref.shape[1] // 8
            ref[:, s * size:(s + 1) * size] = piece[:, at:at + size]
            at += size

    norms = m.norms

    def set_norm(key, mean_sum, square_sum, count, gain, shift):
        ref = norms[key]
        mean = mean_sum / count
        var = square_sum / count - mean * mean
        scaler = lax.rsqrt(var + NORM_EPS)
        ref[0:1, :] = mean
        ref[1:2, :] = scaler
        ref[2:3, :] = gain
        ref[3:4, :] = gain * scaler
        ref[4:5, :] = shift - mean * (gain * scaler)

    def set_back(key, first_sum, second_sum, count, at):
        ref = norms[key]
        mean, scaler, gain = ref[0:1, :], ref[1:2, :], ref[2:3, :]
        centred = second_sum - mean * first_sum
        grad_var = -0.5 * gain * centred * scaler * scaler * scaler
        grad_mean = -gain * scaler * first_sum - 2.0 * mean * grad_var
        ref[5:6, :] = grad_mean / count
        ref[6:7, :] = 2.0 * grad_var / count
        size = ref.shape[1]
        gain_at, shift_at = at
        m.norm_out[:, gain_at:gain_at + size] = scaler * centred
        m.norm_out[:, shift_at:shift_at + size] = first_sum

    def rows_of(key, at, size):
        ref = norms[key]
        return [ref[k:k + 1, pl.ds(at, size)] for k in range(8)]

    def norm_of(key, pre, at, size):
        ref = norms[key]
        return pre * ref[3:4, pl.ds(at, size)] + ref[4:5, pl.ds(at, size)]

    def back_of(key, pre, up, valid, at, size):
        ref = norms[key]
        return ref[3:4, pl.ds(at, size)] * up + valid * (ref[5:6, pl.ds(at, size)] + ref[6:7, pl.ds(at, size)] * pre)

    def valid_of(rows, cols):
        one = m.valid[rows, :]
        return jnp.concatenate([one] * (cols // 128), axis=1) if cols > 128 else one

    def colsum(v):
        return jnp.sum(v, axis=0, keepdims=True)

    stat = m.stat

    def chunks(rows, width, body):
        def one(step, carry):
            return body(pl.ds(pl.multiple_of(step * 64, 64), 64), carry)

        zero = jnp.zeros((1, width), F32)
        return lax.fori_loop(0, rows // 64, one, (zero, zero))

    weight(R1)

    def layer1(step, carry):
        rows = pl.ds(pl.multiple_of(step * 256, 256), 256)
        pre = nn(m.pix[rows, :], w[R1][...].reshape(1024, 384))
        m.pre1[rows, :] = pre
        weighed = pre * valid_of(rows, 384)
        return carry[0] + colsum(weighed), carry[1] + colsum(weighed * pre)

    zero = jnp.zeros((1, 384), F32)
    first, second = lax.fori_loop(0, 4, layer1, (zero, zero))
    hi_here = jnp.concatenate([colsum(m.valid[...])] * 3, axis=1)
    lo_here = jnp.concatenate([colsum(m.valid[lo, :])] * 3, axis=1)
    got = total(0, [first, second, hi_here, lo_here])
    count_hi = jnp.maximum(got[2:3, :], 1.0)
    count_lo = jnp.maximum(got[3:4, :], 1.0)
    count_wide = jnp.concatenate([count_lo] * 4, axis=1)
    set_norm(N1, got[0:1, :], got[1:2, :], count_hi, m.gain_a[:, 0:384], m.shift_a[:, 0:384])

    def activate1(rows, carry):
        v = norm_of(N1, m.pre1[rows, :], 0, 384)
        act = v * sigmoid(v)
        m.up1[rows, :] = act
        m.act1[y, rows, :] = act.astype(BF16)
        return carry

    chunks(1024, 384, activate1)
    hand(m.act1.at[y], T.act1)
    for tap in range(9):
        a, b = tap // 3, tap % 3
        pq = (0 if a == 1 else 2) + (0 if b == 1 else 1)
        block = m.up1[pq * 256:pq * 256 + 256, :]
        block = shifted(block, -1 if a == 0 else 0, -1 if b == 0 else 0)
        m.xc2[y, :, tap * 384:(tap + 1) * 384] = block.astype(BF16)
    hand(m.xc2.at[y], T.xc2)

    def statistics(pre, rows, width):
        weighed = pre * valid_of(rows, width)
        return colsum(weighed), colsum(weighed * pre)

    weight(S1)
    pre = nn(m.xc2[y], w[S1][...].reshape(3456, 384))
    m.pre2[...] = pre
    got = total(1, statistics(pre, lo, 384))
    set_norm(N2, got[0:1, :], got[1:2, :], count_lo, m.gain_a[:, 384:768], m.shift_a[:, 384:768])

    def activate2(rows, carry):
        v = norm_of(N2, m.pre2[rows, :], 0, 384)
        m.act2[rows, :] = (v * sigmoid(v)).astype(BF16)
        return carry

    chunks(256, 384, activate2)
    hand(m.act2, T.act2)

    def wide_loop(body, size=256):
        def one(step, carry):
            body(pl.multiple_of(step * size, size))
            return carry

        lax.fori_loop(0, 1536 // size, one, 0)

    def keep_stats(ref, at, size, k):
        first, second = statistics(ref[:, pl.ds(at, size)], lo, size)
        stat[k:k + 1, pl.ds(at, size)] = first
        stat[k + 1:k + 2, pl.ds(at, size)] = second

    weight(E1)

    def layer3(at):
        m.pre3[:, pl.ds(at, 256)] = nn(m.act2[...], w[E1][:, :, :, pl.ds(at, 256)].reshape(384, 256))
        keep_stats(m.pre3, at, 256, 0)

    wide_loop(layer3)
    for n, piece in enumerate(PIECES):
        if piece[0] == P1:
            links.arrived(m.prep.at[:, pl.ds(piece[1], piece[2])], T.hand + n)
    wide_loop(lambda at: keep_stats(m.prep, at, 256, 2))
    got = total(2, [stat[k:k + 1, :] for k in range(4)])
    set_norm(N3, got[0:1, :], got[1:2, :], count_wide, m.gain_a[:, 768:2304], m.shift_a[:, 768:2304])
    set_norm(NP, got[2:3, :], got[3:4, :], count_wide, m.gain_a[:, 2304:3840], m.shift_a[:, 2304:3840])

    def sum_one(at, size):
        cols = pl.ds(at, size)
        return norm_of(N3, m.pre3[:, cols], at, size) + norm_of(NP, m.prep[:, cols], at, size)

    def make_hidden(at):
        v = sum_one(at, 128)
        hidden = v * sigmoid(v)
        m.hidden[:, pl.ds(at, 128)] = hidden
        m.hlow[:, pl.ds(at, 128)] = hidden.astype(BF16)

    wide_loop(make_hidden, 128)
    hand(m.hlow, T.hlow)

    weight(R2)
    pre = nn(m.hlow[...], w[R2][...].reshape(1536, 384))
    m.pre4[...] = pre
    got = total(3, statistics(pre, lo, 384))
    set_norm(N4, got[0:1, :], got[1:2, :], count_lo, m.gain_b[:, 0:384], m.shift_b[:, 0:384])

    def activate4(rows, carry):
        v = norm_of(N4, m.pre4[rows, :], 0, 384)
        act = v * sigmoid(v)
        m.small[rows, :] = act
        m.act4[y, rows, :] = act.astype(BF16)
        return carry

    chunks(256, 384, activate4)
    post(m.act4.at[y], m.act4.at[y], T.act4_y, dy=1, other=True)
    for tap in range(9):
        m.xc5[y, :, tap * 384:(tap + 1) * 384] = shifted(m.small[...], tap // 3 - 1, tap % 3 - 1).astype(BF16)
    hand(m.xc5.at[y], T.xc5)
    weight(S2)
    pre = nn(m.xc5[y], w[S2][...].reshape(3456, 384))
    m.pre5[...] = pre
    got = total(4, statistics(pre, lo, 384))
    set_norm(N5, got[0:1, :], got[1:2, :], count_lo, m.gain_b[:, 384:768], m.shift_b[:, 384:768])

    def activate5(rows, carry):
        v = norm_of(N5, m.pre5[rows, :], 0, 384)
        m.act5[rows, :] = (v * sigmoid(v)).astype(BF16)
        return carry

    chunks(256, 384, activate5)
    hand(m.act5, T.act5)
    weight(E2)

    def layer6(at):
        m.pre6[:, pl.ds(at, 256)] = nn(m.act5[...], w[E2][:, :, :, pl.ds(at, 256)].reshape(384, 256))
        keep_stats(m.pre6, at, 256, 0)

    wide_loop(layer6)
    got = total(5, [stat[k:k + 1, :] for k in range(2)])
    set_norm(N6, got[0:1, :], got[1:2, :], count_wide, m.gain_b[:, 768:2304], m.shift_b[:, 768:2304])
    own_cot.wait()
    links.arrived(m.cot.at[0], T.cot)

    def top(at):
        cols = pl.ds(at, 128)
        pre = m.pre6[:, cols]
        v = norm_of(N6, pre, at, 128) + m.hidden[:, cols]
        sg = sigmoid(v)
        m.acts[:, cols] = (v * sg).astype(BF16)
        up = m.cot[:, :, cols].reshape(256, 128).astype(F32)
        up = up * sg * (1.0 + v * (1.0 - sg))
        m.hidden[:, cols] = up
        stat[0:1, cols] = colsum(up)
        stat[1:2, cols] = colsum(up * pre)

    wide_loop(top, 128)
    out_act = pltpu.make_async_copy(m.acts.at[pl.ds(128, 128)], outs.act, local_sems.at[4])
    out_act.start()
    post(m.acts.at[pl.ds(0, 128)], outs.act, T.out_act, other=True)
    got = total(6, [stat[k:k + 1, :] for k in range(2)])
    b_gain, b_shift = 7680, 9984
    set_back(N6, got[0:1, :], got[1:2, :], count_wide, (b_gain + 768, b_shift + 768))

    def low6(at):
        cols = pl.ds(at, 128)
        m.low6[:, cols] = back_of(N6, m.pre6[:, cols], m.hidden[:, cols], valid_of(lo, 128), at, 128).astype(BF16)

    wide_loop(low6, 128)
    hand(m.low6, T.low6)
    m.small[...] = nt(m.low6[...], w[E2][...].reshape(384, 1536))

    def narrow_up(key, pre):
        def one(rows, carry):
            kept = pre[rows, :]
            up = silu_back(norm_of(key, kept, 0, 384), m.small[rows, :])
            m.small[rows, :] = up
            return carry[0] + colsum(up), carry[1] + colsum(up * kept)

        return chunks(256, 384, one)

    def narrow_low(key, pre, low, slot, far=None):
        def one(rows, carry):
            got = back_of(key, pre[rows, :], m.small[rows, :], valid_of(rows, 384), 0, 384)
            m.small[rows, :] = got
            low[rows, :] = got.astype(BF16)
            return carry

        chunks(256, 384, one)
        hand(low, slot)
        if far is not None:
            post(low, low, far, dy=1, other=True)

    got = total(7, narrow_up(N5, m.pre5))
    set_back(N5, got[0:1, :], got[1:2, :], count_lo, (b_gain + 384, b_shift + 384))
    narrow_low(N5, m.pre5, m.low5.at[y], T.low5, T.low5_y)
    grad = jnp.zeros((256, 384), F32)
    for tap in range(9):
        moved = shifted(m.small[...], 1 - tap // 3, 1 - tap % 3).astype(BF16)
        grad = grad + nt(moved, w[S2][tap].reshape(384, 384))
    m.small[...] = grad
    got = total(8, narrow_up(N4, m.pre4))
    set_back(N4, got[0:1, :], got[1:2, :], count_lo, (b_gain, b_shift))
    narrow_low(N4, m.pre4, m.low4, T.low4)

    def below(step, carry):
        at = pl.multiple_of(step * 384, 128)
        cols = pl.ds(at, 384)
        grad = m.hidden[:, cols] + nt(m.low4[...], w[R2][step].reshape(384, 384))
        up = silu_back(sum_one(at, 384), grad)
        m.pre6[:, cols] = up
        stat[0:1, cols] = colsum(up)
        stat[1:2, cols] = colsum(up * m.pre3[:, cols])
        stat[2:3, cols] = colsum(up * m.prep[:, cols])
        return carry

    lax.fori_loop(0, 4, below, 0)
    got = total(9, [stat[k:k + 1, :] for k in range(3)])
    a_gain, a_shift = 0, 3840
    set_back(N3, got[0:1, :], got[1:2, :], count_wide, (a_gain + 768, a_shift + 768))
    set_back(NP, got[0:1, :], got[2:3, :], count_wide, (a_gain + 2304, a_shift + 2304))

    def low3(at):
        cols = pl.ds(at, 128)
        up, valid = m.pre6[:, cols], valid_of(lo, 128)
        m.low3[:, cols] = back_of(N3, m.pre3[:, cols], up, valid, at, 128).astype(BF16)
        m.lowp[:, cols] = back_of(NP, m.prep[:, cols], up, valid, at, 128).astype(BF16)

    wide_loop(low3, 128)
    theirs, mine = m.lowp.at[:, columns_of(m.lowp, 1 - y)], m.lowp.at[:, columns_of(m.lowp, y)]
    hand(theirs, T.lowp)
    hand(mine, T.lowp_own)
    hand(m.low3, T.low3)
    m.small[...] = nt(m.low3[...], w[E1][...].reshape(384, 1536))
    got = total(10, narrow_up(N2, m.pre2))
    set_back(N2, got[0:1, :], got[1:2, :], count_lo, (a_gain + 384, a_shift + 384))
    narrow_low(N2, m.pre2, m.low2.at[y], T.low2, T.low2_y)
    for pq in range(4):
        p, q = pq // 2, pq % 2
        grad = jnp.zeros((256, 384), F32)
        for a in ((1,) if p == 0 else (0, 2)):
            for b in ((1,) if q == 0 else (0, 2)):
                moved = shifted(m.small[...], 1 if a == 0 else 0, 1 if b == 0 else 0).astype(BF16)
                grad = grad + nt(moved, w[S1][a * 3 + b].reshape(384, 384))
        m.up1[pq * 256:pq * 256 + 256, :] = grad

    def up1(rows, carry):
        kept = m.pre1[rows, :]
        up = silu_back(norm_of(N1, kept, 0, 384), m.up1[rows, :])
        m.up1[rows, :] = up
        return carry[0] + colsum(up), carry[1] + colsum(up * kept)

    got = total(11, chunks(1024, 384, up1))
    set_back(N1, got[0:1, :], got[1:2, :], count_hi, (a_gain, a_shift))
    out_norm = pltpu.make_async_copy(m.norm_out, outs.norm, local_sems.at[5])
    out_norm.start()
    post(m.norm_out, outs.norm, T.out_norm, other=True)

    def low1(rows, carry):
        got = back_of(N1, m.pre1[rows, :], m.up1[rows, :], valid_of(rows, 384), 0, 384)
        m.low1[rows, :] = got.astype(BF16)
        return carry

    chunks(1024, 384, low1)
    hand(m.low1, T.low1)
    links.arrived(m.gsamp, T.gsamp)
    pix_sent.wait_send()
    for pq in range(4):
        grad = nt(m.low1[pq * 256:pq * 256 + 256, :], w[R1][...].reshape(1024, 384))
        if pq == 0:
            grad = grad + m.gsamp[...]
        m.pix[pq * 256:pq * 256 + 256, :] = grad.astype(BF16)
    for b in range(4):
        block = jnp.concatenate([m.pix[pq * 256 + b * 64:pq * 256 + b * 64 + 64, :] for pq in range(4)], axis=0)
        m.raw[b // 2, (b % 2) * 256:(b % 2) * 256 + 256, :] = tn(m.perm[...], block).astype(BF16)
    out_img = pltpu.make_async_copy(m.raw.at[1], outs.gimg, local_sems.at[6])
    out_img.start()
    post(m.raw.at[0], outs.gimg, T.out_gimg, other=True)
    for name in NAMES:
        links.arrived(outs.grads[name], T.out + name)
    out_act.wait()
    out_norm.wait()
    out_img.wait()
    for made in pending:
        made.wait_send()


SUM_ROWS = ((4, 384), (2, 384), (4, 1536), (2, 384), (2, 384), (2, 1536), (2, 1536), (2, 384), (2, 384), (3, 1536), (2, 384), (2, 384))


def fused_kernel(sizes, keys, *refs):
    groups, at = [], 0
    for size in sizes:
        groups.append(refs[at:at + size])
        at += size
    taken, shards_in, given, made, w, g, fin, third, kept, norms, sums, rest = groups
    dp, wide = lax.axis_index("dp"), lax.axis_index("wide")
    core = dp % 2
    send_sems, recv_sems, local_sems, credit = rest
    barrier = pltpu.get_barrier_semaphore()
    greet = Links(send_sems, recv_sems, core, 0)
    everyone = [dict(other=True), dict(dy=1, other=True)] + [
        dict(dy=dy, dz=dz, dx=dx) for dy in (0, 1) for dz in range(4) for dx in (0, 1) if (dy, dz, dx) != (0, 0, 0)]
    for to in everyone:
        pl.semaphore_signal(barrier, inc=1, device_id=greet.device(**to), device_id_type=MESH)
    pl.semaphore_wait(barrier, len(everyone))

    images, mask, cotangent, norm = taken
    act, gimg, norm_out = given
    ins = types.SimpleNamespace(images=images, mask=mask, cotangent=cotangent, norm=norm, weights=shards_in)
    outs = types.SimpleNamespace(act=act, gimg=gimg, norm=norm_out, grads=made)
    m = types.SimpleNamespace(**dict(zip(keys, kept)), norms=norms, local_sems=local_sems, tail=[], seen=[])

    @pl.when(core == 0)
    def _():
        mover(Links(send_sems, recv_sems, 0, 1), ins, outs, w, g, third, fin, m, credit)

    @pl.when(core == 1)
    def _():
        runner(Links(send_sems, recv_sems, 1, 1), ins, outs, w, m, sums)


def finish_kernel(sizes, *refs):
    act, gimg, norms = refs[:3]
    grads, out_act, out_gimg = refs[3:10], refs[10], refs[11]
    out_grads, out_norms = refs[12:19], refs[19:23]
    low, high, row, parts = refs[23:30], refs[30:37], refs[37], refs[38:42]
    held_act, held_gimg, in_sems, out_sems = refs[42:]
    passing = [pltpu.make_async_copy(gimg, held_gimg, in_sems.at[0]), pltpu.make_async_copy(act, held_act, in_sems.at[9])]
    copies = []
    coming = [pltpu.make_async_copy(v, into, in_sems.at[2 + n]) for n, (v, into) in enumerate(zip(grads, low))]
    norm_in = pltpu.make_async_copy(norms, row, in_sems.at[1])
    norm_in.start()
    for made in coming + passing:
        made.start()
    norm_in.wait()
    wide = lax.axis_index("wide")
    at = 0
    for n, size in enumerate((sizes[0], sizes[0], sizes[1], sizes[1])):
        for s in range(8):
            @pl.when(wide == s)
            def _(n=n, size=size, start=at + s * size):
                parts[n][...] = row[:, start:start + size]
        at += 8 * size
        made = pltpu.make_async_copy(parts[n].at[0], out_norms[n], out_sems.at[1 + n])
        made.start()
        copies.append(made)
    for n, (source, into, out) in enumerate(zip(low, high, out_grads)):
        coming[n].wait()
        for i in range(source.shape[0] if len(source.shape) == 3 else 1):
            part = i if len(source.shape) == 3 else slice(None)
            into[part] = source[part].astype(F32)
        made = pltpu.make_async_copy(into, out, out_sems.at[5 + n])
        made.start()
        copies.append(made)
    for n, (source, out) in enumerate(((held_gimg, out_gimg), (held_act, out_act))):
        passing[n].wait()
        made = pltpu.make_async_copy(source, out, out_sems.at[(0, 12)[n]])
        made.start()
        copies.append(made)
    for made in copies:
        made.wait()


def fused_shards(images, pixel_mask, cotangent, reduce_one, spatial_one, expand_one, project_one, gains_one, shifts_one,
                 reduce_two, spatial_two, expand_two, gains_two, shifts_two):
    def split(weight, parts=2):
        return weight.reshape(parts, weight.shape[0] // parts, weight.shape[1])

    def join(weight):
        return weight.reshape(9, weight.shape[2], weight.shape[3])

    weights = (split(reduce_one), join(spatial_one), expand_one, split(project_one), split(reduce_two, 4), join(spatial_two), expand_two)
    local_a, local_b = gains_one.shape[0], gains_two.shape[0]
    row, at = 0.0, 0
    for part in (gains_one, shifts_one, gains_two, shifts_two):
        row = row + jnp.pad(part.astype(F32), (at, 2 * (local_a + local_b) - at - part.shape[0]))
        at += part.shape[0]
    norm = row.reshape(1, -1)
    taken = [images.reshape(512, 1024), pixel_mask.reshape(32, 16), cotangent.reshape(128, 1536), norm]
    given = [jax.ShapeDtypeStruct((128, 1536), BF16), jax.ShapeDtypeStruct((512, 1024), BF16), jax.ShapeDtypeStruct((1, 12288), F32)]
    made = [jax.ShapeDtypeStruct(v.shape, BF16) for v in weights]
    whole = [pltpu.VMEM(whole_shape(KINDS[n], v.shape), BF16) for n, v in enumerate(weights)]
    fin = [pltpu.VMEM(v.shape, BF16) for v in weights]
    partial = list(whole)
    partial[S1] = partial[S2] = pltpu.VMEM((5, 4, 2, 48, 384), BF16)
    partial[P1] = pltpu.VMEM((4, 2, 2, 64, 768), BF16)
    cells = [(5, 48, 384) if KINDS[n] == TAP else (2, 64, 768) if n == P1 else v.shape for n, v in enumerate(weights)]
    third = []
    for n, cell in enumerate(cells):
        orders = [piece[3] for piece in SUMMED if piece[0] == n]
        both = 2 if any(order.index(3) < order.index(1) for order in orders) else 1
        whole_y = any(2 in order and order.index(3) < order.index(2) for order in orders)
        if KINDS[n] == TAP:
            shape = (3, 5, both, 48, 384)
        elif n == P1 or whole_y:
            shape = (3, both) + cell
        elif KINDS[n] == COL:
            shape = (3, both, cell[0], cell[1] // 2)
        else:
            shape = (3, both, cell[0] // 2) + cell[1:]
        third.append(pltpu.VMEM(shape, BF16))
    bf = dict(raw=(2, 512, 1024), cot=(2, 128, 1536), pix=(1024, 1024), perm=(256, 256), xc2=(2, 256, 3456), xc5=(2, 256, 3456),
              act2=(256, 384), act5=(256, 384), hlow=(256, 1536), acts=(256, 1536), low6=(256, 1536), low5=(2, 256, 384), low4=(256, 384),
              low3=(256, 1536), lowp=(256, 1536), low2=(2, 256, 384), low1=(1024, 384),
              samp=(2, 256, 1024), act1=(2, 1024, 384), act4=(2, 256, 384), lowp_y=(256, 768), land=(4, 2, 64, 768))
    f32 = dict(norm_in=(8, 1, 1536), gain_a=(1, 3840), shift_a=(1, 3840), gain_b=(1, 2304), shift_b=(1, 2304), norm_out=(1, 12288),
               valid=(1024, 128), stat=(8, 1536), pre1=(1024, 384), up1=(1024, 384), pre2=(256, 384), pre3=(256, 1536), prep=(256, 1536),
               hidden=(256, 1536), pre4=(256, 384), pre5=(256, 384), pre6=(256, 1536), small=(256, 384), gsamp=(256, 1024))
    kept = {k: pltpu.VMEM(v, BF16) for k, v in bf.items()} | {k: pltpu.VMEM(v, F32) for k, v in f32.items()}
    kept |= dict(mask=pltpu.VMEM((2, 32, 16), jnp.int32))
    norms = [pltpu.VMEM((8, width), F32) for width in (384, 384, 1536, 1536, 384, 384, 1536)]
    sums = [pltpu.VMEM((16 if width < 1536 else 4, rows, width), F32) for rows, width in SUM_ROWS]
    sums += [pltpu.VMEM((4, rows, width) if width == 1536 else (1, 1, 128), F32) for rows, width in SUM_ROWS]
    rest = [pltpu.SemaphoreType.DMA((320,)), pltpu.SemaphoreType.DMA((T.total,)), pltpu.SemaphoreType.DMA((28,)),
            pltpu.SemaphoreType.REGULAR((1,))]
    groups = [taken, weights, given, made, whole, partial, fin, third, list(kept.values()), norms, sums, rest]
    anywhere = pl.BlockSpec(memory_space=pl.ANY)
    got = pl.pallas_call(
        functools.partial(fused_kernel, [len(group) for group in groups], list(kept)),
        out_shape=given + made,
        in_specs=[anywhere] * (len(taken) + len(weights)),
        out_specs=[anywhere] * (len(given) + len(made)),
        scratch_shapes=[v for group in groups[4:] for v in group],
        compiler_params=pltpu.CompilerParams(collective_id=0, has_side_effects=True, vmem_limit_bytes=63 * 2**20),
    )(*taken, *weights)
    act, gimg, norms, *grads = got
    finished = pl.pallas_call(
        functools.partial(finish_kernel, (local_a, local_b)),
        out_shape=[act, gimg] + [jax.ShapeDtypeStruct(v.shape, F32) for v in grads]
        + [jax.ShapeDtypeStruct((size,), F32) for size in (local_a, local_a, local_b, local_b)],
        in_specs=[anywhere] * 10,
        out_specs=[anywhere] * 13,
        scratch_shapes=[pltpu.VMEM(v.shape, BF16) for v in grads] + [pltpu.VMEM(v.shape, F32) for v in grads]
        + [pltpu.VMEM(norms.shape, F32)] + [pltpu.VMEM((1, size), F32) for size in (local_a, local_a, local_b, local_b)]
        + [pltpu.VMEM(act.shape, BF16), pltpu.VMEM(gimg.shape, BF16), pltpu.SemaphoreType.DMA((10,)), pltpu.SemaphoreType.DMA((13,))],
        compiler_params=pltpu.CompilerParams(vmem_limit_bytes=60 * 2**20),
    )(act, gimg, norms, *grads)
    act, gimg = finished[:2]
    grads = [v.reshape(like.shape) for v, like in zip(
        finished[2:9], (reduce_one, spatial_one, expand_one, project_one, reduce_two, spatial_two, expand_two))]
    norm_grads = finished[9:]
    return (
        act.reshape(cotangent.shape),
        gimg.reshape(images.shape),
        grads[0], grads[1], grads[2], grads[3], norm_grads[0], norm_grads[1],
        grads[4], grads[5], grads[6], norm_grads[2], norm_grads[3],
    )


def solution(mesh):
    fused = mesh.shape["dp"] == 4 and mesh.shape["wide"] == 8
    in_specs = (
        P(("dp", "wide"), None, None, None),
        P(("dp", "wide"), None, None),
        P(("dp", "wide"), None, None, None),
        P("wide", None),
        P(None, None, "wide", None),
        P("wide", None),
        P("wide", None),
        P("wide"),
        P("wide"),
        P("wide", None),
        P(None, None, "wide", None),
        P("wide", None),
        P("wide"),
        P("wide"),
    )
    out_specs = (
        P(("dp", "wide"), None, None, None),
        P(("dp", "wide"), None, None, None),
        P("wide", None),
        P(None, None, "wide", None),
        P("wide", None),
        P("wide", None),
        P("wide"),
        P("wide"),
        P("wide", None),
        P(None, None, "wide", None),
        P("wide", None),
        P("wide"),
        P("wide"),
    )
    return jax.shard_map(fused_shards if fused else shards, mesh=mesh, in_specs=in_specs, out_specs=out_specs, check_vma=False)
```

```python
import functools
import types

import jax
import jax.numpy as jnp
from jax import lax
from jax.experimental import pallas as pl
from jax.experimental.pallas import tpu as pltpu
from jax.sharding import PartitionSpec as P

NORM_EPS = 1e-05


def pixel_product(source, kernel):
    return jnp.einsum("bhwc,co->bhwo", source, kernel, preferred_element_type=jnp.float32)


def weight_grad(source, upstream):
    return jnp.einsum("bhwc,bhwo->co", source, upstream, preferred_element_type=jnp.float32)


def input_grad(upstream, kernel):
    return jnp.einsum("bhwo,co->bhwc", upstream, kernel, preferred_element_type=jnp.float32)


def conv_spatial(source, kernel, stride):
    out_h = source.shape[1] // stride
    out_w = source.shape[2] // stride
    padded = jnp.pad(source, ((0, 0), (1, 1), (1, 1), (0, 0)))
    summed = jnp.zeros((source.shape[0], out_h, out_w, kernel.shape[3]), jnp.float32)
    for row_off in range(3):
        for col_off in range(3):
            window = padded[
                :,
                row_off : row_off + stride * out_h : stride,
                col_off : col_off + stride * out_w : stride,
            ]
            summed = summed + pixel_product(window, kernel[row_off, col_off])
    return summed


def conv_back(source, upstream, kernel, stride):
    out_h = upstream.shape[1]
    out_w = upstream.shape[2]
    padded = jnp.pad(source, ((0, 0), (1, 1), (1, 1), (0, 0)))
    grad_src = jnp.zeros(padded.shape, jnp.float32)
    kernel_rows = []
    for row_off in range(3):
        for col_off in range(3):
            window = padded[
                :,
                row_off : row_off + stride * out_h : stride,
                col_off : col_off + stride * out_w : stride,
            ]
            kernel_rows.append(weight_grad(window, upstream))
            grad_src = grad_src.at[
                :,
                row_off : row_off + stride * out_h : stride,
                col_off : col_off + stride * out_w : stride,
            ].add(input_grad(upstream, kernel[row_off, col_off]))
    kernel_grad = jnp.stack(kernel_rows).reshape(kernel.shape)
    return (kernel_grad, grad_src[:, 1:-1, 1:-1])


def norm_forward(pre, valid, count, gain, shift):
    moments = lax.psum(
        (jnp.sum(pre * valid, axis=(0, 1, 2)), jnp.sum(pre * pre * valid, axis=(0, 1, 2))),
        ("dp", "wide"),
    )
    mean_val = moments[0] / count
    variance = moments[1] / count - mean_val * mean_val
    scaler = lax.rsqrt(variance + NORM_EPS)
    normed = (pre - mean_val) * scaler
    return (gain * normed + shift, (mean_val, scaler))


def norm_backward(upstream, pre, valid, count, gain, stats):
    mean_val, scaler = stats
    sums = lax.psum(
        (jnp.sum(upstream, axis=(0, 1, 2)), jnp.sum(upstream * pre, axis=(0, 1, 2))), ("dp", "wide")
    )
    first_sum, second_sum = sums
    centred = second_sum - mean_val * first_sum
    grad_gain = scaler * centred
    grad_var = -0.5 * gain * centred * scaler * scaler * scaler
    grad_mean = -gain * scaler * first_sum - 2.0 * mean_val * grad_var
    grad_pre = gain * scaler * upstream + valid / count * (grad_mean + 2.0 * pre * grad_var)
    return (grad_pre, grad_gain, first_sum)


def silu_grad(pre_act, upstream):
    sigma = jax.nn.sigmoid(pre_act)
    return upstream * sigma * (1.0 + pre_act * (1.0 - sigma))


def own_slice(whole, local_len):
    start = lax.axis_index("wide") * local_len
    return lax.dynamic_slice_in_dim(whole, start, local_len, 0)


def shards(
    images,
    pixel_mask,
    cotangent,
    reduce_one,
    spatial_one,
    expand_one,
    project_one,
    gains_one,
    shifts_one,
    reduce_two,
    spatial_two,
    expand_two,
    gains_two,
    shifts_two,
):
    valid_hi = pixel_mask.astype(jnp.float32)[..., None]
    valid_lo = valid_hi[:, ::2, ::2]
    counts = lax.psum((jnp.sum(valid_hi), jnp.sum(valid_lo)), ("dp", "wide"))
    count_hi = jnp.maximum(counts[0], 1.0)
    count_lo = jnp.maximum(counts[1], 1.0)
    first_full = (
        lax.all_gather(reduce_one, "wide", axis=0, tiled=True),
        lax.all_gather(spatial_one, "wide", axis=2, tiled=True),
        lax.all_gather(expand_one, "wide", axis=0, tiled=True),
        lax.all_gather(project_one, "wide", axis=0, tiled=True),
        lax.all_gather(gains_one, "wide", axis=0, tiled=True),
        lax.all_gather(shifts_one, "wide", axis=0, tiled=True),
    )
    red_a, spa_a, exp_a, proj_a, gain_a, shift_a = first_full
    mid_a = red_a.shape[1]
    mid_b = 2 * mid_a
    out_a = mid_b + exp_a.shape[1]
    out_b = out_a + exp_a.shape[1]
    gain_af = gain_a.astype(jnp.float32)
    shift_af = shift_a.astype(jnp.float32)
    pre_one = pixel_product(images, red_a)
    y_one, stat_one = norm_forward(pre_one, valid_hi, count_hi, gain_af[:mid_a], shift_af[:mid_a])
    act_one = jax.nn.silu(y_one).astype(jnp.bfloat16)
    pre_two = conv_spatial(act_one, spa_a, 2)
    y_two, stat_two = norm_forward(
        pre_two, valid_lo, count_lo, gain_af[mid_a:mid_b], shift_af[mid_a:mid_b]
    )
    act_two = jax.nn.silu(y_two).astype(jnp.bfloat16)
    pre_three = pixel_product(act_two, exp_a)
    y_three, stat_three = norm_forward(
        pre_three, valid_lo, count_lo, gain_af[mid_b:out_a], shift_af[mid_b:out_a]
    )
    sampled = images[:, ::2, ::2]
    pre_proj = pixel_product(sampled, proj_a)
    y_proj, stat_proj = norm_forward(
        pre_proj, valid_lo, count_lo, gain_af[out_a:out_b], shift_af[out_a:out_b]
    )
    sum_one = y_three + y_proj
    hidden = jax.nn.silu(sum_one)
    hidden_low = hidden.astype(jnp.bfloat16)
    second_full = (
        lax.all_gather(reduce_two, "wide", axis=0, tiled=True),
        lax.all_gather(spatial_two, "wide", axis=2, tiled=True),
        lax.all_gather(expand_two, "wide", axis=0, tiled=True),
        lax.all_gather(gains_two, "wide", axis=0, tiled=True),
        lax.all_gather(shifts_two, "wide", axis=0, tiled=True),
    )
    red_b, spa_b, exp_b, gain_b, shift_b = second_full
    gain_bf = gain_b.astype(jnp.float32)
    shift_bf = shift_b.astype(jnp.float32)
    pre_four = pixel_product(hidden_low, red_b)
    y_four, stat_four = norm_forward(
        pre_four, valid_lo, count_lo, gain_bf[:mid_a], shift_bf[:mid_a]
    )
    act_four = jax.nn.silu(y_four).astype(jnp.bfloat16)
    pre_five = conv_spatial(act_four, spa_b, 1)
    y_five, stat_five = norm_forward(
        pre_five, valid_lo, count_lo, gain_bf[mid_a:mid_b], shift_bf[mid_a:mid_b]
    )
    act_five = jax.nn.silu(y_five).astype(jnp.bfloat16)
    pre_six = pixel_product(act_five, exp_b)
    y_six, stat_six = norm_forward(
        pre_six, valid_lo, count_lo, gain_bf[mid_b:out_a], shift_bf[mid_b:out_a]
    )
    sum_two = y_six + hidden
    activations = jax.nn.silu(sum_two).astype(jnp.bfloat16)
    back_two = (
        lax.all_gather(reduce_two, "wide", axis=0, tiled=True),
        lax.all_gather(spatial_two, "wide", axis=2, tiled=True),
        lax.all_gather(expand_two, "wide", axis=0, tiled=True),
        lax.all_gather(gains_two, "wide", axis=0, tiled=True),
    )
    red_b, spa_b, exp_b, gain_b = back_two
    gain_bf = gain_b.astype(jnp.float32)
    upstream = cotangent.astype(jnp.float32)
    grad_sum_two = silu_grad(sum_two, upstream)
    grad_pre6, gain_g6, shift_g6 = norm_backward(
        grad_sum_two, pre_six, valid_lo, count_lo, gain_bf[mid_b:out_a], stat_six
    )
    low_six = grad_pre6.astype(jnp.bfloat16)
    grad_exp_b = weight_grad(act_five, low_six)
    grad_act5 = input_grad(low_six, exp_b)
    grad_pre5, gain_g5, shift_g5 = norm_backward(
        silu_grad(y_five, grad_act5), pre_five, valid_lo, count_lo, gain_bf[mid_a:mid_b], stat_five
    )
    low_five = grad_pre5.astype(jnp.bfloat16)
    grad_spa_b, grad_act4 = conv_back(act_four, low_five, spa_b, 1)
    grad_pre4, gain_g4, shift_g4 = norm_backward(
        silu_grad(y_four, grad_act4), pre_four, valid_lo, count_lo, gain_bf[:mid_a], stat_four
    )
    low_four = grad_pre4.astype(jnp.bfloat16)
    grad_red_b = weight_grad(hidden_low, low_four)
    grad_hidden = grad_sum_two + input_grad(low_four, red_b)
    owned_two = (
        lax.psum_scatter(
            grad_red_b.astype(jnp.bfloat16), "wide", scatter_dimension=0, tiled=True
        ).astype(jnp.float32),
        lax.psum_scatter(
            grad_spa_b.astype(jnp.bfloat16), "wide", scatter_dimension=2, tiled=True
        ).astype(jnp.float32),
        lax.psum_scatter(
            grad_exp_b.astype(jnp.bfloat16), "wide", scatter_dimension=0, tiled=True
        ).astype(jnp.float32),
    )
    owned_two = (
        lax.psum(owned_two[0].astype(jnp.bfloat16), "dp").astype(jnp.float32),
        lax.psum(owned_two[1].astype(jnp.bfloat16), "dp").astype(jnp.float32),
        lax.psum(owned_two[2].astype(jnp.bfloat16), "dp").astype(jnp.float32),
    )
    back_one = (
        lax.all_gather(reduce_one, "wide", axis=0, tiled=True),
        lax.all_gather(spatial_one, "wide", axis=2, tiled=True),
        lax.all_gather(expand_one, "wide", axis=0, tiled=True),
        lax.all_gather(project_one, "wide", axis=0, tiled=True),
        lax.all_gather(gains_one, "wide", axis=0, tiled=True),
    )
    red_a, spa_a, exp_a, proj_a, gain_a = back_one
    gain_af = gain_a.astype(jnp.float32)
    grad_sum_one = silu_grad(sum_one, grad_hidden)
    grad_pre3, gain_g3, shift_g3 = norm_backward(
        grad_sum_one, pre_three, valid_lo, count_lo, gain_af[mid_b:out_a], stat_three
    )
    grad_prep, gain_gp, shift_gp = norm_backward(
        grad_sum_one, pre_proj, valid_lo, count_lo, gain_af[out_a:out_b], stat_proj
    )
    low_three = grad_pre3.astype(jnp.bfloat16)
    low_proj = grad_prep.astype(jnp.bfloat16)
    grad_exp_a = weight_grad(act_two, low_three)
    grad_act2 = input_grad(low_three, exp_a)
    grad_proj_a = weight_grad(sampled, low_proj)
    grad_sampled = input_grad(low_proj, proj_a)
    grad_pre2, gain_g2, shift_g2 = norm_backward(
        silu_grad(y_two, grad_act2), pre_two, valid_lo, count_lo, gain_af[mid_a:mid_b], stat_two
    )
    low_two = grad_pre2.astype(jnp.bfloat16)
    grad_spa_a, grad_act1 = conv_back(act_one, low_two, spa_a, 2)
    grad_pre1, gain_g1, shift_g1 = norm_backward(
        silu_grad(y_one, grad_act1), pre_one, valid_hi, count_hi, gain_af[:mid_a], stat_one
    )
    low_one = grad_pre1.astype(jnp.bfloat16)
    grad_red_a = weight_grad(images, low_one)
    grad_input = input_grad(low_one, red_a)
    grad_input = grad_input.at[:, ::2, ::2].add(grad_sampled)
    grad_images = grad_input.astype(jnp.bfloat16)
    owned_one = (
        lax.psum_scatter(
            grad_red_a.astype(jnp.bfloat16), "wide", scatter_dimension=0, tiled=True
        ).astype(jnp.float32),
        lax.psum_scatter(
            grad_spa_a.astype(jnp.bfloat16), "wide", scatter_dimension=2, tiled=True
        ).astype(jnp.float32),
        lax.psum_scatter(
            grad_exp_a.astype(jnp.bfloat16), "wide", scatter_dimension=0, tiled=True
        ).astype(jnp.float32),
        lax.psum_scatter(
            grad_proj_a.astype(jnp.bfloat16), "wide", scatter_dimension=0, tiled=True
        ).astype(jnp.float32),
    )
    owned_one = (
        lax.psum(owned_one[0].astype(jnp.bfloat16), "dp").astype(jnp.float32),
        lax.psum(owned_one[1].astype(jnp.bfloat16), "dp").astype(jnp.float32),
        lax.psum(owned_one[2].astype(jnp.bfloat16), "dp").astype(jnp.float32),
        lax.psum(owned_one[3].astype(jnp.bfloat16), "dp").astype(jnp.float32),
    )
    gains_grad_a = jnp.concatenate([gain_g1, gain_g2, gain_g3, gain_gp])
    shifts_grad_a = jnp.concatenate([shift_g1, shift_g2, shift_g3, shift_gp])
    gains_grad_b = jnp.concatenate([gain_g4, gain_g5, gain_g6])
    shifts_grad_b = jnp.concatenate([shift_g4, shift_g5, shift_g6])
    local_a = gains_one.shape[0]
    local_b = gains_two.shape[0]
    return (
        activations,
        grad_images,
        owned_one[0],
        owned_one[1],
        owned_one[2],
        owned_one[3],
        own_slice(gains_grad_a, local_a),
        own_slice(shifts_grad_a, local_a),
        owned_two[0],
        owned_two[1],
        owned_two[2],
        own_slice(gains_grad_b, local_b),
        own_slice(shifts_grad_b, local_b),
    )


MESH = pl.DeviceIdType.MESH
F32 = jnp.float32
BF16 = jnp.bfloat16
ALL = slice(None)
NAMES = R1, S1, E1, P1, R2, S2, E2 = range(7)
ROW, TAP, COL = range(3)
KINDS = (ROW, TAP, COL, ROW, ROW, TAP, COL)
NORMS = N1, N2, N3, NP, N4, N5, N6 = range(7)


def nn(left, right):
    return jnp.dot(left, right, preferred_element_type=F32)


def nt(left, right):
    return lax.dot_general(left, right, (((1,), (1,)), ((), ())), preferred_element_type=F32)


def tn(left, right):
    return lax.dot_general(left, right, (((0,), (0,)), ((), ())), preferred_element_type=F32)


def whole_shape(kind, shard):
    if kind == TAP:
        return (shard[0], 4, 2) + tuple(shard[1:])
    return (4, 2) + tuple(shard)


class Links:
    def __init__(self, send_sems, recv_sems, core, base):
        self.send_sems, self.recv_sems = send_sems, recv_sems
        self.dp, self.wide = lax.axis_index("dp"), lax.axis_index("wide")
        self.core = core
        self.y, self.z, self.x = self.dp // 2, self.wide // 2, self.wide % 2
        self.next_send = base

    def device(self, dy=0, dz=0, dx=0, other=False):
        core = 1 - self.core if other else self.core
        y = (self.y + dy) % 2
        z, x = (self.z + dz) % 4, (self.x + dx) % 2
        return {"dp": y * 2 + core, "wide": z * 2 + x}

    def copy(self, src, dst, slot, **to):
        sem = self.send_sems.at[self.next_send]
        self.next_send += 1
        return pltpu.make_async_remote_copy(
            src_ref=src, dst_ref=dst, send_sem=sem, recv_sem=self.recv_sems.at[slot],
            device_id=self.device(**to), device_id_type=MESH)

    def send(self, src, dst, slot, **to):
        made = self.copy(src, dst, slot, **to)
        made.start()
        return made

    def arrived(self, dst, slot):
        pltpu.make_async_remote_copy(
            src_ref=dst, dst_ref=dst, send_sem=self.send_sems.at[0], recv_sem=self.recv_sems.at[slot],
            device_id=self.device(other=True), device_id_type=MESH).wait_recv()


def slot_table(**counts):
    table, at = types.SimpleNamespace(), 0
    for key, count in counts.items():
        setattr(table, key, at)
        at += count
    table.total = at
    return table


T = slot_table(raw=1, mask=1, cot=1, pix=1, xc2=1, act2=1, hlow=1, xc5=1, act5=1, low6=1, low5=1, low4=1, low3=1, lowp=1, low2=1,
               low1=1, gsamp=1, out_act=1, out_norm=1, out_gimg=1, samp_y=1, act1=1, act1_y=1, act4_y=1, low5_y=1, low2_y=1, lowp_own=1, lowp_y=6,
               out=7, hand=28, gather=8 * 28, reduce=6 * 22, norm_in=8, sums=24)


def sigmoid(v):
    return 1.0 / (1.0 + jnp.exp(-v))


def silu_back(v, up):
    sg = sigmoid(v)
    return up * sg * (1.0 + v * (1.0 - sg))


def pixel_ids(rows, cols):
    row = lax.broadcasted_iota(jnp.int32, (rows, cols), 0)
    return (row // 8) % 8, row % 8


def shifted(value, di, dj):
    step = di * 8 + dj
    if step == 0:
        return value
    rows, cols = value.shape
    rolled = pltpu.roll(value, (-step) % rows, 0)
    i, j = pixel_ids(rows, cols)
    keep = None
    for index, d in ((i, di), (j, dj)):
        if d == 0:
            continue
        this = index < 8 - d if d > 0 else index >= -d
        keep = this if keep is None else keep & this
    return jnp.where(keep, rolled, 0.0)


A, B, C, D, E = range(5)
MAKE, MAKE_P1, OTHER = -1, -2, -3
PIECES = (
    (R1, 0, 1, C), (S1, 0, 1, C), (S1, 2, 1, B), (S1, 4, 1, C), (S1, 6, 1, C), (S1, 8, 1, D), (E1, 0, 384, B), (E1, 768, 384, C),
    (P1, 0, 256, D), (P1, 256, 256, D), (P1, 512, 256, B), (P1, 768, 256, C), (P1, 1024, 256, A), (P1, 1280, 256, C), (R2, 0, 1,
    A), (R2, 2, 1, B), (S2, 0, 1, B), (S2, 2, 1, A), (S2, 4, 1, B), (S2, 6, 1, A), (S2, 8, 1, E), (E2, 0, 384, D), (E2, 768, 384,
    E))
GATHER_PLAN = (
    (13, 0), (0, 0), (2, 0), (4, 0), (14, 0), (12, 0), (13, 1), (3, 0), (11, 0), (6, 0), (5, 0), (17, 0), (0, 1), (1, 0), (19, 0),
    (7, 0), (9, 0), (20, 0), (2, 1), (13, 2), (10, 0), (8, 0), (4, 1), (3, 1), (0, 2), (12, 1), (15, 0), (2, 2), (13, 3), (4, 2),
    (16, 0), (3, 2), (5, 1), (1, 1), (11, 1), (6, 1), (0, 3), (7, 1), (2, 3), (14, 1), (18, 0), (5, 3), (4, 3), (9, 1), (19, 1),
    (1, 2), (3, 3), (6, 2), (10, 1), (7, 2), (1, 3), (8, 1), (9, 3), (11, 2), (6, 3), (10, 2), (17, 1), (12, 2), (15, 1), (7, 3),
    (22, 0), (16, 1), (11, 3), (21, 0), (8, 3), (14, 2), (10, 3), (12, 3), (15, 2), (16, 2), (20, 1), (18, 1), (19, 2), (14, 3),
    (15, 3), (17, 2), (18, 2), (22, 1), (19, 3), (16, 3), (21, 1), (17, 3), (20, 3), (18, 3), (21, 3), (22, 3), (OTHER, 0),
    (OTHER, 1))
SUMMED = (
    (E2, 0, 384, (2, 1, 3)), (E2, 768, 384, (2, 1, 3)), (R2, 0, 2, (2, 1, 3)), (E1, 0, 384, (2, 1, 3)), (E1, 768, 384, (2, 1, 3)),
    (R1, 0, 1, (2, 1, 3)), (S2, 0, 1, (1, 3)), (S2, 1, 1, (1, 3)), (S2, 2, 1, (1, 3)), (S2, 3, 1, (1, 3)), (S2, 4, 1, (3, 1)),
    (S1, 0, 1, (1, 3)), (S1, 1, 1, (1, 3)), (S1, 2, 1, (1, 3)), (S1, 3, 1, (1, 3)), (S1, 4, 1, (1, 3)), (P1, 0, 256, (1, 3)), (P1,
    256, 256, (1, 3)), (P1, 512, 256, (1, 3)))
REDUCE_PLAN = (
    (MAKE, E2), (OTHER, 1), (0, 0), (1, 0), (0, 1), (OTHER, 0), (MAKE, R2), (2, 0), (1, 1), (MAKE, S2), (6, 0), (8, 0), (10, 0),
    (1, 2), (0, 2), (9, 0), (7, 0), (6, 1), (OTHER, 2), (MAKE, E1), (2, 1), (8, 1), (OTHER, 3), (1, 3), (9, 1), (MAKE_P1, 0), (16,
    0), (4, 0), (7, 1), (MAKE_P1, 2), (0, 3), (6, 2), (1, 4), (18, 0), (2, 2), (8, 2), (3, 0), (MAKE, S1), (14, 0), (11, 0), (12,
    0), (16, 1), (9, 2), (7, 2), (0, 4), (8, 3), (6, 3), (MAKE, R1), (5, 0), (18, 1), (9, 3), (4, 1), (3, 1), (14, 1), (MAKE_P1,
    1), (2, 3), (11, 1), (12, 1), (16, 2), (17, 0), (7, 3), (10, 1), (4, 2), (18, 2), (5, 1), (2, 4), (13, 0), (3, 2), (14, 2),
    (16, 3), (15, 0), (18, 3), (17, 1), (11, 2), (12, 2), (14, 3), (10, 2), (4, 3), (5, 2), (3, 3), (12, 3), (13, 1), (11, 3),
    (15, 1), (4, 4), (17, 2), (3, 4), (5, 3), (17, 3), (13, 2), (15, 2), (5, 4), (13, 3))
PARTS_P1 = 3
def piece_of(piece, buf, z, x, h):
    name, first, count, order = piece
    kind = KINDS[name]
    if kind == COL or name == P1:
        if kind == COL:
            cols = pl.ds(first, 2 * count) if h is ALL else pl.ds(pl.multiple_of(first + h * count, 128), count)
            return buf.at[z, x, :, cols]
        return buf.at[z, x, h, :, pl.ds(first, count)]
    if name == R1:
        return buf.at[z, x, h]
    part = pl.ds(first, 1) if first == 8 else pl.ds(first, 2) if h is ALL else pl.ds(first + h, 1)
    return buf.at[part, z, x] if kind == TAP else buf.at[z, x, part]


def shard_of(piece, buf, h):
    name, first, count, order = piece
    kind = KINDS[name]
    if kind == COL:
        cols = pl.ds(first, 2 * count) if h is ALL else pl.ds(pl.multiple_of(first + h * count, 128), count)
        return buf.at[:, cols]
    if name == P1:
        return buf.at[h, :, pl.ds(first, count)]
    if name == R1:
        return buf.at[h]
    return buf.at[pl.ds(first, 1) if first == 8 else pl.ds(first, 2) if h is ALL else pl.ds(first + h, 1)]


def columns_of(ref, h):
    return pl.ds(pl.multiple_of(h * (ref.shape[-1] // 2), 128), ref.shape[-1] // 2)


def mover(links, ins, outs, w, g, third, fin, m, credit):
    x, y, z = links.x, links.y, links.z
    pending = []
    local_sems = m.local_sems

    def post(src, dst, slot, **to):
        made = links.send(src, dst, slot, **to)
        pending.append(made)
        return made

    def drain():
        for made in pending:
            made.wait_send()
        pending.clear()

    post(ins.images, m.raw.at[0], T.raw, other=True)
    post(ins.mask, m.mask.at[0], T.mask, other=True)
    own = []
    for n, piece in enumerate(PIECES):
        made = pltpu.make_async_copy(shard_of(piece, ins.weights[piece[0]], ALL), piece_of(piece, w[piece[0]], z, x, ALL), local_sems.at[n])
        made.start()
        own.append(made)

    flight = {}

    def along_z(src, dst, slot):
        return [post(src, dst, slot + dz, dz=dz) for dz in (2, 1, 3)]

    def gather(n, stage):
        piece = PIECES[n]
        buf, shard, order, slot = w[piece[0]], ins.weights[piece[0]], piece[3], T.gather + 8 * n
        if stage == 0:
            h = ALL if order in (D, E) else y
            src, dst = shard_of(piece, shard, h), piece_of(piece, buf, z, x, h)
        else:
            if order == A:
                part = (z, ALL, y) if stage == 1 else (ALL, ALL, y)
            elif order == B:
                part = (ALL, x, y) if stage == 1 else (ALL, x, ALL)
            elif order == C:
                part = (ALL, x, y) if stage == 1 else (ALL, ALL, y)
            elif order == D:
                part = (ALL, x, ALL)
            else:
                part = (z, ALL, ALL)
            src = dst = piece_of(piece, buf, *part)
        axis = ((1, 3, 2), (3, 2, 1), (3, 1, 2), (3, 1), (1, 3))[order][stage]
        if axis == 3:
            flight[n] = along_z(src, dst, slot)
        elif axis == 2:
            both = x if order == B else ALL
            flight[n] = []
            for dz in (1, 2, 3):
                part = piece_of(piece, buf, (z + dz) % 4, both, y)
                flight[n].append(post(part, part, slot + 4 + dz, dy=1))
            if order != B:
                part = piece_of(piece, buf, z, 1 - x, y)
                flight[n].append(post(part, part, slot + 4, dy=1))
        else:
            flight[n] = [post(src, dst, slot, dx=1)]

    def landed(n):
        for made in flight[n]:
            made.wait_recv()

    def gathered(n):
        piece = PIECES[n]
        if piece[0] != P1:
            whole = piece_of(piece, w[piece[0]], ALL, ALL, ALL)
            post(whole, whole, T.hand + n, other=True)
            return
        if not m.seen:
            links.arrived(m.pix, T.pix)
            m.seen.append(0)

        cols = pl.ds(piece[1], piece[2])
        m.prep[:, cols] = nn(m.pix[0:256, :], w[P1][:, :, :, :, cols].reshape(1024, piece[2]))
        cols = m.prep.at[:, pl.ds(piece[1], piece[2])]
        post(cols, cols, T.hand + n, other=True)

    def swap_act1():
        links.arrived(m.act1.at[y], T.act1)
        post(m.act1.at[y], m.act1.at[y], T.act1_y, dy=1)

    def swap_pix():
        if not m.seen:
            links.arrived(m.pix, T.pix)
            m.seen.append(0)
        post(m.pix.at[pl.ds(0, 256)], m.samp.at[y], T.samp_y, dy=1)

    waited = False
    for n, stage in GATHER_PLAN:
        if n == OTHER:
            (swap_act1, swap_pix)[stage]()
            continue
        if stage and not waited:
            for made in own:
                made.wait()
            waited = True
        if stage:
            landed(n)
        if stage == 3:
            gathered(n)
        else:
            gather(n, stage)
    post(ins.cotangent, m.cot.at[0], T.cot, other=True)
    drain()

    for to in (dict(dx=1), dict(dy=1)):
        pl.semaphore_signal(credit.at[0], inc=1, device_id=links.device(**to), device_id_type=MESH)
    pl.semaphore_wait(credit.at[0], 2)

    def windows_one():
        links.arrived(m.act1.at[1 - y], T.act1_y)
        for tap in range(9):
            a, b = tap // 3, tap % 3
            pq = (0 if a == 1 else 2) + (0 if b == 1 else 1)
            block = m.act1[1 - y, pq * 256:pq * 256 + 256, :].astype(F32)
            m.xc2[1 - y, :, tap * 384:(tap + 1) * 384] = shifted(block, -1 if a == 0 else 0, -1 if b == 0 else 0).astype(BF16)

    def windows_two():
        links.arrived(m.act4.at[1 - y], T.act4_y)
        for tap in range(9):
            block = m.act4[1 - y].astype(F32)
            m.xc5[1 - y, :, tap * 384:(tap + 1) * 384] = shifted(block, tap // 3 - 1, tap % 3 - 1).astype(BF16)

    def add(into, own, others):
        got = own[...].astype(F32)
        for other in others:
            got = got + other[...].astype(F32)
        into[...] = got.astype(BF16)

    def reduce(n, stage):
        name, first, count, order = SUMMED[n]
        kind, buf, into, last = KINDS[name], g[name], w[name], fin[name]
        slot = T.reduce + 6 * n
        paired = len(order) == 2
        done = order[:stage]

        def pick(ref, zi, xi, h):
            if kind == TAP:
                return ref.at[pl.ds(first, count), zi, xi]
            if name == P1:
                return ref.at[zi, xi, :, :, pl.ds(first, count)]
            if kind == COL:
                cols = pl.ds(first, 2 * count) if h is ALL else pl.ds(pl.multiple_of(first + h * count, 128), count)
                return ref.at[zi, xi, :, cols]
            return ref.at[zi, xi] if h is ALL else ref.at[zi, xi, pl.ds(h * count, count)]

        def pick_z(k, xi, h):
            ref = third[name].at[k]
            if kind == TAP:
                return ref.at[pl.ds(first, count), xi]
            if name == P1:
                return ref.at[xi, :, :, pl.ds(first, count)]
            if kind == COL:
                thin = ref.shape[-1] < buf.shape[-1]
                return ref.at[xi, :, pl.ds(first, 2 * count) if h is ALL else pl.ds(first // 2 if thin else first, count)]
            return ref.at[xi]

        def pick_last(i):
            if kind == TAP:
                return last.at[8 if first == 4 else 2 * (first + i) + y]
            if name == P1:
                return last.at[:, :, pl.ds(pl.multiple_of(768 * y + first, 128), count)]
            if kind == COL:
                return last.at[:, pl.ds(pl.multiple_of(first + y * count, 128), count)]
            return last.at[pl.ds(y * count, count)]

        def held(axes):
            return z if 3 in axes else ALL, x if 1 in axes else ALL, y if 2 in axes else ALL

        def landing(axes, axis, zi):
            if name == P1:
                return m.land.at[zi, :, :, pl.ds(first, count)]
            if axis == 1:
                return pick(into, zi, 0, ALL if paired or 2 not in axes else 1)
            return pick(into, zi, 1 if 1 in axes else ALL, 0)

        if stage:
            for made in flight[n]:
                made.wait_recv()
        if 0 < stage <= len(order):
            before, axis = order[:stage - 1], order[stage - 1]
            zi, xi, h = held(done)
            taps_here = count if kind == TAP else 1
            many_z, many_x = 4 if zi is ALL else 1, 2 if xi is ALL else 1

            def one(i, carry):
                tap, cell = i // (many_z * many_x), i % (many_z * many_x)
                at_z, at_x = cell // many_x if zi is ALL else zi, cell % many_x if xi is ALL else xi

                def inner(ref):
                    return ref.at[tap] if kind == TAP else ref

                own = inner(pick(buf, at_z, at_x, h))
                if axis == 3:
                    others = [inner(pick_z(k, 0 if 1 in before else at_x, ALL if 2 not in before else 0)) for k in range(3)]
                else:
                    land_x = 0 if axis == 1 else 1 if 1 in before else at_x
                    land_h = (ALL if paired or 2 not in before else 1) if axis == 1 else 0
                    others = [m.land.at[at_z, :, :, pl.ds(first, count)] if name == P1 else inner(pick(into, at_z, land_x, land_h))]
                add(pick_last(tap) if stage == len(order) else own, own, others)
                return carry

            lax.fori_loop(0, taps_here * many_z * many_x, one, 0)
        if stage < len(order):
            axis = order[stage]
            zi, xi, h = held(done)
            if axis == 1:
                flight[n] = [post(pick(buf, zi, 1 - x, h), landing(done, 1, zi), slot, dx=1)]
            elif axis == 2:
                flight[n] = [post(pick(buf, zi, xi, 1 - y), landing(done, 2, zi), slot + 4, dy=1)]
            else:
                flight[n] = [post(pick(buf, (z + dz) % 4, xi, h), pick_z(dz - 1, 0 if 1 in done else ALL, ALL if 2 not in done else 0),
                                  slot + dz, dz=dz) for dz in (2, 1, 3)]
        elif stage == len(order) and not (kind == TAP and first == 4):
            parts = [pick_last(i) for i in range(count if kind == TAP else 1)]
            flight[n] = [post(part, part, slot + (5 if kind != TAP else 4 + i), dy=1) for i, part in enumerate(parts)]
        else:
            left[name] -= 1
            if left[name] == 0:
                made = pltpu.make_async_copy(last, outs.grads[name], local_sems.at[name])
                made.start()
                m.tail.append(made)
                post(last, outs.grads[name], T.out + name, other=True)

    def columns(name, left, right):
        def one(step, carry):
            off = pl.multiple_of(step * 256, 256)
            part = tn(left, right[:, pl.ds(off, 256)])
            g[name][..., pl.ds(off, 256)] = part.astype(BF16).reshape(g[name].shape[:-1] + (256,))
            return carry

        lax.fori_loop(0, right.shape[1] // 256, one, 0)

    def taps(name, windows, low):
        def one(k, carry):
            tap = jnp.where(k == 4, 8, 2 * k + y)
            off = pl.multiple_of(tap * 384, 128)
            part = tn(windows[:, :, pl.ds(off, 384)].reshape(512, 384), low[...].reshape(512, 384))
            g[name][k] = part.astype(BF16).reshape(4, 2, 48, 384)
            return carry

        lax.fori_loop(0, 5, one, 0)

    def make(name):
        if name == E2:
            links.arrived(m.act5, T.act5)
            links.arrived(m.low6, T.low6)
            columns(E2, m.act5[...], m.low6)
        elif name == S2:
            links.arrived(m.xc5.at[y], T.xc5)
            links.arrived(m.low5.at[y], T.low5)
            links.arrived(m.low5.at[1 - y], T.low5_y)
            taps(S2, m.xc5, m.low5)
        elif name == R2:
            links.arrived(m.hlow, T.hlow)
            links.arrived(m.low4, T.low4)

            def one(step, carry):
                part = tn(m.hlow[:, pl.ds(pl.multiple_of(step * 384, 128), 384)], m.low4[...])
                g[R2][step] = part.astype(BF16).reshape(2, 4, 48, 384)
                return carry

            lax.fori_loop(0, 4, one, 0)
        elif name == E1:
            links.arrived(m.act2, T.act2)
            links.arrived(m.low3, T.low3)
            columns(E1, m.act2[...], m.low3)
        elif name == S1:
            links.arrived(m.xc2.at[y], T.xc2)
            links.arrived(m.low2.at[y], T.low2)
            links.arrived(m.low2.at[1 - y], T.low2_y)
            taps(S1, m.xc2, m.low2)
        else:
            links.arrived(m.low1, T.low1)

            def one(step, carry):
                part = tn(m.pix[:, pl.ds(pl.multiple_of(step * 256, 256), 256)], m.low1[...])
                g[R1][step] = part.astype(BF16).reshape(2, 2, 64, 384)
                return carry

            lax.fori_loop(0, 4, one, 0)

    def swap_projection():
        theirs = m.lowp.at[:, columns_of(m.lowp, 1 - y)]
        links.arrived(theirs, T.lowp)
        for k in range(PARTS_P1):
            size = 768 // PARTS_P1
            cols = pl.ds(pl.multiple_of((1 - y) * 768 + k * size, 128), size)
            post(m.lowp.at[:, cols], m.lowp_y.at[:, pl.ds(k * size, size)], T.lowp_y + k, dy=1)

    def project_back():
        links.arrived(m.lowp.at[:, columns_of(m.lowp, y)], T.lowp_own)

        def back(step, carry):
            kern = w[P1][step].reshape(256, 1536)
            m.gsamp[:, pl.ds(pl.multiple_of(step * 256, 256), 256)] = nt(m.lowp[...], kern)
            return carry

        lax.fori_loop(0, 4, back, 0)
        post(m.gsamp, m.gsamp, T.gsamp, other=True)

    def make_projection(k):
        size = 768 // PARTS_P1
        if k == 0:
            links.arrived(m.samp.at[1 - y], T.samp_y)
        links.arrived(m.lowp_y.at[:, pl.ds(k * size, size)], T.lowp_y + k)
        mine = m.lowp[:, pl.ds(pl.multiple_of(y * 768 + k * size, 128), size)]
        theirs = m.lowp_y[:, pl.ds(k * size, size)]

        def one(step, carry):
            cols = pl.ds(pl.multiple_of(step * 256, 256), 256)
            part = tn(m.pix[0:256, cols], mine) + tn(m.samp[1 - y, :, cols], theirs)
            g[P1][step, :, :, :, pl.ds(k * size, size)] = part.astype(BF16).reshape(2, 2, 64, size)
            return carry

        lax.fori_loop(0, 4, one, 0)

    left = [sum(piece[0] == name for piece in SUMMED) for name in NAMES]
    for n, stage in REDUCE_PLAN:
        if n == MAKE:
            make(stage)
        elif n == OTHER:
            (windows_one, windows_two, swap_projection, project_back)[stage]()
        elif n == MAKE_P1:
            make_projection(stage)
        else:
            reduce(n, stage)
    drain()
    for made in m.tail:
        made.wait()
    links.arrived(outs.act, T.out_act)
    links.arrived(outs.norm, T.out_norm)
    links.arrived(outs.gimg, T.out_gimg)


def runner(links, ins, outs, w, m, sums):
    x, y, z = links.x, links.y, links.z
    me = y * 8 + links.wide
    pending = []
    local_sems = m.local_sems

    def post(src, dst, slot, **to):
        made = links.send(src, dst, slot, **to)
        pending.append(made)
        return made

    def hand(ref, slot):
        post(ref, ref, slot, other=True)

    def weight(name):
        for n, piece in enumerate(PIECES):
            if piece[0] == name:
                links.arrived(piece_of(piece, w[name], ALL, ALL, ALL), T.hand + n)

    peers = [(dy, dz, dx) for dz in (2, 1, 3, 0) for dx in (1, 0) for dy in (1, 0) if (dy, dz, dx) != (0, 0, 0)]

    quad = [(dy, 0, dx) for dy, dx in ((1, 1), (0, 1), (1, 0))]
    along = [(0, dz, 0) for dz in (2, 1, 3)]

    def spread(buf, mine, slot, to):
        sem = links.next_send
        links.next_send += 1
        for dy, dz, dx in to:
            pltpu.make_async_remote_copy(
                src_ref=buf.at[mine], dst_ref=buf.at[mine], send_sem=links.send_sems.at[sem], recv_sem=links.recv_sems.at[slot],
                device_id=links.device(dy=dy, dz=dz, dx=dx), device_id_type=MESH).start()
        others = buf.at[pl.ds(0, len(to))]
        return pltpu.make_async_remote_copy(
            src_ref=others, dst_ref=others, send_sem=links.send_sems.at[sem],
            recv_sem=links.recv_sems.at[slot], device_id=links.device(other=True), device_id_type=MESH)

    def added(parts):
        while len(parts) > 1:
            parts = [parts[i] + parts[i + 1] for i in range(0, len(parts), 2)]
        return parts[0]

    def total(which, rows):
        buf = sums[which]
        if rows[0].shape[1] < 1536:
            for r, row in enumerate(rows):
                buf[me, r:r + 1, :] = row
            waiting = spread(buf, me, T.sums + which, peers)
            waiting.wait_recv()
            waiting.wait_send()
            return added([buf[i] for i in range(16)])
        mine = y * 2 + x
        for r, row in enumerate(rows):
            buf[mine, r:r + 1, :] = row
        waiting = spread(buf, mine, T.sums + which, quad)
        waiting.wait_recv()
        waiting.wait_send()
        far = sums[which + 12]
        far[z] = added([buf[i] for i in range(4)])
        waiting = spread(far, z, T.sums + 12 + which, along)
        waiting.wait_recv()
        waiting.wait_send()
        return added([far[i] for i in range(4)])

    own_norm = pltpu.make_async_copy(ins.norm, m.norm_in.at[links.wide], local_sems.at[0])
    own_norm.start()
    own_raw = pltpu.make_async_copy(ins.images, m.raw.at[1], local_sems.at[1])
    own_raw.start()
    own_mask = pltpu.make_async_copy(ins.mask, m.mask.at[1], local_sems.at[2])
    own_mask.start()
    own_cot = pltpu.make_async_copy(ins.cotangent, m.cot.at[1], local_sems.at[3])
    own_cot.start()
    for k, (dz, dx) in enumerate([(dz, dx) for dz in (2, 1, 3, 0) for dx in (1, 0) if (dz, dx) != (0, 0)]):
        post(ins.norm, m.norm_in.at[links.wide], T.norm_in + dz * 2 + dx, dz=dz, dx=dx)

    lo = pl.ds(0, 256)
    r = lax.broadcasted_iota(jnp.int32, (256, 256), 0)
    c = lax.broadcasted_iota(jnp.int32, (256, 256), 1)
    source = (2 * ((r // 8) % 8) + r // 128) * 16 + 2 * (r % 8) + (r // 64) % 2
    perm = jnp.where(c == source, 1.0, 0.0).astype(BF16)
    m.perm[...] = perm

    own_mask.wait()
    links.arrived(m.mask.at[0], T.mask)
    flags = m.mask[...].reshape(64, 16).astype(F32)
    for pq in range(4):
        p, q = pq // 2, pq % 2
        row = lax.broadcasted_iota(jnp.int32, (256, 64), 0)
        line = lax.broadcasted_iota(jnp.int32, (256, 64), 1)
        pick = jnp.where(line == (row // 64) * 16 + 2 * ((row // 8) % 8) + p, 1.0, 0.0)
        lines = nn(pick.astype(BF16), flags.astype(BF16))
        row16 = lax.broadcasted_iota(jnp.int32, (256, 16), 0)
        col16 = lax.broadcasted_iota(jnp.int32, (256, 16), 1)
        one = jnp.sum(jnp.where(col16 == 2 * (row16 % 8) + q, lines, 0.0), axis=1, keepdims=True)
        m.valid[pq * 256:(pq + 1) * 256, :] = jnp.broadcast_to(one, (256, 128))

    own_raw.wait()
    links.arrived(m.raw.at[0], T.raw)
    for b in range(4):
        picked = nn(perm, m.raw[b // 2, (b % 2) * 256:(b % 2) * 256 + 256, :]).astype(BF16)
        for pq in range(4):
            m.pix[pq * 256 + b * 64:pq * 256 + b * 64 + 64, :] = picked[pq * 64:pq * 64 + 64, :]
    pix_sent = links.send(m.pix, m.pix, T.pix, other=True)

    own_norm.wait()
    for dz in range(4):
        for dx in range(2):
            if dz or dx:
                links.arrived(m.norm_in.at[0], T.norm_in + dz * 2 + dx)
    for s in range(8):
        piece = m.norm_in[s]
        at = 0
        for ref in (m.gain_a, m.shift_a, m.gain_b, m.shift_b):
            size = ref.shape[1] // 8
            ref[:, s * size:(s + 1) * size] = piece[:, at:at + size]
            at += size

    norms = m.norms

    def set_norm(key, mean_sum, square_sum, count, gain, shift):
        ref = norms[key]
        mean = mean_sum / count
        var = square_sum / count - mean * mean
        scaler = lax.rsqrt(var + NORM_EPS)
        ref[0:1, :] = mean
        ref[1:2, :] = scaler
        ref[2:3, :] = gain
        ref[3:4, :] = gain * scaler
        ref[4:5, :] = shift - mean * (gain * scaler)

    def set_back(key, first_sum, second_sum, count, at):
        ref = norms[key]
        mean, scaler, gain = ref[0:1, :], ref[1:2, :], ref[2:3, :]
        centred = second_sum - mean * first_sum
        grad_var = -0.5 * gain * centred * scaler * scaler * scaler
        grad_mean = -gain * scaler * first_sum - 2.0 * mean * grad_var
        ref[5:6, :] = grad_mean / count
        ref[6:7, :] = 2.0 * grad_var / count
        size = ref.shape[1]
        gain_at, shift_at = at
        m.norm_out[:, gain_at:gain_at + size] = scaler * centred
        m.norm_out[:, shift_at:shift_at + size] = first_sum

    def rows_of(key, at, size):
        ref = norms[key]
        return [ref[k:k + 1, pl.ds(at, size)] for k in range(8)]

    def norm_of(key, pre, at, size):
        ref = norms[key]
        return pre * ref[3:4, pl.ds(at, size)] + ref[4:5, pl.ds(at, size)]

    def back_of(key, pre, up, valid, at, size):
        ref = norms[key]
        return ref[3:4, pl.ds(at, size)] * up + valid * (ref[5:6, pl.ds(at, size)] + ref[6:7, pl.ds(at, size)] * pre)

    def valid_of(rows, cols):
        one = m.valid[rows, :]
        return jnp.concatenate([one] * (cols // 128), axis=1) if cols > 128 else one

    def colsum(v):
        return jnp.sum(v, axis=0, keepdims=True)

    stat = m.stat

    def chunks(rows, width, body):
        def one(step, carry):
            return body(pl.ds(pl.multiple_of(step * 64, 64), 64), carry)

        zero = jnp.zeros((1, width), F32)
        return lax.fori_loop(0, rows // 64, one, (zero, zero))

    weight(R1)

    def layer1(step, carry):
        rows = pl.ds(pl.multiple_of(step * 256, 256), 256)
        pre = nn(m.pix[rows, :], w[R1][...].reshape(1024, 384))
        m.pre1[rows, :] = pre
        weighed = pre * valid_of(rows, 384)
        return carry[0] + colsum(weighed), carry[1] + colsum(weighed * pre)

    zero = jnp.zeros((1, 384), F32)
    first, second = lax.fori_loop(0, 4, layer1, (zero, zero))
    hi_here = jnp.concatenate([colsum(m.valid[...])] * 3, axis=1)
    lo_here = jnp.concatenate([colsum(m.valid[lo, :])] * 3, axis=1)
    got = total(0, [first, second, hi_here, lo_here])
    count_hi = jnp.maximum(got[2:3, :], 1.0)
    count_lo = jnp.maximum(got[3:4, :], 1.0)
    count_wide = jnp.concatenate([count_lo] * 4, axis=1)
    set_norm(N1, got[0:1, :], got[1:2, :], count_hi, m.gain_a[:, 0:384], m.shift_a[:, 0:384])

    def activate1(rows, carry):
        v = norm_of(N1, m.pre1[rows, :], 0, 384)
        act = v * sigmoid(v)
        m.up1[rows, :] = act
        m.act1[y, rows, :] = act.astype(BF16)
        return carry

    chunks(1024, 384, activate1)
    hand(m.act1.at[y], T.act1)
    for tap in range(9):
        a, b = tap // 3, tap % 3
        pq = (0 if a == 1 else 2) + (0 if b == 1 else 1)
        block = m.up1[pq * 256:pq * 256 + 256, :]
        block = shifted(block, -1 if a == 0 else 0, -1 if b == 0 else 0)
        m.xc2[y, :, tap * 384:(tap + 1) * 384] = block.astype(BF16)
    hand(m.xc2.at[y], T.xc2)

    def statistics(pre, rows, width):
        weighed = pre * valid_of(rows, width)
        return colsum(weighed), colsum(weighed * pre)

    weight(S1)
    pre = nn(m.xc2[y], w[S1][...].reshape(3456, 384))
    m.pre2[...] = pre
    got = total(1, statistics(pre, lo, 384))
    set_norm(N2, got[0:1, :], got[1:2, :], count_lo, m.gain_a[:, 384:768], m.shift_a[:, 384:768])

    def activate2(rows, carry):
        v = norm_of(N2, m.pre2[rows, :], 0, 384)
        m.act2[rows, :] = (v * sigmoid(v)).astype(BF16)
        return carry

    chunks(256, 384, activate2)
    hand(m.act2, T.act2)

    def wide_loop(body, size=256):
        def one(step, carry):
            body(pl.multiple_of(step * size, size))
            return carry

        lax.fori_loop(0, 1536 // size, one, 0)

    def keep_stats(ref, at, size, k):
        first, second = statistics(ref[:, pl.ds(at, size)], lo, size)
        stat[k:k + 1, pl.ds(at, size)] = first
        stat[k + 1:k + 2, pl.ds(at, size)] = second

    weight(E1)

    def layer3(at):
        m.pre3[:, pl.ds(at, 256)] = nn(m.act2[...], w[E1][:, :, :, pl.ds(at, 256)].reshape(384, 256))
        keep_stats(m.pre3, at, 256, 0)

    wide_loop(layer3)
    for n, piece in enumerate(PIECES):
        if piece[0] == P1:
            links.arrived(m.prep.at[:, pl.ds(piece[1], piece[2])], T.hand + n)
    wide_loop(lambda at: keep_stats(m.prep, at, 256, 2))
    got = total(2, [stat[k:k + 1, :] for k in range(4)])
    set_norm(N3, got[0:1, :], got[1:2, :], count_wide, m.gain_a[:, 768:2304], m.shift_a[:, 768:2304])
    set_norm(NP, got[2:3, :], got[3:4, :], count_wide, m.gain_a[:, 2304:3840], m.shift_a[:, 2304:3840])

    def sum_one(at, size):
        cols = pl.ds(at, size)
        return norm_of(N3, m.pre3[:, cols], at, size) + norm_of(NP, m.prep[:, cols], at, size)

    def make_hidden(at):
        v = sum_one(at, 128)
        hidden = v * sigmoid(v)
        m.hidden[:, pl.ds(at, 128)] = hidden
        m.hlow[:, pl.ds(at, 128)] = hidden.astype(BF16)

    wide_loop(make_hidden, 128)
    hand(m.hlow, T.hlow)

    weight(R2)
    pre = nn(m.hlow[...], w[R2][...].reshape(1536, 384))
    m.pre4[...] = pre
    got = total(3, statistics(pre, lo, 384))
    set_norm(N4, got[0:1, :], got[1:2, :], count_lo, m.gain_b[:, 0:384], m.shift_b[:, 0:384])

    def activate4(rows, carry):
        v = norm_of(N4, m.pre4[rows, :], 0, 384)
        act = v * sigmoid(v)
        m.small[rows, :] = act
        m.act4[y, rows, :] = act.astype(BF16)
        return carry

    chunks(256, 384, activate4)
    post(m.act4.at[y], m.act4.at[y], T.act4_y, dy=1, other=True)
    for tap in range(9):
        m.xc5[y, :, tap * 384:(tap + 1) * 384] = shifted(m.small[...], tap // 3 - 1, tap % 3 - 1).astype(BF16)
    hand(m.xc5.at[y], T.xc5)
    weight(S2)
    pre = nn(m.xc5[y], w[S2][...].reshape(3456, 384))
    m.pre5[...] = pre
    got = total(4, statistics(pre, lo, 384))
    set_norm(N5, got[0:1, :], got[1:2, :], count_lo, m.gain_b[:, 384:768], m.shift_b[:, 384:768])

    def activate5(rows, carry):
        v = norm_of(N5, m.pre5[rows, :], 0, 384)
        m.act5[rows, :] = (v * sigmoid(v)).astype(BF16)
        return carry

    chunks(256, 384, activate5)
    hand(m.act5, T.act5)
    weight(E2)

    def layer6(at):
        m.pre6[:, pl.ds(at, 256)] = nn(m.act5[...], w[E2][:, :, :, pl.ds(at, 256)].reshape(384, 256))
        keep_stats(m.pre6, at, 256, 0)

    wide_loop(layer6)
    got = total(5, [stat[k:k + 1, :] for k in range(2)])
    set_norm(N6, got[0:1, :], got[1:2, :], count_wide, m.gain_b[:, 768:2304], m.shift_b[:, 768:2304])
    own_cot.wait()
    links.arrived(m.cot.at[0], T.cot)

    def top(at):
        cols = pl.ds(at, 128)
        pre = m.pre6[:, cols]
        v = norm_of(N6, pre, at, 128) + m.hidden[:, cols]
        sg = sigmoid(v)
        m.acts[:, cols] = (v * sg).astype(BF16)
        up = m.cot[:, :, cols].reshape(256, 128).astype(F32)
        up = up * sg * (1.0 + v * (1.0 - sg))
        m.hidden[:, cols] = up
        stat[0:1, cols] = colsum(up)
        stat[1:2, cols] = colsum(up * pre)

    wide_loop(top, 128)
    out_act = pltpu.make_async_copy(m.acts.at[pl.ds(128, 128)], outs.act, local_sems.at[4])
    out_act.start()
    post(m.acts.at[pl.ds(0, 128)], outs.act, T.out_act, other=True)
    got = total(6, [stat[k:k + 1, :] for k in range(2)])
    b_gain, b_shift = 7680, 9984
    set_back(N6, got[0:1, :], got[1:2, :], count_wide, (b_gain + 768, b_shift + 768))

    def low6(at):
        cols = pl.ds(at, 128)
        m.low6[:, cols] = back_of(N6, m.pre6[:, cols], m.hidden[:, cols], valid_of(lo, 128), at, 128).astype(BF16)

    wide_loop(low6, 128)
    hand(m.low6, T.low6)
    m.small[...] = nt(m.low6[...], w[E2][...].reshape(384, 1536))

    def narrow_up(key, pre):
        def one(rows, carry):
            kept = pre[rows, :]
            up = silu_back(norm_of(key, kept, 0, 384), m.small[rows, :])
            m.small[rows, :] = up
            return carry[0] + colsum(up), carry[1] + colsum(up * kept)

        return chunks(256, 384, one)

    def narrow_low(key, pre, low, slot, far=None):
        def one(rows, carry):
            got = back_of(key, pre[rows, :], m.small[rows, :], valid_of(rows, 384), 0, 384)
            m.small[rows, :] = got
            low[rows, :] = got.astype(BF16)
            return carry

        chunks(256, 384, one)
        hand(low, slot)
        if far is not None:
            post(low, low, far, dy=1, other=True)

    got = total(7, narrow_up(N5, m.pre5))
    set_back(N5, got[0:1, :], got[1:2, :], count_lo, (b_gain + 384, b_shift + 384))
    narrow_low(N5, m.pre5, m.low5.at[y], T.low5, T.low5_y)
    grad = jnp.zeros((256, 384), F32)
    for tap in range(9):
        moved = shifted(m.small[...], 1 - tap // 3, 1 - tap % 3).astype(BF16)
        grad = grad + nt(moved, w[S2][tap].reshape(384, 384))
    m.small[...] = grad
    got = total(8, narrow_up(N4, m.pre4))
    set_back(N4, got[0:1, :], got[1:2, :], count_lo, (b_gain, b_shift))
    narrow_low(N4, m.pre4, m.low4, T.low4)

    def below(step, carry):
        at = pl.multiple_of(step * 384, 128)
        cols = pl.ds(at, 384)
        grad = m.hidden[:, cols] + nt(m.low4[...], w[R2][step].reshape(384, 384))
        up = silu_back(sum_one(at, 384), grad)
        m.pre6[:, cols] = up
        stat[0:1, cols] = colsum(up)
        stat[1:2, cols] = colsum(up * m.pre3[:, cols])
        stat[2:3, cols] = colsum(up * m.prep[:, cols])
        return carry

    lax.fori_loop(0, 4, below, 0)
    got = total(9, [stat[k:k + 1, :] for k in range(3)])
    a_gain, a_shift = 0, 3840
    set_back(N3, got[0:1, :], got[1:2, :], count_wide, (a_gain + 768, a_shift + 768))
    set_back(NP, got[0:1, :], got[2:3, :], count_wide, (a_gain + 2304, a_shift + 2304))

    def low3(at):
        cols = pl.ds(at, 128)
        up, valid = m.pre6[:, cols], valid_of(lo, 128)
        m.low3[:, cols] = back_of(N3, m.pre3[:, cols], up, valid, at, 128).astype(BF16)
        m.lowp[:, cols] = back_of(NP, m.prep[:, cols], up, valid, at, 128).astype(BF16)

    wide_loop(low3, 128)
    theirs, mine = m.lowp.at[:, columns_of(m.lowp, 1 - y)], m.lowp.at[:, columns_of(m.lowp, y)]
    hand(theirs, T.lowp)
    hand(mine, T.lowp_own)
    hand(m.low3, T.low3)
    m.small[...] = nt(m.low3[...], w[E1][...].reshape(384, 1536))
    got = total(10, narrow_up(N2, m.pre2))
    set_back(N2, got[0:1, :], got[1:2, :], count_lo, (a_gain + 384, a_shift + 384))
    narrow_low(N2, m.pre2, m.low2.at[y], T.low2, T.low2_y)
    for pq in range(4):
        p, q = pq // 2, pq % 2
        grad = jnp.zeros((256, 384), F32)
        for a in ((1,) if p == 0 else (0, 2)):
            for b in ((1,) if q == 0 else (0, 2)):
                moved = shifted(m.small[...], 1 if a == 0 else 0, 1 if b == 0 else 0).astype(BF16)
                grad = grad + nt(moved, w[S1][a * 3 + b].reshape(384, 384))
        m.up1[pq * 256:pq * 256 + 256, :] = grad

    def up1(rows, carry):
        kept = m.pre1[rows, :]
        up = silu_back(norm_of(N1, kept, 0, 384), m.up1[rows, :])
        m.up1[rows, :] = up
        return carry[0] + colsum(up), carry[1] + colsum(up * kept)

    got = total(11, chunks(1024, 384, up1))
    set_back(N1, got[0:1, :], got[1:2, :], count_hi, (a_gain, a_shift))
    out_norm = pltpu.make_async_copy(m.norm_out, outs.norm, local_sems.at[5])
    out_norm.start()
    post(m.norm_out, outs.norm, T.out_norm, other=True)

    def low1(rows, carry):
        got = back_of(N1, m.pre1[rows, :], m.up1[rows, :], valid_of(rows, 384), 0, 384)
        m.low1[rows, :] = got.astype(BF16)
        return carry

    chunks(1024, 384, low1)
    hand(m.low1, T.low1)
    links.arrived(m.gsamp, T.gsamp)
    pix_sent.wait_send()
    for pq in range(4):
        grad = nt(m.low1[pq * 256:pq * 256 + 256, :], w[R1][...].reshape(1024, 384))
        if pq == 0:
            grad = grad + m.gsamp[...]
        m.pix[pq * 256:pq * 256 + 256, :] = grad.astype(BF16)
    for b in range(4):
        block = jnp.concatenate([m.pix[pq * 256 + b * 64:pq * 256 + b * 64 + 64, :] for pq in range(4)], axis=0)
        m.raw[b // 2, (b % 2) * 256:(b % 2) * 256 + 256, :] = tn(m.perm[...], block).astype(BF16)
    out_img = pltpu.make_async_copy(m.raw.at[1], outs.gimg, local_sems.at[6])
    out_img.start()
    post(m.raw.at[0], outs.gimg, T.out_gimg, other=True)
    for name in NAMES:
        links.arrived(outs.grads[name], T.out + name)
    out_act.wait()
    out_norm.wait()
    out_img.wait()
    for made in pending:
        made.wait_send()


SUM_ROWS = ((4, 384), (2, 384), (4, 1536), (2, 384), (2, 384), (2, 1536), (2, 1536), (2, 384), (2, 384), (3, 1536), (2, 384), (2, 384))


def fused_kernel(sizes, keys, *refs):
    groups, at = [], 0
    for size in sizes:
        groups.append(refs[at:at + size])
        at += size
    taken, shards_in, given, made, w, g, fin, third, kept, norms, sums, rest = groups
    dp, wide = lax.axis_index("dp"), lax.axis_index("wide")
    core = dp % 2
    send_sems, recv_sems, local_sems, credit = rest
    barrier = pltpu.get_barrier_semaphore()
    greet = Links(send_sems, recv_sems, core, 0)
    everyone = [dict(other=True), dict(dy=1, other=True)] + [
        dict(dy=dy, dz=dz, dx=dx) for dy in (0, 1) for dz in range(4) for dx in (0, 1) if (dy, dz, dx) != (0, 0, 0)]
    for to in everyone:
        pl.semaphore_signal(barrier, inc=1, device_id=greet.device(**to), device_id_type=MESH)
    pl.semaphore_wait(barrier, len(everyone))

    images, mask, cotangent, norm = taken
    act, gimg, norm_out = given
    ins = types.SimpleNamespace(images=images, mask=mask, cotangent=cotangent, norm=norm, weights=shards_in)
    outs = types.SimpleNamespace(act=act, gimg=gimg, norm=norm_out, grads=made)
    m = types.SimpleNamespace(**dict(zip(keys, kept)), norms=norms, local_sems=local_sems, tail=[], seen=[])

    @pl.when(core == 0)
    def _():
        mover(Links(send_sems, recv_sems, 0, 1), ins, outs, w, g, third, fin, m, credit)

    @pl.when(core == 1)
    def _():
        runner(Links(send_sems, recv_sems, 1, 1), ins, outs, w, m, sums)


def finish_kernel(sizes, *refs):
    act, gimg, norms = refs[:3]
    grads, out_act, out_gimg = refs[3:10], refs[10], refs[11]
    out_grads, out_norms = refs[12:19], refs[19:23]
    low, high, row, parts = refs[23:30], refs[30:37], refs[37], refs[38:42]
    held_act, held_gimg, in_sems, out_sems = refs[42:]
    passing = [pltpu.make_async_copy(gimg, held_gimg, in_sems.at[0]), pltpu.make_async_copy(act, held_act, in_sems.at[9])]
    copies = []
    coming = [pltpu.make_async_copy(v, into, in_sems.at[2 + n]) for n, (v, into) in enumerate(zip(grads, low))]
    norm_in = pltpu.make_async_copy(norms, row, in_sems.at[1])
    norm_in.start()
    for made in coming + passing:
        made.start()
    norm_in.wait()
    wide = lax.axis_index("wide")
    at = 0
    for n, size in enumerate((sizes[0], sizes[0], sizes[1], sizes[1])):
        for s in range(8):
            @pl.when(wide == s)
            def _(n=n, size=size, start=at + s * size):
                parts[n][...] = row[:, start:start + size]
        at += 8 * size
        made = pltpu.make_async_copy(parts[n].at[0], out_norms[n], out_sems.at[1 + n])
        made.start()
        copies.append(made)
    for n, (source, into, out) in enumerate(zip(low, high, out_grads)):
        coming[n].wait()
        for i in range(source.shape[0] if len(source.shape) == 3 else 1):
            part = i if len(source.shape) == 3 else slice(None)
            into[part] = source[part].astype(F32)
        made = pltpu.make_async_copy(into, out, out_sems.at[5 + n])
        made.start()
        copies.append(made)
    for n, (source, out) in enumerate(((held_gimg, out_gimg), (held_act, out_act))):
        passing[n].wait()
        made = pltpu.make_async_copy(source, out, out_sems.at[(0, 12)[n]])
        made.start()
        copies.append(made)
    for made in copies:
        made.wait()


def fused_shards(images, pixel_mask, cotangent, reduce_one, spatial_one, expand_one, project_one, gains_one, shifts_one,
                 reduce_two, spatial_two, expand_two, gains_two, shifts_two):
    def split(weight, parts=2):
        return weight.reshape(parts, weight.shape[0] // parts, weight.shape[1])

    def join(weight):
        return weight.reshape(9, weight.shape[2], weight.shape[3])

    weights = (split(reduce_one), join(spatial_one), expand_one, split(project_one), split(reduce_two, 4), join(spatial_two), expand_two)
    local_a, local_b = gains_one.shape[0], gains_two.shape[0]
    row, at = 0.0, 0
    for part in (gains_one, shifts_one, gains_two, shifts_two):
        row = row + jnp.pad(part.astype(F32), (at, 2 * (local_a + local_b) - at - part.shape[0]))
        at += part.shape[0]
    norm = row.reshape(1, -1)
    taken = [images.reshape(512, 1024), pixel_mask.reshape(32, 16), cotangent.reshape(128, 1536), norm]
    given = [jax.ShapeDtypeStruct((128, 1536), BF16), jax.ShapeDtypeStruct((512, 1024), BF16), jax.ShapeDtypeStruct((1, 12288), F32)]
    made = [jax.ShapeDtypeStruct(v.shape, BF16) for v in weights]
    whole = [pltpu.VMEM(whole_shape(KINDS[n], v.shape), BF16) for n, v in enumerate(weights)]
    fin = [pltpu.VMEM(v.shape, BF16) for v in weights]
    partial = list(whole)
    partial[S1] = partial[S2] = pltpu.VMEM((5, 4, 2, 48, 384), BF16)
    partial[P1] = pltpu.VMEM((4, 2, 2, 64, 768), BF16)
    cells = [(5, 48, 384) if KINDS[n] == TAP else (2, 64, 768) if n == P1 else v.shape for n, v in enumerate(weights)]
    third = []
    for n, cell in enumerate(cells):
        orders = [piece[3] for piece in SUMMED if piece[0] == n]
        both = 2 if any(order.index(3) < order.index(1) for order in orders) else 1
        whole_y = any(2 in order and order.index(3) < order.index(2) for order in orders)
        if KINDS[n] == TAP:
            shape = (3, 5, both, 48, 384)
        elif n == P1 or whole_y:
            shape = (3, both) + cell
        elif KINDS[n] == COL:
            shape = (3, both, cell[0], cell[1] // 2)
        else:
            shape = (3, both, cell[0] // 2) + cell[1:]
        third.append(pltpu.VMEM(shape, BF16))
    bf = dict(raw=(2, 512, 1024), cot=(2, 128, 1536), pix=(1024, 1024), perm=(256, 256), xc2=(2, 256, 3456), xc5=(2, 256, 3456),
              act2=(256, 384), act5=(256, 384), hlow=(256, 1536), acts=(256, 1536), low6=(256, 1536), low5=(2, 256, 384), low4=(256, 384),
              low3=(256, 1536), lowp=(256, 1536), low2=(2, 256, 384), low1=(1024, 384),
              samp=(2, 256, 1024), act1=(2, 1024, 384), act4=(2, 256, 384), lowp_y=(256, 768), land=(4, 2, 64, 768))
    f32 = dict(norm_in=(8, 1, 1536), gain_a=(1, 3840), shift_a=(1, 3840), gain_b=(1, 2304), shift_b=(1, 2304), norm_out=(1, 12288),
               valid=(1024, 128), stat=(8, 1536), pre1=(1024, 384), up1=(1024, 384), pre2=(256, 384), pre3=(256, 1536), prep=(256, 1536),
               hidden=(256, 1536), pre4=(256, 384), pre5=(256, 384), pre6=(256, 1536), small=(256, 384), gsamp=(256, 1024))
    kept = {k: pltpu.VMEM(v, BF16) for k, v in bf.items()} | {k: pltpu.VMEM(v, F32) for k, v in f32.items()}
    kept |= dict(mask=pltpu.VMEM((2, 32, 16), jnp.int32))
    norms = [pltpu.VMEM((8, width), F32) for width in (384, 384, 1536, 1536, 384, 384, 1536)]
    sums = [pltpu.VMEM((16 if width < 1536 else 4, rows, width), F32) for rows, width in SUM_ROWS]
    sums += [pltpu.VMEM((4, rows, width) if width == 1536 else (1, 1, 128), F32) for rows, width in SUM_ROWS]
    rest = [pltpu.SemaphoreType.DMA((320,)), pltpu.SemaphoreType.DMA((T.total,)), pltpu.SemaphoreType.DMA((28,)),
            pltpu.SemaphoreType.REGULAR((1,))]
    groups = [taken, weights, given, made, whole, partial, fin, third, list(kept.values()), norms, sums, rest]
    anywhere = pl.BlockSpec(memory_space=pl.ANY)
    got = pl.pallas_call(
        functools.partial(fused_kernel, [len(group) for group in groups], list(kept)),
        out_shape=given + made,
        in_specs=[anywhere] * (len(taken) + len(weights)),
        out_specs=[anywhere] * (len(given) + len(made)),
        scratch_shapes=[v for group in groups[4:] for v in group],
        compiler_params=pltpu.CompilerParams(collective_id=0, has_side_effects=True, vmem_limit_bytes=63 * 2**20),
    )(*taken, *weights)
    act, gimg, norms, *grads = got
    finished = pl.pallas_call(
        functools.partial(finish_kernel, (local_a, local_b)),
        out_shape=[act, gimg] + [jax.ShapeDtypeStruct(v.shape, F32) for v in grads]
        + [jax.ShapeDtypeStruct((size,), F32) for size in (local_a, local_a, local_b, local_b)],
        in_specs=[anywhere] * 10,
        out_specs=[anywhere] * 13,
        scratch_shapes=[pltpu.VMEM(v.shape, BF16) for v in grads] + [pltpu.VMEM(v.shape, F32) for v in grads]
        + [pltpu.VMEM(norms.shape, F32)] + [pltpu.VMEM((1, size), F32) for size in (local_a, local_a, local_b, local_b)]
        + [pltpu.VMEM(act.shape, BF16), pltpu.VMEM(gimg.shape, BF16), pltpu.SemaphoreType.DMA((10,)), pltpu.SemaphoreType.DMA((13,))],
        compiler_params=pltpu.CompilerParams(vmem_limit_bytes=60 * 2**20),
    )(act, gimg, norms, *grads)
    act, gimg = finished[:2]
    grads = [v.reshape(like.shape) for v, like in zip(
        finished[2:9], (reduce_one, spatial_one, expand_one, project_one, reduce_two, spatial_two, expand_two))]
    norm_grads = finished[9:]
    return (
        act.reshape(cotangent.shape),
        gimg.reshape(images.shape),
        grads[0], grads[1], grads[2], grads[3], norm_grads[0], norm_grads[1],
        grads[4], grads[5], grads[6], norm_grads[2], norm_grads[3],
    )


def solution(mesh):
    fused = mesh.shape["dp"] == 4 and mesh.shape["wide"] == 8
    in_specs = (
        P(("dp", "wide"), None, None, None),
        P(("dp", "wide"), None, None),
        P(("dp", "wide"), None, None, None),
        P("wide", None),
        P(None, None, "wide", None),
        P("wide", None),
        P("wide", None),
        P("wide"),
        P("wide"),
        P("wide", None),
        P(None, None, "wide", None),
        P("wide", None),
        P("wide"),
        P("wide"),
    )
    out_specs = (
        P(("dp", "wide"), None, None, None),
        P(("dp", "wide"), None, None, None),
        P("wide", None),
        P(None, None, "wide", None),
        P("wide", None),
        P("wide", None),
        P("wide"),
        P("wide"),
        P("wide", None),
        P(None, None, "wide", None),
        P("wide", None),
        P("wide"),
        P("wide"),
    )
    return jax.shard_map(fused_shards if fused else shards, mesh=mesh, in_specs=in_specs, out_specs=out_specs, check_vma=False)
```

```python
import functools
import types

import jax
import jax.numpy as jnp
from jax import lax
from jax.experimental import pallas as pl
from jax.experimental.pallas import tpu as pltpu
from jax.sharding import PartitionSpec as P

NORM_EPS = 1e-05


def pixel_product(source, kernel):
    return jnp.einsum("bhwc,co->bhwo", source, kernel, preferred_element_type=jnp.float32)


def weight_grad(source, upstream):
    return jnp.einsum("bhwc,bhwo->co", source, upstream, preferred_element_type=jnp.float32)


def input_grad(upstream, kernel):
    return jnp.einsum("bhwo,co->bhwc", upstream, kernel, preferred_element_type=jnp.float32)


def conv_spatial(source, kernel, stride):
    out_h = source.shape[1] // stride
    out_w = source.shape[2] // stride
    padded = jnp.pad(source, ((0, 0), (1, 1), (1, 1), (0, 0)))
    summed = jnp.zeros((source.shape[0], out_h, out_w, kernel.shape[3]), jnp.float32)
    for row_off in range(3):
        for col_off in range(3):
            window = padded[
                :,
                row_off : row_off + stride * out_h : stride,
                col_off : col_off + stride * out_w : stride,
            ]
            summed = summed + pixel_product(window, kernel[row_off, col_off])
    return summed


def conv_back(source, upstream, kernel, stride):
    out_h = upstream.shape[1]
    out_w = upstream.shape[2]
    padded = jnp.pad(source, ((0, 0), (1, 1), (1, 1), (0, 0)))
    grad_src = jnp.zeros(padded.shape, jnp.float32)
    kernel_rows = []
    for row_off in range(3):
        for col_off in range(3):
            window = padded[
                :,
                row_off : row_off + stride * out_h : stride,
                col_off : col_off + stride * out_w : stride,
            ]
            kernel_rows.append(weight_grad(window, upstream))
            grad_src = grad_src.at[
                :,
                row_off : row_off + stride * out_h : stride,
                col_off : col_off + stride * out_w : stride,
            ].add(input_grad(upstream, kernel[row_off, col_off]))
    kernel_grad = jnp.stack(kernel_rows).reshape(kernel.shape)
    return (kernel_grad, grad_src[:, 1:-1, 1:-1])


def norm_forward(pre, valid, count, gain, shift):
    moments = lax.psum(
        (jnp.sum(pre * valid, axis=(0, 1, 2)), jnp.sum(pre * pre * valid, axis=(0, 1, 2))),
        ("dp", "wide"),
    )
    mean_val = moments[0] / count
    variance = moments[1] / count - mean_val * mean_val
    scaler = lax.rsqrt(variance + NORM_EPS)
    normed = (pre - mean_val) * scaler
    return (gain * normed + shift, (mean_val, scaler))


def norm_backward(upstream, pre, valid, count, gain, stats):
    mean_val, scaler = stats
    sums = lax.psum(
        (jnp.sum(upstream, axis=(0, 1, 2)), jnp.sum(upstream * pre, axis=(0, 1, 2))), ("dp", "wide")
    )
    first_sum, second_sum = sums
    centred = second_sum - mean_val * first_sum
    grad_gain = scaler * centred
    grad_var = -0.5 * gain * centred * scaler * scaler * scaler
    grad_mean = -gain * scaler * first_sum - 2.0 * mean_val * grad_var
    grad_pre = gain * scaler * upstream + valid / count * (grad_mean + 2.0 * pre * grad_var)
    return (grad_pre, grad_gain, first_sum)


def silu_grad(pre_act, upstream):
    sigma = jax.nn.sigmoid(pre_act)
    return upstream * sigma * (1.0 + pre_act * (1.0 - sigma))


def own_slice(whole, local_len):
    start = lax.axis_index("wide") * local_len
    return lax.dynamic_slice_in_dim(whole, start, local_len, 0)


def shards(
    images,
    pixel_mask,
    cotangent,
    reduce_one,
    spatial_one,
    expand_one,
    project_one,
    gains_one,
    shifts_one,
    reduce_two,
    spatial_two,
    expand_two,
    gains_two,
    shifts_two,
):
    valid_hi = pixel_mask.astype(jnp.float32)[..., None]
    valid_lo = valid_hi[:, ::2, ::2]
    counts = lax.psum((jnp.sum(valid_hi), jnp.sum(valid_lo)), ("dp", "wide"))
    count_hi = jnp.maximum(counts[0], 1.0)
    count_lo = jnp.maximum(counts[1], 1.0)
    first_full = (
        lax.all_gather(reduce_one, "wide", axis=0, tiled=True),
        lax.all_gather(spatial_one, "wide", axis=2, tiled=True),
        lax.all_gather(expand_one, "wide", axis=0, tiled=True),
        lax.all_gather(project_one, "wide", axis=0, tiled=True),
        lax.all_gather(gains_one, "wide", axis=0, tiled=True),
        lax.all_gather(shifts_one, "wide", axis=0, tiled=True),
    )
    red_a, spa_a, exp_a, proj_a, gain_a, shift_a = first_full
    mid_a = red_a.shape[1]
    mid_b = 2 * mid_a
    out_a = mid_b + exp_a.shape[1]
    out_b = out_a + exp_a.shape[1]
    gain_af = gain_a.astype(jnp.float32)
    shift_af = shift_a.astype(jnp.float32)
    pre_one = pixel_product(images, red_a)
    y_one, stat_one = norm_forward(pre_one, valid_hi, count_hi, gain_af[:mid_a], shift_af[:mid_a])
    act_one = jax.nn.silu(y_one).astype(jnp.bfloat16)
    pre_two = conv_spatial(act_one, spa_a, 2)
    y_two, stat_two = norm_forward(
        pre_two, valid_lo, count_lo, gain_af[mid_a:mid_b], shift_af[mid_a:mid_b]
    )
    act_two = jax.nn.silu(y_two).astype(jnp.bfloat16)
    pre_three = pixel_product(act_two, exp_a)
    y_three, stat_three = norm_forward(
        pre_three, valid_lo, count_lo, gain_af[mid_b:out_a], shift_af[mid_b:out_a]
    )
    sampled = images[:, ::2, ::2]
    pre_proj = pixel_product(sampled, proj_a)
    y_proj, stat_proj = norm_forward(
        pre_proj, valid_lo, count_lo, gain_af[out_a:out_b], shift_af[out_a:out_b]
    )
    sum_one = y_three + y_proj
    hidden = jax.nn.silu(sum_one)
    hidden_low = hidden.astype(jnp.bfloat16)
    second_full = (
        lax.all_gather(reduce_two, "wide", axis=0, tiled=True),
        lax.all_gather(spatial_two, "wide", axis=2, tiled=True),
        lax.all_gather(expand_two, "wide", axis=0, tiled=True),
        lax.all_gather(gains_two, "wide", axis=0, tiled=True),
        lax.all_gather(shifts_two, "wide", axis=0, tiled=True),
    )
    red_b, spa_b, exp_b, gain_b, shift_b = second_full
    gain_bf = gain_b.astype(jnp.float32)
    shift_bf = shift_b.astype(jnp.float32)
    pre_four = pixel_product(hidden_low, red_b)
    y_four, stat_four = norm_forward(
        pre_four, valid_lo, count_lo, gain_bf[:mid_a], shift_bf[:mid_a]
    )
    act_four = jax.nn.silu(y_four).astype(jnp.bfloat16)
    pre_five = conv_spatial(act_four, spa_b, 1)
    y_five, stat_five = norm_forward(
        pre_five, valid_lo, count_lo, gain_bf[mid_a:mid_b], shift_bf[mid_a:mid_b]
    )
    act_five = jax.nn.silu(y_five).astype(jnp.bfloat16)
    pre_six = pixel_product(act_five, exp_b)
    y_six, stat_six = norm_forward(
        pre_six, valid_lo, count_lo, gain_bf[mid_b:out_a], shift_bf[mid_b:out_a]
    )
    sum_two = y_six + hidden
    activations = jax.nn.silu(sum_two).astype(jnp.bfloat16)
    back_two = (
        lax.all_gather(reduce_two, "wide", axis=0, tiled=True),
        lax.all_gather(spatial_two, "wide", axis=2, tiled=True),
        lax.all_gather(expand_two, "wide", axis=0, tiled=True),
        lax.all_gather(gains_two, "wide", axis=0, tiled=True),
    )
    red_b, spa_b, exp_b, gain_b = back_two
    gain_bf = gain_b.astype(jnp.float32)
    upstream = cotangent.astype(jnp.float32)
    grad_sum_two = silu_grad(sum_two, upstream)
    grad_pre6, gain_g6, shift_g6 = norm_backward(
        grad_sum_two, pre_six, valid_lo, count_lo, gain_bf[mid_b:out_a], stat_six
    )
    low_six = grad_pre6.astype(jnp.bfloat16)
    grad_exp_b = weight_grad(act_five, low_six)
    grad_act5 = input_grad(low_six, exp_b)
    grad_pre5, gain_g5, shift_g5 = norm_backward(
        silu_grad(y_five, grad_act5), pre_five, valid_lo, count_lo, gain_bf[mid_a:mid_b], stat_five
    )
    low_five = grad_pre5.astype(jnp.bfloat16)
    grad_spa_b, grad_act4 = conv_back(act_four, low_five, spa_b, 1)
    grad_pre4, gain_g4, shift_g4 = norm_backward(
        silu_grad(y_four, grad_act4), pre_four, valid_lo, count_lo, gain_bf[:mid_a], stat_four
    )
    low_four = grad_pre4.astype(jnp.bfloat16)
    grad_red_b = weight_grad(hidden_low, low_four)
    grad_hidden = grad_sum_two + input_grad(low_four, red_b)
    owned_two = (
        lax.psum_scatter(
            grad_red_b.astype(jnp.bfloat16), "wide", scatter_dimension=0, tiled=True
        ).astype(jnp.float32),
        lax.psum_scatter(
            grad_spa_b.astype(jnp.bfloat16), "wide", scatter_dimension=2, tiled=True
        ).astype(jnp.float32),
        lax.psum_scatter(
            grad_exp_b.astype(jnp.bfloat16), "wide", scatter_dimension=0, tiled=True
        ).astype(jnp.float32),
    )
    owned_two = (
        lax.psum(owned_two[0].astype(jnp.bfloat16), "dp").astype(jnp.float32),
        lax.psum(owned_two[1].astype(jnp.bfloat16), "dp").astype(jnp.float32),
        lax.psum(owned_two[2].astype(jnp.bfloat16), "dp").astype(jnp.float32),
    )
    back_one = (
        lax.all_gather(reduce_one, "wide", axis=0, tiled=True),
        lax.all_gather(spatial_one, "wide", axis=2, tiled=True),
        lax.all_gather(expand_one, "wide", axis=0, tiled=True),
        lax.all_gather(project_one, "wide", axis=0, tiled=True),
        lax.all_gather(gains_one, "wide", axis=0, tiled=True),
    )
    red_a, spa_a, exp_a, proj_a, gain_a = back_one
    gain_af = gain_a.astype(jnp.float32)
    grad_sum_one = silu_grad(sum_one, grad_hidden)
    grad_pre3, gain_g3, shift_g3 = norm_backward(
        grad_sum_one, pre_three, valid_lo, count_lo, gain_af[mid_b:out_a], stat_three
    )
    grad_prep, gain_gp, shift_gp = norm_backward(
        grad_sum_one, pre_proj, valid_lo, count_lo, gain_af[out_a:out_b], stat_proj
    )
    low_three = grad_pre3.astype(jnp.bfloat16)
    low_proj = grad_prep.astype(jnp.bfloat16)
    grad_exp_a = weight_grad(act_two, low_three)
    grad_act2 = input_grad(low_three, exp_a)
    grad_proj_a = weight_grad(sampled, low_proj)
    grad_sampled = input_grad(low_proj, proj_a)
    grad_pre2, gain_g2, shift_g2 = norm_backward(
        silu_grad(y_two, grad_act2), pre_two, valid_lo, count_lo, gain_af[mid_a:mid_b], stat_two
    )
    low_two = grad_pre2.astype(jnp.bfloat16)
    grad_spa_a, grad_act1 = conv_back(act_one, low_two, spa_a, 2)
    grad_pre1, gain_g1, shift_g1 = norm_backward(
        silu_grad(y_one, grad_act1), pre_one, valid_hi, count_hi, gain_af[:mid_a], stat_one
    )
    low_one = grad_pre1.astype(jnp.bfloat16)
    grad_red_a = weight_grad(images, low_one)
    grad_input = input_grad(low_one, red_a)
    grad_input = grad_input.at[:, ::2, ::2].add(grad_sampled)
    grad_images = grad_input.astype(jnp.bfloat16)
    owned_one = (
        lax.psum_scatter(
            grad_red_a.astype(jnp.bfloat16), "wide", scatter_dimension=0, tiled=True
        ).astype(jnp.float32),
        lax.psum_scatter(
            grad_spa_a.astype(jnp.bfloat16), "wide", scatter_dimension=2, tiled=True
        ).astype(jnp.float32),
        lax.psum_scatter(
            grad_exp_a.astype(jnp.bfloat16), "wide", scatter_dimension=0, tiled=True
        ).astype(jnp.float32),
        lax.psum_scatter(
            grad_proj_a.astype(jnp.bfloat16), "wide", scatter_dimension=0, tiled=True
        ).astype(jnp.float32),
    )
    owned_one = (
        lax.psum(owned_one[0].astype(jnp.bfloat16), "dp").astype(jnp.float32),
        lax.psum(owned_one[1].astype(jnp.bfloat16), "dp").astype(jnp.float32),
        lax.psum(owned_one[2].astype(jnp.bfloat16), "dp").astype(jnp.float32),
        lax.psum(owned_one[3].astype(jnp.bfloat16), "dp").astype(jnp.float32),
    )
    gains_grad_a = jnp.concatenate([gain_g1, gain_g2, gain_g3, gain_gp])
    shifts_grad_a = jnp.concatenate([shift_g1, shift_g2, shift_g3, shift_gp])
    gains_grad_b = jnp.concatenate([gain_g4, gain_g5, gain_g6])
    shifts_grad_b = jnp.concatenate([shift_g4, shift_g5, shift_g6])
    local_a = gains_one.shape[0]
    local_b = gains_two.shape[0]
    return (
        activations,
        grad_images,
        owned_one[0],
        owned_one[1],
        owned_one[2],
        owned_one[3],
        own_slice(gains_grad_a, local_a),
        own_slice(shifts_grad_a, local_a),
        owned_two[0],
        owned_two[1],
        owned_two[2],
        own_slice(gains_grad_b, local_b),
        own_slice(shifts_grad_b, local_b),
    )


MESH = pl.DeviceIdType.MESH
F32 = jnp.float32
BF16 = jnp.bfloat16
ALL = slice(None)
NAMES = R1, S1, E1, P1, R2, S2, E2 = range(7)
ROW, TAP, COL = range(3)
KINDS = (ROW, TAP, COL, ROW, ROW, TAP, COL)
NORMS = N1, N2, N3, NP, N4, N5, N6 = range(7)


def nn(left, right):
    return jnp.dot(left, right, preferred_element_type=F32)


def nt(left, right):
    return lax.dot_general(left, right, (((1,), (1,)), ((), ())), preferred_element_type=F32)


def tn(left, right):
    return lax.dot_general(left, right, (((0,), (0,)), ((), ())), preferred_element_type=F32)


def whole_shape(kind, shard):
    if kind == TAP:
        return (shard[0], 4, 2) + tuple(shard[1:])
    return (4, 2) + tuple(shard)


class Links:
    def __init__(self, send_sems, recv_sems, core, base):
        self.send_sems, self.recv_sems = send_sems, recv_sems
        self.dp, self.wide = lax.axis_index("dp"), lax.axis_index("wide")
        self.core = core
        self.y, self.z, self.x = self.dp // 2, self.wide // 2, self.wide % 2
        self.next_send = base

    def device(self, dy=0, dz=0, dx=0, other=False):
        core = 1 - self.core if other else self.core
        y = (self.y + dy) % 2
        z, x = (self.z + dz) % 4, (self.x + dx) % 2
        return {"dp": y * 2 + core, "wide": z * 2 + x}

    def copy(self, src, dst, slot, **to):
        sem = self.send_sems.at[self.next_send]
        self.next_send += 1
        return pltpu.make_async_remote_copy(
            src_ref=src, dst_ref=dst, send_sem=sem, recv_sem=self.recv_sems.at[slot],
            device_id=self.device(**to), device_id_type=MESH)

    def send(self, src, dst, slot, **to):
        made = self.copy(src, dst, slot, **to)
        made.start()
        return made

    def arrived(self, dst, slot):
        pltpu.make_async_remote_copy(
            src_ref=dst, dst_ref=dst, send_sem=self.send_sems.at[0], recv_sem=self.recv_sems.at[slot],
            device_id=self.device(other=True), device_id_type=MESH).wait_recv()


def slot_table(**counts):
    table, at = types.SimpleNamespace(), 0
    for key, count in counts.items():
        setattr(table, key, at)
        at += count
    table.total = at
    return table


T = slot_table(raw=1, mask=1, cot=1, pix=1, xc2=1, act2=1, hlow=1, xc5=1, act5=1, low6=1, low5=1, low4=1, low3=1, lowp=1, low2=1,
               low1=1, gsamp=1, out_act=1, out_norm=1, out_gimg=1, samp_y=1, act1=1, act1_y=1, act4_y=1, low5_y=1, low2_y=1, lowp_own=1, lowp_y=6,
               out=7, hand=28, gather=8 * 28, reduce=6 * 22, norm_in=8, sums=24)


def sigmoid(v):
    return 1.0 / (1.0 + jnp.exp(-v))


def slope(v):
    sg = sigmoid(v)
    return sg * (1.0 + v * (1.0 - sg))


def side_step(value, dj):
    rows, cols = value.shape
    value = value.reshape(rows // 64, 8, 8, cols)
    if dj == 0:
        return value
    j = lax.broadcasted_iota(jnp.int32, value.shape, 2)
    return jnp.where(j < 7 if dj > 0 else j > 0, pltpu.roll(value, (-dj) % 8, 2), 0.0)


def down_step(value, di):
    images, _, _, cols = value.shape
    none = jnp.zeros((images, 1, 8, cols), value.dtype)
    if di > 0:
        value = jnp.concatenate([value[:, 1:], none], axis=1)
    elif di < 0:
        value = jnp.concatenate([none, value[:, :7]], axis=1)
    return value.reshape(images * 64, cols)


def windows_of(value):
    stepped = [side_step(value, dj) for dj in (-1, 0, 1)]
    return [down_step(stepped[tap % 3], tap // 3 - 1) for tap in range(9)]


def strided_windows(block):
    for tap in range(9):
        a, b = tap // 3, tap % 3
        value = block((0 if a == 1 else 2) + (0 if b == 1 else 1))
        yield down_step(side_step(value, -1 if b == 0 else 0), -1 if a == 0 else 0)


A, B, C, D, E = range(5)
MAKE, MAKE_P1, OTHER = -1, -2, -3
PIECES = (
    (R1, 0, 1, C), (S1, 0, 1, C), (S1, 2, 1, B), (S1, 4, 1, C), (S1, 6, 1, C), (S1, 8, 1, D), (E1, 0, 384, B), (E1, 768, 384, C),
    (P1, 0, 256, D), (P1, 256, 256, D), (P1, 512, 256, B), (P1, 768, 256, C), (P1, 1024, 256, A), (P1, 1280, 256, C), (R2, 0, 1,
    A), (R2, 2, 1, B), (S2, 0, 1, B), (S2, 2, 1, A), (S2, 4, 1, B), (S2, 6, 1, A), (S2, 8, 1, E), (E2, 0, 384, D), (E2, 768, 384,
    E))
GATHER_PLAN = (
    (13, 0), (0, 0), (2, 0), (4, 0), (14, 0), (12, 0), (13, 1), (3, 0), (11, 0), (6, 0), (5, 0), (17, 0), (0, 1), (1, 0), (19, 0),
    (7, 0), (9, 0), (20, 0), (2, 1), (13, 2), (10, 0), (8, 0), (4, 1), (3, 1), (0, 2), (12, 1), (15, 0), (2, 2), (13, 3), (4, 2),
    (16, 0), (3, 2), (5, 1), (1, 1), (11, 1), (6, 1), (0, 3), (7, 1), (2, 3), (14, 1), (18, 0), (5, 3), (4, 3), (9, 1), (19, 1),
    (1, 2), (3, 3), (6, 2), (10, 1), (7, 2), (1, 3), (8, 1), (9, 3), (11, 2), (6, 3), (10, 2), (17, 1), (12, 2), (15, 1), (7, 3),
    (22, 0), (16, 1), (11, 3), (21, 0), (8, 3), (14, 2), (10, 3), (12, 3), (15, 2), (16, 2), (20, 1), (18, 1), (19, 2), (14, 3),
    (15, 3), (17, 2), (18, 2), (22, 1), (19, 3), (16, 3), (21, 1), (17, 3), (20, 3), (18, 3), (21, 3), (22, 3), (OTHER, 0),
    (OTHER, 1))
SUMMED = (
    (E2, 0, 384, (2, 1, 3)), (E2, 768, 384, (2, 1, 3)), (R2, 0, 2, (2, 1, 3)), (E1, 0, 384, (2, 1, 3)), (E1, 768, 384, (2, 1, 3)),
    (R1, 0, 1, (2, 1, 3)), (S2, 0, 1, (1, 3)), (S2, 1, 1, (1, 3)), (S2, 2, 1, (1, 3)), (S2, 3, 1, (1, 3)), (S2, 4, 1, (3, 1)),
    (S1, 0, 1, (1, 3)), (S1, 1, 1, (1, 3)), (S1, 2, 1, (1, 3)), (S1, 3, 1, (1, 3)), (S1, 4, 1, (1, 3)), (P1, 0, 256, (1, 3)), (P1,
    256, 256, (1, 3)), (P1, 512, 256, (1, 3)))
REDUCE_PLAN = (
    (MAKE, E2), (OTHER, 1), (0, 0), (1, 0), (0, 1), (OTHER, 0), (MAKE, R2), (2, 0), (1, 1), (MAKE, S2), (6, 0), (8, 0), (10, 0),
    (1, 2), (0, 2), (9, 0), (7, 0), (6, 1), (OTHER, 2), (MAKE, E1), (2, 1), (8, 1), (OTHER, 3), (1, 3), (9, 1), (MAKE_P1, 0), (16,
    0), (4, 0), (7, 1), (MAKE_P1, 2), (0, 3), (6, 2), (1, 4), (18, 0), (2, 2), (8, 2), (3, 0), (MAKE, S1), (14, 0), (11, 0), (12,
    0), (16, 1), (9, 2), (7, 2), (0, 4), (8, 3), (6, 3), (MAKE, R1), (5, 0), (18, 1), (9, 3), (4, 1), (3, 1), (14, 1), (MAKE_P1,
    1), (2, 3), (11, 1), (12, 1), (16, 2), (17, 0), (7, 3), (10, 1), (4, 2), (18, 2), (5, 1), (2, 4), (13, 0), (3, 2), (14, 2),
    (16, 3), (15, 0), (18, 3), (17, 1), (11, 2), (12, 2), (14, 3), (10, 2), (4, 3), (5, 2), (3, 3), (12, 3), (13, 1), (11, 3),
    (15, 1), (4, 4), (17, 2), (3, 4), (5, 3), (17, 3), (13, 2), (15, 2), (5, 4), (13, 3))
PARTS_P1 = 3
def piece_of(piece, buf, z, x, h):
    name, first, count, order = piece
    kind = KINDS[name]
    if kind == COL or name == P1:
        if kind == COL:
            cols = pl.ds(first, 2 * count) if h is ALL else pl.ds(pl.multiple_of(first + h * count, 128), count)
            return buf.at[z, x, :, cols]
        return buf.at[z, x, h, :, pl.ds(first, count)]
    if name == R1:
        return buf.at[z, x, h]
    part = pl.ds(first, 1) if first == 8 else pl.ds(first, 2) if h is ALL else pl.ds(first + h, 1)
    return buf.at[part, z, x] if kind == TAP else buf.at[z, x, part]


def shard_of(piece, buf, h):
    name, first, count, order = piece
    kind = KINDS[name]
    if kind == COL:
        cols = pl.ds(first, 2 * count) if h is ALL else pl.ds(pl.multiple_of(first + h * count, 128), count)
        return buf.at[:, cols]
    if name == P1:
        return buf.at[h, :, pl.ds(first, count)]
    if name == R1:
        return buf.at[h]
    return buf.at[pl.ds(first, 1) if first == 8 else pl.ds(first, 2) if h is ALL else pl.ds(first + h, 1)]


def columns_of(ref, h):
    return pl.ds(pl.multiple_of(h * (ref.shape[-1] // 2), 128), ref.shape[-1] // 2)


def mover(links, ins, outs, w, g, third, fin, m, credit):
    x, y, z = links.x, links.y, links.z
    pending = []
    local_sems = m.local_sems

    def post(src, dst, slot, **to):
        made = links.send(src, dst, slot, **to)
        pending.append(made)
        return made

    def drain():
        for made in pending:
            made.wait_send()
        pending.clear()

    post(ins.images, m.raw.at[0], T.raw, other=True)
    post(ins.mask, m.mask.at[0], T.mask, other=True)
    own = []
    for n, piece in enumerate(PIECES):
        made = pltpu.make_async_copy(shard_of(piece, ins.weights[piece[0]], ALL), piece_of(piece, w[piece[0]], z, x, ALL), local_sems.at[n])
        made.start()
        own.append(made)

    flight = {}

    def along_z(src, dst, slot):
        return [post(src, dst, slot + dz, dz=dz) for dz in (2, 1, 3)]

    def gather(n, stage):
        piece = PIECES[n]
        buf, shard, order, slot = w[piece[0]], ins.weights[piece[0]], piece[3], T.gather + 8 * n
        if stage == 0:
            h = ALL if order in (D, E) else y
            src, dst = shard_of(piece, shard, h), piece_of(piece, buf, z, x, h)
        else:
            if order == A:
                part = (z, ALL, y) if stage == 1 else (ALL, ALL, y)
            elif order == B:
                part = (ALL, x, y) if stage == 1 else (ALL, x, ALL)
            elif order == C:
                part = (ALL, x, y) if stage == 1 else (ALL, ALL, y)
            elif order == D:
                part = (ALL, x, ALL)
            else:
                part = (z, ALL, ALL)
            src = dst = piece_of(piece, buf, *part)
        axis = ((1, 3, 2), (3, 2, 1), (3, 1, 2), (3, 1), (1, 3))[order][stage]
        if axis == 3:
            flight[n] = along_z(src, dst, slot)
        elif axis == 2:
            both = x if order == B else ALL
            flight[n] = []
            for dz in (1, 2, 3):
                part = piece_of(piece, buf, (z + dz) % 4, both, y)
                flight[n].append(post(part, part, slot + 4 + dz, dy=1))
            if order != B:
                part = piece_of(piece, buf, z, 1 - x, y)
                flight[n].append(post(part, part, slot + 4, dy=1))
        else:
            flight[n] = [post(src, dst, slot, dx=1)]

    def landed(n):
        for made in flight[n]:
            made.wait_recv()

    def gathered(n):
        piece = PIECES[n]
        if piece[0] != P1:
            whole = piece_of(piece, w[piece[0]], ALL, ALL, ALL)
            post(whole, whole, T.hand + n, other=True)
            return
        if not m.seen:
            links.arrived(m.pix, T.pix)
            m.seen.append(0)

        cols = pl.ds(piece[1], piece[2])
        m.prep[:, cols] = nn(m.pix[0:256, :], w[P1][:, :, :, :, cols].reshape(1024, piece[2]))
        cols = m.prep.at[:, pl.ds(piece[1], piece[2])]
        post(cols, cols, T.hand + n, other=True)

    def swap_act1():
        links.arrived(m.act1.at[y], T.act1)
        post(m.act1.at[y], m.act1.at[y], T.act1_y, dy=1)

    def swap_pix():
        if not m.seen:
            links.arrived(m.pix, T.pix)
            m.seen.append(0)
        post(m.pix.at[pl.ds(0, 256)], m.samp.at[y], T.samp_y, dy=1)

    waited = False
    for n, stage in GATHER_PLAN:
        if n == OTHER:
            (swap_act1, swap_pix)[stage]()
            continue
        if stage and not waited:
            for made in own:
                made.wait()
            waited = True
        if stage:
            landed(n)
        if stage == 3:
            gathered(n)
        else:
            gather(n, stage)
    post(ins.cotangent, m.cot.at[0], T.cot, other=True)
    drain()

    for to in (dict(dx=1), dict(dy=1)):
        pl.semaphore_signal(credit.at[0], inc=1, device_id=links.device(**to), device_id_type=MESH)
    pl.semaphore_wait(credit.at[0], 2)

    def windows_one():
        links.arrived(m.act1.at[1 - y], T.act1_y)
        for tap, window in enumerate(strided_windows(lambda pq: m.act1[1 - y, pq * 256:pq * 256 + 256, :].astype(F32))):
            m.xc2[1 - y, :, tap * 384:(tap + 1) * 384] = window.astype(BF16)

    def windows_two():
        links.arrived(m.act4.at[1 - y], T.act4_y)
        for tap, window in enumerate(windows_of(m.act4[1 - y].astype(F32))):
            m.xc5[1 - y, :, tap * 384:(tap + 1) * 384] = window.astype(BF16)

    def add(into, own, others):
        if len(others) == 1:
            into[...] = own[...] + others[0][...]
            return
        got = own[...].astype(F32)
        for other in others:
            got = got + other[...].astype(F32)
        into[...] = got.astype(BF16)

    def reduce(n, stage):
        name, first, count, order = SUMMED[n]
        kind, buf, into, last = KINDS[name], g[name], w[name], fin[name]
        slot = T.reduce + 6 * n
        paired = len(order) == 2
        done = order[:stage]

        def pick(ref, zi, xi, h):
            if kind == TAP:
                return ref.at[pl.ds(first, count), zi, xi]
            if name == P1:
                return ref.at[zi, xi, :, :, pl.ds(first, count)]
            if kind == COL:
                cols = pl.ds(first, 2 * count) if h is ALL else pl.ds(pl.multiple_of(first + h * count, 128), count)
                return ref.at[zi, xi, :, cols]
            return ref.at[zi, xi] if h is ALL else ref.at[zi, xi, pl.ds(h * count, count)]

        def pick_z(k, xi, h):
            ref = third[name].at[k]
            if kind == TAP:
                return ref.at[pl.ds(first, count), xi]
            if name == P1:
                return ref.at[xi, :, :, pl.ds(first, count)]
            if kind == COL:
                thin = ref.shape[-1] < buf.shape[-1]
                return ref.at[xi, :, pl.ds(first, 2 * count) if h is ALL else pl.ds(first // 2 if thin else first, count)]
            return ref.at[xi]

        def pick_last(i):
            if kind == TAP:
                return last.at[8 if first == 4 else 2 * (first + i) + y]
            if name == P1:
                return last.at[:, :, pl.ds(pl.multiple_of(768 * y + first, 128), count)]
            if kind == COL:
                return last.at[:, pl.ds(pl.multiple_of(first + y * count, 128), count)]
            return last.at[pl.ds(y * count, count)]

        def held(axes):
            return z if 3 in axes else ALL, x if 1 in axes else ALL, y if 2 in axes else ALL

        def landing(axes, axis, zi):
            if name == P1:
                return m.land.at[zi, :, :, pl.ds(first, count)]
            if axis == 1:
                return pick(into, zi, 0, ALL if paired or 2 not in axes else 1)
            return pick(into, zi, 1 if 1 in axes else ALL, 0)

        if stage:
            for made in flight[n]:
                made.wait_recv()
        if 0 < stage <= len(order):
            before, axis = order[:stage - 1], order[stage - 1]
            zi, xi, h = held(done)
            taps_here = count if kind == TAP else 1
            many_z = 4 if zi is ALL and kind != TAP else 1

            def one(i, carry):
                at_z = i if many_z == 4 else zi

                def inner(ref):
                    return ref.at[i] if kind == TAP else ref

                own = inner(pick(buf, at_z, xi, h))
                if axis == 3:
                    others = [inner(pick_z(k, 0 if 1 in before else xi, ALL if 2 not in before else 0)) for k in range(3)]
                else:
                    land_x = 0 if axis == 1 else 1 if 1 in before else xi
                    land_h = (ALL if paired or 2 not in before else 1) if axis == 1 else 0
                    others = [m.land.at[at_z, :, :, pl.ds(first, count)] if name == P1 else inner(pick(into, at_z, land_x, land_h))]
                add(pick_last(i) if stage == len(order) else own, own, others)
                return carry

            lax.fori_loop(0, taps_here * many_z, one, 0)
        if stage < len(order):
            axis = order[stage]
            zi, xi, h = held(done)
            if axis == 1:
                flight[n] = [post(pick(buf, zi, 1 - x, h), landing(done, 1, zi), slot, dx=1)]
            elif axis == 2:
                flight[n] = [post(pick(buf, zi, xi, 1 - y), landing(done, 2, zi), slot + 4, dy=1)]
            else:
                flight[n] = [post(pick(buf, (z + dz) % 4, xi, h), pick_z(dz - 1, 0 if 1 in done else ALL, ALL if 2 not in done else 0),
                                  slot + dz, dz=dz) for dz in (2, 1, 3)]
        elif stage == len(order) and not (kind == TAP and first == 4):
            parts = [pick_last(i) for i in range(count if kind == TAP else 1)]
            flight[n] = [post(part, part, slot + (5 if kind != TAP else 4 + i), dy=1) for i, part in enumerate(parts)]
        else:
            left[name] -= 1
            if left[name] == 0:
                made = pltpu.make_async_copy(last, outs.grads[name], local_sems.at[name])
                made.start()
                m.tail.append(made)
                post(last, outs.grads[name], T.out + name, other=True)

    def columns(name, left, right):
        def one(step, carry):
            off = pl.multiple_of(step * 256, 256)
            part = tn(left, right[:, pl.ds(off, 256)])
            g[name][..., pl.ds(off, 256)] = part.astype(BF16).reshape(g[name].shape[:-1] + (256,))
            return carry

        lax.fori_loop(0, right.shape[1] // 256, one, 0)

    def taps(name, windows, low):
        def one(k, carry):
            tap = jnp.where(k == 4, 8, 2 * k + y)
            off = pl.multiple_of(tap * 384, 128)
            part = tn(windows[:, :, pl.ds(off, 384)].reshape(512, 384), low[...].reshape(512, 384))
            g[name][k] = part.astype(BF16).reshape(4, 2, 48, 384)
            return carry

        lax.fori_loop(0, 5, one, 0)

    def make(name):
        if name == E2:
            links.arrived(m.act5, T.act5)
            links.arrived(m.low6, T.low6)
            columns(E2, m.act5[...], m.low6)
        elif name == S2:
            links.arrived(m.xc5.at[y], T.xc5)
            links.arrived(m.low5.at[y], T.low5)
            links.arrived(m.low5.at[1 - y], T.low5_y)
            taps(S2, m.xc5, m.low5)
        elif name == R2:
            links.arrived(m.hlow, T.hlow)
            links.arrived(m.low4, T.low4)

            def one(step, carry):
                part = tn(m.hlow[:, pl.ds(pl.multiple_of(step * 384, 128), 384)], m.low4[...])
                g[R2][step] = part.astype(BF16).reshape(2, 4, 48, 384)
                return carry

            lax.fori_loop(0, 4, one, 0)
        elif name == E1:
            links.arrived(m.act2, T.act2)
            links.arrived(m.low3, T.low3)
            columns(E1, m.act2[...], m.low3)
        elif name == S1:
            links.arrived(m.xc2.at[y], T.xc2)
            links.arrived(m.low2.at[y], T.low2)
            links.arrived(m.low2.at[1 - y], T.low2_y)
            taps(S1, m.xc2, m.low2)
        else:
            links.arrived(m.low1, T.low1)

            def one(step, carry):
                part = tn(m.pix[:, pl.ds(pl.multiple_of(step * 256, 256), 256)], m.low1[...])
                g[R1][step] = part.astype(BF16).reshape(2, 2, 64, 384)
                return carry

            lax.fori_loop(0, 4, one, 0)

    def swap_projection():
        theirs = m.lowp.at[:, columns_of(m.lowp, 1 - y)]
        links.arrived(theirs, T.lowp)
        for k in range(PARTS_P1):
            size = 768 // PARTS_P1
            cols = pl.ds(pl.multiple_of((1 - y) * 768 + k * size, 128), size)
            post(m.lowp.at[:, cols], m.lowp_y.at[:, pl.ds(k * size, size)], T.lowp_y + k, dy=1)

    def project_back():
        links.arrived(m.lowp.at[:, columns_of(m.lowp, y)], T.lowp_own)

        def back(step, carry):
            kern = w[P1][step].reshape(256, 1536)
            m.gsamp[:, pl.ds(pl.multiple_of(step * 256, 256), 256)] = nt(m.lowp[...], kern)
            return carry

        lax.fori_loop(0, 4, back, 0)
        post(m.gsamp, m.gsamp, T.gsamp, other=True)

    def make_projection(k):
        size = 768 // PARTS_P1
        if k == 0:
            links.arrived(m.samp.at[1 - y], T.samp_y)
        links.arrived(m.lowp_y.at[:, pl.ds(k * size, size)], T.lowp_y + k)
        mine = m.lowp[:, pl.ds(pl.multiple_of(y * 768 + k * size, 128), size)]
        theirs = m.lowp_y[:, pl.ds(k * size, size)]

        def one(step, carry):
            cols = pl.ds(pl.multiple_of(step * 256, 256), 256)
            part = tn(m.pix[0:256, cols], mine) + tn(m.samp[1 - y, :, cols], theirs)
            g[P1][step, :, :, :, pl.ds(k * size, size)] = part.astype(BF16).reshape(2, 2, 64, size)
            return carry

        lax.fori_loop(0, 4, one, 0)

    left = [sum(piece[0] == name for piece in SUMMED) for name in NAMES]
    for n, stage in REDUCE_PLAN:
        if n == MAKE:
            make(stage)
        elif n == OTHER:
            (windows_one, windows_two, swap_projection, project_back)[stage]()
        elif n == MAKE_P1:
            make_projection(stage)
        else:
            reduce(n, stage)
    drain()
    for made in m.tail:
        made.wait()
    links.arrived(outs.act, T.out_act)
    links.arrived(outs.norm, T.out_norm)
    links.arrived(outs.gimg, T.out_gimg)


def runner(links, ins, outs, w, m, sums):
    x, y, z = links.x, links.y, links.z
    me = y * 8 + links.wide
    pending = []
    local_sems = m.local_sems

    def post(src, dst, slot, **to):
        made = links.send(src, dst, slot, **to)
        pending.append(made)
        return made

    def hand(ref, slot):
        post(ref, ref, slot, other=True)

    def weight(name):
        for n, piece in enumerate(PIECES):
            if piece[0] == name:
                links.arrived(piece_of(piece, w[name], ALL, ALL, ALL), T.hand + n)

    peers = [(dy, dz, dx) for dz in (2, 1, 3, 0) for dx in (1, 0) for dy in (1, 0) if (dy, dz, dx) != (0, 0, 0)]

    quad = [(dy, 0, dx) for dy, dx in ((1, 1), (0, 1), (1, 0))]
    along = [(0, dz, 0) for dz in (2, 1, 3)]

    later = []

    def send_later():
        for ref, slot, far in later:
            if far:
                post(ref, ref, slot, dy=1, other=True)
            else:
                hand(ref, slot)
        later.clear()

    def spread(buf, mine, slot, to):
        sem = links.next_send
        links.next_send += 1
        for dy, dz, dx in to:
            pltpu.make_async_remote_copy(
                src_ref=buf.at[mine], dst_ref=buf.at[mine], send_sem=links.send_sems.at[sem], recv_sem=links.recv_sems.at[slot],
                device_id=links.device(dy=dy, dz=dz, dx=dx), device_id_type=MESH).start()
        others = buf.at[pl.ds(0, len(to))]
        return pltpu.make_async_remote_copy(
            src_ref=others, dst_ref=others, send_sem=links.send_sems.at[sem],
            recv_sem=links.recv_sems.at[slot], device_id=links.device(other=True), device_id_type=MESH)

    def added(parts):
        while len(parts) > 1:
            parts = [parts[i] + parts[i + 1] for i in range(0, len(parts), 2)]
        return parts[0]

    def total(which, rows, meanwhile=None):
        def pause():
            send_later()
            if meanwhile is not None:
                meanwhile()

        buf = sums[which]
        if which not in LONG_SUMS:
            for r, row in enumerate(rows):
                buf[me, r:r + 1, :] = row
            waiting = spread(buf, me, T.sums + which, peers)
            pause()
            waiting.wait_recv()
            pending.append(waiting)
            return added([buf[i] for i in range(16)])
        mine = y * 2 + x
        for r, row in enumerate(rows):
            buf[mine, r:r + 1, :] = row
        waiting = spread(buf, mine, T.sums + which, quad)
        pause()
        waiting.wait_recv()
        pending.append(waiting)
        far = sums[which + 12]
        far[z] = added([buf[i] for i in range(4)])
        waiting = spread(far, z, T.sums + 12 + which, along)
        waiting.wait_recv()
        pending.append(waiting)
        return added([far[i] for i in range(4)])

    own_norm = pltpu.make_async_copy(ins.norm, m.norm_in.at[links.wide], local_sems.at[0])
    own_norm.start()
    own_raw = pltpu.make_async_copy(ins.images, m.raw.at[1], local_sems.at[1])
    own_raw.start()
    own_mask = pltpu.make_async_copy(ins.mask, m.mask.at[1], local_sems.at[2])
    own_mask.start()
    own_cot = pltpu.make_async_copy(ins.cotangent, m.cot.at[1], local_sems.at[3])
    own_cot.start()
    for k, (dz, dx) in enumerate([(dz, dx) for dz in (2, 1, 3, 0) for dx in (1, 0) if (dz, dx) != (0, 0)]):
        post(ins.norm, m.norm_in.at[links.wide], T.norm_in + dz * 2 + dx, dz=dz, dx=dx)

    lo = pl.ds(0, 256)
    r = lax.broadcasted_iota(jnp.int32, (256, 256), 0)
    c = lax.broadcasted_iota(jnp.int32, (256, 256), 1)
    source = (2 * ((r // 8) % 8) + r // 128) * 16 + 2 * (r % 8) + (r // 64) % 2
    perm = jnp.where(c == source, 1.0, 0.0).astype(BF16)
    m.perm[...] = perm

    own_mask.wait()
    links.arrived(m.mask.at[0], T.mask)
    flags = m.mask[...].reshape(64, 16).astype(F32)
    for pq in range(4):
        p, q = pq // 2, pq % 2
        row = lax.broadcasted_iota(jnp.int32, (256, 64), 0)
        line = lax.broadcasted_iota(jnp.int32, (256, 64), 1)
        pick = jnp.where(line == (row // 64) * 16 + 2 * ((row // 8) % 8) + p, 1.0, 0.0)
        lines = nn(pick.astype(BF16), flags.astype(BF16))
        row16 = lax.broadcasted_iota(jnp.int32, (256, 16), 0)
        col16 = lax.broadcasted_iota(jnp.int32, (256, 16), 1)
        one = jnp.sum(jnp.where(col16 == 2 * (row16 % 8) + q, lines, 0.0), axis=1, keepdims=True)
        m.valid[pq * 256:(pq + 1) * 256, :] = jnp.broadcast_to(one, (256, 128))

    own_raw.wait()
    links.arrived(m.raw.at[0], T.raw)
    for b in range(4):
        picked = nn(perm, m.raw[b // 2, (b % 2) * 256:(b % 2) * 256 + 256, :]).astype(BF16)
        for pq in range(4):
            m.pix[pq * 256 + b * 64:pq * 256 + b * 64 + 64, :] = picked[pq * 64:pq * 64 + 64, :]
    pix_sent = links.send(m.pix, m.pix, T.pix, other=True)

    own_norm.wait()
    for dz in range(4):
        for dx in range(2):
            if dz or dx:
                links.arrived(m.norm_in.at[0], T.norm_in + dz * 2 + dx)
    for s in range(8):
        piece = m.norm_in[s]
        at = 0
        for ref in (m.gain_a, m.shift_a, m.gain_b, m.shift_b):
            size = ref.shape[1] // 8
            ref[:, s * size:(s + 1) * size] = piece[:, at:at + size]
            at += size

    norms = m.norms

    def set_norm(key, mean_sum, square_sum, count, gain, shift):
        ref = norms[key]
        mean = mean_sum / count
        var = square_sum / count - mean * mean
        scaler = lax.rsqrt(var + NORM_EPS)
        ref[0:1, :] = mean
        ref[1:2, :] = scaler
        ref[2:3, :] = gain
        ref[3:4, :] = gain * scaler
        ref[4:5, :] = shift - mean * (gain * scaler)

    def set_back(key, first_sum, second_sum, count, at):
        ref = norms[key]
        mean, scaler, gain = ref[0:1, :], ref[1:2, :], ref[2:3, :]
        centred = second_sum - mean * first_sum
        grad_var = -0.5 * gain * centred * scaler * scaler * scaler
        grad_mean = -gain * scaler * first_sum - 2.0 * mean * grad_var
        ref[5:6, :] = grad_mean / count
        ref[6:7, :] = 2.0 * grad_var / count
        size = ref.shape[1]
        gain_at, shift_at = at
        m.norm_out[:, gain_at:gain_at + size] = scaler * centred
        m.norm_out[:, shift_at:shift_at + size] = first_sum

    def rows_of(key, at, size):
        ref = norms[key]
        return [ref[k:k + 1, pl.ds(at, size)] for k in range(8)]

    def norm_of(key, pre, at, size):
        ref = norms[key]
        return pre * ref[3:4, pl.ds(at, size)] + ref[4:5, pl.ds(at, size)]

    def back_of(key, pre, up, valid, at, size):
        ref = norms[key]
        return ref[3:4, pl.ds(at, size)] * up + valid * (ref[5:6, pl.ds(at, size)] + ref[6:7, pl.ds(at, size)] * pre)

    def valid_of(rows, cols):
        one = m.valid[rows, :]
        return jnp.concatenate([one] * (cols // 128), axis=1) if cols > 128 else one

    def colsum(v):
        return jnp.sum(v, axis=0, keepdims=True)

    stat = m.stat

    def chunks(rows, width, body):
        def one(step, carry):
            return body(pl.ds(pl.multiple_of(step * 64, 64), 64), carry)

        zero = jnp.zeros((1, width), F32)
        return lax.fori_loop(0, rows // 64, one, (zero, zero))

    weight(R1)

    def layer1(step, carry):
        rows = pl.ds(pl.multiple_of(step * 256, 256), 256)
        pre = nn(m.pix[rows, :], w[R1][...].reshape(1024, 384))
        m.pre1[rows, :] = pre
        weighed = pre * valid_of(rows, 384)
        return carry[0] + colsum(weighed), carry[1] + colsum(weighed * pre)

    zero = jnp.zeros((1, 384), F32)
    first, second = lax.fori_loop(0, 4, layer1, (zero, zero))
    hi_here = jnp.concatenate([colsum(m.valid[...])] * 3, axis=1)
    lo_here = jnp.concatenate([colsum(m.valid[lo, :])] * 3, axis=1)
    got = total(0, [first, second, hi_here, lo_here])
    count_hi = jnp.maximum(got[2:3, :], 1.0)
    count_lo = jnp.maximum(got[3:4, :], 1.0)
    count_wide = jnp.concatenate([count_lo] * 4, axis=1)
    set_norm(N1, got[0:1, :], got[1:2, :], count_hi, m.gain_a[:, 0:384], m.shift_a[:, 0:384])

    def activate1(rows, carry):
        v = norm_of(N1, m.pre1[rows, :], 0, 384)
        act = v * sigmoid(v)
        m.up1[rows, :] = act
        m.act1[y, rows, :] = act.astype(BF16)
        return carry

    chunks(1024, 384, activate1)
    later.append((m.act1.at[y], T.act1, False))
    for tap, window in enumerate(strided_windows(lambda pq: m.up1[pq * 256:pq * 256 + 256, :])):
        m.xc2[y, :, tap * 384:(tap + 1) * 384] = window.astype(BF16)
    later.append((m.xc2.at[y], T.xc2, False))

    def statistics(pre, rows, width):
        weighed = pre * valid_of(rows, width)
        return colsum(weighed), colsum(weighed * pre)

    weight(S1)
    pre = nn(m.xc2[y], w[S1][...].reshape(3456, 384))
    m.pre2[...] = pre
    got = total(1, statistics(pre, lo, 384))
    set_norm(N2, got[0:1, :], got[1:2, :], count_lo, m.gain_a[:, 384:768], m.shift_a[:, 384:768])

    def activate2(rows, carry):
        v = norm_of(N2, m.pre2[rows, :], 0, 384)
        m.act2[rows, :] = (v * sigmoid(v)).astype(BF16)
        return carry

    chunks(256, 384, activate2)
    later.append((m.act2, T.act2, False))

    def wide_loop(body, size=256):
        def one(step, carry):
            body(pl.multiple_of(step * size, size))
            return carry

        lax.fori_loop(0, 1536 // size, one, 0)

    def keep_stats(ref, at, size, k):
        first, second = statistics(ref[:, pl.ds(at, size)], lo, size)
        stat[k:k + 1, pl.ds(at, size)] = first
        stat[k + 1:k + 2, pl.ds(at, size)] = second

    weight(E1)

    def layer3(at):
        m.pre3[:, pl.ds(at, 256)] = nn(m.act2[...], w[E1][:, :, :, pl.ds(at, 256)].reshape(384, 256))
        keep_stats(m.pre3, at, 256, 0)

    wide_loop(layer3)
    for n, piece in enumerate(PIECES):
        if piece[0] == P1:
            links.arrived(m.prep.at[:, pl.ds(piece[1], piece[2])], T.hand + n)
    wide_loop(lambda at: keep_stats(m.prep, at, 256, 2))
    got = total(2, [stat[k:k + 1, :] for k in range(4)])
    set_norm(N3, got[0:1, :], got[1:2, :], count_wide, m.gain_a[:, 768:2304], m.shift_a[:, 768:2304])
    set_norm(NP, got[2:3, :], got[3:4, :], count_wide, m.gain_a[:, 2304:3840], m.shift_a[:, 2304:3840])

    def sum_one(at, size):
        cols = pl.ds(at, size)
        return norm_of(N3, m.pre3[:, cols], at, size) + norm_of(NP, m.prep[:, cols], at, size)

    def make_hidden(at):
        v = sum_one(at, 128)
        hidden = v * sigmoid(v)
        m.hidden[:, pl.ds(at, 128)] = hidden
        m.hlow[:, pl.ds(at, 128)] = hidden.astype(BF16)

    wide_loop(make_hidden, 128)
    later.append((m.hlow, T.hlow, False))

    weight(R2)
    pre = nn(m.hlow[...], w[R2][...].reshape(1536, 384))
    m.pre4[...] = pre
    got = total(3, statistics(pre, lo, 384))
    set_norm(N4, got[0:1, :], got[1:2, :], count_lo, m.gain_b[:, 0:384], m.shift_b[:, 0:384])

    def activate4(rows, carry):
        v = norm_of(N4, m.pre4[rows, :], 0, 384)
        act = v * sigmoid(v)
        m.small[rows, :] = act
        m.act4[y, rows, :] = act.astype(BF16)
        return carry

    chunks(256, 384, activate4)
    later.append((m.act4.at[y], T.act4_y, True))
    for tap, window in enumerate(windows_of(m.small[...])):
        m.xc5[y, :, tap * 384:(tap + 1) * 384] = window.astype(BF16)
    later.append((m.xc5.at[y], T.xc5, False))
    weight(S2)
    pre = nn(m.xc5[y], w[S2][...].reshape(3456, 384))
    m.pre5[...] = pre
    got = total(4, statistics(pre, lo, 384))
    set_norm(N5, got[0:1, :], got[1:2, :], count_lo, m.gain_b[:, 384:768], m.shift_b[:, 384:768])

    def activate5(rows, carry):
        v = norm_of(N5, m.pre5[rows, :], 0, 384)
        m.act5[rows, :] = (v * sigmoid(v)).astype(BF16)
        return carry

    chunks(256, 384, activate5)
    later.append((m.act5, T.act5, False))
    weight(E2)

    def layer6(at):
        m.pre6[:, pl.ds(at, 256)] = nn(m.act5[...], w[E2][:, :, :, pl.ds(at, 256)].reshape(384, 256))
        keep_stats(m.pre6, at, 256, 0)

    wide_loop(layer6)
    got = total(5, [stat[k:k + 1, :] for k in range(2)])
    set_norm(N6, got[0:1, :], got[1:2, :], count_wide, m.gain_b[:, 768:2304], m.shift_b[:, 768:2304])
    own_cot.wait()
    links.arrived(m.cot.at[0], T.cot)

    def top(at):
        cols = pl.ds(at, 128)
        pre = m.pre6[:, cols]
        v = norm_of(N6, pre, at, 128) + m.hidden[:, cols]
        sg = sigmoid(v)
        m.acts[:, cols] = (v * sg).astype(BF16)
        up = m.cot[:, :, cols].reshape(256, 128).astype(F32)
        up = up * sg * (1.0 + v * (1.0 - sg))
        m.hidden[:, cols] = up
        stat[0:1, cols] = colsum(up)
        stat[1:2, cols] = colsum(up * pre)

    wide_loop(top, 128)
    out_act = pltpu.make_async_copy(m.acts.at[pl.ds(128, 128)], outs.act, local_sems.at[4])
    out_act.start()
    post(m.acts.at[pl.ds(0, 128)], outs.act, T.out_act, other=True)

    def slopes_two():
        m.slopes[0] = slope(norm_of(N5, m.pre5[...], 0, 384))
        m.slopes[1] = slope(norm_of(N4, m.pre4[...], 0, 384))

        def one(step, carry):
            m.up1[pl.ds(pl.multiple_of(step * 256, 256), 256), :] = slope(sum_one(pl.multiple_of(step * 384, 128), 384))
            return carry

        lax.fori_loop(0, 4, one, 0)

    def slopes_one():
        m.slopes[0] = slope(norm_of(N2, m.pre2[...], 0, 384))

        def one(rows, carry):
            m.up1[rows, :] = slope(norm_of(N1, m.pre1[rows, :], 0, 384))
            return carry

        chunks(1024, 384, one)

    got = total(6, [stat[k:k + 1, :] for k in range(2)], slopes_two)
    b_gain, b_shift = 7680, 9984
    set_back(N6, got[0:1, :], got[1:2, :], count_wide, (b_gain + 768, b_shift + 768))

    def low6(at):
        cols = pl.ds(at, 128)
        m.low6[:, cols] = back_of(N6, m.pre6[:, cols], m.hidden[:, cols], valid_of(lo, 128), at, 128).astype(BF16)

    wide_loop(low6, 128)
    hand(m.low6, T.low6)
    m.small[...] = nt(m.low6[...], w[E2][...].reshape(384, 1536))

    def narrow_up(pre, which):
        def one(rows, carry):
            kept = pre[rows, :]
            up = m.small[rows, :] * m.slopes[which, rows, :]
            m.small[rows, :] = up
            return carry[0] + colsum(up), carry[1] + colsum(up * kept)

        return chunks(256, 384, one)

    def narrow_low(key, pre, low, slot, far=None):
        def one(rows, carry):
            got = back_of(key, pre[rows, :], m.small[rows, :], valid_of(rows, 384), 0, 384)
            m.small[rows, :] = got
            low[rows, :] = got.astype(BF16)
            return carry

        chunks(256, 384, one)
        hand(low, slot)
        if far is not None:
            post(low, low, far, dy=1, other=True)

    got = total(7, narrow_up(m.pre5, 0))
    set_back(N5, got[0:1, :], got[1:2, :], count_lo, (b_gain + 384, b_shift + 384))
    narrow_low(N5, m.pre5, m.low5.at[y], T.low5, T.low5_y)
    grad = jnp.zeros((256, 384), F32)
    for tap, window in enumerate(windows_of(m.small[...])):
        grad = grad + nt(window.astype(BF16), w[S2][8 - tap].reshape(384, 384))
    m.small[...] = grad
    got = total(8, narrow_up(m.pre4, 1))
    set_back(N4, got[0:1, :], got[1:2, :], count_lo, (b_gain, b_shift))
    narrow_low(N4, m.pre4, m.low4, T.low4)

    def below(step, carry):
        at = pl.multiple_of(step * 384, 128)
        cols = pl.ds(at, 384)
        grad = m.hidden[:, cols] + nt(m.low4[...], w[R2][step].reshape(384, 384))
        up = grad * m.up1[pl.ds(pl.multiple_of(step * 256, 256), 256), :]
        m.pre6[:, cols] = up
        stat[0:1, cols] = colsum(up)
        stat[1:2, cols] = colsum(up * m.pre3[:, cols])
        stat[2:3, cols] = colsum(up * m.prep[:, cols])
        return carry

    lax.fori_loop(0, 4, below, 0)
    got = total(9, [stat[k:k + 1, :] for k in range(3)], slopes_one)
    a_gain, a_shift = 0, 3840
    set_back(N3, got[0:1, :], got[1:2, :], count_wide, (a_gain + 768, a_shift + 768))
    set_back(NP, got[0:1, :], got[2:3, :], count_wide, (a_gain + 2304, a_shift + 2304))

    def low3(at):
        cols = pl.ds(at, 128)
        up, valid = m.pre6[:, cols], valid_of(lo, 128)
        m.low3[:, cols] = back_of(N3, m.pre3[:, cols], up, valid, at, 128).astype(BF16)
        m.lowp[:, cols] = back_of(NP, m.prep[:, cols], up, valid, at, 128).astype(BF16)

    wide_loop(low3, 128)
    theirs, mine = m.lowp.at[:, columns_of(m.lowp, 1 - y)], m.lowp.at[:, columns_of(m.lowp, y)]
    hand(theirs, T.lowp)
    hand(mine, T.lowp_own)
    hand(m.low3, T.low3)
    m.small[...] = nt(m.low3[...], w[E1][...].reshape(384, 1536))
    got = total(10, narrow_up(m.pre2, 0))
    set_back(N2, got[0:1, :], got[1:2, :], count_lo, (a_gain + 384, a_shift + 384))
    narrow_low(N2, m.pre2, m.low2.at[y], T.low2, T.low2_y)
    for pq in range(4):
        p, q = pq // 2, pq % 2
        grad = jnp.zeros((256, 384), F32)
        for b in ((1,) if q == 0 else (0, 2)):
            stepped = side_step(m.small[...], 1 if b == 0 else 0)
            for a in ((1,) if p == 0 else (0, 2)):
                moved = down_step(stepped, 1 if a == 0 else 0).astype(BF16)
                grad = grad + nt(moved, w[S1][a * 3 + b].reshape(384, 384))
        rows = pl.ds(pq * 256, 256)
        m.up1[rows, :] = grad * m.up1[rows, :]

    def up1(rows, carry):
        kept = m.pre1[rows, :]
        up = m.up1[rows, :]
        return carry[0] + colsum(up), carry[1] + colsum(up * kept)

    got = total(11, chunks(1024, 384, up1))
    set_back(N1, got[0:1, :], got[1:2, :], count_hi, (a_gain, a_shift))
    out_norm = pltpu.make_async_copy(m.norm_out, outs.norm, local_sems.at[5])
    out_norm.start()
    post(m.norm_out, outs.norm, T.out_norm, other=True)

    def low1(rows, carry):
        got = back_of(N1, m.pre1[rows, :], m.up1[rows, :], valid_of(rows, 384), 0, 384)
        m.low1[rows, :] = got.astype(BF16)
        return carry

    chunks(1024, 384, low1)
    hand(m.low1, T.low1)
    links.arrived(m.gsamp, T.gsamp)
    pix_sent.wait_send()
    for pq in range(4):
        grad = nt(m.low1[pq * 256:pq * 256 + 256, :], w[R1][...].reshape(1024, 384))
        if pq == 0:
            grad = grad + m.gsamp[...]
        m.pix[pq * 256:pq * 256 + 256, :] = grad.astype(BF16)
    for b in range(4):
        block = jnp.concatenate([m.pix[pq * 256 + b * 64:pq * 256 + b * 64 + 64, :] for pq in range(4)], axis=0)
        m.raw[b // 2, (b % 2) * 256:(b % 2) * 256 + 256, :] = tn(m.perm[...], block).astype(BF16)
    out_img = pltpu.make_async_copy(m.raw.at[1], outs.gimg, local_sems.at[6])
    out_img.start()
    post(m.raw.at[0], outs.gimg, T.out_gimg, other=True)
    for name in NAMES:
        links.arrived(outs.grads[name], T.out + name)
    out_act.wait()
    out_norm.wait()
    out_img.wait()
    for made in pending:
        made.wait_send()


SUM_ROWS = ((4, 384), (2, 384), (4, 1536), (2, 384), (2, 384), (2, 1536), (2, 1536), (2, 384), (2, 384), (3, 1536), (2, 384), (2, 384))


LONG_SUMS = (2, 5, 6, 9)


def fused_kernel(sizes, keys, *refs):
    groups, at = [], 0
    for size in sizes:
        groups.append(refs[at:at + size])
        at += size
    taken, shards_in, given, made, w, g, fin, third, kept, norms, sums, rest = groups
    dp, wide = lax.axis_index("dp"), lax.axis_index("wide")
    core = dp % 2
    send_sems, recv_sems, local_sems, credit = rest
    barrier = pltpu.get_barrier_semaphore()
    greet = Links(send_sems, recv_sems, core, 0)
    everyone = [dict(other=True), dict(dy=1, other=True)] + [
        dict(dy=dy, dz=dz, dx=dx) for dy in (0, 1) for dz in range(4) for dx in (0, 1) if (dy, dz, dx) != (0, 0, 0)]
    for to in everyone:
        pl.semaphore_signal(barrier, inc=1, device_id=greet.device(**to), device_id_type=MESH)
    pl.semaphore_wait(barrier, len(everyone))

    images, mask, cotangent, norm = taken
    act, gimg, norm_out = given
    ins = types.SimpleNamespace(images=images, mask=mask, cotangent=cotangent, norm=norm, weights=shards_in)
    outs = types.SimpleNamespace(act=act, gimg=gimg, norm=norm_out, grads=made)
    m = types.SimpleNamespace(**dict(zip(keys, kept)), norms=norms, local_sems=local_sems, tail=[], seen=[])

    @pl.when(core == 0)
    def _():
        mover(Links(send_sems, recv_sems, 0, 1), ins, outs, w, g, third, fin, m, credit)

    @pl.when(core == 1)
    def _():
        runner(Links(send_sems, recv_sems, 1, 1), ins, outs, w, m, sums)


def finish_kernel(sizes, *refs):
    act, gimg, norms = refs[:3]
    grads, out_act, out_gimg = refs[3:10], refs[10], refs[11]
    out_grads, out_norms = refs[12:19], refs[19:23]
    low, high, row, parts = refs[23:30], refs[30:37], refs[37], refs[38:42]
    held_act, held_gimg, in_sems, out_sems = refs[42:]
    passing = [pltpu.make_async_copy(gimg, held_gimg, in_sems.at[0]), pltpu.make_async_copy(act, held_act, in_sems.at[9])]
    copies = []
    coming = [pltpu.make_async_copy(v, into, in_sems.at[2 + n]) for n, (v, into) in enumerate(zip(grads, low))]
    norm_in = pltpu.make_async_copy(norms, row, in_sems.at[1])
    norm_in.start()
    for made in coming + passing:
        made.start()
    norm_in.wait()
    wide = lax.axis_index("wide")
    at = 0
    for n, size in enumerate((sizes[0], sizes[0], sizes[1], sizes[1])):
        for s in range(8):
            @pl.when(wide == s)
            def _(n=n, size=size, start=at + s * size):
                parts[n][...] = row[:, start:start + size]
        at += 8 * size
        made = pltpu.make_async_copy(parts[n].at[0], out_norms[n], out_sems.at[1 + n])
        made.start()
        copies.append(made)
    for n, (source, into, out) in enumerate(zip(low, high, out_grads)):
        coming[n].wait()
        for i in range(source.shape[0] if len(source.shape) == 3 else 1):
            part = i if len(source.shape) == 3 else slice(None)
            into[part] = source[part].astype(F32)
        made = pltpu.make_async_copy(into, out, out_sems.at[5 + n])
        made.start()
        copies.append(made)
    for n, (source, out) in enumerate(((held_gimg, out_gimg), (held_act, out_act))):
        passing[n].wait()
        made = pltpu.make_async_copy(source, out, out_sems.at[(0, 12)[n]])
        made.start()
        copies.append(made)
    for made in copies:
        made.wait()


def fused_shards(images, pixel_mask, cotangent, reduce_one, spatial_one, expand_one, project_one, gains_one, shifts_one,
                 reduce_two, spatial_two, expand_two, gains_two, shifts_two):
    def split(weight, parts=2):
        return weight.reshape(parts, weight.shape[0] // parts, weight.shape[1])

    def join(weight):
        return weight.reshape(9, weight.shape[2], weight.shape[3])

    weights = (split(reduce_one), join(spatial_one), expand_one, split(project_one), split(reduce_two, 4), join(spatial_two), expand_two)
    local_a, local_b = gains_one.shape[0], gains_two.shape[0]
    row, at = 0.0, 0
    for part in (gains_one, shifts_one, gains_two, shifts_two):
        row = row + jnp.pad(part.astype(F32), (at, 2 * (local_a + local_b) - at - part.shape[0]))
        at += part.shape[0]
    norm = row.reshape(1, -1)
    taken = [images.reshape(512, 1024), pixel_mask.reshape(32, 16), cotangent.reshape(128, 1536), norm]
    given = [jax.ShapeDtypeStruct((128, 1536), BF16), jax.ShapeDtypeStruct((512, 1024), BF16), jax.ShapeDtypeStruct((1, 12288), F32)]
    made = [jax.ShapeDtypeStruct(v.shape, BF16) for v in weights]
    whole = [pltpu.VMEM(whole_shape(KINDS[n], v.shape), BF16) for n, v in enumerate(weights)]
    fin = [pltpu.VMEM(v.shape, BF16) for v in weights]
    partial = list(whole)
    partial[S1] = partial[S2] = pltpu.VMEM((5, 4, 2, 48, 384), BF16)
    partial[P1] = pltpu.VMEM((4, 2, 2, 64, 768), BF16)
    cells = [(5, 48, 384) if KINDS[n] == TAP else (2, 64, 768) if n == P1 else v.shape for n, v in enumerate(weights)]
    third = []
    for n, cell in enumerate(cells):
        orders = [piece[3] for piece in SUMMED if piece[0] == n]
        both = 2 if any(order.index(3) < order.index(1) for order in orders) else 1
        whole_y = any(2 in order and order.index(3) < order.index(2) for order in orders)
        if KINDS[n] == TAP:
            shape = (3, 5, both, 48, 384)
        elif n == P1 or whole_y:
            shape = (3, both) + cell
        elif KINDS[n] == COL:
            shape = (3, both, cell[0], cell[1] // 2)
        else:
            shape = (3, both, cell[0] // 2) + cell[1:]
        third.append(pltpu.VMEM(shape, BF16))
    bf = dict(raw=(2, 512, 1024), cot=(2, 128, 1536), pix=(1024, 1024), perm=(256, 256), xc2=(2, 256, 3456), xc5=(2, 256, 3456),
              act2=(256, 384), act5=(256, 384), hlow=(256, 1536), acts=(256, 1536), low6=(256, 1536), low5=(2, 256, 384), low4=(256, 384),
              low3=(256, 1536), lowp=(256, 1536), low2=(2, 256, 384), low1=(1024, 384),
              samp=(2, 256, 1024), act1=(2, 1024, 384), act4=(2, 256, 384), lowp_y=(256, 768), land=(4, 2, 64, 768))
    f32 = dict(norm_in=(8, 1, 1536), gain_a=(1, 3840), shift_a=(1, 3840), gain_b=(1, 2304), shift_b=(1, 2304), norm_out=(1, 12288),
               valid=(1024, 128), stat=(8, 1536), pre1=(1024, 384), up1=(1024, 384), pre2=(256, 384), pre3=(256, 1536), prep=(256, 1536),
               hidden=(256, 1536), pre4=(256, 384), pre5=(256, 384), pre6=(256, 1536), small=(256, 384), gsamp=(256, 1024), slopes=(2, 256, 384))
    kept = {k: pltpu.VMEM(v, BF16) for k, v in bf.items()} | {k: pltpu.VMEM(v, F32) for k, v in f32.items()}
    kept |= dict(mask=pltpu.VMEM((2, 32, 16), jnp.int32))
    norms = [pltpu.VMEM((8, width), F32) for width in (384, 384, 1536, 1536, 384, 384, 1536)]
    sums = [pltpu.VMEM((4 if n in LONG_SUMS else 16, rows, width), F32) for n, (rows, width) in enumerate(SUM_ROWS)]
    sums += [pltpu.VMEM((4, rows, width) if n in LONG_SUMS else (1, 1, 128), F32) for n, (rows, width) in enumerate(SUM_ROWS)]
    rest = [pltpu.SemaphoreType.DMA((320,)), pltpu.SemaphoreType.DMA((T.total,)), pltpu.SemaphoreType.DMA((28,)),
            pltpu.SemaphoreType.REGULAR((1,))]
    groups = [taken, weights, given, made, whole, partial, fin, third, list(kept.values()), norms, sums, rest]
    anywhere = pl.BlockSpec(memory_space=pl.ANY)
    got = pl.pallas_call(
        functools.partial(fused_kernel, [len(group) for group in groups], list(kept)),
        out_shape=given + made,
        in_specs=[anywhere] * (len(taken) + len(weights)),
        out_specs=[anywhere] * (len(given) + len(made)),
        scratch_shapes=[v for group in groups[4:] for v in group],
        compiler_params=pltpu.CompilerParams(collective_id=0, has_side_effects=True, vmem_limit_bytes=63 * 2**20),
    )(*taken, *weights)
    act, gimg, norms, *grads = got
    finished = pl.pallas_call(
        functools.partial(finish_kernel, (local_a, local_b)),
        out_shape=[act, gimg] + [jax.ShapeDtypeStruct(v.shape, F32) for v in grads]
        + [jax.ShapeDtypeStruct((size,), F32) for size in (local_a, local_a, local_b, local_b)],
        in_specs=[anywhere] * 10,
        out_specs=[anywhere] * 13,
        scratch_shapes=[pltpu.VMEM(v.shape, BF16) for v in grads] + [pltpu.VMEM(v.shape, F32) for v in grads]
        + [pltpu.VMEM(norms.shape, F32)] + [pltpu.VMEM((1, size), F32) for size in (local_a, local_a, local_b, local_b)]
        + [pltpu.VMEM(act.shape, BF16), pltpu.VMEM(gimg.shape, BF16), pltpu.SemaphoreType.DMA((10,)), pltpu.SemaphoreType.DMA((13,))],
        compiler_params=pltpu.CompilerParams(vmem_limit_bytes=60 * 2**20),
    )(act, gimg, norms, *grads)
    act, gimg = finished[:2]
    grads = [v.reshape(like.shape) for v, like in zip(
        finished[2:9], (reduce_one, spatial_one, expand_one, project_one, reduce_two, spatial_two, expand_two))]
    norm_grads = finished[9:]
    return (
        act.reshape(cotangent.shape),
        gimg.reshape(images.shape),
        grads[0], grads[1], grads[2], grads[3], norm_grads[0], norm_grads[1],
        grads[4], grads[5], grads[6], norm_grads[2], norm_grads[3],
    )


def solution(mesh):
    fused = mesh.shape["dp"] == 4 and mesh.shape["wide"] == 8
    in_specs = (
        P(("dp", "wide"), None, None, None),
        P(("dp", "wide"), None, None),
        P(("dp", "wide"), None, None, None),
        P("wide", None),
        P(None, None, "wide", None),
        P("wide", None),
        P("wide", None),
        P("wide"),
        P("wide"),
        P("wide", None),
        P(None, None, "wide", None),
        P("wide", None),
        P("wide"),
        P("wide"),
    )
    out_specs = (
        P(("dp", "wide"), None, None, None),
        P(("dp", "wide"), None, None, None),
        P("wide", None),
        P(None, None, "wide", None),
        P("wide", None),
        P("wide", None),
        P("wide"),
        P("wide"),
        P("wide", None),
        P(None, None, "wide", None),
        P("wide", None),
        P("wide"),
        P("wide"),
    )
    return jax.shard_map(fused_shards if fused else shards, mesh=mesh, in_specs=in_specs, out_specs=out_specs, check_vma=False)
```
